32 devices in a mesh: rows: 8 (over z, core), cols: 4 (over y, x).
Axes of the slice: x: 2, y: 2, z: 4, core: 2. Of those that a mesh axis runs over, the one named last changes fastest.
Arguments:
- slm_field: float32 [2, 2048, 1024], P(None, 'rows', 'cols'), may hold values from -6 to 6
- target_light: float32 [16, 8, 256], P('rows', 'cols'), may hold values from 0 to 0.5
Outputs:
- gradient: float32 [2, 2048, 1024], P(None, 'rows', 'cols')
- light_field: float32 [16, 8, 256], P('rows', 'cols')
The draws below stay inside these ranges and needn't reach their ends.
All inputs are finite; a program needn't handle non-finite values.
Results may differ from the reference program's by a relative error of at most 0.012.
Values may be sent and summed in bfloat16 or wider, within the bound.
No kernel may reach another device: no remote copies, remote signals or barrier semaphores. Data moves between devices by JAX's collectives and lax.ppermute only.
A program may use at most 64 MiB of HBM per device.

```python
import math
import jax
import jax.numpy as jnp
from jax import lax

WIN = 256
VIEWS = 16
STRIDE = 128
BIN = 16
FIELD_ROWS = 2048
FIELD_COLS = 1024
HOGEL_ROWS = 16
HOGEL_COLS = 8


def levels(key, dims, split, smallest, high):
    loudness, own = 1.0, jax.random.fold_in(key, 6)
    for dim, shards_of in split:
        draws = jnp.exp(jax.random.uniform(jax.random.fold_in(own, dim), (shards_of,), jnp.float32, smallest / len(split), high / len(split)))
        loudness = loudness * jnp.repeat(draws, dims[dim] // shards_of).reshape([-1 if axis == dim else 1 for axis in range(len(dims))])
    return loudness


def normal_values(key, shape, deviation, bound, shards=(), held_as=jnp.bfloat16):
    level = levels(key, shape, shards, -0.22, 0.18) if shards else 1.0
    drawn = jax.random.normal(key, shape, jnp.float32) * deviation * level
    return jnp.minimum(jnp.maximum(drawn, -bound), bound).astype(held_as)


def setup_inputs(seed: int = 0) -> dict:
    arg_keys = jax.random.split(jax.random.key(seed), 3)
    return {
        "slm_field": normal_values(arg_keys[0], (2, FIELD_ROWS, FIELD_COLS), 1.0, 6.0, ((1, 8), (2, 4)), jnp.float32),
        "target_light": jnp.clip(0.5 * jax.random.uniform(arg_keys[1], (HOGEL_ROWS, HOGEL_COLS, VIEWS * VIEWS), jnp.float32) ** levels(arg_keys[1], (HOGEL_ROWS, HOGEL_COLS, VIEWS * VIEWS), ((0, 8), (1, 4)), -0.2, 0.2), 0.0, 0.5),
    }


distance_px = 16000.0
index_ratio = 15.0

def freq_of(positions, count):
    return ((positions + count // 2) % count - count // 2).astype(jnp.float32) / count

def phase_of(freq_rows, freq_cols):
    radial = freq_rows * freq_rows + freq_cols * freq_cols
    return -2.0 * math.pi * distance_px * radial / (jnp.sqrt(index_ratio * index_ratio - radial) + index_ratio)

def hogel_tables():
    positions = jnp.arange(WIN, dtype=jnp.int32)
    tapers = jnp.sin(math.pi * (positions.astype(jnp.float32) + 0.5) / WIN) ** 2
    angles = -2.0 * math.pi / WIN * (positions[:, None] * positions[None, :] % WIN).astype(jnp.float32)
    cosine = tapers[:, None] * jnp.cos(angles)
    sine_part = tapers[:, None] * jnp.sin(angles)
    return (cosine.astype(jnp.bfloat16), sine_part.astype(jnp.bfloat16), (cosine / WIN).astype(jnp.bfloat16), (sine_part / WIN).astype(jnp.bfloat16))

def complex_product(pattern, left_re, left_im, right_re, right_im):

    def multiply(first, second):
        return jnp.einsum(pattern, first.astype(jnp.float32), second.astype(jnp.float32), precision=lax.Precision.HIGHEST)
    return (multiply(left_re, right_re) - multiply(left_im, right_im), multiply(left_re, right_im) + multiply(left_im, right_re))

def propagate(values, phase_sign):
    spectrum = jnp.fft.fft2(lax.complex(values[0], values[1]))
    freq_rows = freq_of(jnp.arange(FIELD_ROWS, dtype=jnp.int32), FIELD_ROWS)[:, None]
    freq_cols = freq_of(jnp.arange(FIELD_COLS, dtype=jnp.int32), FIELD_COLS)[None, :]
    phase = phase_of(freq_rows, freq_cols)
    kernel = lax.complex(jnp.cos(phase), phase_sign * jnp.sin(phase))
    result = jnp.fft.ifft2(spectrum * kernel)
    return jnp.stack([jnp.real(result), jnp.imag(result)])

def inner_forward(padded, col_re, col_im):
    count = padded.shape[1]
    hogels = padded.shape[2] // STRIDE - 1
    halves = padded.reshape(2, count, hogels + 1, STRIDE)
    windows = jnp.concatenate([halves[:, :, :-1], halves[:, :, 1:]], axis=3)
    lines_re, lines_im = complex_product('xjc,cq->xjq', windows[0], windows[1], col_re, col_im)
    return jnp.stack([lines_re, lines_im]).astype(jnp.bfloat16)

def hogel_step(window_rows, goal_rows, row_re, row_im):
    hogels = window_rows.shape[2]
    spec_re, spec_im = complex_product('rp,rjq->jpq', row_re, row_im, window_rows[0], window_rows[1])
    power = spec_re * spec_re + spec_im * spec_im
    light_row = power.reshape(hogels, VIEWS, BIN, VIEWS, BIN).sum(axis=(2, 4)) / (BIN * BIN)
    weights = 4.0 * (light_row - goal_rows.reshape(hogels, VIEWS, VIEWS))
    spread = jnp.broadcast_to(weights[:, :, None, :, None], (hogels, VIEWS, BIN, VIEWS, BIN)).reshape(hogels, WIN, WIN)
    weighted_re = (spread * spec_re).astype(jnp.bfloat16)
    weighted_im = (spread * spec_im).astype(jnp.bfloat16)
    back_re, back_im = complex_product('rp,jpq->rjq', row_re, -row_im, weighted_re, weighted_im)
    return (light_row.reshape(hogels, VIEWS * VIEWS), back_re, back_im)

def inner_adjoint(block, col_re, col_im):
    spread_re, spread_im = complex_product('xjq,cq->xjc', block[0], block[1], col_re, -col_im)
    spread = jnp.stack([spread_re, spread_im])
    first_half = spread[..., :STRIDE]
    second_half = spread[..., STRIDE:]
    joined = first_half + jnp.roll(second_half, 1, axis=2)
    return joined.reshape(2, block.shape[1], -1)

def reference(slm_field, target_light):
    col_re, col_im, row_re, row_im = hogel_tables()
    near_field = propagate(slm_field, 1.0).astype(jnp.bfloat16)
    padded = jnp.concatenate([near_field, near_field[:, :, :STRIDE]], axis=2)
    bands = padded.reshape(2, HOGEL_ROWS, STRIDE, FIELD_COLS + STRIDE).transpose(1, 0, 2, 3)
    spectra = lax.map(lambda band_data: inner_forward(band_data, col_re, col_im), bands)

    def hogel_row(pending, position):
        upper = lax.dynamic_index_in_dim(spectra, position, 0, keepdims=False)
        lower = lax.dynamic_index_in_dim(spectra, (position + 1) % HOGEL_ROWS, 0, keepdims=False)
        window_rows = jnp.concatenate([upper, lower], axis=1)
        goal_rows = lax.dynamic_index_in_dim(target_light, position, 0, keepdims=False)
        light_row, back_re, back_im = hogel_step(window_rows, goal_rows, row_re, row_im)
        returned = jnp.stack([back_re, back_im])
        return (returned[:, STRIDE:], (light_row, returned[:, :STRIDE] + pending))
    start = jnp.zeros((2, STRIDE, HOGEL_COLS, WIN), jnp.float32)
    last, (lights, blocks) = lax.scan(hogel_row, start, jnp.arange(HOGEL_ROWS, dtype=jnp.int32))
    blocks = blocks.at[0].add(last)
    back_lines = blocks.astype(jnp.bfloat16)
    rows_back = lax.map(lambda block: inner_adjoint(block, col_re, col_im), back_lines)
    back_near = rows_back.transpose(1, 0, 2, 3).reshape(2, FIELD_ROWS, FIELD_COLS)
    gradient = propagate(back_near, -1.0)
    return (gradient, lights)
```

```python
import math

import jax
import jax.numpy as jnp
import ml_dtypes
import numpy as np
from jax import lax
from jax.experimental import pallas as pl
from jax.experimental.pallas import tpu as pltpu
from jax.sharding import PartitionSpec as P

WIN = 256
VIEWS = 16
STRIDE = 128
BIN = 16

distance_px = 16000.0
index_ratio = 15.0

BF16 = jnp.bfloat16
F32 = jnp.float32
BOTH_MINOR = (((1,), (1,)), ((), ()))


def call(body, outs, args, scratch=(), flops=0):
    nbytes = sum(math.prod(a.shape) * a.dtype.itemsize for a in (*outs, *args))
    return pl.pallas_call(
        body,
        out_shape=outs,
        scratch_shapes=list(scratch),
        compiler_params=pltpu.CompilerParams(vmem_limit_bytes=24 * 2**20),
        cost_estimate=pl.CostEstimate(flops=flops, bytes_accessed=nbytes, transcendentals=0),
    )(*args)


def shape_of(dims, dtype):
    return jax.ShapeDtypeStruct(dims, dtype)


def high_low(table):
    table = np.asarray(table, np.float32)
    high = table.astype(ml_dtypes.bfloat16)
    low = (table - high.astype(np.float32)).astype(ml_dtypes.bfloat16)
    return np.stack([high, low])


def split(values):
    high = values.astype(BF16)
    return high, (values - high.astype(F32)).astype(BF16)


def times_i(values):
    half = values.shape[-1] // 2
    if values.shape[-1] == 128:
        lanes = lax.broadcasted_iota(jnp.int32, values.shape, values.ndim - 1)
        turned = pltpu.roll(values, half, values.ndim - 1)
        return jnp.where(lanes < half, -turned, turned)
    return jnp.concatenate([-values[..., half:], values[..., :half]], axis=-1)


def scaled(value, factor):
    return value if factor == 1.0 else value * factor


def small_dft(points, sign):
    count = len(points)
    if count == 1:
        return points
    even = small_dft(points[0::2], sign)
    odd = small_dft(points[1::2], sign)
    front, back = [], []
    for k in range(count // 2):
        re, im = odd[k]
        angle = sign * 2.0 * math.pi * k / count
        cosine, sine = math.cos(angle), math.sin(angle)
        if k == 0:
            pass
        elif 4 * k == count:
            re, im = (-im, re) if sign > 0 else (im, -re)
        elif 8 * k == count:
            re, im = cosine * (re - sign * im), cosine * (im + sign * re)
        elif 8 * k == 3 * count:
            re, im = cosine * (re + sign * im), cosine * (im - sign * re)
        else:
            re, im = re * cosine - im * sine, re * sine + im * cosine
        even_re, even_im = even[k]
        front.append((even_re + re, even_im + im))
        back.append((even_re - re, even_im - im))
    return front + back


def packed_dft(points, sign):
    count = len(points)
    if count == 1:
        return points
    even = packed_dft(points[0::2], sign)
    odd = packed_dft(points[1::2], sign)
    front, back = [], []
    for k in range(count // 2):
        term = odd[k]
        angle = sign * 2.0 * math.pi * k / count
        if 4 * k == count:
            term = times_i(term) if sign > 0 else -times_i(term)
        elif k:
            term = math.cos(angle) * term + math.sin(angle) * times_i(term)
        front.append(even[k] + term)
        back.append(even[k] - term)
    return front + back


def turn(rows, cols, period, sign):
    angles = sign * 2.0 * np.pi / period * ((np.arange(rows)[:, None] * np.arange(cols)) % period)
    return np.cos(angles), np.sin(angles)


def block_diagonal(block, copies):
    return np.kron(np.eye(copies), block)


class Plan:
    def __init__(self, rows_count, cols_count, rows_dev, cols_dev):
        self.R, self.C = rows_count, cols_count
        self.D = rows_count * cols_count
        self.X = cols_dev
        self.m = rows_dev // cols_count
        self.lanes = 2 * self.m
        self.P = 128 // self.m
        self.span = cols_dev // rows_count
        self.f = self.span // self.P
        self.total_rows = rows_dev * rows_count
        self.total_cols = cols_dev * cols_count
        self.outer = 8
        self.inner = self.D // 8

    def line_tables(self, sign):
        cosine, sine = turn(self.X, self.X, self.X, sign)
        weights = high_low(np.concatenate([cosine, sine], axis=1))
        twist = turn(self.X, self.C, self.total_cols, sign)
        return weights, np.concatenate(twist, axis=1).astype(np.float32)

    def pencil_tables(self):
        cosine, sine = turn(self.m, self.m, self.m, -1.0)
        cosine, sine = block_diagonal(cosine, self.P), block_diagonal(sine, self.P)
        ahead = np.block([[cosine, sine], [-sine, cosine]])
        behind = np.block([[cosine, -sine], [sine, cosine]]) / (self.total_rows * self.total_cols)
        twist = turn(self.D, self.m, self.total_rows, -1.0)
        twist = np.stack([np.tile(part, (1, self.P)) for part in twist]).astype(np.float32)
        return high_low(ahead), high_low(behind), twist


def hogel_tables():
    positions = np.arange(WIN)
    tapers = np.sin(np.pi * (positions + 0.5) / WIN) ** 2
    angles = -2.0 * np.pi / WIN * (positions[:, None] * positions[None, :] % WIN)
    cosine = (tapers[:, None] * np.cos(angles)).astype(np.float32)
    sine = (tapers[:, None] * np.sin(angles)).astype(np.float32)
    col = cosine.astype(ml_dtypes.bfloat16), sine.astype(ml_dtypes.bfloat16)
    row = (cosine / WIN).astype(ml_dtypes.bfloat16), (sine / WIN).astype(ml_dtypes.bfloat16)
    return col, row


def pack_kernel(plan, field, out):
    m = plan.m
    for c in range(plan.C):
        block = jnp.concatenate(
            [field[0, m * c : m * c + m, :], field[1, m * c : m * c + m, :]], axis=0
        )
        out[c] = block.T.astype(BF16)


def unpack_kernel(plan, slabs, out):
    m = plan.m
    for c in range(plan.C):
        block = slabs[c].astype(F32).T
        out[0, m * c : m * c + m, :] = block[:m]
        out[1, m * c : m * c + m, :] = block[m:]


def rows_forward_kernel(plan, halo, slabs, weights, twist, out, high, low):
    C, X, lanes = plan.C, plan.X, plan.lanes
    step = 64
    for start in range(0, X, step):
        points = []
        for c in range(C):
            point = slabs[c, start : start + step, :].astype(F32)
            if halo and start < halo:
                beside = slabs[(c - 1) % C, X + start : X + start + step, :]
                point = point + beside.astype(F32)
            points.append(point)
        points = packed_dft(points, -1.0)
        for k in range(C):
            cosine = twist[start : start + step, k : k + 1]
            sine = twist[start : start + step, C + k : C + k + 1]
            across = times_i(points[k])
            if k:
                value = points[k] * cosine + across * sine
                across = across * cosine - points[k] * sine
            else:
                value = points[k]
            place = slice(k * lanes, k * lanes + lanes)
            for offset, part in ((0, value), (X, across)):
                part_high, part_low = split(part)
                high[offset + start : offset + start + step, place] = part_high
                low[offset + start : offset + start + step, place] = part_low
    first, second = high[...], low[...]
    for r in range(plan.R):
        place = slice(r * plan.span, (r + 1) * plan.span)
        result = (
            jnp.dot(weights[0, place, :], first, preferred_element_type=F32)
            + jnp.dot(weights[0, place, :], second, preferred_element_type=F32)
            + jnp.dot(weights[1, place, :], first, preferred_element_type=F32)
        )
        for k in range(C):
            parts = [
                result[p * plan.f : (p + 1) * plan.f, k * lanes : (k + 1) * lanes]
                for p in range(plan.P)
            ]
            real = jnp.concatenate([part[:, : plan.m] for part in parts], axis=1)
            imag = jnp.concatenate([part[:, plan.m :] for part in parts], axis=1)
            out[k * plan.R + r] = jnp.concatenate([real, imag], axis=0).astype(BF16)


def rows_inverse_kernel(plan, halo, pencils, weights, twist, out, packed):
    C, X, lanes, m = plan.C, plan.X, plan.lanes, plan.m
    for k in range(C):
        for r in range(plan.R):
            chunk = pencils[k * plan.R + r].astype(F32)
            real, imag = chunk[: plan.f], chunk[plan.f :]
            block = jnp.concatenate(
                [
                    jnp.concatenate([real[:, p * m : (p + 1) * m], imag[:, p * m : (p + 1) * m]], axis=1)
                    for p in range(plan.P)
                ],
                axis=0,
            )
            place = slice(k * lanes, k * lanes + lanes)
            packed[r * plan.span : (r + 1) * plan.span, place] = block.astype(BF16)
            packed[X + r * plan.span : X + (r + 1) * plan.span, place] = times_i(block).astype(BF16)
    first = packed[...]
    step = 64
    for start in range(0, X, step):
        result = jnp.dot(
            weights[0, start : start + step, :], first, preferred_element_type=F32
        ) + jnp.dot(weights[1, start : start + step, :], first, preferred_element_type=F32)
        points = []
        for k in range(C):
            value = result[:, k * lanes : (k + 1) * lanes]
            if k:
                cosine = twist[start : start + step, k : k + 1]
                sine = twist[start : start + step, C + k : C + k + 1]
                value = value * cosine + times_i(value) * sine
            points.append(value)
        points = packed_dft(points, 1.0)
        for c in range(C):
            rounded = points[c].astype(BF16)
            out[c, start : start + step, :] = rounded
            if halo and start < halo:
                out[(c - 1) % C, X + start : X + start + step, :] = rounded


def columns_kernel(plan, sign, pencils, steer_re, steer_im, ahead, behind, twist, out, *scratch):
    D, f, outer, inner = plan.D, plan.f, plan.outer, plan.inner
    half_re, half_im, high, low = scratch
    for b in range(inner):
        points = []
        for a in range(outer):
            chunk = pencils[inner * a + b].astype(F32)
            points.append((chunk[:f], chunk[f:]))
        for alpha, (re, im) in enumerate(small_dft(points, -1.0)):
            angle = -2.0 * math.pi * b * alpha / D
            cosine, sine = math.cos(angle), math.sin(angle)
            if b * alpha:
                re, im = re * cosine - im * sine, re * sine + im * cosine
            half_re[alpha * inner + b] = re
            half_im[alpha * inner + b] = im
    for alpha in range(outer):
        points = [(half_re[alpha * inner + b], half_im[alpha * inner + b]) for b in range(inner)]
        for beta, (re, im) in enumerate(small_dft(points, -1.0)):
            k = alpha + outer * beta
            cosine, sine = twist[0, k : k + 1, :], twist[1, k : k + 1, :]
            for offset, part in ((0, re * cosine - im * sine), (128, re * sine + im * cosine)):
                part_high, part_low = split(part)
                high[k, :, offset : offset + 128] = part_high
                low[k, :, offset : offset + 128] = part_low
    group = D // 4
    for start in range(0, D, group):
        place = slice(start, start + group)

        def multiply(matrix):
            first = high[place].reshape(group * f, 256)
            second = low[place].reshape(group * f, 256)
            return (
                jnp.dot(first, matrix[0], preferred_element_type=F32)
                + jnp.dot(second, matrix[0], preferred_element_type=F32)
                + jnp.dot(first, matrix[1], preferred_element_type=F32)
            ).reshape(group, f, 256)

        result = multiply(ahead)
        re, im = result[:, :, :128], result[:, :, 128:]
        factor_re, factor_im = steer_re[place], sign * steer_im[place]
        for offset, part in (
            (0, re * factor_re - im * factor_im),
            (128, re * factor_im + im * factor_re),
        ):
            part_high, part_low = split(part)
            high[place, :, offset : offset + 128] = part_high
            low[place, :, offset : offset + 128] = part_low
        result = multiply(behind)
        half_re[place] = result[:, :, :128]
        half_im[place] = result[:, :, 128:]
    for alpha in range(outer):
        points = []
        for beta in range(inner):
            k = alpha + outer * beta
            cosine, sine = twist[0, k : k + 1, :], twist[1, k : k + 1, :]
            re, im = half_re[k], half_im[k]
            points.append((re * cosine + im * sine, im * cosine - re * sine))
        for b, (re, im) in enumerate(small_dft(points, 1.0)):
            angle = 2.0 * math.pi * b * alpha / D
            cosine, sine = math.cos(angle), math.sin(angle)
            if b * alpha:
                re, im = re * cosine - im * sine, re * sine + im * cosine
            half_re[alpha + outer * b] = re
            half_im[alpha + outer * b] = im
    for b in range(inner):
        points = [(half_re[alpha + outer * b], half_im[alpha + outer * b]) for alpha in range(outer)]
        for a, (re, im) in enumerate(small_dft(points, 1.0)):
            out[inner * a + b] = jnp.concatenate([re, im], axis=0).astype(BF16)


def hogel_kernel(plan, near, rim, goal, col, row, picks, spreads, lights, own, spill, *scratch):
    C, X, lanes = plan.C, plan.X, plan.lanes
    field, lines, spectra, bright, weights = scratch
    rims = rim.shape[0]
    width = C * lanes
    chunks = [near[c] for c in range(C)] + [rim[c] for c in range(rims)]
    for index, chunk in enumerate(chunks):
        place = slice(index * lanes, (index + 1) * lanes)
        field[0, :, place] = chunk
        field[1, :, place] = times_i(chunk.astype(F32)).astype(BF16)
    hogel_cols = X // STRIDE
    hogel_rows = 2
    for j in range(hogel_cols):
        window = slice(STRIDE * j, STRIDE * j + WIN)
        lines[j] = (
            lax.dot_general(
                col[0], field[0, window, :], (((0,), (0,)), ((), ())), preferred_element_type=F32
            )
            + lax.dot_general(
                col[1], field[1, window, :], (((0,), (0,)), ((), ())), preferred_element_type=F32
            )
        ).astype(BF16)
    shift = STRIDE // plan.m * lanes
    for i in range(hogel_rows):
        for j in range(hogel_cols):
            h = i * hogel_cols + j
            result = jnp.dot(
                lines[j, :, i * shift : i * shift + width], row[...], preferred_element_type=F32
            )
            spectra[h] = result
            power = result[:, :WIN] * result[:, :WIN] + result[:, WIN:] * result[:, WIN:]
            bright[h * VIEWS : (h + 1) * VIEWS, :] = power.reshape(VIEWS, BIN, WIN).sum(axis=1)
    light = jnp.dot(
        bright[...], picks[...], preferred_element_type=F32, precision=lax.Precision.HIGHEST
    )
    lights[...] = light
    weights[...] = jnp.dot(
        4.0 * (light - goal[...]),
        spreads[...],
        preferred_element_type=F32,
        precision=lax.Precision.HIGHEST,
    )
    for j in range(hogel_cols):
        backs = []
        for i in range(hogel_rows):
            h = i * hogel_cols + j
            blocks = []
            for view in range(VIEWS):
                factor = weights[h * VIEWS + view : h * VIEWS + view + 1, :]
                factor = jnp.concatenate([factor, factor], axis=1)
                blocks.append(
                    (spectra[h, view * BIN : (view + 1) * BIN, :] * factor).astype(BF16)
                )
            backs.append(
                lax.dot_general(
                    jnp.concatenate(blocks, axis=0),
                    row[...],
                    BOTH_MINOR,
                    preferred_element_type=F32,
                )
            )
        own[j, :, :shift] = backs[0][:, :shift]
        own[j, :, shift:] = backs[0][:, shift:] + backs[1][:, : width - shift]
        spill[j] = backs[1][:, width - shift :].astype(BF16)


def adjoint_kernel(plan, own, spill, col, out, *scratch):
    C, X, lanes = plan.C, plan.X, plan.lanes
    (pair,) = scratch
    shift = STRIDE // plan.m * lanes
    hogel_cols = X // STRIDE
    pending = None
    for j in range(hogel_cols):
        for c in range(C):
            place = slice(c * lanes, (c + 1) * lanes)
            value = own[j, :, place]
            if c * lanes < shift:
                value = value + spill[j, :, place].astype(F32)
            value = value.astype(BF16)
            pair[0, :, place] = value
            pair[1, :, place] = (-times_i(value.astype(F32))).astype(BF16)
        result = jnp.dot(col[0], pair[0], preferred_element_type=F32) + jnp.dot(
            col[1], pair[1], preferred_element_type=F32
        )
        lead = result[:STRIDE]
        if pending is not None:
            lead = lead + pending
        pending = result[STRIDE:]
        for c in range(C):
            out[c, STRIDE * j : STRIDE * (j + 1), :] = lead[:, c * lanes : (c + 1) * lanes].astype(BF16)
    for c in range(C):
        out[c, X:, :] = pending[:, c * lanes : (c + 1) * lanes].astype(BF16)


def steer_table(plan):
    index = lax.axis_index(("rows", "cols"))
    shape = (plan.D, plan.f, 128)
    k = lax.broadcasted_iota(jnp.int32, shape, 0)
    line = lax.broadcasted_iota(jnp.int32, shape, 1)
    lane = lax.broadcasted_iota(jnp.int32, shape, 2)
    u = k + plan.D * (lane % plan.m)
    v = index // plan.R + plan.C * (
        plan.span * (index % plan.R) + plan.f * (lane // plan.m) + line
    )

    def freq(position, count):
        return ((position + count // 2) % count - count // 2).astype(F32) / count

    freq_rows, freq_cols = freq(u, plan.total_rows), freq(v, plan.total_cols)
    radial = freq_rows * freq_rows + freq_cols * freq_cols
    phase = (
        -2.0
        * math.pi
        * distance_px
        * radial
        / (jnp.sqrt(index_ratio * index_ratio - radial) + index_ratio)
    )
    return jnp.cos(phase), jnp.sin(phase)


def exchange(chunks, axes):
    return lax.all_to_all(chunks, axes, split_axis=0, concat_axis=0, tiled=True)


def shifted(block, axis, distance):
    count = lax.axis_size(axis)
    return lax.ppermute(block, axis, [((i - distance) % count, i) for i in range(count)])


def local(slm_field, target_light):
    rows_count, cols_count = lax.axis_size("rows"), lax.axis_size("cols")
    plan = Plan(rows_count, cols_count, slm_field.shape[1], slm_field.shape[2])
    R, C, D, X, lanes, f = plan.R, plan.C, plan.D, plan.X, plan.lanes, plan.f
    whole = ("rows", "cols")

    ahead, behind, twist = (jnp.asarray(t) for t in plan.pencil_tables())
    weights_ahead, twist_ahead = (jnp.asarray(t) for t in plan.line_tables(-1.0))
    weights_behind, twist_behind = (jnp.asarray(t) for t in plan.line_tables(1.0))
    (col_re, col_im), (row_re, row_im) = hogel_tables()
    col = jnp.asarray(np.stack([col_re, col_im]))
    slabs_in_window = WIN // plan.m
    row_blocks = [
        np.concatenate(
            [
                np.concatenate([row_re[part], row_im[part]], axis=1),
                np.concatenate([-row_im[part], row_re[part]], axis=1),
            ],
            axis=0,
        )
        for part in (slice(s * plan.m, (s + 1) * plan.m) for s in range(slabs_in_window))
    ]
    row = jnp.asarray(np.concatenate(row_blocks, axis=0))
    groups = np.kron(np.eye(VIEWS), np.ones((BIN, 1))).astype(np.float32)
    picks, spreads = jnp.asarray(groups / (BIN * BIN)), jnp.asarray(groups.T.copy())

    steer_re, steer_im = steer_table(plan)
    pencil_shape = shape_of((D, 2 * f, 128), BF16)
    tall = pltpu.VMEM((2 * X, C * lanes), BF16)

    def forward_rows(slabs, halo):
        return call(
            lambda *refs: rows_forward_kernel(plan, halo, *refs),
            (pencil_shape,),
            (slabs, weights_ahead, twist_ahead),
            (tall, tall),
            flops=6 * X * 2 * X * C * lanes,
        )[0]

    def inverse_rows(pencils, halo):
        return call(
            lambda *refs: rows_inverse_kernel(plan, halo, *refs),
            (shape_of((C, X + halo, lanes), BF16),),
            (pencils, weights_behind, twist_behind),
            (tall,),
            flops=4 * X * 2 * X * C * lanes,
        )[0]

    def columns(pencils, sign):
        return call(
            lambda *refs: columns_kernel(plan, sign, *refs),
            (pencil_shape,),
            (pencils, steer_re, steer_im, ahead, behind, twist),
            (
                pltpu.VMEM((D, f, 128), F32),
                pltpu.VMEM((D, f, 128), F32),
                pltpu.VMEM((D, f, 256), BF16),
                pltpu.VMEM((D, f, 256), BF16),
            ),
            flops=12 * D * f * 256 * 256,
        )[0]

    def travel(slabs, sign, halo_in, halo_out):
        pencils = exchange(forward_rows(slabs, halo_in), whole)
        pencils = exchange(columns(pencils, sign), whole)
        return inverse_rows(pencils, halo_out)

    slabs = call(
        lambda *refs: pack_kernel(plan, *refs), (shape_of((C, X, lanes), BF16),), (slm_field,)
    )[0]
    near = travel(exchange(slabs, "cols"), 1.0, 0, STRIDE)
    near = exchange(near, "cols")
    rims = STRIDE // plan.m
    rim = shifted(near[:rims], "rows", -1)

    hogel_rows, hogel_cols = target_light.shape[:2]
    hogels = hogel_rows * hogel_cols
    goal = target_light.reshape(hogels, VIEWS, VIEWS).swapaxes(1, 2).reshape(hogels * VIEWS, VIEWS)
    breadth = (C + rims) * lanes
    lights, own, spill = call(
        lambda *refs: hogel_kernel(plan, *refs),
        (
            shape_of((hogels * VIEWS, VIEWS), F32),
            shape_of((hogel_cols, WIN, C * lanes), F32),
            shape_of((hogel_cols, WIN, rims * lanes), BF16),
        ),
        (near, rim, goal, col, row, picks, spreads),
        (
            pltpu.VMEM((2, X + STRIDE, breadth), BF16),
            pltpu.VMEM((hogel_cols, WIN, breadth), BF16),
            pltpu.VMEM((hogels, WIN, 2 * WIN), F32),
            pltpu.VMEM((hogels * VIEWS, WIN), F32),
            pltpu.VMEM((hogels * VIEWS, WIN), F32),
        ),
        flops=2 * hogels * 4 * WIN**3 * 2 + 2 * hogel_cols * WIN * 2 * WIN * breadth,
    )
    spill = shifted(spill, "rows", 1)
    slabs = call(
        lambda *refs: adjoint_kernel(plan, *refs),
        (shape_of((C, X + STRIDE, lanes), BF16),),
        (own, spill, col),
        (pltpu.VMEM((2, WIN, C * lanes), BF16),),
        flops=2 * hogel_cols * WIN * 2 * WIN * C * lanes,
    )[0]
    slabs = travel(exchange(slabs, "cols"), -1.0, STRIDE, 0)
    gradient = call(
        lambda *refs: unpack_kernel(plan, *refs),
        (shape_of(slm_field.shape, F32),),
        (exchange(slabs, "cols"),),
    )[0]
    light_field = lights.reshape(hogels, VIEWS, VIEWS).swapaxes(1, 2).reshape(target_light.shape)
    return gradient, light_field


def solution(mesh):
    return jax.shard_map(
        local,
        mesh=mesh,
        in_specs=(P(None, "rows", "cols"), P("rows", "cols", None)),
        out_specs=(P(None, "rows", "cols"), P("rows", "cols", None)),
        check_vma=False,
    )
```

```python
import math

import jax
import jax.numpy as jnp
import ml_dtypes
import numpy as np
from jax import lax
from jax.experimental import pallas as pl
from jax.experimental.pallas import tpu as pltpu
from jax.sharding import PartitionSpec as P

WIN = 256
VIEWS = 16
STRIDE = 128
BIN = 16

distance_px = 16000.0
index_ratio = 15.0

BF16 = jnp.bfloat16
F32 = jnp.float32
BOTH_MINOR = (((1,), (1,)), ((), ()))


def call(body, outs, args, scratch=(), flops=0):
    nbytes = sum(math.prod(a.shape) * a.dtype.itemsize for a in (*outs, *args))
    return pl.pallas_call(
        body,
        out_shape=outs,
        scratch_shapes=list(scratch),
        compiler_params=pltpu.CompilerParams(vmem_limit_bytes=24 * 2**20),
        cost_estimate=pl.CostEstimate(flops=flops, bytes_accessed=nbytes, transcendentals=0),
    )(*args)


def shape_of(dims, dtype):
    return jax.ShapeDtypeStruct(dims, dtype)


def high_low(table):
    table = np.asarray(table, np.float32)
    high = table.astype(ml_dtypes.bfloat16)
    low = (table - high.astype(np.float32)).astype(ml_dtypes.bfloat16)
    return np.stack([high, low])


def split(values):
    high = values.astype(BF16)
    return high, (values - high.astype(F32)).astype(BF16)


def times_i(values):
    half = values.shape[-1] // 2
    if values.shape[-1] == 128:
        lanes = lax.broadcasted_iota(jnp.int32, values.shape, values.ndim - 1)
        turned = pltpu.roll(values, half, values.ndim - 1)
        return jnp.where(lanes < half, -turned, turned)
    return jnp.concatenate([-values[..., half:], values[..., :half]], axis=-1)


def scaled(value, factor):
    return value if factor == 1.0 else value * factor


def small_dft(points, sign):
    count = len(points)
    if count == 1:
        return points
    even = small_dft(points[0::2], sign)
    odd = small_dft(points[1::2], sign)
    front, back = [], []
    for k in range(count // 2):
        re, im = odd[k]
        angle = sign * 2.0 * math.pi * k / count
        cosine, sine = math.cos(angle), math.sin(angle)
        if k == 0:
            pass
        elif 4 * k == count:
            re, im = (-im, re) if sign > 0 else (im, -re)
        elif 8 * k == count:
            re, im = cosine * (re - sign * im), cosine * (im + sign * re)
        elif 8 * k == 3 * count:
            re, im = cosine * (re + sign * im), cosine * (im - sign * re)
        else:
            re, im = re * cosine - im * sine, re * sine + im * cosine
        even_re, even_im = even[k]
        front.append((even_re + re, even_im + im))
        back.append((even_re - re, even_im - im))
    return front + back


def packed_dft(points, sign):
    count = len(points)
    if count == 1:
        return points
    even = packed_dft(points[0::2], sign)
    odd = packed_dft(points[1::2], sign)
    front, back = [], []
    for k in range(count // 2):
        term = odd[k]
        angle = sign * 2.0 * math.pi * k / count
        if 4 * k == count:
            term = times_i(term) if sign > 0 else -times_i(term)
        elif k:
            term = math.cos(angle) * term + math.sin(angle) * times_i(term)
        front.append(even[k] + term)
        back.append(even[k] - term)
    return front + back


def turn(rows, cols, period, sign):
    angles = sign * 2.0 * np.pi / period * ((np.arange(rows)[:, None] * np.arange(cols)) % period)
    return np.cos(angles), np.sin(angles)


def block_diagonal(block, copies):
    return np.kron(np.eye(copies), block)


class Plan:
    def __init__(self, rows_count, cols_count, rows_dev, cols_dev):
        self.R, self.C = rows_count, cols_count
        self.D = rows_count * cols_count
        self.X = cols_dev
        self.m = rows_dev // cols_count
        self.lanes = 2 * self.m
        self.P = 128 // self.m
        self.span = cols_dev // rows_count
        self.f = self.span // self.P
        self.total_rows = rows_dev * rows_count
        self.total_cols = cols_dev * cols_count
        self.outer = 8
        self.inner = self.D // 8

    def line_tables(self, sign):
        cosine, sine = turn(self.X, self.X, self.X, sign)
        weights = high_low(np.concatenate([cosine, sine], axis=1))
        twist = turn(self.X, self.C, self.total_cols, sign)
        return weights, np.concatenate(twist, axis=1).astype(np.float32)

    def pencil_tables(self):
        cosine, sine = turn(self.m, self.m, self.m, -1.0)
        cosine, sine = block_diagonal(cosine, self.P), block_diagonal(sine, self.P)
        ahead = np.block([[cosine, sine], [-sine, cosine]])
        behind = np.block([[cosine, -sine], [sine, cosine]]) / (self.total_rows * self.total_cols)
        twist = turn(self.D, self.m, self.total_rows, -1.0)
        twist = np.stack([np.tile(part, (1, self.P)) for part in twist]).astype(np.float32)
        return high_low(ahead), high_low(behind), twist


def hogel_tables():
    positions = np.arange(WIN)
    tapers = np.sin(np.pi * (positions + 0.5) / WIN) ** 2
    angles = -2.0 * np.pi / WIN * (positions[:, None] * positions[None, :] % WIN)
    cosine = (tapers[:, None] * np.cos(angles)).astype(np.float32)
    sine = (tapers[:, None] * np.sin(angles)).astype(np.float32)
    col = cosine.astype(ml_dtypes.bfloat16), sine.astype(ml_dtypes.bfloat16)
    row = (cosine / WIN).astype(ml_dtypes.bfloat16), (sine / WIN).astype(ml_dtypes.bfloat16)
    return col, row


def gather_chunks(arrived, chunks):
    mine = lax.axis_index("cols")
    for t, chunk in enumerate(arrived):
        chunks[mine ^ t] = chunk[...]


def scatter_chunks(chunks, leaving):
    mine = lax.axis_index("cols")
    for t, chunk in enumerate(leaving):
        chunk[...] = chunks[mine ^ t]


def pack_kernel(plan, field, *refs):
    m = plan.m
    leaving, out = refs[: plan.C], refs[plan.C]
    for c in range(plan.C):
        block = jnp.concatenate(
            [field[0, m * c : m * c + m, :], field[1, m * c : m * c + m, :]], axis=0
        )
        out[c] = block.T.astype(BF16)
    scatter_chunks(out, leaving)


def unpack_kernel(plan, *refs):
    m = plan.m
    arrived, (out, slabs) = refs[: plan.C], refs[plan.C :]
    gather_chunks(arrived, slabs)
    for c in range(plan.C):
        block = slabs[c].astype(F32).T
        out[0, m * c : m * c + m, :] = block[:m]
        out[1, m * c : m * c + m, :] = block[m:]


def rows_forward_kernel(plan, halo, *refs):
    C, X, lanes = plan.C, plan.X, plan.lanes
    arrived, (weights, twist, out, high, low, slabs) = refs[:C], refs[C:]
    gather_chunks(arrived, slabs)
    step = 64
    for start in range(0, X, step):
        points = []
        for c in range(C):
            point = slabs[c, start : start + step, :].astype(F32)
            if halo and start < halo:
                beside = slabs[(c - 1) % C, X + start : X + start + step, :]
                point = point + beside.astype(F32)
            points.append(point)
        points = packed_dft(points, -1.0)
        for k in range(C):
            cosine = twist[start : start + step, k : k + 1]
            sine = twist[start : start + step, C + k : C + k + 1]
            across = times_i(points[k])
            if k:
                value = points[k] * cosine + across * sine
                across = across * cosine - points[k] * sine
            else:
                value = points[k]
            place = slice(k * lanes, k * lanes + lanes)
            for offset, part in ((0, value), (X, across)):
                part_high, part_low = split(part)
                high[offset + start : offset + start + step, place] = part_high
                low[offset + start : offset + start + step, place] = part_low
    first, second = high[...], low[...]
    for r in range(plan.R):
        place = slice(r * plan.span, (r + 1) * plan.span)
        result = (
            jnp.dot(weights[0, place, :], first, preferred_element_type=F32)
            + jnp.dot(weights[0, place, :], second, preferred_element_type=F32)
            + jnp.dot(weights[1, place, :], first, preferred_element_type=F32)
        )
        for k in range(C):
            parts = [
                result[p * plan.f : (p + 1) * plan.f, k * lanes : (k + 1) * lanes]
                for p in range(plan.P)
            ]
            real = jnp.concatenate([part[:, : plan.m] for part in parts], axis=1)
            imag = jnp.concatenate([part[:, plan.m :] for part in parts], axis=1)
            out[k * plan.R + r] = jnp.concatenate([real, imag], axis=0).astype(BF16)


def rows_inverse_kernel(plan, halo, pencils, weights, twist, *refs):
    C, X, lanes, m = plan.C, plan.X, plan.lanes, plan.m
    leaving, (packed, out) = refs[:C], refs[C:]
    for k in range(C):
        for r in range(plan.R):
            chunk = pencils[k * plan.R + r].astype(F32)
            real, imag = chunk[: plan.f], chunk[plan.f :]
            block = jnp.concatenate(
                [
                    jnp.concatenate([real[:, p * m : (p + 1) * m], imag[:, p * m : (p + 1) * m]], axis=1)
                    for p in range(plan.P)
                ],
                axis=0,
            )
            place = slice(k * lanes, k * lanes + lanes)
            packed[r * plan.span : (r + 1) * plan.span, place] = block.astype(BF16)
            packed[X + r * plan.span : X + (r + 1) * plan.span, place] = times_i(block).astype(BF16)
    first = packed[...]
    step = 64
    for start in range(0, X, step):
        result = jnp.dot(
            weights[0, start : start + step, :], first, preferred_element_type=F32
        ) + jnp.dot(weights[1, start : start + step, :], first, preferred_element_type=F32)
        points = []
        for k in range(C):
            value = result[:, k * lanes : (k + 1) * lanes]
            if k:
                cosine = twist[start : start + step, k : k + 1]
                sine = twist[start : start + step, C + k : C + k + 1]
                value = value * cosine + times_i(value) * sine
            points.append(value)
        points = packed_dft(points, 1.0)
        for c in range(C):
            rounded = points[c].astype(BF16)
            out[c, start : start + step, :] = rounded
            if halo and start < halo:
                out[(c - 1) % C, X + start : X + start + step, :] = rounded
    scatter_chunks(out, leaving)


def columns_kernel(plan, sign, pencils, steer_re, steer_im, ahead, behind, twist, out, *scratch):
    D, f, outer, inner = plan.D, plan.f, plan.outer, plan.inner
    half_re, half_im, high, low = scratch
    for b in range(inner):
        points = []
        for a in range(outer):
            chunk = pencils[inner * a + b].astype(F32)
            points.append((chunk[:f], chunk[f:]))
        for alpha, (re, im) in enumerate(small_dft(points, -1.0)):
            angle = -2.0 * math.pi * b * alpha / D
            cosine, sine = math.cos(angle), math.sin(angle)
            if b * alpha:
                re, im = re * cosine - im * sine, re * sine + im * cosine
            half_re[alpha * inner + b] = re
            half_im[alpha * inner + b] = im
    for alpha in range(outer):
        points = [(half_re[alpha * inner + b], half_im[alpha * inner + b]) for b in range(inner)]
        for beta, (re, im) in enumerate(small_dft(points, -1.0)):
            k = alpha + outer * beta
            cosine, sine = twist[0, k : k + 1, :], twist[1, k : k + 1, :]
            for offset, part in ((0, re * cosine - im * sine), (128, re * sine + im * cosine)):
                part_high, part_low = split(part)
                high[k, :, offset : offset + 128] = part_high
                low[k, :, offset : offset + 128] = part_low
    group = D // 4
    for start in range(0, D, group):
        place = slice(start, start + group)

        def multiply(matrix):
            first = high[place].reshape(group * f, 256)
            second = low[place].reshape(group * f, 256)
            return (
                jnp.dot(first, matrix[0], preferred_element_type=F32)
                + jnp.dot(second, matrix[0], preferred_element_type=F32)
                + jnp.dot(first, matrix[1], preferred_element_type=F32)
            ).reshape(group, f, 256)

        result = multiply(ahead)
        re, im = result[:, :, :128], result[:, :, 128:]
        factor_re, factor_im = steer_re[place], sign * steer_im[place]
        for offset, part in (
            (0, re * factor_re - im * factor_im),
            (128, re * factor_im + im * factor_re),
        ):
            part_high, part_low = split(part)
            high[place, :, offset : offset + 128] = part_high
            low[place, :, offset : offset + 128] = part_low
        result = multiply(behind)
        half_re[place] = result[:, :, :128]
        half_im[place] = result[:, :, 128:]
    for alpha in range(outer):
        points = []
        for beta in range(inner):
            k = alpha + outer * beta
            cosine, sine = twist[0, k : k + 1, :], twist[1, k : k + 1, :]
            re, im = half_re[k], half_im[k]
            points.append((re * cosine + im * sine, im * cosine - re * sine))
        for b, (re, im) in enumerate(small_dft(points, 1.0)):
            angle = 2.0 * math.pi * b * alpha / D
            cosine, sine = math.cos(angle), math.sin(angle)
            if b * alpha:
                re, im = re * cosine - im * sine, re * sine + im * cosine
            half_re[alpha + outer * b] = re
            half_im[alpha + outer * b] = im
    for b in range(inner):
        points = [(half_re[alpha + outer * b], half_im[alpha + outer * b]) for alpha in range(outer)]
        for a, (re, im) in enumerate(small_dft(points, 1.0)):
            out[inner * a + b] = jnp.concatenate([re, im], axis=0).astype(BF16)


def hogel_kernel(plan, *refs):
    C, X, lanes = plan.C, plan.X, plan.lanes
    arrived, (rim, goal, col, row, picks, spreads, lights, own, spill, *scratch) = refs[:C], refs[C:]
    near, field, lines, spectra, bright, weights = scratch
    gather_chunks(arrived, near)
    rims = rim.shape[0]
    odd = lax.axis_index("cols") & (rims - 1)
    width = C * lanes
    chunks = [near[c] for c in range(C)] + [rim[odd ^ c] for c in range(rims)]
    for index, chunk in enumerate(chunks):
        place = slice(index * lanes, (index + 1) * lanes)
        field[0, :, place] = chunk
        field[1, :, place] = times_i(chunk.astype(F32)).astype(BF16)
    hogel_cols = X // STRIDE
    hogel_rows = 2
    for j in range(hogel_cols):
        window = slice(STRIDE * j, STRIDE * j + WIN)
        lines[j] = (
            lax.dot_general(
                col[0], field[0, window, :], (((0,), (0,)), ((), ())), preferred_element_type=F32
            )
            + lax.dot_general(
                col[1], field[1, window, :], (((0,), (0,)), ((), ())), preferred_element_type=F32
            )
        ).astype(BF16)
    shift = STRIDE // plan.m * lanes
    for i in range(hogel_rows):
        for j in range(hogel_cols):
            h = i * hogel_cols + j
            result = jnp.dot(
                lines[j, :, i * shift : i * shift + width], row[...], preferred_element_type=F32
            )
            spectra[h] = result
            power = result[:, :WIN] * result[:, :WIN] + result[:, WIN:] * result[:, WIN:]
            bright[h * VIEWS : (h + 1) * VIEWS, :] = power.reshape(VIEWS, BIN, WIN).sum(axis=1)
    light = jnp.dot(
        bright[...], picks[...], preferred_element_type=F32, precision=lax.Precision.HIGHEST
    )
    lights[...] = light
    weights[...] = jnp.dot(
        4.0 * (light - goal[...]),
        spreads[...],
        preferred_element_type=F32,
        precision=lax.Precision.HIGHEST,
    )
    for j in range(hogel_cols):
        backs = []
        for i in range(hogel_rows):
            h = i * hogel_cols + j
            blocks = []
            for view in range(VIEWS):
                factor = weights[h * VIEWS + view : h * VIEWS + view + 1, :]
                factor = jnp.concatenate([factor, factor], axis=1)
                blocks.append(
                    (spectra[h, view * BIN : (view + 1) * BIN, :] * factor).astype(BF16)
                )
            backs.append(
                lax.dot_general(
                    jnp.concatenate(blocks, axis=0),
                    row[...],
                    BOTH_MINOR,
                    preferred_element_type=F32,
                )
            )
        own[j, :, :shift] = backs[0][:, :shift]
        own[j, :, shift:] = backs[0][:, shift:] + backs[1][:, : width - shift]
        spill[j] = backs[1][:, width - shift :].astype(BF16)


def adjoint_kernel(plan, own, spill, col, *refs):
    C, X, lanes = plan.C, plan.X, plan.lanes
    leaving, (pair, out) = refs[:C], refs[C:]
    shift = STRIDE // plan.m * lanes
    hogel_cols = X // STRIDE
    pending = None
    for j in range(hogel_cols):
        for c in range(C):
            place = slice(c * lanes, (c + 1) * lanes)
            value = own[j, :, place]
            if c * lanes < shift:
                value = value + spill[j, :, place].astype(F32)
            value = value.astype(BF16)
            pair[0, :, place] = value
            pair[1, :, place] = (-times_i(value.astype(F32))).astype(BF16)
        result = jnp.dot(col[0], pair[0], preferred_element_type=F32) + jnp.dot(
            col[1], pair[1], preferred_element_type=F32
        )
        lead = result[:STRIDE]
        if pending is not None:
            lead = lead + pending
        pending = result[STRIDE:]
        for c in range(C):
            out[c, STRIDE * j : STRIDE * (j + 1), :] = lead[:, c * lanes : (c + 1) * lanes].astype(BF16)
    for c in range(C):
        out[c, X:, :] = pending[:, c * lanes : (c + 1) * lanes].astype(BF16)
    scatter_chunks(out, leaving)


def steer_table(plan):
    index = lax.axis_index(("rows", "cols"))
    shape = (plan.D, plan.f, 128)
    k = lax.broadcasted_iota(jnp.int32, shape, 0)
    line = lax.broadcasted_iota(jnp.int32, shape, 1)
    lane = lax.broadcasted_iota(jnp.int32, shape, 2)
    u = k + plan.D * (lane % plan.m)
    v = index // plan.R + plan.C * (
        plan.span * (index % plan.R) + plan.f * (lane // plan.m) + line
    )

    def freq(position, count):
        return ((position + count // 2) % count - count // 2).astype(F32) / count

    freq_rows, freq_cols = freq(u, plan.total_rows), freq(v, plan.total_cols)
    radial = freq_rows * freq_rows + freq_cols * freq_cols
    phase = (
        -2.0
        * math.pi
        * distance_px
        * radial
        / (jnp.sqrt(index_ratio * index_ratio - radial) + index_ratio)
    )
    return jnp.cos(phase), jnp.sin(phase)


def exchange(chunks, axes):
    return lax.all_to_all(chunks, axes, split_axis=0, concat_axis=0, tiled=True)


def shifted(block, axis, distance):
    count = lax.axis_size(axis)
    return lax.ppermute(block, axis, [((i - distance) % count, i) for i in range(count)])


def swap_columns(chunks):
    count = lax.axis_size("cols")
    return tuple(
        chunk if t == 0 else lax.ppermute(chunk, "cols", [(i, i ^ t) for i in range(count)])
        for t, chunk in enumerate(chunks)
    )


def local(slm_field, target_light):
    rows_count, cols_count = lax.axis_size("rows"), lax.axis_size("cols")
    plan = Plan(rows_count, cols_count, slm_field.shape[1], slm_field.shape[2])
    C, D, X, lanes, f = plan.C, plan.D, plan.X, plan.lanes, plan.f
    whole = ("rows", "cols")

    ahead, behind, twist = (jnp.asarray(t) for t in plan.pencil_tables())
    weights_ahead, twist_ahead = (jnp.asarray(t) for t in plan.line_tables(-1.0))
    weights_behind, twist_behind = (jnp.asarray(t) for t in plan.line_tables(1.0))
    (col_re, col_im), (row_re, row_im) = hogel_tables()
    col = jnp.asarray(np.stack([col_re, col_im]))
    slabs_in_window = WIN // plan.m
    row_blocks = [
        np.concatenate(
            [
                np.concatenate([row_re[part], row_im[part]], axis=1),
                np.concatenate([-row_im[part], row_re[part]], axis=1),
            ],
            axis=0,
        )
        for part in (slice(s * plan.m, (s + 1) * plan.m) for s in range(slabs_in_window))
    ]
    row = jnp.asarray(np.concatenate(row_blocks, axis=0))
    groups = np.kron(np.eye(VIEWS), np.ones((BIN, 1))).astype(np.float32)
    picks, spreads = jnp.asarray(groups / (BIN * BIN)), jnp.asarray(groups.T.copy())

    steer_re, steer_im = steer_table(plan)
    pencil_shape = shape_of((D, 2 * f, 128), BF16)
    tall = pltpu.VMEM((2 * X, C * lanes), BF16)

    def slabs_shapes(halo):
        return (shape_of((X + halo, lanes), BF16),) * C

    def slabs_scratch(halo):
        return pltpu.VMEM((C, X + halo, lanes), BF16)

    def forward_rows(slabs, halo):
        return call(
            lambda *refs: rows_forward_kernel(plan, halo, *refs),
            (pencil_shape,),
            (*slabs, weights_ahead, twist_ahead),
            (tall, tall, slabs_scratch(halo)),
            flops=6 * X * 2 * X * C * lanes,
        )[0]

    def inverse_rows(pencils, halo):
        return call(
            lambda *refs: rows_inverse_kernel(plan, halo, *refs),
            slabs_shapes(halo),
            (pencils, weights_behind, twist_behind),
            (tall, slabs_scratch(halo)),
            flops=4 * X * 2 * X * C * lanes,
        )

    def columns(pencils, sign):
        return call(
            lambda *refs: columns_kernel(plan, sign, *refs),
            (pencil_shape,),
            (pencils, steer_re, steer_im, ahead, behind, twist),
            (
                pltpu.VMEM((D, f, 128), F32),
                pltpu.VMEM((D, f, 128), F32),
                pltpu.VMEM((D, f, 256), BF16),
                pltpu.VMEM((D, f, 256), BF16),
            ),
            flops=12 * D * f * 256 * 256,
        )[0]

    def travel(slabs, sign, halo_in, halo_out):
        pencils = exchange(forward_rows(swap_columns(slabs), halo_in), whole)
        pencils = exchange(columns(pencils, sign), whole)
        return swap_columns(inverse_rows(pencils, halo_out))

    slabs = call(
        lambda *refs: pack_kernel(plan, *refs), slabs_shapes(0), (slm_field,), (slabs_scratch(0),)
    )
    near = travel(slabs, 1.0, 0, STRIDE)
    rims = STRIDE // plan.m
    mine = lax.axis_index("cols")
    rim = jnp.stack(
        [
            lax.select_n(mine // rims, *(near[q * rims + s] for q in range(C // rims)))
            for s in range(rims)
        ]
    )
    rim = shifted(rim, "rows", -1)

    hogel_rows, hogel_cols = target_light.shape[:2]
    hogels = hogel_rows * hogel_cols
    goal = target_light.reshape(hogels, VIEWS, VIEWS).swapaxes(1, 2).reshape(hogels * VIEWS, VIEWS)
    breadth = (C + rims) * lanes
    lights, own, spill = call(
        lambda *refs: hogel_kernel(plan, *refs),
        (
            shape_of((hogels * VIEWS, VIEWS), F32),
            shape_of((hogel_cols, WIN, C * lanes), F32),
            shape_of((hogel_cols, WIN, rims * lanes), BF16),
        ),
        (*near, rim, goal, col, row, picks, spreads),
        (
            slabs_scratch(STRIDE),
            pltpu.VMEM((2, X + STRIDE, breadth), BF16),
            pltpu.VMEM((hogel_cols, WIN, breadth), BF16),
            pltpu.VMEM((hogels, WIN, 2 * WIN), F32),
            pltpu.VMEM((hogels * VIEWS, WIN), F32),
            pltpu.VMEM((hogels * VIEWS, WIN), F32),
        ),
        flops=2 * hogels * 4 * WIN**3 * 2 + 2 * hogel_cols * WIN * 2 * WIN * breadth,
    )
    spill = shifted(spill, "rows", 1)
    slabs = call(
        lambda *refs: adjoint_kernel(plan, *refs),
        slabs_shapes(STRIDE),
        (own, spill, col),
        (pltpu.VMEM((2, WIN, C * lanes), BF16), slabs_scratch(STRIDE)),
        flops=2 * hogel_cols * WIN * 2 * WIN * C * lanes,
    )
    slabs = travel(slabs, -1.0, STRIDE, 0)
    gradient = call(
        lambda *refs: unpack_kernel(plan, *refs),
        (shape_of(slm_field.shape, F32),),
        slabs,
        (slabs_scratch(0),),
    )[0]
    light_field = lights.reshape(hogels, VIEWS, VIEWS).swapaxes(1, 2).reshape(target_light.shape)
    return gradient, light_field


def solution(mesh):
    return jax.shard_map(
        local,
        mesh=mesh,
        in_specs=(P(None, "rows", "cols"), P("rows", "cols", None)),
        out_specs=(P(None, "rows", "cols"), P("rows", "cols", None)),
        check_vma=False,
    )
```

```python
import math

import jax
import jax.numpy as jnp
import ml_dtypes
import numpy as np
from jax import lax
from jax.experimental import pallas as pl
from jax.experimental.pallas import tpu as pltpu
from jax.sharding import PartitionSpec as P

WIN = 256
VIEWS = 16
STRIDE = 128
BIN = 16

distance_px = 16000.0
index_ratio = 15.0

BF16 = jnp.bfloat16
F32 = jnp.float32
BOTH_MINOR = (((1,), (1,)), ((), ()))


def call(body, outs, args, scratch=(), flops=0):
    nbytes = sum(math.prod(a.shape) * a.dtype.itemsize for a in (*outs, *args))
    return pl.pallas_call(
        body,
        out_shape=outs,
        scratch_shapes=list(scratch),
        compiler_params=pltpu.CompilerParams(vmem_limit_bytes=24 * 2**20),
        cost_estimate=pl.CostEstimate(flops=flops, bytes_accessed=nbytes, transcendentals=0),
    )(*args)


def shape_of(dims, dtype):
    return jax.ShapeDtypeStruct(dims, dtype)


def high_low(table):
    table = np.asarray(table, np.float32)
    high = table.astype(ml_dtypes.bfloat16)
    low = (table - high.astype(np.float32)).astype(ml_dtypes.bfloat16)
    return np.stack([high, low])


def split(values):
    high = values.astype(BF16)
    return high, (values - high.astype(F32)).astype(BF16)


def times_i(values):
    half = values.shape[-1] // 2
    if values.shape[-1] == 128:
        lanes = lax.broadcasted_iota(jnp.int32, values.shape, values.ndim - 1)
        turned = pltpu.roll(values, half, values.ndim - 1)
        return jnp.where(lanes < half, -turned, turned)
    return jnp.concatenate([-values[..., half:], values[..., :half]], axis=-1)


def scaled(value, factor):
    return value if factor == 1.0 else value * factor


def small_dft(points, sign):
    count = len(points)
    if count == 1:
        return points
    even = small_dft(points[0::2], sign)
    odd = small_dft(points[1::2], sign)
    front, back = [], []
    for k in range(count // 2):
        re, im = odd[k]
        angle = sign * 2.0 * math.pi * k / count
        cosine, sine = math.cos(angle), math.sin(angle)
        if k == 0:
            pass
        elif 4 * k == count:
            re, im = (-im, re) if sign > 0 else (im, -re)
        elif 8 * k == count:
            re, im = cosine * (re - sign * im), cosine * (im + sign * re)
        elif 8 * k == 3 * count:
            re, im = cosine * (re + sign * im), cosine * (im - sign * re)
        else:
            re, im = re * cosine - im * sine, re * sine + im * cosine
        even_re, even_im = even[k]
        front.append((even_re + re, even_im + im))
        back.append((even_re - re, even_im - im))
    return front + back


def packed_dft(points, sign):
    count = len(points)
    if count == 1:
        return points
    even = packed_dft(points[0::2], sign)
    odd = packed_dft(points[1::2], sign)
    front, back = [], []
    for k in range(count // 2):
        term = odd[k]
        angle = sign * 2.0 * math.pi * k / count
        if 4 * k == count:
            term = times_i(term) if sign > 0 else -times_i(term)
        elif k:
            term = math.cos(angle) * term + math.sin(angle) * times_i(term)
        front.append(even[k] + term)
        back.append(even[k] - term)
    return front + back


def turn(rows, cols, period, sign):
    angles = sign * 2.0 * np.pi / period * ((np.arange(rows)[:, None] * np.arange(cols)) % period)
    return np.cos(angles), np.sin(angles)


def block_diagonal(block, copies):
    return np.kron(np.eye(copies), block)


class Plan:
    def __init__(self, rows_count, cols_count, rows_dev, cols_dev):
        self.R, self.C = rows_count, cols_count
        self.D = rows_count * cols_count
        self.X = cols_dev
        self.m = rows_dev // cols_count
        self.lanes = 2 * self.m
        self.P = 128 // self.m
        self.span = cols_dev // rows_count
        self.f = self.span // self.P
        self.total_rows = rows_dev * rows_count
        self.total_cols = cols_dev * cols_count
        self.outer = 8
        self.inner = self.D // 8
        self.shift = STRIDE // self.m
        self.hogel_rows = self.total_rows // STRIDE
        self.hogel_cols = self.total_cols // STRIDE
        self.parts = self.D // self.hogel_rows
        self.pp = WIN // self.parts
        self.views = VIEWS // self.parts
        self.own_cols = cols_dev // STRIDE

    def line_tables(self, sign):
        cosine, sine = turn(self.X, self.X, self.X, sign)
        weights = high_low(np.concatenate([cosine, sine], axis=1))
        twist = turn(self.X, self.C, self.total_cols, sign)
        return weights, np.concatenate(twist, axis=1).astype(np.float32)

    def pencil_tables(self):
        cosine, sine = turn(self.m, self.m, self.m, -1.0)
        cosine, sine = block_diagonal(cosine, self.P), block_diagonal(sine, self.P)
        ahead = np.block([[cosine, sine], [-sine, cosine]])
        behind = np.block([[cosine, -sine], [sine, cosine]]) / (self.total_rows * self.total_cols)
        twist = turn(self.D, self.m, self.total_rows, -1.0)
        twist = np.stack([np.tile(part, (1, self.P)) for part in twist]).astype(np.float32)
        return high_low(ahead), high_low(behind), twist

    def row_table(self, real, imag):
        blocks = []
        for slab in range(WIN // self.m):
            rows = slice(slab * self.m, (slab + 1) * self.m)
            for left, right in ((real[rows], imag[rows]), (-imag[rows], real[rows])):
                pieces = []
                for part in range(self.parts):
                    cols = slice(part * self.pp, (part + 1) * self.pp)
                    pieces += [left[:, cols], right[:, cols]]
                blocks.append(np.concatenate(pieces, axis=1))
        return np.concatenate(blocks, axis=0)

    def view_tables(self):
        places = np.zeros((3, self.own_cols, self.views, self.lanes))
        for piece in range(3):
            for j in range(self.own_cols):
                for a in range(self.views):
                    places[piece, j, a, (j * 3 + piece) * self.views + a] = 1.0
        into = np.zeros((self.parts, 3, self.own_cols, VIEWS, self.lanes))
        for part in range(self.parts):
            into[part, :, :, part * self.views : (part + 1) * self.views] = places
        into = into.reshape(self.parts, 3, self.own_cols * VIEWS, self.lanes)
        joined = places.sum(axis=0)
        groups = np.kron(np.eye(self.views), np.ones((1, BIN)))
        expand = np.stack([joined[j].T @ groups for j in range(self.own_cols)])
        flat = np.zeros((self.parts, self.own_cols, self.lanes, VIEWS * VIEWS))
        for part in range(self.parts):
            start = part * self.views * VIEWS
            flat[part, :, :, start : start + self.views * VIEWS] = expand
        own = np.kron(np.ones((1, VIEWS)), np.eye(VIEWS))
        return (
            into.astype(ml_dtypes.bfloat16),
            places.astype(ml_dtypes.bfloat16),
            expand.astype(ml_dtypes.bfloat16),
            flat.astype(ml_dtypes.bfloat16),
            own.astype(np.float32),
            (groups.T / (BIN * BIN)).astype(np.float32),
            (groups.T @ groups / (BIN * BIN)).astype(np.float32),
        )


def hogel_tables():
    positions = np.arange(WIN)
    tapers = np.sin(np.pi * (positions + 0.5) / WIN) ** 2
    angles = -2.0 * np.pi / WIN * (positions[:, None] * positions[None, :] % WIN)
    cosine = (tapers[:, None] * np.cos(angles)).astype(np.float32)
    sine = (tapers[:, None] * np.sin(angles)).astype(np.float32)
    col = np.stack([cosine, sine]).astype(ml_dtypes.bfloat16)
    row = np.stack([cosine / WIN, sine / WIN]).astype(ml_dtypes.bfloat16)
    return col, row


def three_pieces(values):
    first = values.astype(BF16)
    rest = values - first.astype(F32)
    second = rest.astype(BF16)
    return first, second, (rest - second.astype(F32)).astype(BF16)


def matmul(left, right):
    return jnp.dot(left, right, preferred_element_type=F32)


def gather_chunks(arrived, chunks):
    mine = lax.axis_index("cols")
    for t, chunk in enumerate(arrived):
        chunks[mine ^ t] = chunk[...]


def scatter_chunks(chunks, leaving):
    mine = lax.axis_index("cols")
    for t, chunk in enumerate(leaving):
        chunk[...] = chunks[mine ^ t]


def pack_kernel(plan, field, goal, into, *refs):
    m, X = plan.m, plan.X
    leaving, (out,) = refs[: plan.C], refs[plan.C :]
    for c in range(plan.C):
        block = jnp.concatenate(
            [field[0, m * c : m * c + m, :], field[1, m * c : m * c + m, :]], axis=0
        )
        out[c, :X, :] = block.T.astype(BF16)
        pieces = three_pieces(goal[c // plan.parts])
        part = c % plan.parts
        out[c, X:, :] = sum(matmul(pieces[n], into[part, n]) for n in range(3)).astype(BF16)
    scatter_chunks(out, leaving)


def unpack_kernel(plan, flat, own, *refs):
    m, X = plan.m, plan.X
    arrived, (out, light, slabs) = refs[: plan.C], refs[plan.C :]
    gather_chunks(arrived, slabs)
    for c in range(plan.C):
        block = slabs[c, :X, :].astype(F32).T
        out[0, m * c : m * c + m, :] = block[:m]
        out[1, m * c : m * c + m, :] = block[m:]
    for i in range(plan.C // plan.parts):
        for j in range(plan.own_cols):
            total = sum(
                matmul(slabs[i * plan.parts + part, X:, :], flat[part, j])
                for part in range(plan.parts)
            )
            light[i, j : j + 1, :] = jnp.sum(total * own[...], axis=0, keepdims=True)


def lines_forward(plan, lanes, load, emit, weights, twist, high, low):
    C, X = plan.C, plan.X
    step = 64
    for start in range(0, X, step):
        points = packed_dft([load(c, start, step) for c in range(C)], -1.0)
        for k in range(C):
            cosine = twist[start : start + step, k : k + 1]
            sine = twist[start : start + step, C + k : C + k + 1]
            across = times_i(points[k])
            if k:
                value = points[k] * cosine + across * sine
                across = across * cosine - points[k] * sine
            else:
                value = points[k]
            place = slice(k * lanes, k * lanes + lanes)
            for offset, part in ((0, value), (X, across)):
                part_high, part_low = split(part)
                high[offset + start : offset + start + step, place] = part_high
                low[offset + start : offset + start + step, place] = part_low
    for r in range(plan.R):
        place = slice(r * plan.span, (r + 1) * plan.span)
        result = (
            matmul(weights[0, place, :], high[...])
            + matmul(weights[0, place, :], low[...])
            + matmul(weights[1, place, :], high[...])
        )
        for k in range(C):
            emit(k * plan.R + r, result[:, k * lanes : (k + 1) * lanes])


def lines_inverse(plan, lanes, packed, emit, weights, twist):
    C, X = plan.C, plan.X
    step = 64
    for start in range(0, X, step):
        result = matmul(weights[0, start : start + step, :], packed[...]) + matmul(
            weights[1, start : start + step, :], packed[...]
        )
        points = []
        for k in range(C):
            value = result[:, k * lanes : (k + 1) * lanes]
            if k:
                cosine = twist[start : start + step, k : k + 1]
                sine = twist[start : start + step, C + k : C + k + 1]
                value = value * cosine + times_i(value) * sine
            points.append(value)
        for c, value in enumerate(packed_dft(points, 1.0)):
            emit(c, start, step, value)


def to_planes(plan, block):
    parts = [block[p * plan.f : (p + 1) * plan.f, :] for p in range(plan.P)]
    real = jnp.concatenate([part[:, : plan.m] for part in parts], axis=1)
    imag = jnp.concatenate([part[:, plan.m :] for part in parts], axis=1)
    return real, imag


def from_planes(plan, real, imag):
    m = plan.m
    return jnp.concatenate(
        [
            jnp.concatenate([real[:, p * m : (p + 1) * m], imag[:, p * m : (p + 1) * m]], axis=1)
            for p in range(plan.P)
        ],
        axis=0,
    )


def rows_forward_kernel(plan, weights, twist, *refs):
    C, X = plan.C, plan.X
    arrived, (out, goals, high, low, slabs) = refs[:C], refs[C:]
    gather_chunks(arrived, slabs)
    goals[...] = slabs[:, X:, :]

    def load(c, start, step):
        return slabs[c, start : start + step, :].astype(F32)

    def emit(d, block):
        out[d] = jnp.concatenate(to_planes(plan, block), axis=0).astype(BF16)

    lines_forward(plan, plan.lanes, load, emit, weights, twist, high, low)


def rows_inverse_kernel(plan, pencils, lights, weights, twist, *refs):
    C, X, lanes = plan.C, plan.X, plan.lanes
    leaving, (packed, out) = refs[:C], refs[C:]
    for k in range(C):
        for r in range(plan.R):
            chunk = pencils[k * plan.R + r].astype(F32)
            block = from_planes(plan, chunk[: plan.f], chunk[plan.f :])
            place = slice(k * lanes, k * lanes + lanes)
            packed[r * plan.span : (r + 1) * plan.span, place] = block.astype(BF16)
            packed[X + r * plan.span : X + (r + 1) * plan.span, place] = times_i(block).astype(BF16)

    def emit(c, start, step, value):
        out[c, start : start + step, :] = value.astype(BF16)

    lines_inverse(plan, lanes, packed, emit, weights, twist)
    out[:, X:, :] = lights[...]
    scatter_chunks(out, leaving)


def columns(plan, sign, load, store, steer_re, steer_im, ahead, behind, twist, scratch):
    D, f, outer, inner = plan.D, plan.f, plan.outer, plan.inner
    half_re, half_im, high, low = scratch
    for b in range(inner):
        points = [load(inner * a + b) for a in range(outer)]
        for alpha, (re, im) in enumerate(small_dft(points, -1.0)):
            angle = -2.0 * math.pi * b * alpha / D
            cosine, sine = math.cos(angle), math.sin(angle)
            if b * alpha:
                re, im = re * cosine - im * sine, re * sine + im * cosine
            half_re[alpha * inner + b] = re
            half_im[alpha * inner + b] = im
    for alpha in range(outer):
        points = [(half_re[alpha * inner + b], half_im[alpha * inner + b]) for b in range(inner)]
        for beta, (re, im) in enumerate(small_dft(points, -1.0)):
            k = alpha + outer * beta
            cosine, sine = twist[0, k : k + 1, :], twist[1, k : k + 1, :]
            for offset, part in ((0, re * cosine - im * sine), (128, re * sine + im * cosine)):
                part_high, part_low = split(part)
                high[k, :, offset : offset + 128] = part_high
                low[k, :, offset : offset + 128] = part_low
    group = D // 4
    for start in range(0, D, group):
        place = slice(start, start + group)

        def multiply(matrix):
            first = high[place].reshape(group * f, 256)
            second = low[place].reshape(group * f, 256)
            return (
                matmul(first, matrix[0]) + matmul(second, matrix[0]) + matmul(first, matrix[1])
            ).reshape(group, f, 256)

        result = multiply(ahead)
        re, im = result[:, :, :128], result[:, :, 128:]
        factor_re, factor_im = steer_re[place], sign * steer_im[place]
        for offset, part in (
            (0, re * factor_re - im * factor_im),
            (128, re * factor_im + im * factor_re),
        ):
            part_high, part_low = split(part)
            high[place, :, offset : offset + 128] = part_high
            low[place, :, offset : offset + 128] = part_low
        result = multiply(behind)
        half_re[place] = result[:, :, :128]
        half_im[place] = result[:, :, 128:]
    for alpha in range(outer):
        points = []
        for beta in range(inner):
            k = alpha + outer * beta
            cosine, sine = twist[0, k : k + 1, :], twist[1, k : k + 1, :]
            re, im = half_re[k], half_im[k]
            points.append((re * cosine + im * sine, im * cosine - re * sine))
        for b, (re, im) in enumerate(small_dft(points, 1.0)):
            angle = 2.0 * math.pi * b * alpha / D
            cosine, sine = math.cos(angle), math.sin(angle)
            if b * alpha:
                re, im = re * cosine - im * sine, re * sine + im * cosine
            half_re[alpha + outer * b] = re
            half_im[alpha + outer * b] = im
    for b in range(inner):
        points = [(half_re[alpha + outer * b], half_im[alpha + outer * b]) for alpha in range(outer)]
        for a, (re, im) in enumerate(small_dft(points, 1.0)):
            store(inner * a + b, re, im)


def pencil_forward_kernel(plan, pencils, *refs):
    steer_re, steer_im, ahead, behind, twist, row, out, windows, *scratch = refs
    f, lanes, span = plan.f, plan.lanes, plan.span

    def load(s):
        chunk = pencils[s].astype(F32)
        return chunk[:f], chunk[f:]

    def store(s, re, im):
        block = from_planes(plan, re, im).astype(BF16)
        i, slab = s // plan.shift, s % plan.shift
        windows[i, :, slab * lanes : (slab + 1) * lanes] = block
        slab += plan.shift
        windows[(i - 1) % plan.hogel_rows, :, slab * lanes : (slab + 1) * lanes] = block

    columns(plan, 1.0, load, store, steer_re, steer_im, ahead, behind, twist, scratch)
    group = plan.hogel_rows // 4
    for start in range(0, plan.hogel_rows, group):
        result = matmul(
            windows[start : start + group].reshape(group * span, 2 * WIN), row[...]
        ).astype(BF16)
        for i in range(group):
            for part in range(plan.parts):
                out[(start + i) * plan.parts + part] = result[
                    i * span : (i + 1) * span, part * 2 * plan.pp : (part + 1) * 2 * plan.pp
                ]


def pencil_back_kernel(plan, lines, *refs):
    steer_re, steer_im, ahead, behind, twist, row, out, windows, *scratch = refs
    lanes, span, parts = plan.lanes, plan.span, plan.parts
    group = plan.hogel_rows // 4
    for start in range(0, plan.hogel_rows, group):
        left = jnp.concatenate(
            [
                jnp.concatenate([lines[i * parts + part] for part in range(parts)], axis=1)
                for i in range(start, start + group)
            ],
            axis=0,
        )
        result = lax.dot_general(left, row[...], BOTH_MINOR, preferred_element_type=F32)
        windows[start : start + group] = result.reshape(group, span, 2 * WIN)

    def load(s):
        i, slab = s // plan.shift, s % plan.shift
        block = windows[i, :, slab * lanes : (slab + 1) * lanes]
        slab += plan.shift
        block = block + windows[(i - 1) % plan.hogel_rows, :, slab * lanes : (slab + 1) * lanes]
        return to_planes(plan, block)

    def store(s, re, im):
        out[s] = jnp.concatenate([re, im], axis=0).astype(BF16)

    columns(plan, -1.0, load, store, steer_re, steer_im, ahead, behind, twist, scratch)


def hogel_kernel(plan, lines, goals, *refs):
    weights_behind, twist_behind, weights_ahead, twist_ahead, col, places, expand, picks, same = refs[:9]
    out, lights, high, low, field, spectra, bright, factors, back = refs[9:]
    C, X, lanes, pp = plan.C, plan.X, 2 * plan.pp, plan.pp
    total = plan.total_cols
    for k in range(C):
        block = lines[k * plan.R : (k + 1) * plan.R].reshape(X, lanes)
        place = slice(k * lanes, (k + 1) * lanes)
        high[:X, place] = block
        high[X:, place] = times_i(block.astype(F32)).astype(BF16)

    def emit_near(c, start, step, value):
        for n, part in enumerate((value, times_i(value))):
            rounded = part.astype(BF16)
            field[n, c * X + start : c * X + start + step, :] = rounded
            if c == 0 and start < STRIDE:
                field[n, total + start : total + start + step, :] = rounded

    lines_inverse(plan, lanes, high, emit_near, weights_behind, twist_behind)
    transposed = (((0,), (0,)), ((), ()))
    for j in range(plan.hogel_cols):
        window = slice(STRIDE * j, STRIDE * j + WIN)
        result = lax.dot_general(
            col[0], field[0, window, :], transposed, preferred_element_type=F32
        ) + lax.dot_general(col[1], field[1, window, :], transposed, preferred_element_type=F32)
        spectra[j] = result
        power = result[:, :pp] * result[:, :pp] + result[:, pp:] * result[:, pp:]
        bright[j * VIEWS : (j + 1) * VIEWS, :] = power.reshape(VIEWS, BIN, pp).sum(axis=1)
    exact = lax.Precision.HIGHEST
    light = jnp.dot(bright[...], picks[...], preferred_element_type=F32, precision=exact)
    spread = jnp.dot(bright[...], same[...], preferred_element_type=F32, precision=exact)
    pieces = three_pieces(light)
    for c in range(C):
        chunk = 0.0
        for j in range(plan.own_cols):
            h = c * plan.own_cols + j
            rows = slice(h * VIEWS, (h + 1) * VIEWS)
            chunk = chunk + sum(matmul(pieces[n][rows, :], places[n, j]) for n in range(3))
            factors[rows, :] = 4.0 * (spread[rows, :] - matmul(goals[c], expand[j]))
        lights[c] = chunk.astype(BF16)
    for j in range(plan.hogel_cols):
        straight, across = [], []
        for view in range(VIEWS):
            factor = factors[j * VIEWS + view : j * VIEWS + view + 1, :]
            block = spectra[j, view * BIN : (view + 1) * BIN, :]
            block = block * jnp.concatenate([factor, factor], axis=1)
            straight.append(block.astype(BF16))
            across.append((-times_i(block)).astype(BF16))
        result = matmul(col[0], jnp.concatenate(straight, axis=0)) + matmul(
            col[1], jnp.concatenate(across, axis=0)
        )
        first, second = slice(STRIDE * j, STRIDE * j + STRIDE), STRIDE * (j + 1) % total
        if j == 0:
            back[first] = result[:STRIDE]
        else:
            back[first] = back[first] + result[:STRIDE]
        if j < plan.hogel_cols - 1:
            back[second : second + STRIDE] = result[STRIDE:]
        else:
            back[:STRIDE] = back[:STRIDE] + result[STRIDE:]

    def load(c, start, step):
        return back[c * X + start : c * X + start + step, :]

    def emit(d, block):
        out[d] = block.astype(BF16)

    lines_forward(plan, lanes, load, emit, weights_ahead, twist_ahead, high, low)


def steer_table(plan):
    index = lax.axis_index(("rows", "cols"))
    shape = (plan.D, plan.f, 128)
    k = lax.broadcasted_iota(jnp.int32, shape, 0)
    line = lax.broadcasted_iota(jnp.int32, shape, 1)
    lane = lax.broadcasted_iota(jnp.int32, shape, 2)
    u = k + plan.D * (lane % plan.m)
    v = index // plan.R + plan.C * (
        plan.span * (index % plan.R) + plan.f * (lane // plan.m) + line
    )

    def freq(position, count):
        return ((position + count // 2) % count - count // 2).astype(F32) / count

    freq_rows, freq_cols = freq(u, plan.total_rows), freq(v, plan.total_cols)
    radial = freq_rows * freq_rows + freq_cols * freq_cols
    phase = (
        -2.0
        * math.pi
        * distance_px
        * radial
        / (jnp.sqrt(index_ratio * index_ratio - radial) + index_ratio)
    )
    return jnp.cos(phase), jnp.sin(phase)


def exchange(chunks):
    return lax.all_to_all(chunks, ("rows", "cols"), split_axis=0, concat_axis=0, tiled=True)


def swap_columns(chunks):
    count = lax.axis_size("cols")
    return tuple(
        chunk if t == 0 else lax.ppermute(chunk, "cols", [(i, i ^ t) for i in range(count)])
        for t, chunk in enumerate(chunks)
    )


def local(slm_field, target_light):
    rows_count, cols_count = lax.axis_size("rows"), lax.axis_size("cols")
    plan = Plan(rows_count, cols_count, slm_field.shape[1], slm_field.shape[2])
    C, D, X, lanes, f = plan.C, plan.D, plan.X, plan.lanes, plan.f
    span, wide = plan.span, 2 * plan.pp

    ahead, behind, twist = (jnp.asarray(t) for t in plan.pencil_tables())
    weights_ahead, twist_ahead = (jnp.asarray(t) for t in plan.line_tables(-1.0))
    weights_behind, twist_behind = (jnp.asarray(t) for t in plan.line_tables(1.0))
    col, row = hogel_tables()
    col, row = jnp.asarray(col), jnp.asarray(plan.row_table(row[0], row[1]))
    into, places, expand, flat, own, picks, same = (jnp.asarray(t) for t in plan.view_tables())
    steer_re, steer_im = steer_table(plan)

    slabs_shapes = (shape_of((X + VIEWS, lanes), BF16),) * C
    slabs_scratch = pltpu.VMEM((C, X + VIEWS, lanes), BF16)
    views_shape = shape_of((C, VIEWS, lanes), BF16)
    pencil_shape = shape_of((D, 2 * f, 128), BF16)
    lines_shape = shape_of((D, span, wide), BF16)
    columns_scratch = (
        pltpu.VMEM((D, f, 128), F32),
        pltpu.VMEM((D, f, 128), F32),
        pltpu.VMEM((D, f, 256), BF16),
        pltpu.VMEM((D, f, 256), BF16),
    )
    pencil_tables = (steer_re, steer_im, ahead, behind, twist, row)
    columns_flops = 12 * D * f * 256 * 256 + 2 * plan.hogel_rows * span * (2 * WIN) ** 2

    goal = target_light.reshape(*target_light.shape[:2], VIEWS, VIEWS).transpose(0, 3, 1, 2)
    goal = goal.reshape(target_light.shape[0], VIEWS, plan.own_cols * VIEWS)
    slabs = call(
        lambda *refs: pack_kernel(plan, *refs),
        slabs_shapes,
        (slm_field, goal, into),
        (slabs_scratch,),
    )
    tall = pltpu.VMEM((2 * X, C * lanes), BF16)
    pencils, goals = call(
        lambda *refs: rows_forward_kernel(plan, *refs),
        (pencil_shape, views_shape),
        (weights_ahead, twist_ahead, *swap_columns(slabs)),
        (tall, tall, slabs_scratch),
        flops=6 * X * 2 * X * C * lanes,
    )
    (lines,) = call(
        lambda *refs: pencil_forward_kernel(plan, *refs),
        (lines_shape,),
        (exchange(pencils), *pencil_tables),
        (pltpu.VMEM((plan.hogel_rows, span, 2 * WIN), BF16), *columns_scratch),
        flops=columns_flops,
    )
    tall = pltpu.VMEM((2 * X, C * wide), BF16)
    lines, lights = call(
        lambda *refs: hogel_kernel(plan, *refs),
        (lines_shape, views_shape),
        (
            exchange(lines),
            goals,
            weights_behind,
            twist_behind,
            weights_ahead,
            twist_ahead,
            col,
            places,
            expand,
            picks,
            same,
        ),
        (
            tall,
            tall,
            pltpu.VMEM((2, plan.total_cols + STRIDE, wide), BF16),
            pltpu.VMEM((plan.hogel_cols, WIN, wide), F32),
            pltpu.VMEM((plan.hogel_cols * VIEWS, plan.pp), F32),
            pltpu.VMEM((plan.hogel_cols * VIEWS, plan.pp), F32),
            pltpu.VMEM((plan.total_cols, wide), F32),
        ),
        flops=10 * X * 2 * X * C * wide + 4 * plan.hogel_cols * WIN * 2 * WIN * wide,
    )
    (pencils,) = call(
        lambda *refs: pencil_back_kernel(plan, *refs),
        (pencil_shape,),
        (exchange(lines), *pencil_tables),
        (pltpu.VMEM((plan.hogel_rows, span, 2 * WIN), F32), *columns_scratch),
        flops=columns_flops,
    )
    tall = pltpu.VMEM((2 * X, C * lanes), BF16)
    slabs = call(
        lambda *refs: rows_inverse_kernel(plan, *refs),
        slabs_shapes,
        (exchange(pencils), lights, weights_behind, twist_behind),
        (tall, slabs_scratch),
        flops=4 * X * 2 * X * C * lanes,
    )
    return call(
        lambda *refs: unpack_kernel(plan, *refs),
        (shape_of(slm_field.shape, F32), shape_of(target_light.shape, F32)),
        (flat, own, *swap_columns(slabs)),
        (slabs_scratch,),
    )


def solution(mesh):
    return jax.shard_map(
        local,
        mesh=mesh,
        in_specs=(P(None, "rows", "cols"), P("rows", "cols", None)),
        out_specs=(P(None, "rows", "cols"), P("rows", "cols", None)),
        check_vma=False,
    )
```

```python
import math

import jax
import jax.numpy as jnp
import ml_dtypes
import numpy as np
from jax import lax
from jax.experimental import pallas as pl
from jax.experimental.pallas import tpu as pltpu
from jax.sharding import PartitionSpec as P

WIN = 256
VIEWS = 16
STRIDE = 128
BIN = 16

distance_px = 16000.0
index_ratio = 15.0

BF16 = jnp.bfloat16
F32 = jnp.float32
BOTH_MINOR = (((1,), (1,)), ((), ()))


def call(body, outs, args, scratch=(), flops=0, in_specs=None, out_specs=None):
    nbytes = sum(math.prod(a.shape) * a.dtype.itemsize for a in (*outs, *args))
    specs = {}
    if in_specs:
        whole = pl.BlockSpec(memory_space=pltpu.VMEM)
        specs["in_specs"] = [in_specs.get(n, whole) for n in range(len(args))]
    if out_specs:
        specs["out_specs"] = out_specs
    return pl.pallas_call(
        body,
        out_shape=outs,
        scratch_shapes=list(scratch),
        compiler_params=pltpu.CompilerParams(vmem_limit_bytes=24 * 2**20),
        cost_estimate=pl.CostEstimate(flops=flops, bytes_accessed=nbytes, transcendentals=0),
        **specs,
    )(*args)


def shape_of(dims, dtype):
    return jax.ShapeDtypeStruct(dims, dtype)


def high_low(table):
    table = np.asarray(table, np.float32)
    high = table.astype(ml_dtypes.bfloat16)
    low = (table - high.astype(np.float32)).astype(ml_dtypes.bfloat16)
    return np.concatenate([high, low], axis=0)


def split(values):
    high = values.astype(BF16)
    return high, (values - high.astype(F32)).astype(BF16)


def times_i(values):
    half = values.shape[-1] // 2
    if values.shape[-1] == 128:
        lanes = lax.broadcasted_iota(jnp.int32, values.shape, values.ndim - 1)
        turned = pltpu.roll(values, half, values.ndim - 1)
        return jnp.where(lanes < half, -turned, turned)
    return jnp.concatenate([-values[..., half:], values[..., :half]], axis=-1)


def scaled(value, factor):
    return value if factor == 1.0 else value * factor


def small_dft(points, sign):
    count = len(points)
    if count == 1:
        return points
    even = small_dft(points[0::2], sign)
    odd = small_dft(points[1::2], sign)
    front, back = [], []
    for k in range(count // 2):
        re, im = odd[k]
        angle = sign * 2.0 * math.pi * k / count
        cosine, sine = math.cos(angle), math.sin(angle)
        if k == 0:
            pass
        elif 4 * k == count:
            re, im = (-im, re) if sign > 0 else (im, -re)
        elif 8 * k == count:
            re, im = cosine * (re - sign * im), cosine * (im + sign * re)
        elif 8 * k == 3 * count:
            re, im = cosine * (re + sign * im), cosine * (im - sign * re)
        else:
            re, im = re * cosine - im * sine, re * sine + im * cosine
        even_re, even_im = even[k]
        front.append((even_re + re, even_im + im))
        back.append((even_re - re, even_im - im))
    return front + back


def packed_dft(points, sign):
    count = len(points)
    if count == 1:
        return points
    even = packed_dft(points[0::2], sign)
    odd = packed_dft(points[1::2], sign)
    front, back = [], []
    for k in range(count // 2):
        term = odd[k]
        angle = sign * 2.0 * math.pi * k / count
        if 4 * k == count:
            term = times_i(term) if sign > 0 else -times_i(term)
        elif k:
            term = math.cos(angle) * term + math.sin(angle) * times_i(term)
        front.append(even[k] + term)
        back.append(even[k] - term)
    return front + back


def turn(rows, cols, period, sign):
    angles = sign * 2.0 * np.pi / period * ((np.arange(rows)[:, None] * np.arange(cols)) % period)
    return np.cos(angles), np.sin(angles)


def block_diagonal(block, copies):
    return np.kron(np.eye(copies), block)


class Plan:
    def __init__(self, rows_count, cols_count, rows_dev, cols_dev):
        self.R, self.C = rows_count, cols_count
        self.D = rows_count * cols_count
        self.X = cols_dev
        self.m = rows_dev // cols_count
        self.lanes = 2 * self.m
        self.P = 128 // self.m
        self.span = cols_dev // rows_count
        self.f = self.span // self.P
        self.total_rows = rows_dev * rows_count
        self.total_cols = cols_dev * cols_count
        self.outer = 8
        self.inner = self.D // 8
        self.shift = STRIDE // self.m
        self.hogel_rows = self.total_rows // STRIDE
        self.hogel_cols = self.total_cols // STRIDE
        self.parts = self.D // self.hogel_rows
        self.pp = WIN // self.parts
        self.views = VIEWS // self.parts
        self.own_cols = cols_dev // STRIDE

    def line_tables(self, sign):
        cosine, sine = turn(self.X, self.X, self.X, sign)
        weights = high_low(np.concatenate([cosine, sine], axis=1))
        twist = turn(self.X, self.C, self.total_cols, sign)
        return weights, np.concatenate(twist, axis=1).astype(np.float32)

    def pencil_tables(self):
        cosine, sine = turn(self.m, self.m, self.m, -1.0)
        cosine, sine = block_diagonal(cosine, self.P), block_diagonal(sine, self.P)
        ahead = np.block([[cosine, sine], [-sine, cosine]])
        behind = np.block([[cosine, -sine], [sine, cosine]]) / (self.total_rows * self.total_cols)
        twist = turn(self.D, self.m, self.total_rows, -1.0)
        twist = np.stack([np.tile(part, (1, self.P)) for part in twist]).astype(np.float32)
        return high_low(ahead), high_low(behind), twist

    def row_table(self, real, imag):
        blocks = []
        for slab in range(WIN // self.m):
            rows = slice(slab * self.m, (slab + 1) * self.m)
            for left, right in ((real[rows], imag[rows]), (-imag[rows], real[rows])):
                pieces = []
                for part in range(self.parts):
                    cols = slice(part * self.pp, (part + 1) * self.pp)
                    pieces += [left[:, cols], right[:, cols]]
                blocks.append(np.concatenate(pieces, axis=1))
        return np.concatenate(blocks, axis=0)

    def group_table(self):
        return np.kron(np.eye(self.views), np.ones((BIN, BIN))).astype(np.float32)


def hogel_tables():
    positions = np.arange(WIN)
    tapers = np.sin(np.pi * (positions + 0.5) / WIN) ** 2
    angles = -2.0 * np.pi / WIN * (positions[:, None] * positions[None, :] % WIN)
    cosine = (tapers[:, None] * np.cos(angles)).astype(np.float32)
    sine = (tapers[:, None] * np.sin(angles)).astype(np.float32)
    col = np.concatenate([cosine, sine], axis=1).astype(ml_dtypes.bfloat16)
    col_turned = np.concatenate([cosine.T, sine.T], axis=1).astype(ml_dtypes.bfloat16)
    row = np.stack([cosine / WIN, sine / WIN]).astype(ml_dtypes.bfloat16)
    return col, col_turned, row


def three_pieces(values):
    first = values.astype(BF16)
    rest = values - first.astype(F32)
    second = rest.astype(BF16)
    return first, second, (rest - second.astype(F32)).astype(BF16)


def matmul(left, right):
    return jnp.dot(left, right, preferred_element_type=F32)


def gather_chunks(arrived, chunks):
    mine = lax.axis_index("cols")
    for t, chunk in enumerate(arrived):
        chunks[mine ^ t] = chunk[...]


def scatter_chunks(chunks, leaving):
    mine = lax.axis_index("cols")
    for t, chunk in enumerate(leaving):
        chunk[...] = chunks[mine ^ t]


def pack_kernel(plan, field, goal, *refs):
    C, m, X = plan.C, plan.m, plan.X
    leaving, (out, arriving, sems) = refs[:C], refs[C:]

    def block_copy(c, part):
        return pltpu.make_async_copy(
            field.at[part, pl.ds(c * m, m), :],
            arriving.at[c, pl.ds(part * m, m), :],
            sems.at[2 * c + part],
        )

    for c in range(C):
        block_copy(c, 0).start()
        block_copy(c, 1).start()
    out[:, X:, :] = jnp.zeros((C, VIEWS, plan.lanes), BF16)
    for c in range(C):
        i, start = c // plan.parts, c % plan.parts * plan.lanes
        rows = goal[i, :, start : start + plan.lanes]
        put_views(plan, out, c, X, rows)
    for c in range(C):
        block_copy(c, 0).wait()
        block_copy(c, 1).wait()
        out[c, :X, :] = arriving[c].T.astype(BF16)
    scatter_chunks(out, leaving)


def put_views(plan, out, c, start, rows):
    pad = jnp.zeros((VIEWS - 3 * plan.own_cols, plan.lanes), F32)
    pieces = [piece.astype(F32) for piece in three_pieces(rows)]
    out[c, start : start + VIEWS, :] = jnp.concatenate([*pieces, pad], axis=0).astype(BF16)


def get_views(plan, chunk):
    chunk = chunk.astype(F32)
    n = plan.own_cols
    return chunk[:n] + chunk[n : 2 * n] + chunk[2 * n : 3 * n]


def unpack_kernel(plan, *refs):
    C, m, X = plan.C, plan.m, plan.X
    arrived, (out, light, slabs, leaving, sems) = refs[:C], refs[C:]
    gather_chunks(arrived, slabs)

    def block_copy(c, part):
        return pltpu.make_async_copy(
            leaving.at[c, pl.ds(part * m, m), :],
            out.at[part, pl.ds(c * m, m), :],
            sems.at[2 * c + part],
        )

    for c in range(C):
        leaving[c] = slabs[c, :X, :].astype(F32).T
        block_copy(c, 0).start()
        block_copy(c, 1).start()
    for c in range(C):
        i, start = c // plan.parts, c % plan.parts * plan.lanes
        light[i, :, start : start + plan.lanes] = get_views(plan, slabs[c, X:, :])
    for c in range(C):
        block_copy(c, 0).wait()
        block_copy(c, 1).wait()


def lines_forward(plan, lanes, load, emit, weights, twist, high, low):
    C, X = plan.C, plan.X
    step = 64
    for start in range(0, X, step):
        points = packed_dft([load(c, start, step) for c in range(C)], -1.0)
        for k in range(C):
            cosine = twist[start : start + step, k : k + 1]
            sine = twist[start : start + step, C + k : C + k + 1]
            across = times_i(points[k])
            if k:
                value = points[k] * cosine + across * sine
                across = across * cosine - points[k] * sine
            else:
                value = points[k]
            place = slice(k * lanes, k * lanes + lanes)
            for offset, part in ((0, value), (X, across)):
                part_high, part_low = split(part)
                high[offset + start : offset + start + step, place] = part_high
                low[offset + start : offset + start + step, place] = part_low
    for k in range(C):
        place = slice(k * lanes, k * lanes + lanes)
        both = matmul(weights[...], high[:, place])
        result = both[:X] + both[X:] + matmul(weights[:X, :], low[:, place])
        for r in range(plan.R):
            emit(k * plan.R + r, result[r * plan.span : (r + 1) * plan.span])


def lines_inverse(plan, lanes, packed, turned, emit, weights, twist):
    C, X = plan.C, plan.X
    for k in range(C):
        both = matmul(weights[...], packed[:, k * lanes : (k + 1) * lanes])
        value = both[:X] + both[X:]
        if k:
            value = value * twist[:, k : k + 1] + times_i(value) * twist[:, C + k : C + k + 1]
        turned[k] = value
    step = 64
    for start in range(0, X, step):
        points = [turned[k, start : start + step, :] for k in range(C)]
        for c, value in enumerate(packed_dft(points, 1.0)):
            emit(c, start, step, value)


def trade_halves(first, second):
    half = first.shape[-1] // 2
    low = lax.broadcasted_iota(jnp.int32, first.shape, first.ndim - 1) < half
    return (
        jnp.where(low, first, pltpu.roll(second, half, first.ndim - 1)),
        jnp.where(low, pltpu.roll(first, half, first.ndim - 1), second),
    )


def to_planes(plan, block):
    if plan.P == 2:
        return trade_halves(block[: plan.f], block[plan.f :])
    parts = [block[p * plan.f : (p + 1) * plan.f, :] for p in range(plan.P)]
    real = jnp.concatenate([part[:, : plan.m] for part in parts], axis=1)
    imag = jnp.concatenate([part[:, plan.m :] for part in parts], axis=1)
    return real, imag


def from_planes(plan, real, imag):
    m = plan.m
    if plan.P == 2:
        return jnp.concatenate(trade_halves(real, imag), axis=0)
    return jnp.concatenate(
        [
            jnp.concatenate([real[:, p * m : (p + 1) * m], imag[:, p * m : (p + 1) * m]], axis=1)
            for p in range(plan.P)
        ],
        axis=0,
    )


def rows_forward_kernel(plan, weights, twist, *refs):
    C, X = plan.C, plan.X
    arrived, (_, _, out, goals, high, low, slabs) = refs[:C], refs[C:]
    gather_chunks(arrived, slabs)
    goals[...] = slabs[:, X:, :]

    def load(c, start, step):
        return slabs[c, start : start + step, :].astype(F32)

    def emit(d, block):
        out[d] = jnp.concatenate(to_planes(plan, block), axis=0).astype(BF16)

    lines_forward(plan, plan.lanes, load, emit, weights, twist, high, low)


def rows_inverse_kernel(plan, pencils, lights, weights, twist, *refs):
    C, X, lanes = plan.C, plan.X, plan.lanes
    leaving, (packed, turned, out) = refs[:C], refs[C:]
    for k in range(C):
        for r in range(plan.R):
            chunk = pencils[k * plan.R + r].astype(F32)
            block = from_planes(plan, chunk[: plan.f], chunk[plan.f :])
            place = slice(k * lanes, k * lanes + lanes)
            packed[r * plan.span : (r + 1) * plan.span, place] = block.astype(BF16)
            packed[X + r * plan.span : X + (r + 1) * plan.span, place] = times_i(block).astype(BF16)

    def emit(c, start, step, value):
        out[c, start : start + step, :] = value.astype(BF16)

    lines_inverse(plan, lanes, packed, turned, emit, weights, twist)
    out[:, X:, :] = lights[...]
    scatter_chunks(out, leaving)


def columns(plan, sign, load, store, steer_re, steer_im, ahead, behind, twist, scratch):
    D, f, outer, inner = plan.D, plan.f, plan.outer, plan.inner
    half_re, half_im, high, low = scratch
    for b in range(inner):
        points = [load(inner * a + b) for a in range(outer)]
        for alpha, (re, im) in enumerate(small_dft(points, -1.0)):
            angle = -2.0 * math.pi * b * alpha / D
            cosine, sine = math.cos(angle), math.sin(angle)
            if b * alpha:
                re, im = re * cosine - im * sine, re * sine + im * cosine
            half_re[alpha * inner + b] = re
            half_im[alpha * inner + b] = im
    for alpha in range(outer):
        points = [(half_re[alpha * inner + b], half_im[alpha * inner + b]) for b in range(inner)]
        for beta, (re, im) in enumerate(small_dft(points, -1.0)):
            k = alpha + outer * beta
            cosine, sine = twist[0, k : k + 1, :], twist[1, k : k + 1, :]
            for offset, part in ((0, re * cosine - im * sine), (128, re * sine + im * cosine)):
                part_high, part_low = split(part)
                high[k, :, offset : offset + 128] = part_high
                low[k, :, offset : offset + 128] = part_low
    group = D // 2
    for start in range(0, D, group):
        place = slice(start, start + group)

        def multiply(matrix):
            first = high[place].reshape(group * f, 256)
            second = low[place].reshape(group * f, 256)
            return (
                matmul(first, matrix[:256, :])
                + matmul(second, matrix[:256, :])
                + matmul(first, matrix[256:, :])
            ).reshape(group, f, 256)

        result = multiply(ahead)
        re, im = result[:, :, :128], result[:, :, 128:]
        factor_re, factor_im = steer_re[place], sign * steer_im[place]
        for offset, part in (
            (0, re * factor_re - im * factor_im),
            (128, re * factor_im + im * factor_re),
        ):
            part_high, part_low = split(part)
            high[place, :, offset : offset + 128] = part_high
            low[place, :, offset : offset + 128] = part_low
        result = multiply(behind)
        half_re[place] = result[:, :, :128]
        half_im[place] = result[:, :, 128:]
    for alpha in range(outer):
        points = []
        for beta in range(inner):
            k = alpha + outer * beta
            cosine, sine = twist[0, k : k + 1, :], twist[1, k : k + 1, :]
            re, im = half_re[k], half_im[k]
            points.append((re * cosine + im * sine, im * cosine - re * sine))
        for b, (re, im) in enumerate(small_dft(points, 1.0)):
            angle = 2.0 * math.pi * b * alpha / D
            cosine, sine = math.cos(angle), math.sin(angle)
            if b * alpha:
                re, im = re * cosine - im * sine, re * sine + im * cosine
            half_re[alpha + outer * b] = re
            half_im[alpha + outer * b] = im
    for b in range(inner):
        points = [(half_re[alpha + outer * b], half_im[alpha + outer * b]) for alpha in range(outer)]
        for a, (re, im) in enumerate(small_dft(points, 1.0)):
            store(inner * a + b, re, im)


def pencil_forward_kernel(plan, pencils, *refs):
    steer_re, steer_im, ahead, behind, twist, row, out, windows, *scratch = refs
    f, lanes, span = plan.f, plan.lanes, plan.span

    def load(s):
        chunk = pencils[s].astype(F32)
        return chunk[:f], chunk[f:]

    def store(s, re, im):
        block = from_planes(plan, re, im).astype(BF16)
        i, slab = s // plan.shift, s % plan.shift
        windows[i, :, slab * lanes : (slab + 1) * lanes] = block
        slab += plan.shift
        windows[(i - 1) % plan.hogel_rows, :, slab * lanes : (slab + 1) * lanes] = block

    columns(plan, 1.0, load, store, steer_re, steer_im, ahead, behind, twist, scratch)
    count = plan.hogel_rows
    result = matmul(windows[...].reshape(count * span, 2 * WIN), row[...]).astype(BF16)
    for i in range(count):
        for part in range(plan.parts):
            out[i * plan.parts + part] = result[
                i * span : (i + 1) * span, part * 2 * plan.pp : (part + 1) * 2 * plan.pp
            ]


def pencil_back_kernel(plan, lines, *refs):
    steer_re, steer_im, ahead, behind, twist, row, out, windows, *scratch = refs
    lanes, span, parts = plan.lanes, plan.span, plan.parts
    count, wide = plan.hogel_rows, 2 * plan.pp
    by_part = lines[...].reshape(count, parts, span, wide)
    result = sum(
        matmul(by_part[:, n].reshape(count * span, wide), row[n * wide : (n + 1) * wide, :])
        for n in range(parts)
    )
    windows[...] = result.reshape(count, span, 2 * WIN)

    def load(s):
        i, slab = s // plan.shift, s % plan.shift
        block = windows[i, :, slab * lanes : (slab + 1) * lanes]
        slab += plan.shift
        block = block + windows[(i - 1) % plan.hogel_rows, :, slab * lanes : (slab + 1) * lanes]
        return to_planes(plan, block)

    def store(s, re, im):
        out[s] = jnp.concatenate([re, im], axis=0).astype(BF16)

    columns(plan, -1.0, load, store, steer_re, steer_im, ahead, behind, twist, scratch)


def hogel_kernel(plan, lines, goals, *refs):
    weights_behind, twist_behind, weights_ahead, twist_ahead, col, col_turned, same = refs[:7]
    out, lights, high, low, turned, field, spectra, bright, marks, factors, weighted, back = refs[7:]
    C, X, lanes, pp = plan.C, plan.X, 2 * plan.pp, plan.pp
    total = plan.total_cols
    for k in range(C):
        block = lines[k * plan.R : (k + 1) * plan.R].reshape(X, lanes)
        place = slice(k * lanes, (k + 1) * lanes)
        high[:X, place] = block
        high[X:, place] = times_i(block.astype(F32)).astype(BF16)

    def emit_near(c, start, step, value):
        for n, part in enumerate((value, times_i(value))):
            rounded = part.astype(BF16)
            field[n, c * X + start : c * X + start + step, :] = rounded
            if c == 0 and start < STRIDE:
                field[n, total + start : total + start + step, :] = rounded

    lines_inverse(plan, lanes, high, turned, emit_near, weights_behind, twist_behind)
    for j in range(plan.hogel_cols):
        window = slice(STRIDE * j, STRIDE * j + WIN)
        result = matmul(
            col_turned[...], jnp.concatenate([field[0, window, :], field[1, window, :]], axis=0)
        )
        spectra[j] = result
        power = result[:, :pp] * result[:, :pp] + result[:, pp:] * result[:, pp:]
        bright[j * VIEWS : (j + 1) * VIEWS, :] = power.reshape(VIEWS, BIN, pp).sum(axis=1)
    exact = lax.Precision.HIGHEST
    own = lax.broadcasted_iota(jnp.int32, (VIEWS, pp), 0) == (
        lax.broadcasted_iota(jnp.int32, (VIEWS, pp), 1) % VIEWS
    )
    for c in range(C):
        target = get_views(plan, goals[c])
        for j in range(plan.own_cols):
            h = c * plan.own_cols + j
            marks[h * VIEWS : (h + 1) * VIEWS, :] = jnp.where(own, target[j : j + 1, :], 0.0)
    scale = 1.0 / (BIN * BIN)
    light = scale * jnp.dot(bright[...], same[...], preferred_element_type=F32, precision=exact)
    target = jnp.dot(marks[...], same[...], preferred_element_type=F32, precision=exact)
    factors[...] = 4.0 * (light - target)
    bright[...] = light
    for c in range(C):
        rows = []
        for j in range(plan.own_cols):
            h = c * plan.own_cols + j
            block = jnp.where(own, bright[h * VIEWS : (h + 1) * VIEWS, :], 0.0)
            rows.append(jnp.sum(block, axis=0, keepdims=True))
        put_views(plan, lights, c, 0, jnp.concatenate(rows, axis=0))
    for j in range(plan.hogel_cols):
        for view in range(VIEWS):
            factor = factors[j * VIEWS + view : j * VIEWS + view + 1, :]
            block = slice(view * BIN, (view + 1) * BIN)
            below = slice(WIN + view * BIN, WIN + (view + 1) * BIN)
            real = (spectra[j, block, :pp] * factor).astype(BF16)
            imag = (spectra[j, block, pp:] * factor).astype(BF16)
            weighted[block, :pp] = real
            weighted[block, pp:] = imag
            weighted[below, :pp] = imag
            weighted[below, pp:] = -real
        result = matmul(col[...], weighted[...])
        first, second = STRIDE * j, STRIDE * (j + 1) % total
        if j == 0:
            back[:STRIDE] = result[:STRIDE]
        else:
            back[first : first + STRIDE] = back[first : first + STRIDE] + result[:STRIDE]
        if j < plan.hogel_cols - 1:
            back[second : second + STRIDE] = result[STRIDE:]
        else:
            back[:STRIDE] = back[:STRIDE] + result[STRIDE:]

    def load(c, start, step):
        return back[c * X + start : c * X + start + step, :]

    def emit(d, block):
        out[d] = block.astype(BF16)

    lines_forward(plan, lanes, load, emit, weights_ahead, twist_ahead, high, low)


def steer_table(plan):
    index = lax.axis_index(("rows", "cols"))
    shape = (plan.D, plan.f, 128)
    k = lax.broadcasted_iota(jnp.int32, shape, 0)
    line = lax.broadcasted_iota(jnp.int32, shape, 1)
    lane = lax.broadcasted_iota(jnp.int32, shape, 2)
    u = k + plan.D * (lane % plan.m)
    v = index // plan.R + plan.C * (
        plan.span * (index % plan.R) + plan.f * (lane // plan.m) + line
    )

    def freq(position, count):
        return ((position + count // 2) % count - count // 2).astype(F32) / count

    freq_rows, freq_cols = freq(u, plan.total_rows), freq(v, plan.total_cols)
    radial = freq_rows * freq_rows + freq_cols * freq_cols
    phase = (
        -2.0
        * math.pi
        * distance_px
        * radial
        / (jnp.sqrt(index_ratio * index_ratio - radial) + index_ratio)
    )
    return jnp.cos(phase), jnp.sin(phase)


def exchange(chunks):
    return lax.all_to_all(chunks, ("rows", "cols"), split_axis=0, concat_axis=0, tiled=True)


def swap_columns(chunks):
    count = lax.axis_size("cols")
    return tuple(
        chunk if t == 0 else lax.ppermute(chunk, "cols", [(i, i ^ t) for i in range(count)])
        for t, chunk in enumerate(chunks)
    )


def local(slm_field, target_light):
    rows_count, cols_count = lax.axis_size("rows"), lax.axis_size("cols")
    plan = Plan(rows_count, cols_count, slm_field.shape[1], slm_field.shape[2])
    C, D, X, lanes, f = plan.C, plan.D, plan.X, plan.lanes, plan.f
    span, wide = plan.span, 2 * plan.pp

    ahead, behind, twist = (jnp.asarray(t) for t in plan.pencil_tables())
    weights_ahead, twist_ahead = (jnp.asarray(t) for t in plan.line_tables(-1.0))
    weights_behind, twist_behind = (jnp.asarray(t) for t in plan.line_tables(1.0))
    col, col_turned, row = hogel_tables()
    row = plan.row_table(row[0], row[1])
    col, col_turned, row, row_turned, same = (
        jnp.asarray(t) for t in (col, col_turned, row, row.T.copy(), plan.group_table())
    )
    steer_re, steer_im = steer_table(plan)

    slabs_shapes = (shape_of((X + VIEWS, lanes), BF16),) * C
    slabs_scratch = pltpu.VMEM((C, X + VIEWS, lanes), BF16)
    views_shape = shape_of((C, VIEWS, lanes), BF16)
    pencil_shape = shape_of((D, 2 * f, 128), BF16)
    lines_shape = shape_of((D, span, wide), BF16)
    columns_scratch = (
        pltpu.VMEM((D, f, 128), F32),
        pltpu.VMEM((D, f, 128), F32),
        pltpu.VMEM((D, f, 256), BF16),
        pltpu.VMEM((D, f, 256), BF16),
    )
    pencil_tables = (steer_re, steer_im, ahead, behind, twist)
    columns_flops = 12 * D * f * 256 * 256 + 2 * plan.hogel_rows * span * (2 * WIN) ** 2

    apart = pl.BlockSpec(memory_space=pltpu.HBM)
    apart_any = pl.BlockSpec(memory_space=pl.ANY)
    blocks_scratch = (pltpu.VMEM((C, lanes, X), F32), pltpu.SemaphoreType.DMA((2 * C,)))
    slabs = call(
        lambda *refs: pack_kernel(plan, *refs),
        slabs_shapes,
        (slm_field, target_light),
        (slabs_scratch, *blocks_scratch),
        in_specs={0: apart},
    )
    tall = pltpu.VMEM((2 * X, C * lanes), BF16)
    pencils, goals = call(
        lambda *refs: rows_forward_kernel(plan, *refs),
        (pencil_shape, views_shape),
        (weights_ahead, twist_ahead, *swap_columns(slabs), steer_re, steer_im),
        (tall, tall, slabs_scratch),
        flops=6 * X * 2 * X * C * lanes,
        in_specs={C + 2: apart_any, C + 3: apart_any},
    )
    (lines,) = call(
        lambda *refs: pencil_forward_kernel(plan, *refs),
        (lines_shape,),
        (exchange(pencils), *pencil_tables, row),
        (pltpu.VMEM((plan.hogel_rows, span, 2 * WIN), BF16), *columns_scratch),
        flops=columns_flops,
    )
    tall = pltpu.VMEM((2 * X, C * wide), BF16)
    lines, lights = call(
        lambda *refs: hogel_kernel(plan, *refs),
        (lines_shape, views_shape),
        (
            exchange(lines),
            goals,
            weights_behind,
            twist_behind,
            weights_ahead,
            twist_ahead,
            col,
            col_turned,
            same,
        ),
        (
            tall,
            tall,
            pltpu.VMEM((C, X, wide), F32),
            pltpu.VMEM((2, plan.total_cols + STRIDE, wide), BF16),
            pltpu.VMEM((plan.hogel_cols, WIN, wide), F32),
            pltpu.VMEM((plan.hogel_cols * VIEWS, plan.pp), F32),
            pltpu.VMEM((plan.hogel_cols * VIEWS, plan.pp), F32),
            pltpu.VMEM((plan.hogel_cols * VIEWS, plan.pp), F32),
            pltpu.VMEM((2 * WIN, wide), BF16),
            pltpu.VMEM((plan.total_cols, wide), F32),
        ),
        flops=10 * X * 2 * X * C * wide + 4 * plan.hogel_cols * WIN * 2 * WIN * wide,
    )
    (pencils,) = call(
        lambda *refs: pencil_back_kernel(plan, *refs),
        (pencil_shape,),
        (exchange(lines), *pencil_tables, row_turned),
        (pltpu.VMEM((plan.hogel_rows, span, 2 * WIN), F32), *columns_scratch),
        flops=columns_flops,
    )
    tall = pltpu.VMEM((2 * X, C * lanes), BF16)
    slabs = call(
        lambda *refs: rows_inverse_kernel(plan, *refs),
        slabs_shapes,
        (exchange(pencils), lights, weights_behind, twist_behind),
        (tall, pltpu.VMEM((C, X, lanes), F32), slabs_scratch),
        flops=4 * X * 2 * X * C * lanes,
    )
    return call(
        lambda *refs: unpack_kernel(plan, *refs),
        (shape_of(slm_field.shape, F32), shape_of(target_light.shape, F32)),
        swap_columns(slabs),
        (slabs_scratch, *blocks_scratch),
        out_specs=(apart, pl.BlockSpec(memory_space=pltpu.VMEM)),
    )


def solution(mesh):
    return jax.shard_map(
        local,
        mesh=mesh,
        in_specs=(P(None, "rows", "cols"), P("rows", "cols", None)),
        out_specs=(P(None, "rows", "cols"), P("rows", "cols", None)),
        check_vma=False,
    )
```

```python
import math

import jax
import jax.numpy as jnp
import ml_dtypes
import numpy as np
from jax import lax
from jax.experimental import pallas as pl
from jax.experimental.pallas import tpu as pltpu
from jax.sharding import PartitionSpec as P

WIN = 256
VIEWS = 16
STRIDE = 128
BIN = 16

distance_px = 16000.0
index_ratio = 15.0

BF16 = jnp.bfloat16
F32 = jnp.float32
BOTH_MINOR = (((1,), (1,)), ((), ()))


def call(body, outs, args, scratch=(), flops=0, in_specs=None, out_specs=None):
    nbytes = sum(math.prod(a.shape) * a.dtype.itemsize for a in (*outs, *args))
    specs = {}
    if in_specs:
        whole = pl.BlockSpec(memory_space=pltpu.VMEM)
        specs["in_specs"] = [in_specs.get(n, whole) for n in range(len(args))]
    if out_specs:
        specs["out_specs"] = out_specs
    return pl.pallas_call(
        body,
        out_shape=outs,
        scratch_shapes=list(scratch),
        compiler_params=pltpu.CompilerParams(vmem_limit_bytes=24 * 2**20),
        cost_estimate=pl.CostEstimate(flops=flops, bytes_accessed=nbytes, transcendentals=0),
        **specs,
    )(*args)


def shape_of(dims, dtype):
    return jax.ShapeDtypeStruct(dims, dtype)


def high_low(table):
    table = np.asarray(table, np.float32)
    high = table.astype(ml_dtypes.bfloat16)
    low = (table - high.astype(np.float32)).astype(ml_dtypes.bfloat16)
    return np.concatenate([high, low], axis=0)


def split(values):
    high = values.astype(BF16)
    return high, (values - high.astype(F32)).astype(BF16)


def times_i(values):
    half = values.shape[-1] // 2
    if values.shape[-1] == 128:
        lanes = lax.broadcasted_iota(jnp.int32, values.shape, values.ndim - 1)
        turned = pltpu.roll(values, half, values.ndim - 1)
        return jnp.where(lanes < half, -turned, turned)
    return jnp.concatenate([-values[..., half:], values[..., :half]], axis=-1)


def scaled(value, factor):
    return value if factor == 1.0 else value * factor


def small_dft(points, sign):
    count = len(points)
    if count == 1:
        return points
    even = small_dft(points[0::2], sign)
    odd = small_dft(points[1::2], sign)
    front, back = [], []
    for k in range(count // 2):
        re, im = odd[k]
        angle = sign * 2.0 * math.pi * k / count
        cosine, sine = math.cos(angle), math.sin(angle)
        if k == 0:
            pass
        elif 4 * k == count:
            re, im = (-im, re) if sign > 0 else (im, -re)
        elif 8 * k == count:
            re, im = cosine * (re - sign * im), cosine * (im + sign * re)
        elif 8 * k == 3 * count:
            re, im = cosine * (re + sign * im), cosine * (im - sign * re)
        else:
            re, im = re * cosine - im * sine, re * sine + im * cosine
        even_re, even_im = even[k]
        front.append((even_re + re, even_im + im))
        back.append((even_re - re, even_im - im))
    return front + back


def packed_dft(points, sign):
    count = len(points)
    if count == 1:
        return points
    even = packed_dft(points[0::2], sign)
    odd = packed_dft(points[1::2], sign)
    front, back = [], []
    for k in range(count // 2):
        term = odd[k]
        angle = sign * 2.0 * math.pi * k / count
        if 4 * k == count:
            term = times_i(term) if sign > 0 else -times_i(term)
        elif k:
            term = math.cos(angle) * term + math.sin(angle) * times_i(term)
        front.append(even[k] + term)
        back.append(even[k] - term)
    return front + back


def turn(rows, cols, period, sign):
    angles = sign * 2.0 * np.pi / period * ((np.arange(rows)[:, None] * np.arange(cols)) % period)
    return np.cos(angles), np.sin(angles)


def block_diagonal(block, copies):
    return np.kron(np.eye(copies), block)


class Plan:
    def __init__(self, rows_count, cols_count, rows_dev, cols_dev):
        self.R, self.C = rows_count, cols_count
        self.D = rows_count * cols_count
        self.X = cols_dev
        self.m = rows_dev // cols_count
        self.lanes = 2 * self.m
        self.P = 128 // self.m
        self.span = cols_dev // rows_count
        self.f = self.span // self.P
        self.total_rows = rows_dev * rows_count
        self.total_cols = cols_dev * cols_count
        self.outer = 8
        self.inner = self.D // 8
        self.shift = STRIDE // self.m
        self.hogel_rows = self.total_rows // STRIDE
        self.hogel_cols = self.total_cols // STRIDE
        self.parts = self.D // self.hogel_rows
        self.pp = WIN // self.parts
        self.views = VIEWS // self.parts
        self.own_cols = cols_dev // STRIDE

    def line_tables(self, sign):
        cosine, sine = turn(self.X, self.X, self.X, sign)
        weights = np.concatenate([cosine, sine], axis=1).astype(ml_dtypes.bfloat16)
        twist = turn(self.X, self.C, self.total_cols, sign)
        return weights, np.concatenate(twist, axis=1).astype(np.float32)

    def pencil_tables(self):
        cosine, sine = turn(self.m, self.m, self.m, -1.0)
        cosine, sine = block_diagonal(cosine, self.P), block_diagonal(sine, self.P)
        ahead = np.block([[cosine, sine], [-sine, cosine]])
        behind = np.block([[cosine, -sine], [sine, cosine]]) / (self.total_rows * self.total_cols)
        twist = turn(self.D, self.m, self.total_rows, -1.0)
        twist = np.stack([np.tile(part, (1, self.P)) for part in twist]).astype(np.float32)
        return high_low(ahead), high_low(behind), twist

    def row_table(self, real, imag):
        blocks = []
        for slab in range(WIN // self.m):
            rows = slice(slab * self.m, (slab + 1) * self.m)
            for left, right in ((real[rows], imag[rows]), (-imag[rows], real[rows])):
                pieces = []
                for part in range(self.parts):
                    cols = slice(part * self.pp, (part + 1) * self.pp)
                    pieces += [left[:, cols], right[:, cols]]
                blocks.append(np.concatenate(pieces, axis=1))
        return np.concatenate(blocks, axis=0)

    def group_table(self):
        return np.kron(np.eye(self.views), np.ones((BIN, BIN))).astype(np.float32)


def hogel_tables():
    positions = np.arange(WIN)
    tapers = np.sin(np.pi * (positions + 0.5) / WIN) ** 2
    angles = -2.0 * np.pi / WIN * (positions[:, None] * positions[None, :] % WIN)
    cosine = (tapers[:, None] * np.cos(angles)).astype(np.float32)
    sine = (tapers[:, None] * np.sin(angles)).astype(np.float32)
    col = np.concatenate([cosine, sine], axis=1).astype(ml_dtypes.bfloat16)
    col_turned = np.concatenate([cosine.T, sine.T], axis=1).astype(ml_dtypes.bfloat16)
    row = np.stack([cosine / WIN, sine / WIN]).astype(ml_dtypes.bfloat16)
    return col, col_turned, row


def matmul(left, right):
    return jnp.dot(left, right, preferred_element_type=F32)


def gather_chunks(arrived, chunks):
    mine = lax.axis_index("cols")
    for t, chunk in enumerate(arrived):
        chunks[mine ^ t] = chunk[...]


def scatter_chunks(chunks, leaving):
    mine = lax.axis_index("cols")
    for t, chunk in enumerate(leaving):
        chunk[...] = chunks[mine ^ t]


def pack_kernel(plan, field, *refs):
    C, m = plan.C, plan.m
    leaving, (out,) = refs[:C], refs[C:]
    for c in range(C):
        rows = slice(c * m, (c + 1) * m)
        out[c] = jnp.concatenate([field[0, rows, :], field[1, rows, :]], axis=0).T.astype(BF16)
    scatter_chunks(out, leaving)


def unpack_kernel(plan, lights, *refs):
    C, m = plan.C, plan.m
    arrived, (out, light, slabs) = refs[:C], refs[C:]
    gather_chunks(arrived, slabs)
    for c in range(C):
        block = slabs[c].astype(F32).T
        out[0, m * c : m * c + m, :] = block[:m]
        out[1, m * c : m * c + m, :] = block[m:]
    mine = lax.axis_index("cols")
    for c in range(C):
        i, start = c // plan.parts, c % plan.parts * plan.lanes
        light[i, :, start : start + plan.lanes] = lights[c, mine]


def lines_forward(plan, lanes, load, emit, weights, twist, turned):
    C, X = plan.C, plan.X
    step = 64
    for start in range(0, X, step):
        points = packed_dft([load(c, start, step) for c in range(C)], -1.0)
        for k in range(C):
            cosine = twist[start : start + step, k : k + 1]
            sine = twist[start : start + step, C + k : C + k + 1]
            across = times_i(points[k])
            if k:
                value = points[k] * cosine + across * sine
                across = across * cosine - points[k] * sine
            else:
                value = points[k]
            place = slice(k * lanes, k * lanes + lanes)
            turned[start : start + step, place] = value.astype(BF16)
            turned[X + start : X + start + step, place] = across.astype(BF16)
    group = max(1, 256 // lanes)
    for first in range(0, C, group):
        result = matmul(weights[...], turned[:, first * lanes : (first + group) * lanes])
        for k in range(group):
            for r in range(plan.R):
                rows = slice(r * plan.span, (r + 1) * plan.span)
                emit((first + k) * plan.R + r, result[rows, k * lanes : (k + 1) * lanes])


def lines_inverse(plan, lanes, packed, turned, emit, weights, twist):
    C, X = plan.C, plan.X
    group = max(1, 256 // lanes)
    for first in range(0, C, group):
        result = matmul(weights[...], packed[:, first * lanes : (first + group) * lanes])
        for k in range(first, first + group):
            value = result[:, (k - first) * lanes : (k - first + 1) * lanes]
            if k:
                value = value * twist[:, k : k + 1] + times_i(value) * twist[:, C + k : C + k + 1]
            turned[k] = value
    step = 64
    for start in range(0, X, step):
        points = [turned[k, start : start + step, :] for k in range(C)]
        for c, value in enumerate(packed_dft(points, 1.0)):
            emit(c, start, step, value)


def trade_halves(first, second):
    half = first.shape[-1] // 2
    low = lax.broadcasted_iota(jnp.int32, first.shape, first.ndim - 1) < half
    return (
        jnp.where(low, first, pltpu.roll(second, half, first.ndim - 1)),
        jnp.where(low, pltpu.roll(first, half, first.ndim - 1), second),
    )


def to_planes(plan, block):
    if plan.P == 2:
        return trade_halves(block[: plan.f], block[plan.f :])
    parts = [block[p * plan.f : (p + 1) * plan.f, :] for p in range(plan.P)]
    real = jnp.concatenate([part[:, : plan.m] for part in parts], axis=1)
    imag = jnp.concatenate([part[:, plan.m :] for part in parts], axis=1)
    return real, imag


def from_planes(plan, real, imag):
    m = plan.m
    if plan.P == 2:
        return jnp.concatenate(trade_halves(real, imag), axis=0)
    return jnp.concatenate(
        [
            jnp.concatenate([real[:, p * m : (p + 1) * m], imag[:, p * m : (p + 1) * m]], axis=1)
            for p in range(plan.P)
        ],
        axis=0,
    )


def rows_forward_kernel(plan, weights, twist, *refs):
    C = plan.C
    arrived, (_, _, out, turned, slabs) = refs[:C], refs[C:]
    gather_chunks(arrived, slabs)

    def load(c, start, step):
        return slabs[c, start : start + step, :].astype(F32)

    def emit(d, block):
        out[d] = jnp.concatenate(to_planes(plan, block), axis=0).astype(BF16)

    lines_forward(plan, plan.lanes, load, emit, weights, twist, turned)


def rows_inverse_kernel(plan, pencils, weights, twist, *refs):
    C, X, lanes = plan.C, plan.X, plan.lanes
    leaving, (packed, turned, out) = refs[:C], refs[C:]
    for k in range(C):
        for r in range(plan.R):
            chunk = pencils[k * plan.R + r].astype(F32)
            block = from_planes(plan, chunk[: plan.f], chunk[plan.f :])
            place = slice(k * lanes, k * lanes + lanes)
            packed[r * plan.span : (r + 1) * plan.span, place] = block.astype(BF16)
            packed[X + r * plan.span : X + (r + 1) * plan.span, place] = times_i(block).astype(BF16)

    def emit(c, start, step, value):
        out[c, start : start + step, :] = value.astype(BF16)

    lines_inverse(plan, lanes, packed, turned, emit, weights, twist)
    scatter_chunks(out, leaving)


def columns(plan, sign, load, store, steer_re, steer_im, ahead, behind, twist, scratch):
    D, f, outer, inner = plan.D, plan.f, plan.outer, plan.inner
    half_re, half_im, high, low = scratch
    for b in range(inner):
        points = [load(inner * a + b) for a in range(outer)]
        for alpha, (re, im) in enumerate(small_dft(points, -1.0)):
            angle = -2.0 * math.pi * b * alpha / D
            cosine, sine = math.cos(angle), math.sin(angle)
            if b * alpha:
                re, im = re * cosine - im * sine, re * sine + im * cosine
            half_re[alpha * inner + b] = re
            half_im[alpha * inner + b] = im
    for alpha in range(outer):
        points = [(half_re[alpha * inner + b], half_im[alpha * inner + b]) for b in range(inner)]
        for beta, (re, im) in enumerate(small_dft(points, -1.0)):
            k = alpha + outer * beta
            cosine, sine = twist[0, k : k + 1, :], twist[1, k : k + 1, :]
            for offset, part in ((0, re * cosine - im * sine), (128, re * sine + im * cosine)):
                part_high, part_low = split(part)
                high[k, :, offset : offset + 128] = part_high
                low[k, :, offset : offset + 128] = part_low
    group = D // 2
    for start in range(0, D, group):
        place = slice(start, start + group)

        def multiply(matrix):
            first = high[place].reshape(group * f, 256)
            second = low[place].reshape(group * f, 256)
            return (
                matmul(first, matrix[:256, :])
                + matmul(second, matrix[:256, :])
                + matmul(first, matrix[256:, :])
            ).reshape(group, f, 256)

        result = multiply(ahead)
        re, im = result[:, :, :128], result[:, :, 128:]
        factor_re, factor_im = steer_re[place], sign * steer_im[place]
        for offset, part in (
            (0, re * factor_re - im * factor_im),
            (128, re * factor_im + im * factor_re),
        ):
            part_high, part_low = split(part)
            high[place, :, offset : offset + 128] = part_high
            low[place, :, offset : offset + 128] = part_low
        result = multiply(behind)
        half_re[place] = result[:, :, :128]
        half_im[place] = result[:, :, 128:]
    for alpha in range(outer):
        points = []
        for beta in range(inner):
            k = alpha + outer * beta
            cosine, sine = twist[0, k : k + 1, :], twist[1, k : k + 1, :]
            re, im = half_re[k], half_im[k]
            points.append((re * cosine + im * sine, im * cosine - re * sine))
        for b, (re, im) in enumerate(small_dft(points, 1.0)):
            angle = 2.0 * math.pi * b * alpha / D
            cosine, sine = math.cos(angle), math.sin(angle)
            if b * alpha:
                re, im = re * cosine - im * sine, re * sine + im * cosine
            half_re[alpha + outer * b] = re
            half_im[alpha + outer * b] = im
    for b in range(inner):
        points = [(half_re[alpha + outer * b], half_im[alpha + outer * b]) for alpha in range(outer)]
        for a, (re, im) in enumerate(small_dft(points, 1.0)):
            store(inner * a + b, re, im)


def pencil_forward_kernel(plan, pencils, *refs):
    steer_re, steer_im, ahead, behind, twist, row, out, windows, *scratch = refs
    f, lanes, span = plan.f, plan.lanes, plan.span

    def load(s):
        chunk = pencils[s].astype(F32)
        return chunk[:f], chunk[f:]

    def store(s, re, im):
        block = from_planes(plan, re, im).astype(BF16)
        i, slab = s // plan.shift, s % plan.shift
        windows[i, :, slab * lanes : (slab + 1) * lanes] = block
        slab += plan.shift
        windows[(i - 1) % plan.hogel_rows, :, slab * lanes : (slab + 1) * lanes] = block

    columns(plan, 1.0, load, store, steer_re, steer_im, ahead, behind, twist, scratch)
    count = plan.hogel_rows
    result = matmul(windows[...].reshape(count * span, 2 * WIN), row[...]).astype(BF16)
    for i in range(count):
        for part in range(plan.parts):
            out[i * plan.parts + part] = result[
                i * span : (i + 1) * span, part * 2 * plan.pp : (part + 1) * 2 * plan.pp
            ]


def pencil_back_kernel(plan, lines, *refs):
    steer_re, steer_im, ahead, behind, twist, row, out, windows, *scratch = refs
    lanes, span, parts = plan.lanes, plan.span, plan.parts
    count, wide = plan.hogel_rows, 2 * plan.pp
    by_part = lines[...].reshape(count, parts, span, wide)
    result = sum(
        matmul(by_part[:, n].reshape(count * span, wide), row[n * wide : (n + 1) * wide, :])
        for n in range(parts)
    )
    windows[...] = result.reshape(count, span, 2 * WIN)

    def load(s):
        i, slab = s // plan.shift, s % plan.shift
        block = windows[i, :, slab * lanes : (slab + 1) * lanes]
        slab += plan.shift
        block = block + windows[(i - 1) % plan.hogel_rows, :, slab * lanes : (slab + 1) * lanes]
        return to_planes(plan, block)

    def store(s, re, im):
        out[s] = jnp.concatenate([re, im], axis=0).astype(BF16)

    columns(plan, -1.0, load, store, steer_re, steer_im, ahead, behind, twist, scratch)


def hogel_kernel(plan, lines, goals, *refs):
    weights_behind, twist_behind, weights_ahead, twist_ahead, col, col_turned, same = refs[:7]
    out, lights, packed, turned, field, spectra, bright, marks, factors, weighted, back = refs[7:]
    C, X, lanes, pp = plan.C, plan.X, 2 * plan.pp, plan.pp
    total = plan.total_cols
    for k in range(C):
        block = lines[k * plan.R : (k + 1) * plan.R].reshape(X, lanes)
        place = slice(k * lanes, (k + 1) * lanes)
        packed[:X, place] = block
        packed[X:, place] = times_i(block.astype(F32)).astype(BF16)

    def emit_near(c, start, step, value):
        for n, part in enumerate((value, times_i(value))):
            rounded = part.astype(BF16)
            field[n, c * X + start : c * X + start + step, :] = rounded
            if c == 0 and start < STRIDE:
                field[n, total + start : total + start + step, :] = rounded

    lines_inverse(plan, lanes, packed, turned, emit_near, weights_behind, twist_behind)
    for j in range(plan.hogel_cols):
        window = slice(STRIDE * j, STRIDE * j + WIN)
        result = matmul(
            col_turned[...], jnp.concatenate([field[0, window, :], field[1, window, :]], axis=0)
        )
        spectra[j] = result
        power = result[:, :pp] * result[:, :pp] + result[:, pp:] * result[:, pp:]
        bright[j * VIEWS : (j + 1) * VIEWS, :] = power.reshape(VIEWS, BIN, pp).sum(axis=1)
    exact = lax.Precision.HIGHEST
    own = lax.broadcasted_iota(jnp.int32, (VIEWS, pp), 0) == (
        lax.broadcasted_iota(jnp.int32, (VIEWS, pp), 1) % VIEWS
    )
    mine = lax.axis_index("cols")
    row, part = mine // plan.parts, mine % plan.parts
    for c in range(C):
        band = goals[c, row]
        target = band[:, :pp]
        for n in range(1, plan.parts):
            target = jnp.where(part == n, band[:, n * pp : (n + 1) * pp], target)
        for j in range(plan.own_cols):
            h = c * plan.own_cols + j
            marks[h * VIEWS : (h + 1) * VIEWS, :] = jnp.where(own, target[j : j + 1, :], 0.0)
    scale = 1.0 / (BIN * BIN)
    light = scale * jnp.dot(bright[...], same[...], preferred_element_type=F32, precision=exact)
    target = jnp.dot(marks[...], same[...], preferred_element_type=F32, precision=exact)
    factors[...] = 4.0 * (light - target)
    bright[...] = light
    for c in range(C):
        for j in range(plan.own_cols):
            h = c * plan.own_cols + j
            block = jnp.where(own, bright[h * VIEWS : (h + 1) * VIEWS, :], 0.0)
            lights[c, j : j + 1, :] = jnp.sum(block, axis=0, keepdims=True)
    for j in range(plan.hogel_cols):
        for view in range(VIEWS):
            factor = factors[j * VIEWS + view : j * VIEWS + view + 1, :]
            block = slice(view * BIN, (view + 1) * BIN)
            below = slice(WIN + view * BIN, WIN + (view + 1) * BIN)
            real = (spectra[j, block, :pp] * factor).astype(BF16)
            imag = (spectra[j, block, pp:] * factor).astype(BF16)
            weighted[block, :pp] = real
            weighted[block, pp:] = imag
            weighted[below, :pp] = imag
            weighted[below, pp:] = -real
        result = matmul(col[...], weighted[...])
        first, second = STRIDE * j, STRIDE * (j + 1) % total
        if j == 0:
            back[:STRIDE] = result[:STRIDE]
        else:
            back[first : first + STRIDE] = back[first : first + STRIDE] + result[:STRIDE]
        if j < plan.hogel_cols - 1:
            back[second : second + STRIDE] = result[STRIDE:]
        else:
            back[:STRIDE] = back[:STRIDE] + result[STRIDE:]

    def load(c, start, step):
        return back[c * X + start : c * X + start + step, :]

    def emit(d, block):
        out[d] = block.astype(BF16)

    lines_forward(plan, lanes, load, emit, weights_ahead, twist_ahead, packed)


def steer_table(plan):
    index = lax.axis_index(("rows", "cols"))
    shape = (plan.D, plan.f, 128)
    k = lax.broadcasted_iota(jnp.int32, shape, 0)
    line = lax.broadcasted_iota(jnp.int32, shape, 1)
    lane = lax.broadcasted_iota(jnp.int32, shape, 2)
    u = k + plan.D * (lane % plan.m)
    v = index // plan.R + plan.C * (
        plan.span * (index % plan.R) + plan.f * (lane // plan.m) + line
    )

    def freq(position, count):
        return ((position + count // 2) % count - count // 2).astype(F32) / count

    freq_rows, freq_cols = freq(u, plan.total_rows), freq(v, plan.total_cols)
    radial = freq_rows * freq_rows + freq_cols * freq_cols
    phase = (
        -2.0
        * math.pi
        * distance_px
        * radial
        / (jnp.sqrt(index_ratio * index_ratio - radial) + index_ratio)
    )
    return jnp.cos(phase), jnp.sin(phase)


def exchange(chunks):
    return lax.all_to_all(chunks, ("rows", "cols"), split_axis=0, concat_axis=0, tiled=True)


def swap_columns(chunks):
    count = lax.axis_size("cols")
    return tuple(
        chunk if t == 0 else lax.ppermute(chunk, "cols", [(i, i ^ t) for i in range(count)])
        for t, chunk in enumerate(chunks)
    )


def local(slm_field, target_light):
    rows_count, cols_count = lax.axis_size("rows"), lax.axis_size("cols")
    plan = Plan(rows_count, cols_count, slm_field.shape[1], slm_field.shape[2])
    C, D, X, lanes, f = plan.C, plan.D, plan.X, plan.lanes, plan.f
    span, wide = plan.span, 2 * plan.pp

    ahead, behind, twist = (jnp.asarray(t) for t in plan.pencil_tables())
    weights_ahead, twist_ahead = (jnp.asarray(t) for t in plan.line_tables(-1.0))
    weights_behind, twist_behind = (jnp.asarray(t) for t in plan.line_tables(1.0))
    col, col_turned, row = hogel_tables()
    row = plan.row_table(row[0], row[1])
    col, col_turned, row, row_turned, same = (
        jnp.asarray(t) for t in (col, col_turned, row, row.T.copy(), plan.group_table())
    )
    steer_re, steer_im = steer_table(plan)

    slabs_shapes = (shape_of((X, lanes), BF16),) * C
    slabs_scratch = pltpu.VMEM((C, X, lanes), BF16)
    lights_shape = shape_of((C, plan.own_cols, plan.pp), F32)
    pencil_shape = shape_of((D, 2 * f, 128), BF16)
    lines_shape = shape_of((D, span, wide), BF16)
    columns_scratch = (
        pltpu.VMEM((D, f, 128), F32),
        pltpu.VMEM((D, f, 128), F32),
        pltpu.VMEM((D, f, 256), BF16),
        pltpu.VMEM((D, f, 256), BF16),
    )
    pencil_tables = (steer_re, steer_im, ahead, behind, twist)
    columns_flops = 12 * D * f * 256 * 256 + 2 * plan.hogel_rows * span * (2 * WIN) ** 2

    apart_any = pl.BlockSpec(memory_space=pl.ANY)
    slabs = call(
        lambda *refs: pack_kernel(plan, *refs), slabs_shapes, (slm_field,), (slabs_scratch,)
    )
    tall = pltpu.VMEM((2 * X, C * lanes), BF16)
    (pencils,) = call(
        lambda *refs: rows_forward_kernel(plan, *refs),
        (pencil_shape,),
        (weights_ahead, twist_ahead, *swap_columns(slabs), steer_re, steer_im),
        (tall, slabs_scratch),
        flops=2 * X * 2 * X * C * lanes,
        in_specs={C + 2: apart_any, C + 3: apart_any},
    )
    (lines,) = call(
        lambda *refs: pencil_forward_kernel(plan, *refs),
        (lines_shape,),
        (exchange(pencils), *pencil_tables, row),
        (pltpu.VMEM((plan.hogel_rows, span, 2 * WIN), BF16), *columns_scratch),
        flops=columns_flops,
    )
    tall = pltpu.VMEM((2 * X, C * wide), BF16)
    lines, lights = call(
        lambda *refs: hogel_kernel(plan, *refs),
        (lines_shape, lights_shape),
        (
            exchange(lines),
            lax.all_gather(target_light, "cols"),
            weights_behind,
            twist_behind,
            weights_ahead,
            twist_ahead,
            col,
            col_turned,
            same,
        ),
        (
            tall,
            pltpu.VMEM((C, X, wide), F32),
            pltpu.VMEM((2, plan.total_cols + STRIDE, wide), BF16),
            pltpu.VMEM((plan.hogel_cols, WIN, wide), F32),
            pltpu.VMEM((plan.hogel_cols * VIEWS, plan.pp), F32),
            pltpu.VMEM((plan.hogel_cols * VIEWS, plan.pp), F32),
            pltpu.VMEM((plan.hogel_cols * VIEWS, plan.pp), F32),
            pltpu.VMEM((2 * WIN, wide), BF16),
            pltpu.VMEM((plan.total_cols, wide), F32),
        ),
        flops=4 * X * 2 * X * C * wide + 4 * plan.hogel_cols * WIN * 2 * WIN * wide,
    )
    (pencils,) = call(
        lambda *refs: pencil_back_kernel(plan, *refs),
        (pencil_shape,),
        (exchange(lines), *pencil_tables, row_turned),
        (pltpu.VMEM((plan.hogel_rows, span, 2 * WIN), F32), *columns_scratch),
        flops=columns_flops,
    )
    tall = pltpu.VMEM((2 * X, C * lanes), BF16)
    slabs = call(
        lambda *refs: rows_inverse_kernel(plan, *refs),
        slabs_shapes,
        (exchange(pencils), weights_behind, twist_behind),
        (tall, pltpu.VMEM((C, X, lanes), F32), slabs_scratch),
        flops=2 * X * 2 * X * C * lanes,
    )
    return call(
        lambda *refs: unpack_kernel(plan, *refs),
        (shape_of(slm_field.shape, F32), shape_of(target_light.shape, F32)),
        (lax.all_gather(lights, "cols"), *swap_columns(slabs)),
        (slabs_scratch,),
    )


def solution(mesh):
    return jax.shard_map(
        local,
        mesh=mesh,
        in_specs=(P(None, "rows", "cols"), P("rows", "cols", None)),
        out_specs=(P(None, "rows", "cols"), P("rows", "cols", None)),
        check_vma=False,
    )
```

```python
import math

import jax
import jax.numpy as jnp
import ml_dtypes
import numpy as np
from jax import lax
from jax.experimental import pallas as pl
from jax.experimental.pallas import tpu as pltpu
from jax.sharding import PartitionSpec as P

WIN = 256
VIEWS = 16
STRIDE = 128
BIN = 16

distance_px = 16000.0
index_ratio = 15.0

BF16 = jnp.bfloat16
F32 = jnp.float32
BOTH_MINOR = (((1,), (1,)), ((), ()))


def call(body, outs, args, scratch=(), flops=0, in_specs=None, out_specs=None):
    nbytes = sum(math.prod(a.shape) * a.dtype.itemsize for a in (*outs, *args))
    specs = {}
    if in_specs:
        whole = pl.BlockSpec(memory_space=pltpu.VMEM)
        specs["in_specs"] = [in_specs.get(n, whole) for n in range(len(args))]
    if out_specs:
        specs["out_specs"] = out_specs
    return pl.pallas_call(
        body,
        out_shape=outs,
        scratch_shapes=list(scratch),
        compiler_params=pltpu.CompilerParams(vmem_limit_bytes=24 * 2**20),
        cost_estimate=pl.CostEstimate(flops=flops, bytes_accessed=nbytes, transcendentals=0),
        **specs,
    )(*args)


def shape_of(dims, dtype):
    return jax.ShapeDtypeStruct(dims, dtype)


def high_low(table):
    table = np.asarray(table, np.float32)
    high = table.astype(ml_dtypes.bfloat16)
    low = (table - high.astype(np.float32)).astype(ml_dtypes.bfloat16)
    return np.concatenate([high, low], axis=0)


def times_i(values):
    half = values.shape[-1] // 2
    if values.shape[-1] == 128:
        lanes = lax.broadcasted_iota(jnp.int32, values.shape, values.ndim - 1)
        turned = pltpu.roll(values, half, values.ndim - 1)
        return jnp.where(lanes < half, -turned, turned)
    return jnp.concatenate([-values[..., half:], values[..., :half]], axis=-1)


def scaled(value, factor):
    return value if factor == 1.0 else value * factor


def small_dft(points, sign):
    count = len(points)
    if count == 1:
        return points
    even = small_dft(points[0::2], sign)
    odd = small_dft(points[1::2], sign)
    front, back = [], []
    for k in range(count // 2):
        re, im = odd[k]
        angle = sign * 2.0 * math.pi * k / count
        cosine, sine = math.cos(angle), math.sin(angle)
        if k == 0:
            pass
        elif 4 * k == count:
            re, im = (-im, re) if sign > 0 else (im, -re)
        elif 8 * k == count:
            re, im = cosine * (re - sign * im), cosine * (im + sign * re)
        elif 8 * k == 3 * count:
            re, im = cosine * (re + sign * im), cosine * (im - sign * re)
        else:
            re, im = re * cosine - im * sine, re * sine + im * cosine
        even_re, even_im = even[k]
        front.append((even_re + re, even_im + im))
        back.append((even_re - re, even_im - im))
    return front + back


def packed_dft(points, sign):
    count = len(points)
    if count == 1:
        return points
    even = packed_dft(points[0::2], sign)
    odd = packed_dft(points[1::2], sign)
    front, back = [], []
    for k in range(count // 2):
        term = odd[k]
        angle = sign * 2.0 * math.pi * k / count
        if 4 * k == count:
            term = times_i(term) if sign > 0 else -times_i(term)
        elif k:
            term = math.cos(angle) * term + math.sin(angle) * times_i(term)
        front.append(even[k] + term)
        back.append(even[k] - term)
    return front + back


def turn(rows, cols, period, sign):
    angles = sign * 2.0 * np.pi / period * ((np.arange(rows)[:, None] * np.arange(cols)) % period)
    return np.cos(angles), np.sin(angles)


def block_diagonal(block, copies):
    return np.kron(np.eye(copies), block)


class Plan:
    def __init__(self, rows_count, cols_count, rows_dev, cols_dev):
        self.R, self.C = rows_count, cols_count
        self.D = rows_count * cols_count
        self.X = cols_dev
        self.m = rows_dev // cols_count
        self.lanes = 2 * self.m
        self.P = 128 // self.m
        self.span = cols_dev // rows_count
        self.f = self.span // self.P
        self.total_rows = rows_dev * rows_count
        self.total_cols = cols_dev * cols_count
        self.outer = 8
        self.inner = self.D // 8
        self.shift = STRIDE // self.m
        self.hogel_rows = self.total_rows // STRIDE
        self.hogel_cols = self.total_cols // STRIDE
        self.parts = self.D // self.hogel_rows
        self.pp = WIN // self.parts
        self.views = VIEWS // self.parts
        self.own_cols = cols_dev // STRIDE

    def line_tables(self, sign):
        cosine, sine = turn(self.X, self.X, self.X, sign)
        weights = np.concatenate([cosine, sine], axis=1).astype(ml_dtypes.bfloat16)
        twist = turn(self.X, self.C, self.total_cols, sign)
        return weights, np.concatenate(twist, axis=1).astype(np.float32)

    def pencil_tables(self):
        cosine, sine = turn(self.m, self.m, self.m, -1.0)
        cosine, sine = block_diagonal(cosine, self.P), block_diagonal(sine, self.P)
        ahead = np.block([[cosine, sine], [-sine, cosine]])
        behind = np.block([[cosine, -sine], [sine, cosine]]) / (self.total_rows * self.total_cols)
        twist = turn(self.D, self.m, self.total_rows, -1.0)
        twist = np.stack([np.tile(part, (1, self.P)) for part in twist]).astype(np.float32)
        return high_low(ahead), high_low(behind), twist

    def row_table(self, real, imag):
        blocks = []
        for slab in range(WIN // self.m):
            rows = slice(slab * self.m, (slab + 1) * self.m)
            for left, right in ((real[rows], imag[rows]), (-imag[rows], real[rows])):
                pieces = []
                for part in range(self.parts):
                    cols = slice(part * self.pp, (part + 1) * self.pp)
                    pieces += [left[:, cols], right[:, cols]]
                blocks.append(np.concatenate(pieces, axis=1))
        return np.concatenate(blocks, axis=0)

    def group_table(self):
        return np.kron(np.eye(self.views), np.ones((BIN, BIN))).astype(np.float32)


def hogel_tables():
    positions = np.arange(WIN)
    tapers = np.sin(np.pi * (positions + 0.5) / WIN) ** 2
    angles = -2.0 * np.pi / WIN * (positions[:, None] * positions[None, :] % WIN)
    cosine = (tapers[:, None] * np.cos(angles)).astype(np.float32)
    sine = (tapers[:, None] * np.sin(angles)).astype(np.float32)
    col = np.concatenate([cosine, sine], axis=1).astype(ml_dtypes.bfloat16)
    col_turned = np.concatenate([cosine.T, sine.T], axis=1).astype(ml_dtypes.bfloat16)
    row = np.stack([cosine / WIN, sine / WIN]).astype(ml_dtypes.bfloat16)
    return col, col_turned, row


def three_pieces(values):
    first = values.astype(BF16)
    rest = values - first.astype(F32)
    second = rest.astype(BF16)
    return first, second, (rest - second.astype(F32)).astype(BF16)


def matmul(left, right):
    return jnp.dot(left, right, preferred_element_type=F32)


def gather_chunks(arrived, chunks):
    mine = lax.axis_index("cols")
    for t, chunk in enumerate(arrived):
        chunks[mine ^ t] = chunk[...]


def scatter_chunks(chunks, leaving):
    mine = lax.axis_index("cols")
    for t, chunk in enumerate(leaving):
        chunk[...] = chunks[mine ^ t]


def put_views(plan, rows):
    pad = jnp.zeros((VIEWS - 3 * plan.own_cols, plan.lanes), F32)
    pieces = [piece.astype(F32) for piece in three_pieces(rows)]
    return jnp.concatenate([*pieces, pad], axis=0).astype(BF16)


def get_views(plan, chunk):
    chunk = chunk.astype(F32)
    n = plan.own_cols
    return chunk[:n] + chunk[n : 2 * n] + chunk[2 * n : 3 * n]


def pack_kernel(plan, field, goal, *refs):
    C, m, X = plan.C, plan.m, plan.X
    leaving, (out,) = refs[:C], refs[C:]
    for c in range(C):
        rows = slice(c * m, (c + 1) * m)
        block = jnp.concatenate([field[0, rows, :], field[1, rows, :]], axis=0)
        out[c, :X, :] = block.astype(F32).T.astype(BF16)
        i, start = c // plan.parts, c % plan.parts * plan.lanes
        out[c, X:, :] = put_views(plan, goal[i, :, start : start + plan.lanes])
    scatter_chunks(out, leaving)


def unpack_kernel(plan, *refs):
    C, m, X = plan.C, plan.m, plan.X
    arrived, (out, light, slabs) = refs[:C], refs[C:]
    gather_chunks(arrived, slabs)
    for c in range(C):
        block = slabs[c, :X, :].astype(F32).T
        out[0, m * c : m * c + m, :] = block[:m]
        out[1, m * c : m * c + m, :] = block[m:]
        i, start = c // plan.parts, c % plan.parts * plan.lanes
        light[i, :, start : start + plan.lanes] = get_views(plan, slabs[c, X:, :])


def lines_forward(plan, lanes, load, emit, weights, twist, turned):
    C, X = plan.C, plan.X
    step = 64
    for start in range(0, X, step):
        points = packed_dft([load(c, start, step) for c in range(C)], -1.0)
        for k in range(C):
            cosine = twist[start : start + step, k : k + 1]
            sine = twist[start : start + step, C + k : C + k + 1]
            across = times_i(points[k])
            if k:
                value = points[k] * cosine + across * sine
                across = across * cosine - points[k] * sine
            else:
                value = points[k]
            place = slice(k * lanes, k * lanes + lanes)
            turned[start : start + step, place] = value.astype(BF16)
            turned[X + start : X + start + step, place] = across.astype(BF16)
    group = max(1, 256 // lanes)
    for first in range(0, C, group):
        result = matmul(weights[...], turned[:, first * lanes : (first + group) * lanes])
        for k in range(group):
            for r in range(plan.R):
                rows = slice(r * plan.span, (r + 1) * plan.span)
                emit((first + k) * plan.R + r, result[rows, k * lanes : (k + 1) * lanes])


def lines_inverse(plan, lanes, packed, emit, weights, twist, step):
    C, X = plan.C, plan.X
    for start in range(0, X, step):
        result = matmul(weights[start : start + step, :], packed[...])
        points = []
        for k in range(C):
            value = result[:, k * lanes : (k + 1) * lanes]
            if k:
                cosine = twist[start : start + step, k : k + 1]
                sine = twist[start : start + step, C + k : C + k + 1]
                value = value * cosine + times_i(value) * sine
            points.append(value)
        for c, value in enumerate(packed_dft(points, 1.0)):
            emit(c, start, step, value)


def trade_halves(first, second):
    half = first.shape[-1] // 2
    low = lax.broadcasted_iota(jnp.int32, first.shape, first.ndim - 1) < half
    return (
        jnp.where(low, first, pltpu.roll(second, half, first.ndim - 1)),
        jnp.where(low, pltpu.roll(first, half, first.ndim - 1), second),
    )


def to_planes(plan, block):
    if plan.P == 2:
        return trade_halves(block[: plan.f], block[plan.f :])
    parts = [block[p * plan.f : (p + 1) * plan.f, :] for p in range(plan.P)]
    real = jnp.concatenate([part[:, : plan.m] for part in parts], axis=1)
    imag = jnp.concatenate([part[:, plan.m :] for part in parts], axis=1)
    return real, imag


def from_planes(plan, real, imag):
    m = plan.m
    if plan.P == 2:
        return jnp.concatenate(trade_halves(real, imag), axis=0)
    return jnp.concatenate(
        [
            jnp.concatenate([real[:, p * m : (p + 1) * m], imag[:, p * m : (p + 1) * m]], axis=1)
            for p in range(plan.P)
        ],
        axis=0,
    )


def rows_forward_kernel(plan, weights, twist, *refs):
    C, X = plan.C, plan.X
    arrived, (_, _, out, goals, turned, slabs) = refs[:C], refs[C:]
    gather_chunks(arrived, slabs)
    goals[...] = slabs[:, X:, :]

    def load(c, start, step):
        return slabs[c, start : start + step, :].astype(F32)

    def emit(d, block):
        out[d] = jnp.concatenate(to_planes(plan, block), axis=0).astype(BF16)

    lines_forward(plan, plan.lanes, load, emit, weights, twist, turned)


def rows_inverse_kernel(plan, pencils, lights, weights, twist, *refs):
    C, X, lanes = plan.C, plan.X, plan.lanes
    leaving, (packed, out) = refs[:C], refs[C:]
    for k in range(C):
        for r in range(plan.R):
            chunk = pencils[k * plan.R + r].astype(F32)
            block = from_planes(plan, chunk[: plan.f], chunk[plan.f :])
            place = slice(k * lanes, k * lanes + lanes)
            packed[r * plan.span : (r + 1) * plan.span, place] = block.astype(BF16)
            packed[X + r * plan.span : X + (r + 1) * plan.span, place] = times_i(block).astype(BF16)

    def emit(c, start, step, value):
        out[c, start : start + step, :] = value.astype(BF16)

    lines_inverse(plan, lanes, packed, emit, weights, twist, 64)
    out[:, X:, :] = lights[...]
    scatter_chunks(out, leaving)


def columns(plan, sign, load, store, steer_re, steer_im, ahead, behind, twist, scratch):
    D, f, outer, inner = plan.D, plan.f, plan.outer, plan.inner
    half_re, half_im, rounded = scratch
    for b in range(inner):
        points = [load(inner * a + b) for a in range(outer)]
        for alpha, (re, im) in enumerate(small_dft(points, -1.0)):
            angle = -2.0 * math.pi * b * alpha / D
            cosine, sine = math.cos(angle), math.sin(angle)
            if b * alpha:
                re, im = re * cosine - im * sine, re * sine + im * cosine
            half_re[alpha * inner + b] = re
            half_im[alpha * inner + b] = im
    for alpha in range(outer):
        points = [(half_re[alpha * inner + b], half_im[alpha * inner + b]) for b in range(inner)]
        for beta, (re, im) in enumerate(small_dft(points, -1.0)):
            k = alpha + outer * beta
            cosine, sine = twist[0, k : k + 1, :], twist[1, k : k + 1, :]
            for offset, part in ((0, re * cosine - im * sine), (128, re * sine + im * cosine)):
                rounded[k, :, offset : offset + 128] = part.astype(BF16)
    group = D // 2
    for start in range(0, D, group):
        place = slice(start, start + group)

        def multiply(matrix):
            left = rounded[place].reshape(group * f, 256)
            product = matmul(left, matrix[:256, :]) + matmul(left, matrix[256:, :])
            return product.reshape(group, f, 256)

        result = multiply(ahead)
        re, im = result[:, :, :128], result[:, :, 128:]
        factor_re, factor_im = steer_re[place], sign * steer_im[place]
        for offset, part in (
            (0, re * factor_re - im * factor_im),
            (128, re * factor_im + im * factor_re),
        ):
            rounded[place, :, offset : offset + 128] = part.astype(BF16)
        result = multiply(behind)
        half_re[place] = result[:, :, :128]
        half_im[place] = result[:, :, 128:]
    for alpha in range(outer):
        points = []
        for beta in range(inner):
            k = alpha + outer * beta
            cosine, sine = twist[0, k : k + 1, :], twist[1, k : k + 1, :]
            re, im = half_re[k], half_im[k]
            points.append((re * cosine + im * sine, im * cosine - re * sine))
        for b, (re, im) in enumerate(small_dft(points, 1.0)):
            angle = 2.0 * math.pi * b * alpha / D
            cosine, sine = math.cos(angle), math.sin(angle)
            if b * alpha:
                re, im = re * cosine - im * sine, re * sine + im * cosine
            half_re[alpha + outer * b] = re
            half_im[alpha + outer * b] = im
    for b in range(inner):
        points = [(half_re[alpha + outer * b], half_im[alpha + outer * b]) for alpha in range(outer)]
        for a, (re, im) in enumerate(small_dft(points, 1.0)):
            store(inner * a + b, re, im)


def pencil_forward_kernel(plan, pencils, *refs):
    steer_re, steer_im, ahead, behind, twist, row, out, windows, *scratch = refs
    f, lanes, span = plan.f, plan.lanes, plan.span

    def load(s):
        chunk = pencils[s].astype(F32)
        return chunk[:f], chunk[f:]

    def store(s, re, im):
        block = from_planes(plan, re, im).astype(BF16)
        i, slab = s // plan.shift, s % plan.shift
        windows[i, :, slab * lanes : (slab + 1) * lanes] = block
        slab += plan.shift
        windows[(i - 1) % plan.hogel_rows, :, slab * lanes : (slab + 1) * lanes] = block

    columns(plan, 1.0, load, store, steer_re, steer_im, ahead, behind, twist, scratch)
    count = plan.hogel_rows
    result = matmul(windows[...].reshape(count * span, 2 * WIN), row[...]).astype(BF16)
    for i in range(count):
        for part in range(plan.parts):
            out[i * plan.parts + part] = result[
                i * span : (i + 1) * span, part * 2 * plan.pp : (part + 1) * 2 * plan.pp
            ]


def pencil_back_kernel(plan, lines, *refs):
    steer_re, steer_im, ahead, behind, twist, row, out, windows, *scratch = refs
    lanes, span, parts = plan.lanes, plan.span, plan.parts
    count, wide = plan.hogel_rows, 2 * plan.pp
    by_part = lines[...].reshape(count, parts, span, wide)
    result = sum(
        matmul(by_part[:, n].reshape(count * span, wide), row[n * wide : (n + 1) * wide, :])
        for n in range(parts)
    )
    windows[...] = result.reshape(count, span, 2 * WIN)

    def load(s):
        i, slab = s // plan.shift, s % plan.shift
        block = windows[i, :, slab * lanes : (slab + 1) * lanes]
        slab += plan.shift
        block = block + windows[(i - 1) % plan.hogel_rows, :, slab * lanes : (slab + 1) * lanes]
        return to_planes(plan, block)

    def store(s, re, im):
        out[s] = jnp.concatenate([re, im], axis=0).astype(BF16)

    columns(plan, -1.0, load, store, steer_re, steer_im, ahead, behind, twist, scratch)


def hogel_kernel(plan, lines, goals, *refs):
    weights_behind, twist_behind, weights_ahead, twist_ahead, col, col_turned, same = refs[:7]
    out, lights, packed, field, spectra, bright, marks, factors, weighted, back = refs[7:]
    C, X, lanes, pp = plan.C, plan.X, 2 * plan.pp, plan.pp
    total = plan.total_cols
    for k in range(C):
        block = lines[k * plan.R : (k + 1) * plan.R].reshape(X, lanes)
        place = slice(k * lanes, (k + 1) * lanes)
        packed[:X, place] = block
        packed[X:, place] = times_i(block.astype(F32)).astype(BF16)

    def emit_near(c, start, step, value):
        for n, part in enumerate((value, times_i(value))):
            rounded = part.astype(BF16)
            field[n, c * X + start : c * X + start + step, :] = rounded
            if c == 0 and start < STRIDE:
                field[n, total + start : total + start + step, :] = rounded

    lines_inverse(plan, lanes, packed, emit_near, weights_behind, twist_behind, 128)
    for j in range(plan.hogel_cols):
        window = slice(STRIDE * j, STRIDE * j + WIN)
        result = matmul(
            col_turned[...], jnp.concatenate([field[0, window, :], field[1, window, :]], axis=0)
        )
        spectra[j] = result
        power = result[:, :pp] * result[:, :pp] + result[:, pp:] * result[:, pp:]
        bright[j * VIEWS : (j + 1) * VIEWS, :] = power.reshape(VIEWS, BIN, pp).sum(axis=1)
    exact = lax.Precision.HIGHEST
    own = lax.broadcasted_iota(jnp.int32, (VIEWS, pp), 0) == (
        lax.broadcasted_iota(jnp.int32, (VIEWS, pp), 1) % VIEWS
    )
    for c in range(C):
        target = get_views(plan, goals[c])
        for j in range(plan.own_cols):
            h = c * plan.own_cols + j
            marks[h * VIEWS : (h + 1) * VIEWS, :] = jnp.where(own, target[j : j + 1, :], 0.0)
    scale = 1.0 / (BIN * BIN)
    light = scale * jnp.dot(bright[...], same[...], preferred_element_type=F32, precision=exact)
    target = jnp.dot(marks[...], same[...], preferred_element_type=F32, precision=exact)
    factors[...] = 4.0 * (light - target)
    bright[...] = light
    for c in range(C):
        rows = []
        for j in range(plan.own_cols):
            h = c * plan.own_cols + j
            block = jnp.where(own, bright[h * VIEWS : (h + 1) * VIEWS, :], 0.0)
            rows.append(jnp.sum(block, axis=0, keepdims=True))
        lights[c] = put_views(plan, jnp.concatenate(rows, axis=0))
    for j in range(plan.hogel_cols):
        for view in range(VIEWS):
            factor = factors[j * VIEWS + view : j * VIEWS + view + 1, :]
            block = slice(view * BIN, (view + 1) * BIN)
            below = slice(WIN + view * BIN, WIN + (view + 1) * BIN)
            real = (spectra[j, block, :pp] * factor).astype(BF16)
            imag = (spectra[j, block, pp:] * factor).astype(BF16)
            weighted[block, :pp] = real
            weighted[block, pp:] = imag
            weighted[below, :pp] = imag
            weighted[below, pp:] = -real
        result = matmul(col[...], weighted[...])
        first, second = STRIDE * j, STRIDE * (j + 1) % total
        if j == 0:
            back[:STRIDE] = result[:STRIDE]
        else:
            back[first : first + STRIDE] = back[first : first + STRIDE] + result[:STRIDE]
        if j < plan.hogel_cols - 1:
            back[second : second + STRIDE] = result[STRIDE:]
        else:
            back[:STRIDE] = back[:STRIDE] + result[STRIDE:]

    def load(c, start, step):
        return back[c * X + start : c * X + start + step, :]

    def emit(d, block):
        out[d] = block.astype(BF16)

    lines_forward(plan, lanes, load, emit, weights_ahead, twist_ahead, packed)


def steer_table(plan):
    index = lax.axis_index(("rows", "cols"))
    shape = (plan.D, plan.f, 128)
    k = lax.broadcasted_iota(jnp.int32, shape, 0)
    line = lax.broadcasted_iota(jnp.int32, shape, 1)
    lane = lax.broadcasted_iota(jnp.int32, shape, 2)
    u = k + plan.D * (lane % plan.m)
    v = index // plan.R + plan.C * (
        plan.span * (index % plan.R) + plan.f * (lane // plan.m) + line
    )

    def freq(position, count):
        return ((position + count // 2) % count - count // 2).astype(F32) / count

    freq_rows, freq_cols = freq(u, plan.total_rows), freq(v, plan.total_cols)
    radial = freq_rows * freq_rows + freq_cols * freq_cols
    phase = (
        -2.0
        * math.pi
        * distance_px
        * radial
        / (jnp.sqrt(index_ratio * index_ratio - radial) + index_ratio)
    )
    return jnp.cos(phase), jnp.sin(phase)


def exchange(chunks):
    return lax.all_to_all(chunks, ("rows", "cols"), split_axis=0, concat_axis=0, tiled=True)


def swap_columns(chunks):
    count = lax.axis_size("cols")
    return tuple(
        chunk if t == 0 else lax.ppermute(chunk, "cols", [(i, i ^ t) for i in range(count)])
        for t, chunk in enumerate(chunks)
    )


def local(slm_field, target_light):
    rows_count, cols_count = lax.axis_size("rows"), lax.axis_size("cols")
    plan = Plan(rows_count, cols_count, slm_field.shape[1], slm_field.shape[2])
    C, D, X, lanes, f = plan.C, plan.D, plan.X, plan.lanes, plan.f
    span, wide = plan.span, 2 * plan.pp

    ahead, behind, twist = (jnp.asarray(t) for t in plan.pencil_tables())
    weights_ahead, twist_ahead = (jnp.asarray(t) for t in plan.line_tables(-1.0))
    weights_behind, twist_behind = (jnp.asarray(t) for t in plan.line_tables(1.0))
    col, col_turned, row = hogel_tables()
    row = plan.row_table(row[0], row[1])
    col, col_turned, row, row_turned, same = (
        jnp.asarray(t) for t in (col, col_turned, row, row.T.copy(), plan.group_table())
    )
    steer_re, steer_im = steer_table(plan)

    slabs_shapes = (shape_of((X + VIEWS, lanes), BF16),) * C
    slabs_scratch = pltpu.VMEM((C, X + VIEWS, lanes), BF16)
    views_shape = shape_of((C, VIEWS, lanes), BF16)
    pencil_shape = shape_of((D, 2 * f, 128), BF16)
    lines_shape = shape_of((D, span, wide), BF16)
    columns_scratch = (
        pltpu.VMEM((D, f, 128), F32),
        pltpu.VMEM((D, f, 128), F32),
        pltpu.VMEM((D, f, 256), BF16),
    )
    pencil_tables = (steer_re, steer_im, ahead, behind, twist)
    columns_flops = 8 * D * f * 256 * 256 + 2 * plan.hogel_rows * span * (2 * WIN) ** 2

    apart_any = pl.BlockSpec(memory_space=pl.ANY)
    slabs = call(
        lambda *refs: pack_kernel(plan, *refs),
        slabs_shapes,
        (slm_field.astype(BF16), target_light),
        (slabs_scratch,),
    )
    tall = pltpu.VMEM((2 * X, C * lanes), BF16)
    pencils, goals = call(
        lambda *refs: rows_forward_kernel(plan, *refs),
        (pencil_shape, views_shape),
        (weights_ahead, twist_ahead, *swap_columns(slabs), steer_re, steer_im),
        (tall, slabs_scratch),
        flops=2 * X * 2 * X * C * lanes,
        in_specs={C + 2: apart_any, C + 3: apart_any},
    )
    (lines,) = call(
        lambda *refs: pencil_forward_kernel(plan, *refs),
        (lines_shape,),
        (exchange(pencils), *pencil_tables, row),
        (pltpu.VMEM((plan.hogel_rows, span, 2 * WIN), BF16), *columns_scratch),
        flops=columns_flops,
    )
    tall = pltpu.VMEM((2 * X, C * wide), BF16)
    lines, lights = call(
        lambda *refs: hogel_kernel(plan, *refs),
        (lines_shape, views_shape),
        (
            exchange(lines),
            goals,
            weights_behind,
            twist_behind,
            weights_ahead,
            twist_ahead,
            col,
            col_turned,
            same,
        ),
        (
            tall,
            pltpu.VMEM((2, plan.total_cols + STRIDE, wide), BF16),
            pltpu.VMEM((plan.hogel_cols, WIN, wide), F32),
            pltpu.VMEM((plan.hogel_cols * VIEWS, plan.pp), F32),
            pltpu.VMEM((plan.hogel_cols * VIEWS, plan.pp), F32),
            pltpu.VMEM((plan.hogel_cols * VIEWS, plan.pp), F32),
            pltpu.VMEM((2 * WIN, wide), BF16),
            pltpu.VMEM((plan.total_cols, wide), F32),
        ),
        flops=4 * X * 2 * X * C * wide + 4 * plan.hogel_cols * WIN * 2 * WIN * wide,
    )
    (pencils,) = call(
        lambda *refs: pencil_back_kernel(plan, *refs),
        (pencil_shape,),
        (exchange(lines), *pencil_tables, row_turned),
        (pltpu.VMEM((plan.hogel_rows, span, 2 * WIN), F32), *columns_scratch),
        flops=columns_flops,
    )
    tall = pltpu.VMEM((2 * X, C * lanes), BF16)
    slabs = call(
        lambda *refs: rows_inverse_kernel(plan, *refs),
        slabs_shapes,
        (exchange(pencils), lights, weights_behind, twist_behind),
        (tall, slabs_scratch),
        flops=2 * X * 2 * X * C * lanes,
    )
    return call(
        lambda *refs: unpack_kernel(plan, *refs),
        (shape_of(slm_field.shape, F32), shape_of(target_light.shape, F32)),
        swap_columns(slabs),
        (slabs_scratch,),
    )


def solution(mesh):
    return jax.shard_map(
        local,
        mesh=mesh,
        in_specs=(P(None, "rows", "cols"), P("rows", "cols", None)),
        out_specs=(P(None, "rows", "cols"), P("rows", "cols", None)),
        check_vma=False,
    )
```

```python
import math

import jax
import jax.numpy as jnp
import ml_dtypes
import numpy as np
from jax import lax
from jax.experimental import pallas as pl
from jax.experimental.pallas import tpu as pltpu
from jax.sharding import PartitionSpec as P

WIN = 256
VIEWS = 16
STRIDE = 128
BIN = 16

distance_px = 16000.0
index_ratio = 15.0

BF16 = jnp.bfloat16
F32 = jnp.float32
BOTH_MINOR = (((1,), (1,)), ((), ()))


def call(body, outs, args, scratch=(), flops=0, in_specs=None, out_specs=None):
    nbytes = sum(math.prod(a.shape) * a.dtype.itemsize for a in (*outs, *args))
    specs = {}
    if in_specs:
        whole = pl.BlockSpec(memory_space=pltpu.VMEM)
        specs["in_specs"] = [in_specs.get(n, whole) for n in range(len(args))]
    if out_specs:
        specs["out_specs"] = out_specs
    return pl.pallas_call(
        body,
        out_shape=outs,
        scratch_shapes=list(scratch),
        compiler_params=pltpu.CompilerParams(vmem_limit_bytes=24 * 2**20),
        cost_estimate=pl.CostEstimate(flops=flops, bytes_accessed=nbytes, transcendentals=0),
        **specs,
    )(*args)


def shape_of(dims, dtype):
    return jax.ShapeDtypeStruct(dims, dtype)


def high_low(table):
    table = np.asarray(table, np.float32)
    high = table.astype(ml_dtypes.bfloat16)
    low = (table - high.astype(np.float32)).astype(ml_dtypes.bfloat16)
    return np.concatenate([high, low], axis=0)


def times_i(values):
    half = values.shape[-1] // 2
    if values.shape[-1] == 128:
        lanes = lax.broadcasted_iota(jnp.int32, values.shape, values.ndim - 1)
        turned = pltpu.roll(values, half, values.ndim - 1)
        return jnp.where(lanes < half, -turned, turned)
    return jnp.concatenate([-values[..., half:], values[..., :half]], axis=-1)


def scaled(value, factor):
    return value if factor == 1.0 else value * factor


def small_dft(points, sign):
    count = len(points)
    if count == 1:
        return points
    even = small_dft(points[0::2], sign)
    odd = small_dft(points[1::2], sign)
    front, back = [], []
    for k in range(count // 2):
        re, im = odd[k]
        angle = sign * 2.0 * math.pi * k / count
        cosine, sine = math.cos(angle), math.sin(angle)
        if k == 0:
            pass
        elif 4 * k == count:
            re, im = (-im, re) if sign > 0 else (im, -re)
        elif 8 * k == count:
            re, im = cosine * (re - sign * im), cosine * (im + sign * re)
        elif 8 * k == 3 * count:
            re, im = cosine * (re + sign * im), cosine * (im - sign * re)
        else:
            re, im = re * cosine - im * sine, re * sine + im * cosine
        even_re, even_im = even[k]
        front.append((even_re + re, even_im + im))
        back.append((even_re - re, even_im - im))
    return front + back


def packed_dft(points, sign):
    count = len(points)
    if count == 1:
        return points
    even = packed_dft(points[0::2], sign)
    odd = packed_dft(points[1::2], sign)
    front, back = [], []
    for k in range(count // 2):
        term = odd[k]
        angle = sign * 2.0 * math.pi * k / count
        if 4 * k == count:
            term = times_i(term) if sign > 0 else -times_i(term)
        elif k:
            term = math.cos(angle) * term + math.sin(angle) * times_i(term)
        front.append(even[k] + term)
        back.append(even[k] - term)
    return front + back


def turn(rows, cols, period, sign):
    angles = sign * 2.0 * np.pi / period * ((np.arange(rows)[:, None] * np.arange(cols)) % period)
    return np.cos(angles), np.sin(angles)


def block_diagonal(block, copies):
    return np.kron(np.eye(copies), block)


class Plan:
    def __init__(self, rows_count, cols_count, rows_dev, cols_dev):
        self.R, self.C = rows_count, cols_count
        self.D = rows_count * cols_count
        self.X = cols_dev
        self.m = rows_dev // cols_count
        self.lanes = 2 * self.m
        self.P = 128 // self.m
        self.span = cols_dev // rows_count
        self.f = self.span // self.P
        self.total_rows = rows_dev * rows_count
        self.total_cols = cols_dev * cols_count
        self.outer = 8
        self.inner = self.D // 8
        self.shift = STRIDE // self.m
        self.hogel_rows = self.total_rows // STRIDE
        self.hogel_cols = self.total_cols // STRIDE
        self.parts = self.D // self.hogel_rows
        self.pp = WIN // self.parts
        self.views = VIEWS // self.parts
        self.own_cols = cols_dev // STRIDE

    def line_tables(self, sign):
        cosine, sine = turn(self.X, self.X, self.X, sign)
        weights = np.concatenate([cosine, sine], axis=1).astype(ml_dtypes.bfloat16)
        twist = turn(self.X, self.C, self.total_cols, sign)
        return weights, np.concatenate(twist, axis=1).astype(np.float32)

    def pencil_tables(self):
        cosine, sine = turn(self.m, self.m, self.m, -1.0)
        cosine, sine = block_diagonal(cosine, self.P), block_diagonal(sine, self.P)
        ahead = np.block([[cosine, sine], [-sine, cosine]])
        behind = np.block([[cosine, -sine], [sine, cosine]]) / (self.total_rows * self.total_cols)
        twist = turn(self.D, self.m, self.total_rows, -1.0)
        twist = np.stack([np.tile(part, (1, self.P)) for part in twist]).astype(np.float32)
        return high_low(ahead), high_low(behind), twist

    def row_table(self, real, imag):
        blocks = []
        for slab in range(WIN // self.m):
            rows = slice(slab * self.m, (slab + 1) * self.m)
            for left, right in ((real[rows], imag[rows]), (-imag[rows], real[rows])):
                pieces = []
                for part in range(self.parts):
                    cols = slice(part * self.pp, (part + 1) * self.pp)
                    pieces += [left[:, cols], right[:, cols]]
                blocks.append(np.concatenate(pieces, axis=1))
        return np.concatenate(blocks, axis=0)

    def group_table(self):
        return np.kron(np.eye(self.views), np.ones((BIN, BIN))).astype(np.float32)


def hogel_tables():
    positions = np.arange(WIN)
    tapers = np.sin(np.pi * (positions + 0.5) / WIN) ** 2
    angles = -2.0 * np.pi / WIN * (positions[:, None] * positions[None, :] % WIN)
    cosine = (tapers[:, None] * np.cos(angles)).astype(np.float32)
    sine = (tapers[:, None] * np.sin(angles)).astype(np.float32)
    col = np.concatenate([cosine, sine], axis=1).astype(ml_dtypes.bfloat16)
    col_turned = np.concatenate([cosine.T, sine.T], axis=1).astype(ml_dtypes.bfloat16)
    row = np.stack([cosine / WIN, sine / WIN]).astype(ml_dtypes.bfloat16)
    return col, col_turned, row


def three_pieces(values):
    first = values.astype(BF16)
    rest = values - first.astype(F32)
    second = rest.astype(BF16)
    return first, second, (rest - second.astype(F32)).astype(BF16)


def matmul(left, right):
    return jnp.dot(left, right, preferred_element_type=F32)


def gather_chunks(arrived, chunks):
    mine = lax.axis_index("cols")
    for t, chunk in enumerate(arrived):
        chunks[mine ^ t] = chunk[...]


def scatter_chunks(chunks, leaving):
    mine = lax.axis_index("cols")
    for t, chunk in enumerate(leaving):
        chunk[...] = chunks[mine ^ t]


def put_views(plan, rows):
    pad = jnp.zeros((VIEWS - 3 * plan.own_cols, plan.lanes), F32)
    pieces = [piece.astype(F32) for piece in three_pieces(rows)]
    return jnp.concatenate([*pieces, pad], axis=0).astype(BF16)


def get_views(plan, chunk):
    chunk = chunk.astype(F32)
    n = plan.own_cols
    return chunk[:n] + chunk[n : 2 * n] + chunk[2 * n : 3 * n]


def pack_kernel(plan, field, goal, *refs):
    C, m, X = plan.C, plan.m, plan.X
    leaving, (out,) = refs[:C], refs[C:]
    for c in range(C):
        rows = slice(c * m, (c + 1) * m)
        block = jnp.concatenate([field[0, rows, :], field[1, rows, :]], axis=0)
        out[c, :X, :] = block.astype(F32).T.astype(BF16)
        i, start = c // plan.parts, c % plan.parts * plan.lanes
        out[c, X:, :] = put_views(plan, goal[i, :, start : start + plan.lanes])
    scatter_chunks(out, leaving)


def unpack_kernel(plan, *refs):
    C, m, X = plan.C, plan.m, plan.X
    arrived, (out, light, slabs) = refs[:C], refs[C:]
    gather_chunks(arrived, slabs)
    for c in range(C):
        block = slabs[c, :X, :].astype(F32).T
        out[0, m * c : m * c + m, :] = block[:m]
        out[1, m * c : m * c + m, :] = block[m:]
        i, start = c // plan.parts, c % plan.parts * plan.lanes
        light[i, :, start : start + plan.lanes] = get_views(plan, slabs[c, X:, :])


def lines_forward(plan, lanes, load, emit, weights, twist, turned):
    C, X = plan.C, plan.X
    step = 64
    for start in range(0, X, step):
        points = packed_dft([load(c, start, step) for c in range(C)], -1.0)
        for k in range(C):
            cosine = twist[start : start + step, k : k + 1]
            sine = twist[start : start + step, C + k : C + k + 1]
            across = times_i(points[k])
            if k:
                value = points[k] * cosine + across * sine
                across = across * cosine - points[k] * sine
            else:
                value = points[k]
            place = slice(k * lanes, k * lanes + lanes)
            turned[start : start + step, place] = value.astype(BF16)
            turned[X + start : X + start + step, place] = across.astype(BF16)
    group = max(1, 256 // lanes)
    for first in range(0, C, group):
        result = matmul(weights[...], turned[:, first * lanes : (first + group) * lanes])
        for k in range(group):
            for r in range(plan.R):
                rows = slice(r * plan.span, (r + 1) * plan.span)
                emit((first + k) * plan.R + r, result[rows, k * lanes : (k + 1) * lanes])


def lines_inverse(plan, lanes, packed, emit, weights, twist, step):
    C, X = plan.C, plan.X
    for start in range(0, X, step):
        result = matmul(weights[start : start + step, :], packed[...])
        points = []
        for k in range(C):
            value = result[:, k * lanes : (k + 1) * lanes]
            if k:
                cosine = twist[start : start + step, k : k + 1]
                sine = twist[start : start + step, C + k : C + k + 1]
                value = value * cosine + times_i(value) * sine
            points.append(value)
        for c, value in enumerate(packed_dft(points, 1.0)):
            emit(c, start, step, value)


def to_planes(plan, block):
    parts = [block[p * plan.f : (p + 1) * plan.f, :] for p in range(plan.P)]
    real = jnp.concatenate([part[:, : plan.m] for part in parts], axis=1)
    imag = jnp.concatenate([part[:, plan.m :] for part in parts], axis=1)
    return real, imag


def from_planes(plan, real, imag):
    m = plan.m
    return jnp.concatenate(
        [
            jnp.concatenate([real[:, p * m : (p + 1) * m], imag[:, p * m : (p + 1) * m]], axis=1)
            for p in range(plan.P)
        ],
        axis=0,
    )


def rows_forward_kernel(plan, weights, twist, *refs):
    C, X = plan.C, plan.X
    arrived, (_, _, out, goals, turned, slabs) = refs[:C], refs[C:]
    gather_chunks(arrived, slabs)
    goals[...] = slabs[:, X:, :]

    def load(c, start, step):
        return slabs[c, start : start + step, :].astype(F32)

    def emit(d, block):
        out[d] = jnp.concatenate(to_planes(plan, block), axis=0).astype(BF16)

    lines_forward(plan, plan.lanes, load, emit, weights, twist, turned)


def rows_inverse_kernel(plan, pencils, lights, weights, twist, *refs):
    C, X, lanes = plan.C, plan.X, plan.lanes
    leaving, (packed, out) = refs[:C], refs[C:]
    for k in range(C):
        for r in range(plan.R):
            chunk = pencils[k * plan.R + r].astype(F32)
            block = from_planes(plan, chunk[: plan.f], chunk[plan.f :])
            place = slice(k * lanes, k * lanes + lanes)
            packed[r * plan.span : (r + 1) * plan.span, place] = block.astype(BF16)
            packed[X + r * plan.span : X + (r + 1) * plan.span, place] = times_i(block).astype(BF16)

    def emit(c, start, step, value):
        out[c, start : start + step, :] = value.astype(BF16)

    lines_inverse(plan, lanes, packed, emit, weights, twist, 64)
    out[:, X:, :] = lights[...]
    scatter_chunks(out, leaving)


def columns(plan, sign, load, store, steer_re, steer_im, ahead, behind, twist, scratch):
    D, f, outer, inner = plan.D, plan.f, plan.outer, plan.inner
    half_re, half_im, rounded = scratch
    for b in range(inner):
        points = [load(inner * a + b) for a in range(outer)]
        for alpha, (re, im) in enumerate(small_dft(points, -1.0)):
            angle = -2.0 * math.pi * b * alpha / D
            cosine, sine = math.cos(angle), math.sin(angle)
            if b * alpha:
                re, im = re * cosine - im * sine, re * sine + im * cosine
            half_re[alpha * inner + b] = re
            half_im[alpha * inner + b] = im
    for alpha in range(outer):
        points = [(half_re[alpha * inner + b], half_im[alpha * inner + b]) for b in range(inner)]
        for beta, (re, im) in enumerate(small_dft(points, -1.0)):
            k = alpha + outer * beta
            cosine, sine = twist[0, k : k + 1, :], twist[1, k : k + 1, :]
            for offset, part in ((0, re * cosine - im * sine), (128, re * sine + im * cosine)):
                rounded[k, :, offset : offset + 128] = part.astype(BF16)
    group = D // 2
    for start in range(0, D, group):
        place = slice(start, start + group)

        def multiply(matrix):
            left = rounded[place].reshape(group * f, 256)
            product = matmul(left, matrix[:256, :]) + matmul(left, matrix[256:, :])
            return product.reshape(group, f, 256)

        result = multiply(ahead)
        re, im = result[:, :, :128], result[:, :, 128:]
        factor_re, factor_im = steer_re[place], sign * steer_im[place]
        for offset, part in (
            (0, re * factor_re - im * factor_im),
            (128, re * factor_im + im * factor_re),
        ):
            rounded[place, :, offset : offset + 128] = part.astype(BF16)
        result = multiply(behind)
        half_re[place] = result[:, :, :128]
        half_im[place] = result[:, :, 128:]
    for alpha in range(outer):
        points = []
        for beta in range(inner):
            k = alpha + outer * beta
            cosine, sine = twist[0, k : k + 1, :], twist[1, k : k + 1, :]
            re, im = half_re[k], half_im[k]
            points.append((re * cosine + im * sine, im * cosine - re * sine))
        for b, (re, im) in enumerate(small_dft(points, 1.0)):
            angle = 2.0 * math.pi * b * alpha / D
            cosine, sine = math.cos(angle), math.sin(angle)
            if b * alpha:
                re, im = re * cosine - im * sine, re * sine + im * cosine
            half_re[alpha + outer * b] = re
            half_im[alpha + outer * b] = im
    for b in range(inner):
        points = [(half_re[alpha + outer * b], half_im[alpha + outer * b]) for alpha in range(outer)]
        for a, (re, im) in enumerate(small_dft(points, 1.0)):
            store(inner * a + b, re, im)


def pencil_forward_kernel(plan, pencils, *refs):
    steer_re, steer_im, ahead, behind, twist, row, out, windows, *scratch = refs
    f, lanes, span = plan.f, plan.lanes, plan.span

    def load(s):
        chunk = pencils[s].astype(F32)
        return chunk[:f], chunk[f:]

    def store(s, re, im):
        block = from_planes(plan, re, im).astype(BF16)
        i, slab = s // plan.shift, s % plan.shift
        windows[i, :, slab * lanes : (slab + 1) * lanes] = block
        slab += plan.shift
        windows[(i - 1) % plan.hogel_rows, :, slab * lanes : (slab + 1) * lanes] = block

    columns(plan, 1.0, load, store, steer_re, steer_im, ahead, behind, twist, scratch)
    count = plan.hogel_rows
    result = matmul(windows[...].reshape(count * span, 2 * WIN), row[...]).astype(BF16)
    for i in range(count):
        for part in range(plan.parts):
            out[i * plan.parts + part] = result[
                i * span : (i + 1) * span, part * 2 * plan.pp : (part + 1) * 2 * plan.pp
            ]


def pencil_back_kernel(plan, lines, *refs):
    steer_re, steer_im, ahead, behind, twist, row, out, windows, *scratch = refs
    lanes, span, parts = plan.lanes, plan.span, plan.parts
    count, wide = plan.hogel_rows, 2 * plan.pp
    by_part = lines[...].reshape(count, parts, span, wide)
    result = sum(
        matmul(by_part[:, n].reshape(count * span, wide), row[n * wide : (n + 1) * wide, :])
        for n in range(parts)
    )
    windows[...] = result.reshape(count, span, 2 * WIN)

    def load(s):
        i, slab = s // plan.shift, s % plan.shift
        block = windows[i, :, slab * lanes : (slab + 1) * lanes]
        slab += plan.shift
        block = block + windows[(i - 1) % plan.hogel_rows, :, slab * lanes : (slab + 1) * lanes]
        return to_planes(plan, block)

    def store(s, re, im):
        out[s] = jnp.concatenate([re, im], axis=0).astype(BF16)

    columns(plan, -1.0, load, store, steer_re, steer_im, ahead, behind, twist, scratch)


def hogel_kernel(plan, lines, goals, *refs):
    weights_behind, twist_behind, weights_ahead, twist_ahead, col, col_turned, same = refs[:7]
    out, lights, packed, field, spectra, bright, marks, factors, weighted, back = refs[7:]
    C, X, lanes, pp = plan.C, plan.X, 2 * plan.pp, plan.pp
    total = plan.total_cols
    for k in range(C):
        block = lines[k * plan.R : (k + 1) * plan.R].reshape(X, lanes)
        place = slice(k * lanes, (k + 1) * lanes)
        packed[:X, place] = block
        packed[X:, place] = times_i(block.astype(F32)).astype(BF16)

    def emit_near(c, start, step, value):
        for n, part in enumerate((value, times_i(value))):
            rounded = part.astype(BF16)
            field[n, c * X + start : c * X + start + step, :] = rounded
            if c == 0 and start < STRIDE:
                field[n, total + start : total + start + step, :] = rounded

    lines_inverse(plan, lanes, packed, emit_near, weights_behind, twist_behind, 128)
    for j in range(plan.hogel_cols):
        window = slice(STRIDE * j, STRIDE * j + WIN)
        result = matmul(
            col_turned[...], jnp.concatenate([field[0, window, :], field[1, window, :]], axis=0)
        )
        spectra[j] = result
        power = result[:, :pp] * result[:, :pp] + result[:, pp:] * result[:, pp:]
        bright[j * VIEWS : (j + 1) * VIEWS, :] = power.reshape(VIEWS, BIN, pp).sum(axis=1)
    exact = lax.Precision.HIGHEST
    own = lax.broadcasted_iota(jnp.int32, (VIEWS, pp), 0) == (
        lax.broadcasted_iota(jnp.int32, (VIEWS, pp), 1) % VIEWS
    )
    for c in range(C):
        target = get_views(plan, goals[c])
        for j in range(plan.own_cols):
            h = c * plan.own_cols + j
            marks[h * VIEWS : (h + 1) * VIEWS, :] = jnp.where(own, target[j : j + 1, :], 0.0)
    scale = 1.0 / (BIN * BIN)
    light = scale * jnp.dot(bright[...], same[...], preferred_element_type=F32, precision=exact)
    target = jnp.dot(marks[...], same[...], preferred_element_type=F32, precision=exact)
    factors[...] = 4.0 * (light - target)
    bright[...] = light
    for c in range(C):
        rows = []
        for j in range(plan.own_cols):
            h = c * plan.own_cols + j
            block = jnp.where(own, bright[h * VIEWS : (h + 1) * VIEWS, :], 0.0)
            rows.append(jnp.sum(block, axis=0, keepdims=True))
        lights[c] = put_views(plan, jnp.concatenate(rows, axis=0))
    for j in range(plan.hogel_cols):
        for view in range(VIEWS):
            factor = factors[j * VIEWS + view : j * VIEWS + view + 1, :]
            block = slice(view * BIN, (view + 1) * BIN)
            below = slice(WIN + view * BIN, WIN + (view + 1) * BIN)
            real = (spectra[j, block, :pp] * factor).astype(BF16)
            imag = (spectra[j, block, pp:] * factor).astype(BF16)
            weighted[block, :pp] = real
            weighted[block, pp:] = imag
            weighted[below, :pp] = imag
            weighted[below, pp:] = -real
        result = matmul(col[...], weighted[...])
        first, second = STRIDE * j, STRIDE * (j + 1) % total
        if j == 0:
            back[:STRIDE] = result[:STRIDE]
        else:
            back[first : first + STRIDE] = back[first : first + STRIDE] + result[:STRIDE]
        if j < plan.hogel_cols - 1:
            back[second : second + STRIDE] = result[STRIDE:]
        else:
            back[:STRIDE] = back[:STRIDE] + result[STRIDE:]

    def load(c, start, step):
        return back[c * X + start : c * X + start + step, :]

    def emit(d, block):
        out[d] = block.astype(BF16)

    lines_forward(plan, lanes, load, emit, weights_ahead, twist_ahead, packed)


def steer_table(plan):
    index = lax.axis_index(("rows", "cols"))
    shape = (plan.D, plan.f, 128)
    k = lax.broadcasted_iota(jnp.int32, shape, 0)
    line = lax.broadcasted_iota(jnp.int32, shape, 1)
    lane = lax.broadcasted_iota(jnp.int32, shape, 2)
    u = k + plan.D * (lane % plan.m)
    v = index // plan.R + plan.C * (
        plan.span * (index % plan.R) + plan.f * (lane // plan.m) + line
    )

    def freq(position, count):
        return ((position + count // 2) % count - count // 2).astype(F32) / count

    freq_rows, freq_cols = freq(u, plan.total_rows), freq(v, plan.total_cols)
    radial = freq_rows * freq_rows + freq_cols * freq_cols
    phase = (
        -2.0
        * math.pi
        * distance_px
        * radial
        / (jnp.sqrt(index_ratio * index_ratio - radial) + index_ratio)
    )
    return jnp.cos(phase), jnp.sin(phase)


def exchange(chunks):
    return lax.all_to_all(chunks, ("rows", "cols"), split_axis=0, concat_axis=0, tiled=True)


def swap_columns(chunks):
    count = lax.axis_size("cols")
    return tuple(
        chunk if t == 0 else lax.ppermute(chunk, "cols", [(i, i ^ t) for i in range(count)])
        for t, chunk in enumerate(chunks)
    )


def local(slm_field, target_light):
    rows_count, cols_count = lax.axis_size("rows"), lax.axis_size("cols")
    plan = Plan(rows_count, cols_count, slm_field.shape[1], slm_field.shape[2])
    C, D, X, lanes, f = plan.C, plan.D, plan.X, plan.lanes, plan.f
    span, wide = plan.span, 2 * plan.pp

    ahead, behind, twist = (jnp.asarray(t) for t in plan.pencil_tables())
    weights_ahead, twist_ahead = (jnp.asarray(t) for t in plan.line_tables(-1.0))
    weights_behind, twist_behind = (jnp.asarray(t) for t in plan.line_tables(1.0))
    col, col_turned, row = hogel_tables()
    row = plan.row_table(row[0], row[1])
    col, col_turned, row, row_turned, same = (
        jnp.asarray(t) for t in (col, col_turned, row, row.T.copy(), plan.group_table())
    )
    steer_re, steer_im = steer_table(plan)

    slabs_shapes = (shape_of((X + VIEWS, lanes), BF16),) * C
    slabs_scratch = pltpu.VMEM((C, X + VIEWS, lanes), BF16)
    views_shape = shape_of((C, VIEWS, lanes), BF16)
    pencil_shape = shape_of((D, 2 * f, 128), BF16)
    lines_shape = shape_of((D, span, wide), BF16)
    columns_scratch = (
        pltpu.VMEM((D, f, 128), F32),
        pltpu.VMEM((D, f, 128), F32),
        pltpu.VMEM((D, f, 256), BF16),
    )
    pencil_tables = (steer_re, steer_im, ahead, behind, twist)
    columns_flops = 8 * D * f * 256 * 256 + 2 * plan.hogel_rows * span * (2 * WIN) ** 2

    apart_any = pl.BlockSpec(memory_space=pl.ANY)
    slabs = call(
        lambda *refs: pack_kernel(plan, *refs),
        slabs_shapes,
        (slm_field.astype(BF16), target_light),
        (slabs_scratch,),
    )
    tall = pltpu.VMEM((2 * X, C * lanes), BF16)
    pencils, goals = call(
        lambda *refs: rows_forward_kernel(plan, *refs),
        (pencil_shape, views_shape),
        (weights_ahead, twist_ahead, *swap_columns(slabs), steer_re, steer_im),
        (tall, slabs_scratch),
        flops=2 * X * 2 * X * C * lanes,
        in_specs={C + 2: apart_any, C + 3: apart_any},
    )
    (lines,) = call(
        lambda *refs: pencil_forward_kernel(plan, *refs),
        (lines_shape,),
        (exchange(pencils), *pencil_tables, row),
        (pltpu.VMEM((plan.hogel_rows, span, 2 * WIN), BF16), *columns_scratch),
        flops=columns_flops,
    )
    tall = pltpu.VMEM((2 * X, C * wide), BF16)
    lines, lights = call(
        lambda *refs: hogel_kernel(plan, *refs),
        (lines_shape, views_shape),
        (
            exchange(lines),
            goals,
            weights_behind,
            twist_behind,
            weights_ahead,
            twist_ahead,
            col,
            col_turned,
            same,
        ),
        (
            tall,
            pltpu.VMEM((2, plan.total_cols + STRIDE, wide), BF16),
            pltpu.VMEM((plan.hogel_cols, WIN, wide), F32),
            pltpu.VMEM((plan.hogel_cols * VIEWS, plan.pp), F32),
            pltpu.VMEM((plan.hogel_cols * VIEWS, plan.pp), F32),
            pltpu.VMEM((plan.hogel_cols * VIEWS, plan.pp), F32),
            pltpu.VMEM((2 * WIN, wide), BF16),
            pltpu.VMEM((plan.total_cols, wide), F32),
        ),
        flops=4 * X * 2 * X * C * wide + 4 * plan.hogel_cols * WIN * 2 * WIN * wide,
    )
    (pencils,) = call(
        lambda *refs: pencil_back_kernel(plan, *refs),
        (pencil_shape,),
        (exchange(lines), *pencil_tables, row_turned),
        (pltpu.VMEM((plan.hogel_rows, span, 2 * WIN), F32), *columns_scratch),
        flops=columns_flops,
    )
    tall = pltpu.VMEM((2 * X, C * lanes), BF16)
    slabs = call(
        lambda *refs: rows_inverse_kernel(plan, *refs),
        slabs_shapes,
        (exchange(pencils), lights, weights_behind, twist_behind),
        (tall, slabs_scratch),
        flops=2 * X * 2 * X * C * lanes,
    )
    return call(
        lambda *refs: unpack_kernel(plan, *refs),
        (shape_of(slm_field.shape, F32), shape_of(target_light.shape, F32)),
        swap_columns(slabs),
        (slabs_scratch,),
    )


def solution(mesh):
    return jax.shard_map(
        local,
        mesh=mesh,
        in_specs=(P(None, "rows", "cols"), P("rows", "cols", None)),
        out_specs=(P(None, "rows", "cols"), P("rows", "cols", None)),
        check_vma=False,
    )
```

```python
import math

import jax
import jax.numpy as jnp
import ml_dtypes
import numpy as np
from jax import lax
from jax.experimental import pallas as pl
from jax.experimental.pallas import tpu as pltpu
from jax.sharding import PartitionSpec as P

WIN = 256
VIEWS = 16
STRIDE = 128
BIN = 16

distance_px = 16000.0
index_ratio = 15.0

BF16 = jnp.bfloat16
F32 = jnp.float32
BOTH_MINOR = (((1,), (1,)), ((), ()))


def call(body, outs, args, scratch=(), flops=0, in_specs=None, out_specs=None):
    nbytes = sum(math.prod(a.shape) * a.dtype.itemsize for a in (*outs, *args))
    specs = {}
    if in_specs:
        whole = pl.BlockSpec(memory_space=pltpu.VMEM)
        specs["in_specs"] = [in_specs.get(n, whole) for n in range(len(args))]
    if out_specs:
        specs["out_specs"] = out_specs
    return pl.pallas_call(
        body,
        out_shape=outs,
        scratch_shapes=list(scratch),
        compiler_params=pltpu.CompilerParams(vmem_limit_bytes=24 * 2**20),
        cost_estimate=pl.CostEstimate(flops=flops, bytes_accessed=nbytes, transcendentals=0),
        **specs,
    )(*args)


def shape_of(dims, dtype):
    return jax.ShapeDtypeStruct(dims, dtype)


def high_low(table):
    table = np.asarray(table, np.float32)
    high = table.astype(ml_dtypes.bfloat16)
    low = (table - high.astype(np.float32)).astype(ml_dtypes.bfloat16)
    return np.concatenate([high, low], axis=0)


def times_i(values):
    half = values.shape[-1] // 2
    if values.shape[-1] == 128:
        lanes = lax.broadcasted_iota(jnp.int32, values.shape, values.ndim - 1)
        turned = pltpu.roll(values, half, values.ndim - 1)
        return jnp.where(lanes < half, -turned, turned)
    return jnp.concatenate([-values[..., half:], values[..., :half]], axis=-1)


def scaled(value, factor):
    return value if factor == 1.0 else value * factor


def small_dft(points, sign):
    count = len(points)
    if count == 1:
        return points
    even = small_dft(points[0::2], sign)
    odd = small_dft(points[1::2], sign)
    front, back = [], []
    for k in range(count // 2):
        re, im = odd[k]
        angle = sign * 2.0 * math.pi * k / count
        cosine, sine = math.cos(angle), math.sin(angle)
        if k == 0:
            pass
        elif 4 * k == count:
            re, im = (-im, re) if sign > 0 else (im, -re)
        elif 8 * k == count:
            re, im = cosine * (re - sign * im), cosine * (im + sign * re)
        elif 8 * k == 3 * count:
            re, im = cosine * (re + sign * im), cosine * (im - sign * re)
        else:
            re, im = re * cosine - im * sine, re * sine + im * cosine
        even_re, even_im = even[k]
        front.append((even_re + re, even_im + im))
        back.append((even_re - re, even_im - im))
    return front + back


def packed_dft(points, sign):
    count = len(points)
    if count == 1:
        return points
    even = packed_dft(points[0::2], sign)
    odd = packed_dft(points[1::2], sign)
    front, back = [], []
    for k in range(count // 2):
        term = odd[k]
        angle = sign * 2.0 * math.pi * k / count
        if 4 * k == count:
            term = times_i(term) if sign > 0 else -times_i(term)
        elif k:
            term = math.cos(angle) * term + math.sin(angle) * times_i(term)
        front.append(even[k] + term)
        back.append(even[k] - term)
    return front + back


def turn(rows, cols, period, sign):
    angles = sign * 2.0 * np.pi / period * ((np.arange(rows)[:, None] * np.arange(cols)) % period)
    return np.cos(angles), np.sin(angles)


def block_diagonal(block, copies):
    return np.kron(np.eye(copies), block)


class Plan:
    def __init__(self, rows_count, cols_count, rows_dev, cols_dev):
        self.R, self.C = rows_count, cols_count
        self.D = rows_count * cols_count
        self.X = cols_dev
        self.m = rows_dev // cols_count
        self.lanes = 2 * self.m
        self.P = 128 // self.m
        self.span = cols_dev // rows_count
        self.f = self.span // self.P
        self.total_rows = rows_dev * rows_count
        self.total_cols = cols_dev * cols_count
        self.outer = 8
        self.inner = self.D // 8
        self.shift = STRIDE // self.m
        self.hogel_rows = self.total_rows // STRIDE
        self.hogel_cols = self.total_cols // STRIDE
        self.parts = self.D // self.hogel_rows
        self.pp = WIN // self.parts
        self.views = VIEWS // self.parts
        self.own_cols = cols_dev // STRIDE

    def line_tables(self, sign):
        cosine, sine = turn(self.X, self.X, self.X, sign)
        weights = np.concatenate([cosine, sine], axis=1).astype(ml_dtypes.bfloat16)
        twist = turn(self.X, self.C, self.total_cols, sign)
        return weights, np.concatenate(twist, axis=1).astype(np.float32)

    def pencil_tables(self):
        cosine, sine = turn(self.m, self.m, self.m, -1.0)
        cosine, sine = block_diagonal(cosine, self.P), block_diagonal(sine, self.P)
        ahead = np.block([[cosine, sine], [-sine, cosine]])
        behind = np.block([[cosine, -sine], [sine, cosine]]) / (self.total_rows * self.total_cols)
        twist = turn(self.D, self.m, self.total_rows, -1.0)
        twist = np.stack([np.tile(part, (1, self.P)) for part in twist]).astype(np.float32)
        return high_low(ahead), high_low(behind), twist

    def row_table(self, real, imag):
        blocks = []
        for slab in range(WIN // self.m):
            rows = slice(slab * self.m, (slab + 1) * self.m)
            for left, right in ((real[rows], imag[rows]), (-imag[rows], real[rows])):
                pieces = []
                for part in range(self.parts):
                    cols = slice(part * self.pp, (part + 1) * self.pp)
                    pieces += [left[:, cols], right[:, cols]]
                blocks.append(np.concatenate(pieces, axis=1))
        return np.concatenate(blocks, axis=0)

    def group_table(self):
        return np.kron(np.eye(self.views), np.ones((BIN, BIN))).astype(np.float32)


def hogel_tables():
    positions = np.arange(WIN)
    tapers = np.sin(np.pi * (positions + 0.5) / WIN) ** 2
    angles = -2.0 * np.pi / WIN * (positions[:, None] * positions[None, :] % WIN)
    cosine = (tapers[:, None] * np.cos(angles)).astype(np.float32)
    sine = (tapers[:, None] * np.sin(angles)).astype(np.float32)
    col = np.concatenate([cosine, sine], axis=1).astype(ml_dtypes.bfloat16)
    col_turned = np.concatenate([cosine.T, sine.T], axis=1).astype(ml_dtypes.bfloat16)
    row = np.stack([cosine / WIN, sine / WIN]).astype(ml_dtypes.bfloat16)
    return col, col_turned, row


def three_pieces(values):
    first = values.astype(BF16)
    rest = values - first.astype(F32)
    second = rest.astype(BF16)
    return first, second, (rest - second.astype(F32)).astype(BF16)


def matmul(left, right):
    return jnp.dot(left, right, preferred_element_type=F32)


def gather_chunks(arrived, chunks):
    mine = lax.axis_index("cols")
    for t, chunk in enumerate(arrived):
        chunks[mine ^ t] = chunk[...]


def scatter_chunks(chunks, leaving):
    mine = lax.axis_index("cols")
    for t, chunk in enumerate(leaving):
        chunk[...] = chunks[mine ^ t]


def put_views(plan, rows):
    pad = jnp.zeros((VIEWS - 3 * plan.own_cols, plan.lanes), F32)
    pieces = [piece.astype(F32) for piece in three_pieces(rows)]
    return jnp.concatenate([*pieces, pad], axis=0).astype(BF16)


def get_views(plan, chunk):
    chunk = chunk.astype(F32)
    n = plan.own_cols
    return chunk[:n] + chunk[n : 2 * n] + chunk[2 * n : 3 * n]


def pack_kernel(plan, field, goal, *refs):
    C, m, X = plan.C, plan.m, plan.X
    leaving, (out,) = refs[:C], refs[C:]
    for c in range(C):
        rows = slice(c * m, (c + 1) * m)
        block = jnp.concatenate([field[0, rows, :], field[1, rows, :]], axis=0)
        out[c, :X, :] = block.astype(F32).T.astype(BF16)
        i, start = c // plan.parts, c % plan.parts * plan.lanes
        out[c, X:, :] = put_views(plan, goal[i, :, start : start + plan.lanes])
    scatter_chunks(out, leaving)


def unpack_kernel(plan, *refs):
    C, m, X = plan.C, plan.m, plan.X
    arrived, (out, light, slabs) = refs[:C], refs[C:]
    gather_chunks(arrived, slabs)
    for c in range(C):
        block = slabs[c, :X, :].astype(F32).T
        out[0, m * c : m * c + m, :] = block[:m]
        out[1, m * c : m * c + m, :] = block[m:]
        i, start = c // plan.parts, c % plan.parts * plan.lanes
        light[i, :, start : start + plan.lanes] = get_views(plan, slabs[c, X:, :])


def lines_forward(plan, lanes, load, emit, weights, twist, turned):
    C, X = plan.C, plan.X
    step = 64
    for start in range(0, X, step):
        points = packed_dft([load(c, start, step) for c in range(C)], -1.0)
        for k in range(C):
            cosine = twist[start : start + step, k : k + 1]
            sine = twist[start : start + step, C + k : C + k + 1]
            across = times_i(points[k])
            if k:
                value = points[k] * cosine + across * sine
                across = across * cosine - points[k] * sine
            else:
                value = points[k]
            place = slice(k * lanes, k * lanes + lanes)
            turned[start : start + step, place] = value.astype(BF16)
            turned[X + start : X + start + step, place] = across.astype(BF16)
    group = max(1, 256 // lanes)
    for first in range(0, C, group):
        result = matmul(weights[...], turned[:, first * lanes : (first + group) * lanes])
        for k in range(group):
            for r in range(plan.R):
                rows = slice(r * plan.span, (r + 1) * plan.span)
                emit((first + k) * plan.R + r, result[rows, k * lanes : (k + 1) * lanes])


def lines_inverse(plan, lanes, packed, emit, weights, twist, step):
    C, X = plan.C, plan.X
    right = packed[...]
    for start in range(0, X, step):
        result = matmul(weights[start : start + step, :], right)
        points = []
        for k in range(C):
            value = result[:, k * lanes : (k + 1) * lanes]
            if k:
                cosine = twist[start : start + step, k : k + 1]
                sine = twist[start : start + step, C + k : C + k + 1]
                value = value * cosine + times_i(value) * sine
            points.append(value)
        for c, value in enumerate(packed_dft(points, 1.0)):
            emit(c, start, step, value)


def to_planes(plan, block):
    parts = [block[p * plan.f : (p + 1) * plan.f, :] for p in range(plan.P)]
    real = jnp.concatenate([part[:, : plan.m] for part in parts], axis=1)
    imag = jnp.concatenate([part[:, plan.m :] for part in parts], axis=1)
    return real, imag


def from_planes(plan, real, imag):
    m = plan.m
    return jnp.concatenate(
        [
            jnp.concatenate([real[:, p * m : (p + 1) * m], imag[:, p * m : (p + 1) * m]], axis=1)
            for p in range(plan.P)
        ],
        axis=0,
    )


def rows_forward_kernel(plan, weights, twist, *refs):
    C, X = plan.C, plan.X
    arrived, (_, _, out, goals, turned, slabs) = refs[:C], refs[C:]
    gather_chunks(arrived, slabs)
    goals[...] = slabs[:, X:, :]

    def load(c, start, step):
        return slabs[c, start : start + step, :].astype(F32)

    def emit(d, block):
        out[d] = jnp.concatenate(to_planes(plan, block), axis=0).astype(BF16)

    lines_forward(plan, plan.lanes, load, emit, weights, twist, turned)


def rows_inverse_kernel(plan, pencils, lights, weights, twist, *refs):
    C, X, lanes = plan.C, plan.X, plan.lanes
    leaving, (packed, out) = refs[:C], refs[C:]
    for k in range(C):
        for r in range(plan.R):
            chunk = pencils[k * plan.R + r].astype(F32)
            block = from_planes(plan, chunk[: plan.f], chunk[plan.f :])
            place = slice(k * lanes, k * lanes + lanes)
            packed[r * plan.span : (r + 1) * plan.span, place] = block.astype(BF16)
            packed[X + r * plan.span : X + (r + 1) * plan.span, place] = times_i(block).astype(BF16)

    def emit(c, start, step, value):
        out[c, start : start + step, :] = value.astype(BF16)

    lines_inverse(plan, lanes, packed, emit, weights, twist, 64)
    out[:, X:, :] = lights[...]
    scatter_chunks(out, leaving)


def columns(plan, sign, load, store, steer_re, steer_im, ahead, behind, twist, scratch):
    D, f, outer, inner = plan.D, plan.f, plan.outer, plan.inner
    half_re, half_im, rounded = scratch
    for b in range(inner):
        points = [load(inner * a + b) for a in range(outer)]
        for alpha, (re, im) in enumerate(small_dft(points, -1.0)):
            angle = -2.0 * math.pi * b * alpha / D
            cosine, sine = math.cos(angle), math.sin(angle)
            if b * alpha:
                re, im = re * cosine - im * sine, re * sine + im * cosine
            half_re[alpha * inner + b] = re
            half_im[alpha * inner + b] = im
    for alpha in range(outer):
        points = [(half_re[alpha * inner + b], half_im[alpha * inner + b]) for b in range(inner)]
        for beta, (re, im) in enumerate(small_dft(points, -1.0)):
            k = alpha + outer * beta
            cosine, sine = twist[0, k : k + 1, :], twist[1, k : k + 1, :]
            for offset, part in ((0, re * cosine - im * sine), (128, re * sine + im * cosine)):
                rounded[k, :, offset : offset + 128] = part.astype(BF16)
    group = D // 2
    for start in range(0, D, group):
        place = slice(start, start + group)

        def multiply(matrix):
            left = rounded[place].reshape(group * f, 256)
            product = matmul(left, matrix[:256, :]) + matmul(left, matrix[256:, :])
            return product.reshape(group, f, 256)

        result = multiply(ahead)
        re, im = result[:, :, :128], result[:, :, 128:]
        factor_re, factor_im = steer_re[place], sign * steer_im[place]
        for offset, part in (
            (0, re * factor_re - im * factor_im),
            (128, re * factor_im + im * factor_re),
        ):
            rounded[place, :, offset : offset + 128] = part.astype(BF16)
        result = multiply(behind)
        half_re[place] = result[:, :, :128]
        half_im[place] = result[:, :, 128:]
    for alpha in range(outer):
        points = []
        for beta in range(inner):
            k = alpha + outer * beta
            cosine, sine = twist[0, k : k + 1, :], twist[1, k : k + 1, :]
            re, im = half_re[k], half_im[k]
            points.append((re * cosine + im * sine, im * cosine - re * sine))
        for b, (re, im) in enumerate(small_dft(points, 1.0)):
            angle = 2.0 * math.pi * b * alpha / D
            cosine, sine = math.cos(angle), math.sin(angle)
            if b * alpha:
                re, im = re * cosine - im * sine, re * sine + im * cosine
            half_re[alpha + outer * b] = re
            half_im[alpha + outer * b] = im
    for b in range(inner):
        points = [(half_re[alpha + outer * b], half_im[alpha + outer * b]) for alpha in range(outer)]
        for a, (re, im) in enumerate(small_dft(points, 1.0)):
            store(inner * a + b, re, im)


def pencil_forward_kernel(plan, pencils, *refs):
    steer_re, steer_im, ahead, behind, twist, row, out, windows, *scratch = refs
    f, lanes, span = plan.f, plan.lanes, plan.span

    def load(s):
        chunk = pencils[s].astype(F32)
        return chunk[:f], chunk[f:]

    def store(s, re, im):
        block = from_planes(plan, re, im).astype(BF16)
        i, slab = s // plan.shift, s % plan.shift
        windows[i, :, slab * lanes : (slab + 1) * lanes] = block
        slab += plan.shift
        windows[(i - 1) % plan.hogel_rows, :, slab * lanes : (slab + 1) * lanes] = block

    columns(plan, 1.0, load, store, steer_re, steer_im, ahead, behind, twist, scratch)
    count = plan.hogel_rows
    result = matmul(windows[...].reshape(count * span, 2 * WIN), row[...]).astype(BF16)
    for i in range(count):
        for part in range(plan.parts):
            out[i * plan.parts + part] = result[
                i * span : (i + 1) * span, part * 2 * plan.pp : (part + 1) * 2 * plan.pp
            ]


def pencil_back_kernel(plan, lines, *refs):
    steer_re, steer_im, ahead, behind, twist, row, out, windows, *scratch = refs
    lanes, span, parts = plan.lanes, plan.span, plan.parts
    count, wide = plan.hogel_rows, 2 * plan.pp
    by_part = lines[...].reshape(count, parts, span, wide)
    result = sum(
        matmul(by_part[:, n].reshape(count * span, wide), row[n * wide : (n + 1) * wide, :])
        for n in range(parts)
    )
    windows[...] = result.reshape(count, span, 2 * WIN)

    def load(s):
        i, slab = s // plan.shift, s % plan.shift
        block = windows[i, :, slab * lanes : (slab + 1) * lanes]
        slab += plan.shift
        block = block + windows[(i - 1) % plan.hogel_rows, :, slab * lanes : (slab + 1) * lanes]
        return to_planes(plan, block)

    def store(s, re, im):
        out[s] = jnp.concatenate([re, im], axis=0).astype(BF16)

    columns(plan, -1.0, load, store, steer_re, steer_im, ahead, behind, twist, scratch)


def hogel_kernel(plan, lines, goals, *refs):
    weights_behind, twist_behind, weights_ahead, twist_ahead, col, col_turned, same = refs[:7]
    out, lights, packed, field, spectra, bright, marks, factors, weighted, back = refs[7:]
    C, X, lanes, pp = plan.C, plan.X, 2 * plan.pp, plan.pp
    total = plan.total_cols
    for k in range(C):
        block = lines[k * plan.R : (k + 1) * plan.R].reshape(X, lanes)
        place = slice(k * lanes, (k + 1) * lanes)
        packed[:X, place] = block
        packed[X:, place] = times_i(block.astype(F32)).astype(BF16)

    def emit_near(c, start, step, value):
        for n, part in enumerate((value, times_i(value))):
            rounded = part.astype(BF16)
            field[n, c * X + start : c * X + start + step, :] = rounded
            if c == 0 and start < STRIDE:
                field[n, total + start : total + start + step, :] = rounded

    lines_inverse(plan, lanes, packed, emit_near, weights_behind, twist_behind, 128)
    for j in range(plan.hogel_cols):
        window = slice(STRIDE * j, STRIDE * j + WIN)
        result = matmul(
            col_turned[...], jnp.concatenate([field[0, window, :], field[1, window, :]], axis=0)
        )
        spectra[j] = result
        power = result[:, :pp] * result[:, :pp] + result[:, pp:] * result[:, pp:]
        bright[j * VIEWS : (j + 1) * VIEWS, :] = power.reshape(VIEWS, BIN, pp).sum(axis=1)
    exact = lax.Precision.HIGHEST
    own = lax.broadcasted_iota(jnp.int32, (VIEWS, pp), 0) == (
        lax.broadcasted_iota(jnp.int32, (VIEWS, pp), 1) % VIEWS
    )
    for c in range(C):
        target = get_views(plan, goals[c])
        for j in range(plan.own_cols):
            h = c * plan.own_cols + j
            marks[h * VIEWS : (h + 1) * VIEWS, :] = jnp.where(own, target[j : j + 1, :], 0.0)
    scale = 1.0 / (BIN * BIN)
    light = scale * jnp.dot(bright[...], same[...], preferred_element_type=F32, precision=exact)
    target = jnp.dot(marks[...], same[...], preferred_element_type=F32, precision=exact)
    factors[...] = 4.0 * (light - target)
    bright[...] = light
    for c in range(C):
        rows = []
        for j in range(plan.own_cols):
            h = c * plan.own_cols + j
            block = jnp.where(own, bright[h * VIEWS : (h + 1) * VIEWS, :], 0.0)
            rows.append(jnp.sum(block, axis=0, keepdims=True))
        lights[c] = put_views(plan, jnp.concatenate(rows, axis=0))
    for j in range(plan.hogel_cols):
        for view in range(VIEWS):
            factor = factors[j * VIEWS + view : j * VIEWS + view + 1, :]
            block = slice(view * BIN, (view + 1) * BIN)
            below = slice(WIN + view * BIN, WIN + (view + 1) * BIN)
            real = (spectra[j, block, :pp] * factor).astype(BF16)
            imag = (spectra[j, block, pp:] * factor).astype(BF16)
            weighted[block, :pp] = real
            weighted[block, pp:] = imag
            weighted[below, :pp] = imag
            weighted[below, pp:] = -real
        result = matmul(col[...], weighted[...])
        first, second = STRIDE * j, STRIDE * (j + 1) % total
        if j == 0:
            back[:STRIDE] = result[:STRIDE]
        else:
            back[first : first + STRIDE] = back[first : first + STRIDE] + result[:STRIDE]
        if j < plan.hogel_cols - 1:
            back[second : second + STRIDE] = result[STRIDE:]
        else:
            back[:STRIDE] = back[:STRIDE] + result[STRIDE:]

    def load(c, start, step):
        return back[c * X + start : c * X + start + step, :]

    def emit(d, block):
        out[d] = block.astype(BF16)

    lines_forward(plan, lanes, load, emit, weights_ahead, twist_ahead, packed)


def steer_table(plan):
    index = lax.axis_index(("rows", "cols"))
    shape = (plan.D, plan.f, 128)
    k = lax.broadcasted_iota(jnp.int32, shape, 0)
    line = lax.broadcasted_iota(jnp.int32, shape, 1)
    lane = lax.broadcasted_iota(jnp.int32, shape, 2)
    u = k + plan.D * (lane % plan.m)
    v = index // plan.R + plan.C * (
        plan.span * (index % plan.R) + plan.f * (lane // plan.m) + line
    )

    def freq(position, count):
        return ((position + count // 2) % count - count // 2).astype(F32) / count

    freq_rows, freq_cols = freq(u, plan.total_rows), freq(v, plan.total_cols)
    radial = freq_rows * freq_rows + freq_cols * freq_cols
    phase = (
        -2.0
        * math.pi
        * distance_px
        * radial
        / (jnp.sqrt(index_ratio * index_ratio - radial) + index_ratio)
    )
    return jnp.cos(phase), jnp.sin(phase)


def exchange(chunks):
    return lax.all_to_all(chunks, ("rows", "cols"), split_axis=0, concat_axis=0, tiled=True)


def swap_columns(chunks):
    count = lax.axis_size("cols")
    arrived = list(chunks)
    for t in sorted(range(1, count), key=lambda t: -t.bit_count()):
        arrived[t] = lax.ppermute(chunks[t], "cols", [(i, i ^ t) for i in range(count)])
    return tuple(arrived)


def local(slm_field, target_light):
    rows_count, cols_count = lax.axis_size("rows"), lax.axis_size("cols")
    plan = Plan(rows_count, cols_count, slm_field.shape[1], slm_field.shape[2])
    C, D, X, lanes, f = plan.C, plan.D, plan.X, plan.lanes, plan.f
    span, wide = plan.span, 2 * plan.pp

    ahead, behind, twist = (jnp.asarray(t) for t in plan.pencil_tables())
    weights_ahead, twist_ahead = (jnp.asarray(t) for t in plan.line_tables(-1.0))
    weights_behind, twist_behind = (jnp.asarray(t) for t in plan.line_tables(1.0))
    col, col_turned, row = hogel_tables()
    row = plan.row_table(row[0], row[1])
    col, col_turned, row, row_turned, same = (
        jnp.asarray(t) for t in (col, col_turned, row, row.T.copy(), plan.group_table())
    )
    steer_re, steer_im = steer_table(plan)

    slabs_shapes = (shape_of((X + VIEWS, lanes), BF16),) * C
    slabs_scratch = pltpu.VMEM((C, X + VIEWS, lanes), BF16)
    views_shape = shape_of((C, VIEWS, lanes), BF16)
    pencil_shape = shape_of((D, 2 * f, 128), BF16)
    lines_shape = shape_of((D, span, wide), BF16)
    columns_scratch = (
        pltpu.VMEM((D, f, 128), F32),
        pltpu.VMEM((D, f, 128), F32),
        pltpu.VMEM((D, f, 256), BF16),
    )
    pencil_tables = (steer_re, steer_im, ahead, behind, twist)
    columns_flops = 8 * D * f * 256 * 256 + 2 * plan.hogel_rows * span * (2 * WIN) ** 2

    apart_any = pl.BlockSpec(memory_space=pl.ANY)
    slabs = call(
        lambda *refs: pack_kernel(plan, *refs),
        slabs_shapes,
        (slm_field.astype(BF16), target_light),
        (slabs_scratch,),
    )
    tall = pltpu.VMEM((2 * X, C * lanes), BF16)
    pencils, goals = call(
        lambda *refs: rows_forward_kernel(plan, *refs),
        (pencil_shape, views_shape),
        (weights_ahead, twist_ahead, *swap_columns(slabs), steer_re, steer_im),
        (tall, slabs_scratch),
        flops=2 * X * 2 * X * C * lanes,
        in_specs={C + 2: apart_any, C + 3: apart_any},
    )
    (lines,) = call(
        lambda *refs: pencil_forward_kernel(plan, *refs),
        (lines_shape,),
        (exchange(pencils), *pencil_tables, row),
        (pltpu.VMEM((plan.hogel_rows, span, 2 * WIN), BF16), *columns_scratch),
        flops=columns_flops,
    )
    tall = pltpu.VMEM((2 * X, C * wide), BF16)
    lines, lights = call(
        lambda *refs: hogel_kernel(plan, *refs),
        (lines_shape, views_shape),
        (
            exchange(lines),
            goals,
            weights_behind,
            twist_behind,
            weights_ahead,
            twist_ahead,
            col,
            col_turned,
            same,
        ),
        (
            tall,
            pltpu.VMEM((2, plan.total_cols + STRIDE, wide), BF16),
            pltpu.VMEM((plan.hogel_cols, WIN, wide), F32),
            pltpu.VMEM((plan.hogel_cols * VIEWS, plan.pp), F32),
            pltpu.VMEM((plan.hogel_cols * VIEWS, plan.pp), F32),
            pltpu.VMEM((plan.hogel_cols * VIEWS, plan.pp), F32),
            pltpu.VMEM((2 * WIN, wide), BF16),
            pltpu.VMEM((plan.total_cols, wide), F32),
        ),
        flops=4 * X * 2 * X * C * wide + 4 * plan.hogel_cols * WIN * 2 * WIN * wide,
    )
    (pencils,) = call(
        lambda *refs: pencil_back_kernel(plan, *refs),
        (pencil_shape,),
        (exchange(lines), *pencil_tables, row_turned),
        (pltpu.VMEM((plan.hogel_rows, span, 2 * WIN), F32), *columns_scratch),
        flops=columns_flops,
    )
    tall = pltpu.VMEM((2 * X, C * lanes), BF16)
    slabs = call(
        lambda *refs: rows_inverse_kernel(plan, *refs),
        slabs_shapes,
        (exchange(pencils), lights, weights_behind, twist_behind),
        (tall, slabs_scratch),
        flops=2 * X * 2 * X * C * lanes,
    )
    return call(
        lambda *refs: unpack_kernel(plan, *refs),
        (shape_of(slm_field.shape, F32), shape_of(target_light.shape, F32)),
        swap_columns(slabs),
        (slabs_scratch,),
    )


def solution(mesh):
    return jax.shard_map(
        local,
        mesh=mesh,
        in_specs=(P(None, "rows", "cols"), P("rows", "cols", None)),
        out_specs=(P(None, "rows", "cols"), P("rows", "cols", None)),
        check_vma=False,
    )
```

```python
import math

import jax
import jax.numpy as jnp
import ml_dtypes
import numpy as np
from jax import lax
from jax.experimental import pallas as pl
from jax.experimental.pallas import tpu as pltpu
from jax.sharding import PartitionSpec as P

WIN = 256
VIEWS = 16
STRIDE = 128
BIN = 16

distance_px = 16000.0
index_ratio = 15.0

BF16 = jnp.bfloat16
F32 = jnp.float32
BOTH_MINOR = (((1,), (1,)), ((), ()))


def call(body, outs, args, scratch=(), flops=0, in_specs=None, out_specs=None):
    nbytes = sum(math.prod(a.shape) * a.dtype.itemsize for a in (*outs, *args))
    specs = {}
    if in_specs:
        whole = pl.BlockSpec(memory_space=pltpu.VMEM)
        specs["in_specs"] = [in_specs.get(n, whole) for n in range(len(args))]
    if out_specs:
        specs["out_specs"] = out_specs
    return pl.pallas_call(
        body,
        out_shape=outs,
        scratch_shapes=list(scratch),
        compiler_params=pltpu.CompilerParams(vmem_limit_bytes=24 * 2**20),
        cost_estimate=pl.CostEstimate(flops=flops, bytes_accessed=nbytes, transcendentals=0),
        **specs,
    )(*args)


def shape_of(dims, dtype):
    return jax.ShapeDtypeStruct(dims, dtype)


def high_low(table):
    table = np.asarray(table, np.float32)
    high = table.astype(ml_dtypes.bfloat16)
    low = (table - high.astype(np.float32)).astype(ml_dtypes.bfloat16)
    return np.concatenate([high, low], axis=0)


def times_i(values):
    half = values.shape[-1] // 2
    if values.shape[-1] == 128:
        lanes = lax.broadcasted_iota(jnp.int32, values.shape, values.ndim - 1)
        turned = pltpu.roll(values, half, values.ndim - 1)
        return jnp.where(lanes < half, -turned, turned)
    return jnp.concatenate([-values[..., half:], values[..., :half]], axis=-1)


def scaled(value, factor):
    return value if factor == 1.0 else value * factor


def small_dft(points, sign):
    count = len(points)
    if count == 1:
        return points
    even = small_dft(points[0::2], sign)
    odd = small_dft(points[1::2], sign)
    front, back = [], []
    for k in range(count // 2):
        re, im = odd[k]
        angle = sign * 2.0 * math.pi * k / count
        cosine, sine = math.cos(angle), math.sin(angle)
        if k == 0:
            pass
        elif 4 * k == count:
            re, im = (-im, re) if sign > 0 else (im, -re)
        elif 8 * k == count:
            re, im = cosine * (re - sign * im), cosine * (im + sign * re)
        elif 8 * k == 3 * count:
            re, im = cosine * (re + sign * im), cosine * (im - sign * re)
        else:
            re, im = re * cosine - im * sine, re * sine + im * cosine
        even_re, even_im = even[k]
        front.append((even_re + re, even_im + im))
        back.append((even_re - re, even_im - im))
    return front + back


def packed_dft(points, sign):
    count = len(points)
    if count == 1:
        return points
    even = packed_dft(points[0::2], sign)
    odd = packed_dft(points[1::2], sign)
    front, back = [], []
    for k in range(count // 2):
        term = odd[k]
        angle = sign * 2.0 * math.pi * k / count
        if 4 * k == count:
            term = times_i(term) if sign > 0 else -times_i(term)
        elif k:
            term = math.cos(angle) * term + math.sin(angle) * times_i(term)
        front.append(even[k] + term)
        back.append(even[k] - term)
    return front + back


def turn(rows, cols, period, sign):
    angles = sign * 2.0 * np.pi / period * ((np.arange(rows)[:, None] * np.arange(cols)) % period)
    return np.cos(angles), np.sin(angles)


def block_diagonal(block, copies):
    return np.kron(np.eye(copies), block)


class Plan:
    def __init__(self, rows_count, cols_count, rows_dev, cols_dev):
        self.R, self.C = rows_count, cols_count
        self.D = rows_count * cols_count
        self.X = cols_dev
        self.m = rows_dev // cols_count
        self.lanes = 2 * self.m
        self.P = 128 // self.m
        self.span = cols_dev // rows_count
        self.f = self.span // self.P
        self.total_rows = rows_dev * rows_count
        self.total_cols = cols_dev * cols_count
        self.outer = 8
        self.inner = self.D // 8
        self.shift = STRIDE // self.m
        self.hogel_rows = self.total_rows // STRIDE
        self.hogel_cols = self.total_cols // STRIDE
        self.parts = self.D // self.hogel_rows
        self.pp = WIN // self.parts
        self.views = VIEWS // self.parts
        self.own_cols = cols_dev // STRIDE

    def line_tables(self, sign):
        cosine, sine = turn(self.X, self.X, self.X, sign)
        weights = np.concatenate([cosine, sine], axis=1).astype(ml_dtypes.bfloat16)
        twist = turn(self.X, self.C, self.total_cols, sign)
        return weights, np.concatenate(twist, axis=1).astype(np.float32)

    def pencil_tables(self):
        cosine, sine = turn(self.m, self.m, self.m, -1.0)
        cosine, sine = block_diagonal(cosine, self.P), block_diagonal(sine, self.P)
        ahead = np.block([[cosine, sine], [-sine, cosine]])
        behind = np.block([[cosine, -sine], [sine, cosine]]) / (self.total_rows * self.total_cols)
        twist = turn(self.D, self.m, self.total_rows, -1.0)
        twist = np.stack([np.tile(part, (1, self.P)) for part in twist]).astype(np.float32)
        return high_low(ahead), high_low(behind), twist

    def row_table(self, real, imag):
        blocks = []
        for slab in range(WIN // self.m):
            rows = slice(slab * self.m, (slab + 1) * self.m)
            for left, right in ((real[rows], imag[rows]), (-imag[rows], real[rows])):
                pieces = []
                for part in range(self.parts):
                    cols = slice(part * self.pp, (part + 1) * self.pp)
                    pieces += [left[:, cols], right[:, cols]]
                blocks.append(np.concatenate(pieces, axis=1))
        return np.concatenate(blocks, axis=0)

    def group_table(self):
        return np.kron(np.eye(self.views), np.ones((BIN, BIN))).astype(np.float32)


def hogel_tables():
    positions = np.arange(WIN)
    tapers = np.sin(np.pi * (positions + 0.5) / WIN) ** 2
    angles = -2.0 * np.pi / WIN * (positions[:, None] * positions[None, :] % WIN)
    cosine = (tapers[:, None] * np.cos(angles)).astype(np.float32)
    sine = (tapers[:, None] * np.sin(angles)).astype(np.float32)
    col = np.concatenate([cosine, sine], axis=1).astype(ml_dtypes.bfloat16)
    col_turned = np.concatenate([cosine.T, sine.T], axis=1).astype(ml_dtypes.bfloat16)
    row = np.stack([cosine / WIN, sine / WIN]).astype(ml_dtypes.bfloat16)
    return col, col_turned, row


def three_pieces(values):
    first = values.astype(BF16)
    rest = values - first.astype(F32)
    second = rest.astype(BF16)
    return first, second, (rest - second.astype(F32)).astype(BF16)


def matmul(left, right):
    return jnp.dot(left, right, preferred_element_type=F32)


def partners(count):
    return sorted(range(count), key=lambda t: (t != 0, -t.bit_count()))


def gather_chunks(arrived, chunks):
    mine = lax.axis_index("cols")
    for t, chunk in zip(partners(len(arrived)), arrived):
        chunks[mine ^ t] = chunk[...]


def scatter_chunks(chunks, leaving):
    mine = lax.axis_index("cols")
    for t, chunk in zip(partners(len(leaving)), leaving):
        chunk[...] = chunks[mine ^ t]


def put_views(plan, rows):
    pad = jnp.zeros((VIEWS - 3 * plan.own_cols, plan.lanes), F32)
    pieces = [piece.astype(F32) for piece in three_pieces(rows)]
    return jnp.concatenate([*pieces, pad], axis=0).astype(BF16)


def get_views(plan, chunk):
    chunk = chunk.astype(F32)
    n = plan.own_cols
    return chunk[:n] + chunk[n : 2 * n] + chunk[2 * n : 3 * n]


def pack_kernel(plan, field, goal, *refs):
    C, m, X = plan.C, plan.m, plan.X
    leaving, (out,) = refs[:C], refs[C:]
    for c in range(C):
        rows = slice(c * m, (c + 1) * m)
        block = jnp.concatenate([field[0, rows, :], field[1, rows, :]], axis=0)
        out[c, :X, :] = block.astype(F32).T.astype(BF16)
        i, start = c // plan.parts, c % plan.parts * plan.lanes
        out[c, X:, :] = put_views(plan, goal[i, :, start : start + plan.lanes])
    scatter_chunks(out, leaving)


def unpack_kernel(plan, *refs):
    C, m, X = plan.C, plan.m, plan.X
    arrived, (out, light, slabs) = refs[:C], refs[C:]
    gather_chunks(arrived, slabs)
    for c in range(C):
        block = slabs[c, :X, :].astype(F32).T
        out[0, m * c : m * c + m, :] = block[:m]
        out[1, m * c : m * c + m, :] = block[m:]
        i, start = c // plan.parts, c % plan.parts * plan.lanes
        light[i, :, start : start + plan.lanes] = get_views(plan, slabs[c, X:, :])


def lines_forward(plan, lanes, load, emit, weights, twist, turned):
    C, X = plan.C, plan.X
    step = 64
    for start in range(0, X, step):
        points = packed_dft([load(c, start, step) for c in range(C)], -1.0)
        for k in range(C):
            cosine = twist[start : start + step, k : k + 1]
            sine = twist[start : start + step, C + k : C + k + 1]
            across = times_i(points[k])
            if k:
                value = points[k] * cosine + across * sine
                across = across * cosine - points[k] * sine
            else:
                value = points[k]
            place = slice(k * lanes, k * lanes + lanes)
            turned[start : start + step, place] = value.astype(BF16)
            turned[X + start : X + start + step, place] = across.astype(BF16)
    group = max(1, 256 // lanes)
    for first in range(0, C, group):
        result = matmul(weights[...], turned[:, first * lanes : (first + group) * lanes])
        for k in range(group):
            for r in range(plan.R):
                rows = slice(r * plan.span, (r + 1) * plan.span)
                emit((first + k) * plan.R + r, result[rows, k * lanes : (k + 1) * lanes])


def lines_inverse(plan, lanes, packed, emit, weights, twist):
    C, X = plan.C, plan.X
    result = matmul(weights[...], packed[...])
    step = 64
    for start in range(0, X, step):
        rows = slice(start, start + step)
        points = []
        for k in range(C):
            value = result[rows, k * lanes : (k + 1) * lanes]
            if k:
                cosine, sine = twist[rows, k : k + 1], twist[rows, C + k : C + k + 1]
                value = value * cosine + times_i(value) * sine
            points.append(value)
        for c, value in enumerate(packed_dft(points, 1.0)):
            emit(c, start, step, value)


def to_planes(plan, block):
    parts = [block[p * plan.f : (p + 1) * plan.f, :] for p in range(plan.P)]
    real = jnp.concatenate([part[:, : plan.m] for part in parts], axis=1)
    imag = jnp.concatenate([part[:, plan.m :] for part in parts], axis=1)
    return real, imag


def from_planes(plan, real, imag):
    m = plan.m
    return jnp.concatenate(
        [
            jnp.concatenate([real[:, p * m : (p + 1) * m], imag[:, p * m : (p + 1) * m]], axis=1)
            for p in range(plan.P)
        ],
        axis=0,
    )


def rows_forward_kernel(plan, weights, twist, *refs):
    C, X = plan.C, plan.X
    arrived, (_, _, out, goals, turned, slabs) = refs[:C], refs[C:]
    gather_chunks(arrived, slabs)
    goals[...] = slabs[:, X:, :]

    def load(c, start, step):
        return slabs[c, start : start + step, :].astype(F32)

    def emit(d, block):
        out[d] = jnp.concatenate(to_planes(plan, block), axis=0).astype(BF16)

    lines_forward(plan, plan.lanes, load, emit, weights, twist, turned)


def rows_inverse_kernel(plan, pencils, lights, weights, twist, *refs):
    C, X, lanes = plan.C, plan.X, plan.lanes
    leaving, (packed, out) = refs[:C], refs[C:]
    for k in range(C):
        for r in range(plan.R):
            chunk = pencils[k * plan.R + r].astype(F32)
            block = from_planes(plan, chunk[: plan.f], chunk[plan.f :])
            place = slice(k * lanes, k * lanes + lanes)
            packed[r * plan.span : (r + 1) * plan.span, place] = block.astype(BF16)
            packed[X + r * plan.span : X + (r + 1) * plan.span, place] = times_i(block).astype(BF16)

    def emit(c, start, step, value):
        out[c, start : start + step, :] = value.astype(BF16)

    lines_inverse(plan, lanes, packed, emit, weights, twist)
    out[:, X:, :] = lights[...]
    scatter_chunks(out, leaving)


def columns(plan, sign, load, store, steer_re, steer_im, ahead, behind, twist, scratch):
    D, f, outer, inner = plan.D, plan.f, plan.outer, plan.inner
    half_re, half_im, rounded = scratch
    for b in range(inner):
        points = [load(inner * a + b) for a in range(outer)]
        for alpha, (re, im) in enumerate(small_dft(points, -1.0)):
            angle = -2.0 * math.pi * b * alpha / D
            cosine, sine = math.cos(angle), math.sin(angle)
            if b * alpha:
                re, im = re * cosine - im * sine, re * sine + im * cosine
            half_re[alpha * inner + b] = re
            half_im[alpha * inner + b] = im
    for alpha in range(outer):
        points = [(half_re[alpha * inner + b], half_im[alpha * inner + b]) for b in range(inner)]
        for beta, (re, im) in enumerate(small_dft(points, -1.0)):
            k = alpha + outer * beta
            cosine, sine = twist[0, k : k + 1, :], twist[1, k : k + 1, :]
            for offset, part in ((0, re * cosine - im * sine), (128, re * sine + im * cosine)):
                rounded[k, :, offset : offset + 128] = part.astype(BF16)
    group = D // 2
    for start in range(0, D, group):
        place = slice(start, start + group)

        def multiply(matrix):
            left = rounded[place].reshape(group * f, 256)
            product = matmul(left, matrix[:256, :]) + matmul(left, matrix[256:, :])
            return product.reshape(group, f, 256)

        result = multiply(ahead)
        re, im = result[:, :, :128], result[:, :, 128:]
        factor_re, factor_im = steer_re[place], sign * steer_im[place]
        for offset, part in (
            (0, re * factor_re - im * factor_im),
            (128, re * factor_im + im * factor_re),
        ):
            rounded[place, :, offset : offset + 128] = part.astype(BF16)
        result = multiply(behind)
        half_re[place] = result[:, :, :128]
        half_im[place] = result[:, :, 128:]
    for alpha in range(outer):
        points = []
        for beta in range(inner):
            k = alpha + outer * beta
            cosine, sine = twist[0, k : k + 1, :], twist[1, k : k + 1, :]
            re, im = half_re[k], half_im[k]
            points.append((re * cosine + im * sine, im * cosine - re * sine))
        for b, (re, im) in enumerate(small_dft(points, 1.0)):
            angle = 2.0 * math.pi * b * alpha / D
            cosine, sine = math.cos(angle), math.sin(angle)
            if b * alpha:
                re, im = re * cosine - im * sine, re * sine + im * cosine
            half_re[alpha + outer * b] = re
            half_im[alpha + outer * b] = im
    for b in range(inner):
        points = [(half_re[alpha + outer * b], half_im[alpha + outer * b]) for alpha in range(outer)]
        for a, (re, im) in enumerate(small_dft(points, 1.0)):
            store(inner * a + b, re, im)


def pencil_forward_kernel(plan, pencils, *refs):
    steer_re, steer_im, ahead, behind, twist, row, out, windows, *scratch = refs
    f, lanes, span = plan.f, plan.lanes, plan.span

    def load(s):
        chunk = pencils[s].astype(F32)
        return chunk[:f], chunk[f:]

    def store(s, re, im):
        block = from_planes(plan, re, im).astype(BF16)
        i, slab = s // plan.shift, s % plan.shift
        windows[i, :, slab * lanes : (slab + 1) * lanes] = block
        slab += plan.shift
        windows[(i - 1) % plan.hogel_rows, :, slab * lanes : (slab + 1) * lanes] = block

    columns(plan, 1.0, load, store, steer_re, steer_im, ahead, behind, twist, scratch)
    count = plan.hogel_rows
    result = matmul(windows[...].reshape(count * span, 2 * WIN), row[...]).astype(BF16)
    for i in range(count):
        for part in range(plan.parts):
            out[i * plan.parts + part] = result[
                i * span : (i + 1) * span, part * 2 * plan.pp : (part + 1) * 2 * plan.pp
            ]


def pencil_back_kernel(plan, lines, *refs):
    steer_re, steer_im, ahead, behind, twist, row, out, windows, *scratch = refs
    lanes, span, parts = plan.lanes, plan.span, plan.parts
    count, wide = plan.hogel_rows, 2 * plan.pp
    by_part = lines[...].reshape(count, parts, span, wide)
    result = sum(
        matmul(by_part[:, n].reshape(count * span, wide), row[n * wide : (n + 1) * wide, :])
        for n in range(parts)
    )
    windows[...] = result.reshape(count, span, 2 * WIN)

    def load(s):
        i, slab = s // plan.shift, s % plan.shift
        block = windows[i, :, slab * lanes : (slab + 1) * lanes]
        slab += plan.shift
        block = block + windows[(i - 1) % plan.hogel_rows, :, slab * lanes : (slab + 1) * lanes]
        return to_planes(plan, block)

    def store(s, re, im):
        out[s] = jnp.concatenate([re, im], axis=0).astype(BF16)

    columns(plan, -1.0, load, store, steer_re, steer_im, ahead, behind, twist, scratch)


def hogel_kernel(plan, lines, goals, *refs):
    weights_behind, twist_behind, weights_ahead, twist_ahead, col, col_turned, same = refs[:7]
    out, lights, packed, field, spectra, bright, marks, factors, weighted, back = refs[7:]
    C, X, lanes, pp = plan.C, plan.X, 2 * plan.pp, plan.pp
    total = plan.total_cols
    for k in range(C):
        block = lines[k * plan.R : (k + 1) * plan.R].reshape(X, lanes)
        place = slice(k * lanes, (k + 1) * lanes)
        packed[:X, place] = block
        packed[X:, place] = times_i(block.astype(F32)).astype(BF16)

    def emit_near(c, start, step, value):
        for n, part in enumerate((value, times_i(value))):
            rounded = part.astype(BF16)
            field[n, c * X + start : c * X + start + step, :] = rounded
            if c == 0 and start < STRIDE:
                field[n, total + start : total + start + step, :] = rounded

    lines_inverse(plan, lanes, packed, emit_near, weights_behind, twist_behind)
    for j in range(plan.hogel_cols):
        window = slice(STRIDE * j, STRIDE * j + WIN)
        result = matmul(
            col_turned[...], jnp.concatenate([field[0, window, :], field[1, window, :]], axis=0)
        )
        spectra[j] = result
        power = result[:, :pp] * result[:, :pp] + result[:, pp:] * result[:, pp:]
        bright[j * VIEWS : (j + 1) * VIEWS, :] = power.reshape(VIEWS, BIN, pp).sum(axis=1)
    exact = lax.Precision.HIGHEST
    own = lax.broadcasted_iota(jnp.int32, (VIEWS, pp), 0) == (
        lax.broadcasted_iota(jnp.int32, (VIEWS, pp), 1) % VIEWS
    )
    for c in range(C):
        target = get_views(plan, goals[c])
        for j in range(plan.own_cols):
            h = c * plan.own_cols + j
            marks[h * VIEWS : (h + 1) * VIEWS, :] = jnp.where(own, target[j : j + 1, :], 0.0)
    scale = 1.0 / (BIN * BIN)
    light = scale * jnp.dot(bright[...], same[...], preferred_element_type=F32, precision=exact)
    target = jnp.dot(marks[...], same[...], preferred_element_type=F32, precision=exact)
    factors[...] = 4.0 * (light - target)
    bright[...] = light
    for c in range(C):
        rows = []
        for j in range(plan.own_cols):
            h = c * plan.own_cols + j
            block = jnp.where(own, bright[h * VIEWS : (h + 1) * VIEWS, :], 0.0)
            rows.append(jnp.sum(block, axis=0, keepdims=True))
        lights[c] = put_views(plan, jnp.concatenate(rows, axis=0))
    for j in range(plan.hogel_cols):
        for view in range(VIEWS):
            factor = factors[j * VIEWS + view : j * VIEWS + view + 1, :]
            block = slice(view * BIN, (view + 1) * BIN)
            below = slice(WIN + view * BIN, WIN + (view + 1) * BIN)
            real = (spectra[j, block, :pp] * factor).astype(BF16)
            imag = (spectra[j, block, pp:] * factor).astype(BF16)
            weighted[block, :pp] = real
            weighted[block, pp:] = imag
            weighted[below, :pp] = imag
            weighted[below, pp:] = -real
        result = matmul(col[...], weighted[...])
        first, second = STRIDE * j, STRIDE * (j + 1) % total
        if j == 0:
            back[:STRIDE] = result[:STRIDE]
        else:
            back[first : first + STRIDE] = back[first : first + STRIDE] + result[:STRIDE]
        if j < plan.hogel_cols - 1:
            back[second : second + STRIDE] = result[STRIDE:]
        else:
            back[:STRIDE] = back[:STRIDE] + result[STRIDE:]

    def load(c, start, step):
        return back[c * X + start : c * X + start + step, :]

    def emit(d, block):
        out[d] = block.astype(BF16)

    lines_forward(plan, lanes, load, emit, weights_ahead, twist_ahead, packed)


def steer_table(plan):
    index = lax.axis_index(("rows", "cols"))
    shape = (plan.D, plan.f, 128)
    k = lax.broadcasted_iota(jnp.int32, shape, 0)
    line = lax.broadcasted_iota(jnp.int32, shape, 1)
    lane = lax.broadcasted_iota(jnp.int32, shape, 2)
    u = k + plan.D * (lane % plan.m)
    v = index // plan.R + plan.C * (
        plan.span * (index % plan.R) + plan.f * (lane // plan.m) + line
    )

    def freq(position, count):
        return ((position + count // 2) % count - count // 2).astype(F32) / count

    freq_rows, freq_cols = freq(u, plan.total_rows), freq(v, plan.total_cols)
    radial = freq_rows * freq_rows + freq_cols * freq_cols
    phase = (
        -2.0
        * math.pi
        * distance_px
        * radial
        / (jnp.sqrt(index_ratio * index_ratio - radial) + index_ratio)
    )
    return jnp.cos(phase), jnp.sin(phase)


def exchange(chunks):
    return lax.all_to_all(chunks, ("rows", "cols"), split_axis=0, concat_axis=0, tiled=True)


def swap_columns(chunks):
    count = lax.axis_size("cols")
    return tuple(
        lax.ppermute(chunk, "cols", [(i, i ^ t) for i in range(count)]) if t else chunk
        for t, chunk in zip(partners(count), chunks)
    )


def local(slm_field, target_light):
    rows_count, cols_count = lax.axis_size("rows"), lax.axis_size("cols")
    plan = Plan(rows_count, cols_count, slm_field.shape[1], slm_field.shape[2])
    C, D, X, lanes, f = plan.C, plan.D, plan.X, plan.lanes, plan.f
    span, wide = plan.span, 2 * plan.pp

    ahead, behind, twist = (jnp.asarray(t) for t in plan.pencil_tables())
    weights_ahead, twist_ahead = (jnp.asarray(t) for t in plan.line_tables(-1.0))
    weights_behind, twist_behind = (jnp.asarray(t) for t in plan.line_tables(1.0))
    col, col_turned, row = hogel_tables()
    row = plan.row_table(row[0], row[1])
    col, col_turned, row, row_turned, same = (
        jnp.asarray(t) for t in (col, col_turned, row, row.T.copy(), plan.group_table())
    )
    steer_re, steer_im = steer_table(plan)

    slabs_shapes = (shape_of((X + VIEWS, lanes), BF16),) * C
    slabs_scratch = pltpu.VMEM((C, X + VIEWS, lanes), BF16)
    views_shape = shape_of((C, VIEWS, lanes), BF16)
    pencil_shape = shape_of((D, 2 * f, 128), BF16)
    lines_shape = shape_of((D, span, wide), BF16)
    columns_scratch = (
        pltpu.VMEM((D, f, 128), F32),
        pltpu.VMEM((D, f, 128), F32),
        pltpu.VMEM((D, f, 256), BF16),
    )
    pencil_tables = (steer_re, steer_im, ahead, behind, twist)
    columns_flops = 8 * D * f * 256 * 256 + 2 * plan.hogel_rows * span * (2 * WIN) ** 2

    apart_any = pl.BlockSpec(memory_space=pl.ANY)
    slabs = call(
        lambda *refs: pack_kernel(plan, *refs),
        slabs_shapes,
        (slm_field.astype(BF16), target_light),
        (slabs_scratch,),
    )
    tall = pltpu.VMEM((2 * X, C * lanes), BF16)
    pencils, goals = call(
        lambda *refs: rows_forward_kernel(plan, *refs),
        (pencil_shape, views_shape),
        (weights_ahead, twist_ahead, *swap_columns(slabs), steer_re, steer_im),
        (tall, slabs_scratch),
        flops=2 * X * 2 * X * C * lanes,
        in_specs={C + 2: apart_any, C + 3: apart_any},
    )
    (lines,) = call(
        lambda *refs: pencil_forward_kernel(plan, *refs),
        (lines_shape,),
        (exchange(pencils), *pencil_tables, row),
        (pltpu.VMEM((plan.hogel_rows, span, 2 * WIN), BF16), *columns_scratch),
        flops=columns_flops,
    )
    tall = pltpu.VMEM((2 * X, C * wide), BF16)
    lines, lights = call(
        lambda *refs: hogel_kernel(plan, *refs),
        (lines_shape, views_shape),
        (
            exchange(lines),
            goals,
            weights_behind,
            twist_behind,
            weights_ahead,
            twist_ahead,
            col,
            col_turned,
            same,
        ),
        (
            tall,
            pltpu.VMEM((2, plan.total_cols + STRIDE, wide), BF16),
            pltpu.VMEM((plan.hogel_cols, WIN, wide), F32),
            pltpu.VMEM((plan.hogel_cols * VIEWS, plan.pp), F32),
            pltpu.VMEM((plan.hogel_cols * VIEWS, plan.pp), F32),
            pltpu.VMEM((plan.hogel_cols * VIEWS, plan.pp), F32),
            pltpu.VMEM((2 * WIN, wide), BF16),
            pltpu.VMEM((plan.total_cols, wide), F32),
        ),
        flops=4 * X * 2 * X * C * wide + 4 * plan.hogel_cols * WIN * 2 * WIN * wide,
    )
    (pencils,) = call(
        lambda *refs: pencil_back_kernel(plan, *refs),
        (pencil_shape,),
        (exchange(lines), *pencil_tables, row_turned),
        (pltpu.VMEM((plan.hogel_rows, span, 2 * WIN), F32), *columns_scratch),
        flops=columns_flops,
    )
    tall = pltpu.VMEM((2 * X, C * lanes), BF16)
    slabs = call(
        lambda *refs: rows_inverse_kernel(plan, *refs),
        slabs_shapes,
        (exchange(pencils), lights, weights_behind, twist_behind),
        (tall, slabs_scratch),
        flops=2 * X * 2 * X * C * lanes,
    )
    return call(
        lambda *refs: unpack_kernel(plan, *refs),
        (shape_of(slm_field.shape, F32), shape_of(target_light.shape, F32)),
        swap_columns(slabs),
        (slabs_scratch,),
    )


def solution(mesh):
    return jax.shard_map(
        local,
        mesh=mesh,
        in_specs=(P(None, "rows", "cols"), P("rows", "cols", None)),
        out_specs=(P(None, "rows", "cols"), P("rows", "cols", None)),
        check_vma=False,
    )
```

```python
import math

import jax
import jax.numpy as jnp
import ml_dtypes
import numpy as np
from jax import lax
from jax.experimental import pallas as pl
from jax.experimental.pallas import tpu as pltpu
from jax.sharding import PartitionSpec as P

WIN = 256
VIEWS = 16
STRIDE = 128
BIN = 16

distance_px = 16000.0
index_ratio = 15.0

BF16 = jnp.bfloat16
F32 = jnp.float32
BOTH_MINOR = (((1,), (1,)), ((), ()))


def call(body, outs, args, scratch=(), flops=0, in_specs=None, out_specs=None):
    nbytes = sum(math.prod(a.shape) * a.dtype.itemsize for a in (*outs, *args))
    specs = {}
    if in_specs:
        whole = pl.BlockSpec(memory_space=pltpu.VMEM)
        specs["in_specs"] = [in_specs.get(n, whole) for n in range(len(args))]
    if out_specs:
        specs["out_specs"] = out_specs
    return pl.pallas_call(
        body,
        out_shape=outs,
        scratch_shapes=list(scratch),
        compiler_params=pltpu.CompilerParams(vmem_limit_bytes=24 * 2**20),
        cost_estimate=pl.CostEstimate(flops=flops, bytes_accessed=nbytes, transcendentals=0),
        **specs,
    )(*args)


def shape_of(dims, dtype):
    return jax.ShapeDtypeStruct(dims, dtype)


def high_low(table):
    table = np.asarray(table, np.float32)
    high = table.astype(ml_dtypes.bfloat16)
    low = (table - high.astype(np.float32)).astype(ml_dtypes.bfloat16)
    return np.concatenate([high, low], axis=0)


def times_i(values):
    half = values.shape[-1] // 2
    if values.shape[-1] == 128:
        lanes = lax.broadcasted_iota(jnp.int32, values.shape, values.ndim - 1)
        turned = pltpu.roll(values, half, values.ndim - 1)
        return jnp.where(lanes < half, -turned, turned)
    return jnp.concatenate([-values[..., half:], values[..., :half]], axis=-1)


def scaled(value, factor):
    return value if factor == 1.0 else value * factor


def small_dft(points, sign):
    count = len(points)
    if count == 1:
        return points
    even = small_dft(points[0::2], sign)
    odd = small_dft(points[1::2], sign)
    front, back = [], []
    for k in range(count // 2):
        re, im = odd[k]
        angle = sign * 2.0 * math.pi * k / count
        cosine, sine = math.cos(angle), math.sin(angle)
        if k == 0:
            pass
        elif 4 * k == count:
            re, im = (-im, re) if sign > 0 else (im, -re)
        elif 8 * k == count:
            re, im = cosine * (re - sign * im), cosine * (im + sign * re)
        elif 8 * k == 3 * count:
            re, im = cosine * (re + sign * im), cosine * (im - sign * re)
        else:
            re, im = re * cosine - im * sine, re * sine + im * cosine
        even_re, even_im = even[k]
        front.append((even_re + re, even_im + im))
        back.append((even_re - re, even_im - im))
    return front + back


def packed_dft(points, sign):
    count = len(points)
    if count == 1:
        return points
    even = packed_dft(points[0::2], sign)
    odd = packed_dft(points[1::2], sign)
    front, back = [], []
    for k in range(count // 2):
        term = odd[k]
        angle = sign * 2.0 * math.pi * k / count
        if 4 * k == count:
            term = times_i(term) if sign > 0 else -times_i(term)
        elif k:
            term = math.cos(angle) * term + math.sin(angle) * times_i(term)
        front.append(even[k] + term)
        back.append(even[k] - term)
    return front + back


def turn(rows, cols, period, sign):
    angles = sign * 2.0 * np.pi / period * ((np.arange(rows)[:, None] * np.arange(cols)) % period)
    return np.cos(angles), np.sin(angles)


def block_diagonal(block, copies):
    return np.kron(np.eye(copies), block)


class Plan:
    def __init__(self, rows_count, cols_count, rows_dev, cols_dev):
        self.R, self.C = rows_count, cols_count
        self.D = rows_count * cols_count
        self.X = cols_dev
        self.m = rows_dev // cols_count
        self.lanes = 2 * self.m
        self.P = 128 // self.m
        self.span = cols_dev // rows_count
        self.f = self.span // self.P
        self.total_rows = rows_dev * rows_count
        self.total_cols = cols_dev * cols_count
        self.outer = 8
        self.inner = self.D // 8
        self.shift = STRIDE // self.m
        self.hogel_rows = self.total_rows // STRIDE
        self.hogel_cols = self.total_cols // STRIDE
        self.parts = self.D // self.hogel_rows
        self.pp = WIN // self.parts
        self.halves = 2
        self.half = self.pp // self.halves
        self.wide = 2 * self.half
        self.own_cols = cols_dev // STRIDE

    def line_tables(self, sign):
        cosine, sine = turn(self.X, self.X, self.X, sign)
        weights = high_low(np.concatenate([cosine, sine], axis=1)).reshape(2, self.X, 2 * self.X)
        twist = turn(self.X, self.C, self.total_cols, sign)
        return weights, np.concatenate(twist, axis=1).astype(np.float32)

    def pencil_tables(self):
        cosine, sine = turn(self.m, self.m, self.m, -1.0)
        cosine, sine = block_diagonal(cosine, self.P), block_diagonal(sine, self.P)
        ahead = np.block([[cosine, sine], [-sine, cosine]])
        behind = np.block([[cosine, -sine], [sine, cosine]]) / (self.total_rows * self.total_cols)
        twist = turn(self.D, self.m, self.total_rows, -1.0)
        twist = np.stack([np.tile(part, (1, self.P)) for part in twist]).astype(np.float32)
        return high_low(ahead), high_low(behind), twist

    def row_table(self, real, imag):
        blocks = []
        for slab in range(WIN // self.m):
            rows = slice(slab * self.m, (slab + 1) * self.m)
            for left, right in ((real[rows], imag[rows]), (-imag[rows], real[rows])):
                pieces = []
                for half in range(self.halves):
                    for part in range(self.parts):
                        start = part * self.pp + half * self.half
                        cols = slice(start, start + self.half)
                        pieces += [left[:, cols], right[:, cols]]
                blocks.append(np.concatenate(pieces, axis=1))
        return np.concatenate(blocks, axis=0)

    def group_table(self):
        return np.kron(np.eye(self.wide // BIN), np.ones((BIN, BIN))).astype(np.float32)


def hogel_tables():
    positions = np.arange(WIN)
    tapers = np.sin(np.pi * (positions + 0.5) / WIN) ** 2
    angles = -2.0 * np.pi / WIN * (positions[:, None] * positions[None, :] % WIN)
    cosine = (tapers[:, None] * np.cos(angles)).astype(np.float32)
    sine = (tapers[:, None] * np.sin(angles)).astype(np.float32)
    col = np.concatenate([cosine, sine], axis=1).astype(ml_dtypes.bfloat16)
    col_turned = np.concatenate([cosine.T, sine.T], axis=1).astype(ml_dtypes.bfloat16)
    row = np.stack([cosine / WIN, sine / WIN]).astype(ml_dtypes.bfloat16)
    return col, col_turned, row


def three_pieces(values):
    first = values.astype(BF16)
    rest = values - first.astype(F32)
    second = rest.astype(BF16)
    return first, second, (rest - second.astype(F32)).astype(BF16)


def matmul(left, right):
    return jnp.dot(left, right, preferred_element_type=F32)


def partners(count):
    return sorted(range(count), key=lambda t: (t != 0, -t.bit_count()))


def gather_chunks(arrived, chunks):
    mine = lax.axis_index("cols")
    for t, chunk in zip(partners(len(arrived)), arrived):
        chunks[mine ^ t] = chunk[...]


def scatter_chunks(chunks, leaving):
    mine = lax.axis_index("cols")
    for t, chunk in zip(partners(len(leaving)), leaving):
        chunk[...] = chunks[mine ^ t]


def put_views(plan, rows):
    pad = jnp.zeros((VIEWS - 3 * plan.own_cols, rows.shape[1]), F32)
    pieces = [piece.astype(F32) for piece in three_pieces(rows)]
    return jnp.concatenate([*pieces, pad], axis=0).astype(BF16)


def get_views(plan, chunk):
    chunk = chunk.astype(F32)
    n = plan.own_cols
    return chunk[:n] + chunk[n : 2 * n] + chunk[2 * n : 3 * n]


def pack_kernel(plan, field, goal, *refs):
    C, m, X = plan.C, plan.m, plan.X
    leaving, (out,) = refs[:C], refs[C:]
    for c in range(C):
        rows = slice(c * m, (c + 1) * m)
        block = jnp.concatenate([field[0, rows, :], field[1, rows, :]], axis=0)
        out[c, :X, :] = block.astype(F32).T.astype(BF16)
        i, start = c // plan.parts, c % plan.parts * plan.lanes
        out[c, X:, :] = put_views(plan, goal[i, :, start : start + plan.lanes])
    scatter_chunks(out, leaving)


def unpack_kernel(plan, *refs):
    C, m, X = plan.C, plan.m, plan.X
    arrived, (out, light, slabs) = refs[:C], refs[C:]
    gather_chunks(arrived, slabs)
    for c in range(C):
        block = slabs[c, :X, :].astype(F32).T
        out[0, m * c : m * c + m, :] = block[:m]
        out[1, m * c : m * c + m, :] = block[m:]
        i, start = c // plan.parts, c % plan.parts * plan.lanes
        light[i, :, start : start + plan.lanes] = get_views(plan, slabs[c, X:, :])


def lines_forward(plan, lanes, load, emit, weights, twist, turned):
    C, X = plan.C, plan.X
    step = 64
    for start in range(0, X, step):
        points = packed_dft([load(c, start, step) for c in range(C)], -1.0)
        for k in range(C):
            cosine = twist[start : start + step, k : k + 1]
            sine = twist[start : start + step, C + k : C + k + 1]
            across = times_i(points[k])
            if k:
                value = points[k] * cosine + across * sine
                across = across * cosine - points[k] * sine
            else:
                value = points[k]
            place = slice(k * lanes, k * lanes + lanes)
            turned[start : start + step, place] = value.astype(BF16)
            turned[X + start : X + start + step, place] = across.astype(BF16)
    group = max(1, 256 // lanes)
    for first in range(0, C, group):
        result = matmul(weights[...], turned[:, first * lanes : (first + group) * lanes])
        for k in range(group):
            for r in range(plan.R):
                rows = slice(r * plan.span, (r + 1) * plan.span)
                emit((first + k) * plan.R + r, result[rows, k * lanes : (k + 1) * lanes])


def lines_inverse(plan, lanes, packed, emit, weights, twist):
    C, X = plan.C, plan.X
    result = matmul(weights[...], packed[...])
    step = 64
    for start in range(0, X, step):
        rows = slice(start, start + step)
        points = []
        for k in range(C):
            value = result[rows, k * lanes : (k + 1) * lanes]
            if k:
                cosine, sine = twist[rows, k : k + 1], twist[rows, C + k : C + k + 1]
                value = value * cosine + times_i(value) * sine
            points.append(value)
        for c, value in enumerate(packed_dft(points, 1.0)):
            emit(c, start, step, value)


def lines_inverse_fine(plan, lanes, packed, emit, weights, twist):
    C, X = plan.C, plan.X
    step = 64
    for start in range(0, X, step):
        rows = slice(start, start + step)
        result = matmul(weights[0, rows, :], packed[...]) + matmul(weights[1, rows, :], packed[...])
        points = []
        for k in range(C):
            value = result[:, k * lanes : (k + 1) * lanes]
            if k:
                cosine, sine = twist[rows, k : k + 1], twist[rows, C + k : C + k + 1]
                value = value * cosine + times_i(value) * sine
            points.append(value)
        for c, value in enumerate(packed_dft(points, 1.0)):
            emit(c, start, step, value)


def to_planes(plan, block):
    parts = [block[p * plan.f : (p + 1) * plan.f, :] for p in range(plan.P)]
    real = jnp.concatenate([part[:, : plan.m] for part in parts], axis=1)
    imag = jnp.concatenate([part[:, plan.m :] for part in parts], axis=1)
    return real, imag


def from_planes(plan, real, imag):
    m = plan.m
    return jnp.concatenate(
        [
            jnp.concatenate([real[:, p * m : (p + 1) * m], imag[:, p * m : (p + 1) * m]], axis=1)
            for p in range(plan.P)
        ],
        axis=0,
    )


def rows_forward_kernel(plan, weights, twist, *refs):
    C, X = plan.C, plan.X
    arrived, (_, _, out, goals, turned, slabs) = refs[:C], refs[C:]
    gather_chunks(arrived, slabs)
    goals[...] = slabs[:, X:, :]

    def load(c, start, step):
        return slabs[c, start : start + step, :].astype(F32)

    def emit(d, block):
        out[d] = jnp.concatenate(to_planes(plan, block), axis=0).astype(BF16)

    lines_forward(plan, plan.lanes, load, emit, weights, twist, turned)


def rows_inverse_kernel(plan, pencils, first, second, weights, twist, *refs):
    C, X, lanes = plan.C, plan.X, plan.lanes
    leaving, (packed, out) = refs[:C], refs[C:]
    for k in range(C):
        for r in range(plan.R):
            chunk = pencils[k * plan.R + r].astype(F32)
            block = from_planes(plan, chunk[: plan.f], chunk[plan.f :])
            place = slice(k * lanes, k * lanes + lanes)
            packed[r * plan.span : (r + 1) * plan.span, place] = block.astype(BF16)
            packed[X + r * plan.span : X + (r + 1) * plan.span, place] = times_i(block).astype(BF16)

    def emit(c, start, step, value):
        out[c, start : start + step, :] = value.astype(BF16)

    lines_inverse_fine(plan, lanes, packed, emit, weights, twist)
    out[:, X:, :] = jnp.concatenate([first[...], second[...]], axis=-1)
    scatter_chunks(out, leaving)


def columns(plan, sign, load, store, steer_re, steer_im, ahead, behind, twist, scratch):
    D, f, outer, inner = plan.D, plan.f, plan.outer, plan.inner
    half_re, half_im, rounded = scratch
    for b in range(inner):
        points = [load(inner * a + b) for a in range(outer)]
        for alpha, (re, im) in enumerate(small_dft(points, -1.0)):
            angle = -2.0 * math.pi * b * alpha / D
            cosine, sine = math.cos(angle), math.sin(angle)
            if b * alpha:
                re, im = re * cosine - im * sine, re * sine + im * cosine
            half_re[alpha * inner + b] = re
            half_im[alpha * inner + b] = im
    for alpha in range(outer):
        points = [(half_re[alpha * inner + b], half_im[alpha * inner + b]) for b in range(inner)]
        for beta, (re, im) in enumerate(small_dft(points, -1.0)):
            k = alpha + outer * beta
            cosine, sine = twist[0, k : k + 1, :], twist[1, k : k + 1, :]
            for offset, part in ((0, re * cosine - im * sine), (128, re * sine + im * cosine)):
                rounded[k, :, offset : offset + 128] = part.astype(BF16)
    group = D // 2
    for start in range(0, D, group):
        place = slice(start, start + group)

        def multiply(matrix):
            left = rounded[place].reshape(group * f, 256)
            product = matmul(left, matrix[:256, :]) + matmul(left, matrix[256:, :])
            return product.reshape(group, f, 256)

        result = multiply(ahead)
        re, im = result[:, :, :128], result[:, :, 128:]
        factor_re, factor_im = steer_re[place], sign * steer_im[place]
        for offset, part in (
            (0, re * factor_re - im * factor_im),
            (128, re * factor_im + im * factor_re),
        ):
            rounded[place, :, offset : offset + 128] = part.astype(BF16)
        result = multiply(behind)
        half_re[place] = result[:, :, :128]
        half_im[place] = result[:, :, 128:]
    for alpha in range(outer):
        points = []
        for beta in range(inner):
            k = alpha + outer * beta
            cosine, sine = twist[0, k : k + 1, :], twist[1, k : k + 1, :]
            re, im = half_re[k], half_im[k]
            points.append((re * cosine + im * sine, im * cosine - re * sine))
        for b, (re, im) in enumerate(small_dft(points, 1.0)):
            angle = 2.0 * math.pi * b * alpha / D
            cosine, sine = math.cos(angle), math.sin(angle)
            if b * alpha:
                re, im = re * cosine - im * sine, re * sine + im * cosine
            half_re[alpha + outer * b] = re
            half_im[alpha + outer * b] = im
    for b in range(inner):
        points = [(half_re[alpha + outer * b], half_im[alpha + outer * b]) for alpha in range(outer)]
        for a, (re, im) in enumerate(small_dft(points, 1.0)):
            store(inner * a + b, re, im)


def pencil_forward_kernel(plan, pencils, *refs):
    steer_re, steer_im, ahead, behind, twist, row, *rest = refs
    outs, (windows, *scratch) = rest[: plan.halves], rest[plan.halves :]
    f, lanes, span = plan.f, plan.lanes, plan.span

    def load(s):
        chunk = pencils[s].astype(F32)
        return chunk[:f], chunk[f:]

    def store(s, re, im):
        block = from_planes(plan, re, im).astype(BF16)
        i, slab = s // plan.shift, s % plan.shift
        windows[i, :, slab * lanes : (slab + 1) * lanes] = block
        slab += plan.shift
        windows[(i - 1) % plan.hogel_rows, :, slab * lanes : (slab + 1) * lanes] = block

    columns(plan, 1.0, load, store, steer_re, steer_im, ahead, behind, twist, scratch)
    count = plan.hogel_rows
    result = matmul(windows[...].reshape(count * span, 2 * WIN), row[...]).astype(BF16)
    for half, out in enumerate(outs):
        for i in range(count):
            for part in range(plan.parts):
                place = (half * plan.parts + part) * plan.wide
                out[i * plan.parts + part] = result[
                    i * span : (i + 1) * span, place : place + plan.wide
                ]


def pencil_back_kernel(plan, *refs):
    both, refs = refs[: plan.halves], refs[plan.halves :]
    steer_re, steer_im, ahead, behind, twist, row, out, windows, *scratch = refs
    lanes, span, parts = plan.lanes, plan.span, plan.parts
    count, depth = plan.hogel_rows, parts * plan.wide
    result = 0.0
    for half, lines in enumerate(both):
        by_part = lines[...].reshape(count, parts, span, plan.wide)
        left = jnp.concatenate([by_part[:, n] for n in range(parts)], axis=-1)
        left = left.reshape(count * span, depth)
        result = result + matmul(left, row[half * depth : (half + 1) * depth, :])
    windows[...] = result.reshape(count, span, 2 * WIN)

    def load(s):
        i, slab = s // plan.shift, s % plan.shift
        block = windows[i, :, slab * lanes : (slab + 1) * lanes]
        slab += plan.shift
        block = block + windows[(i - 1) % plan.hogel_rows, :, slab * lanes : (slab + 1) * lanes]
        return to_planes(plan, block)

    def store(s, re, im):
        out[s] = jnp.concatenate([re, im], axis=0).astype(BF16)

    columns(plan, -1.0, load, store, steer_re, steer_im, ahead, behind, twist, scratch)


def hogel_kernel(plan, half, lines, goals, *refs):
    weights_behind, twist_behind, weights_ahead, twist_ahead, col, col_turned, same = refs[:7]
    out, lights, packed, field, spectra, bright, marks, factors, weighted, back = refs[7:]
    C, X, lanes, count = plan.C, plan.X, plan.wide, plan.half
    total = plan.total_cols
    for k in range(C):
        block = lines[k * plan.R : (k + 1) * plan.R].reshape(X, lanes)
        place = slice(k * lanes, (k + 1) * lanes)
        packed[:X, place] = block
        packed[X:, place] = times_i(block.astype(F32)).astype(BF16)

    def emit_near(c, start, step, value):
        for n, part in enumerate((value, times_i(value))):
            rounded = part.astype(BF16)
            field[n, c * X + start : c * X + start + step, :] = rounded
            if c == 0 and start < STRIDE:
                field[n, total + start : total + start + step, :] = rounded

    lines_inverse(plan, lanes, packed, emit_near, weights_behind, twist_behind)
    group = 256 // lanes
    for start in range(0, plan.hogel_cols, group):
        right = []
        for j in range(start, start + group):
            window = slice(STRIDE * j, STRIDE * j + WIN)
            right.append(jnp.concatenate([field[0, window, :], field[1, window, :]], axis=0))
        result = matmul(col_turned[...], jnp.concatenate(right, axis=1))
        for j in range(start, start + group):
            spectrum = result[:, (j - start) * lanes : (j - start + 1) * lanes]
            spectra[j] = spectrum
            power = (spectrum * spectrum).reshape(VIEWS, BIN, lanes).sum(axis=1)
            bright[j * VIEWS : (j + 1) * VIEWS, :] = power + jnp.concatenate(
                [power[:, count:], power[:, :count]], axis=1
            )
    exact = lax.Precision.HIGHEST
    own = lax.broadcasted_iota(jnp.int32, (VIEWS, lanes), 0) == (
        lax.broadcasted_iota(jnp.int32, (VIEWS, lanes), 1) % VIEWS
    )
    for c in range(C):
        target = get_views(plan, goals[c])[:, half * count : (half + 1) * count]
        target = jnp.concatenate([target, target], axis=1)
        for j in range(plan.own_cols):
            h = c * plan.own_cols + j
            marks[h * VIEWS : (h + 1) * VIEWS, :] = jnp.where(own, target[j : j + 1, :], 0.0)
    scale = 1.0 / (BIN * BIN)
    light = scale * jnp.dot(bright[...], same[...], preferred_element_type=F32, precision=exact)
    target = jnp.dot(marks[...], same[...], preferred_element_type=F32, precision=exact)
    factors[...] = 4.0 * (light - target)
    bright[...] = light
    for c in range(C):
        rows = []
        for j in range(plan.own_cols):
            h = c * plan.own_cols + j
            block = jnp.where(own, bright[h * VIEWS : (h + 1) * VIEWS, :], 0.0)
            rows.append(jnp.sum(block, axis=0, keepdims=True)[:, :count])
        lights[c] = put_views(plan, jnp.concatenate(rows, axis=0))
    for start in range(0, plan.hogel_cols, group):
        for j in range(start, start + group):
            place = slice((j - start) * lanes, (j - start + 1) * lanes)
            for view in range(VIEWS):
                factor = factors[j * VIEWS + view : j * VIEWS + view + 1, :]
                block = spectra[j, view * BIN : (view + 1) * BIN, :] * factor
                weighted[view * BIN : (view + 1) * BIN, place] = block.astype(BF16)
                below = slice(WIN + view * BIN, WIN + (view + 1) * BIN)
                weighted[below, place] = (-times_i(block)).astype(BF16)
        result = matmul(col[...], weighted[...])
        for j in range(start, start + group):
            piece = result[:, (j - start) * lanes : (j - start + 1) * lanes]
            first, second = STRIDE * j, STRIDE * (j + 1) % total
            if j == 0:
                back[:STRIDE] = piece[:STRIDE]
            else:
                back[first : first + STRIDE] = back[first : first + STRIDE] + piece[:STRIDE]
            if j < plan.hogel_cols - 1:
                back[second : second + STRIDE] = piece[STRIDE:]
            else:
                back[:STRIDE] = back[:STRIDE] + piece[STRIDE:]

    def load(c, start, step):
        return back[c * X + start : c * X + start + step, :]

    def emit(d, block):
        out[d] = block.astype(BF16)

    lines_forward(plan, lanes, load, emit, weights_ahead, twist_ahead, packed)


def steer_table(plan):
    index = lax.axis_index(("rows", "cols"))
    shape = (plan.D, plan.f, 128)
    k = lax.broadcasted_iota(jnp.int32, shape, 0)
    line = lax.broadcasted_iota(jnp.int32, shape, 1)
    lane = lax.broadcasted_iota(jnp.int32, shape, 2)
    u = k + plan.D * (lane % plan.m)
    v = index // plan.R + plan.C * (
        plan.span * (index % plan.R) + plan.f * (lane // plan.m) + line
    )

    def freq(position, count):
        return ((position + count // 2) % count - count // 2).astype(F32) / count

    freq_rows, freq_cols = freq(u, plan.total_rows), freq(v, plan.total_cols)
    radial = freq_rows * freq_rows + freq_cols * freq_cols
    phase = (
        -2.0
        * math.pi
        * distance_px
        * radial
        / (jnp.sqrt(index_ratio * index_ratio - radial) + index_ratio)
    )
    return jnp.cos(phase), jnp.sin(phase)


def exchange(chunks):
    return lax.all_to_all(chunks, ("rows", "cols"), split_axis=0, concat_axis=0, tiled=True)


def swap_columns(chunks):
    count = lax.axis_size("cols")
    return tuple(
        lax.ppermute(chunk, "cols", [(i, i ^ t) for i in range(count)]) if t else chunk
        for t, chunk in zip(partners(count), chunks)
    )


def local(slm_field, target_light):
    rows_count, cols_count = lax.axis_size("rows"), lax.axis_size("cols")
    plan = Plan(rows_count, cols_count, slm_field.shape[1], slm_field.shape[2])
    C, D, X, lanes, f = plan.C, plan.D, plan.X, plan.lanes, plan.f
    span, wide = plan.span, plan.wide

    ahead, behind, twist = (jnp.asarray(t) for t in plan.pencil_tables())
    weights_ahead, twist_ahead = plan.line_tables(-1.0)
    weights_ahead, twist_ahead = jnp.asarray(weights_ahead[0]), jnp.asarray(twist_ahead)
    weights_both, twist_behind = (jnp.asarray(t) for t in plan.line_tables(1.0))
    weights_behind = jnp.asarray(plan.line_tables(1.0)[0][0])
    col, col_turned, row = hogel_tables()
    row = plan.row_table(row[0], row[1])
    col, col_turned, row, row_turned, same = (
        jnp.asarray(t) for t in (col, col_turned, row, row.T.copy(), plan.group_table())
    )
    steer_re, steer_im = steer_table(plan)

    slabs_shapes = (shape_of((X + VIEWS, lanes), BF16),) * C
    slabs_scratch = pltpu.VMEM((C, X + VIEWS, lanes), BF16)
    views_shape = shape_of((C, VIEWS, lanes), BF16)
    pencil_shape = shape_of((D, 2 * f, 128), BF16)
    lines_shape = shape_of((D, span, wide), BF16)
    columns_scratch = (
        pltpu.VMEM((D, f, 128), F32),
        pltpu.VMEM((D, f, 128), F32),
        pltpu.VMEM((D, f, 256), BF16),
    )
    pencil_tables = (steer_re, steer_im, ahead, behind, twist)
    columns_flops = 8 * D * f * 256 * 256 + 2 * plan.hogel_rows * span * (2 * WIN) ** 2

    apart_any = pl.BlockSpec(memory_space=pl.ANY)
    slabs = call(
        lambda *refs: pack_kernel(plan, *refs),
        slabs_shapes,
        (slm_field.astype(BF16), target_light),
        (slabs_scratch,),
    )
    tall = pltpu.VMEM((2 * X, C * lanes), BF16)
    pencils, goals = call(
        lambda *refs: rows_forward_kernel(plan, *refs),
        (pencil_shape, views_shape),
        (weights_ahead, twist_ahead, *swap_columns(slabs), steer_re, steer_im),
        (tall, slabs_scratch),
        flops=2 * X * 2 * X * C * lanes,
        in_specs={C + 2: apart_any, C + 3: apart_any},
    )
    lines = call(
        lambda *refs: pencil_forward_kernel(plan, *refs),
        (lines_shape,) * plan.halves,
        (exchange(pencils), *pencil_tables, row),
        (pltpu.VMEM((plan.hogel_rows, span, 2 * WIN), BF16), *columns_scratch),
        flops=columns_flops,
    )
    tall = pltpu.VMEM((2 * X, C * wide), BF16)
    views = pltpu.VMEM((plan.hogel_cols * VIEWS, wide), F32)

    def hogels(half, lines):
        return call(
            lambda *refs: hogel_kernel(plan, half, *refs),
            (lines_shape, shape_of((C, VIEWS, plan.half), BF16)),
            (
                lines,
                goals,
                weights_behind,
                twist_behind,
                weights_ahead,
                twist_ahead,
                col,
                col_turned,
                same,
            ),
            (
                tall,
                pltpu.VMEM((2, plan.total_cols + STRIDE, wide), BF16),
                pltpu.VMEM((plan.hogel_cols, WIN, wide), F32),
                views,
                views,
                views,
                pltpu.VMEM((2 * WIN, 256), BF16),
                pltpu.VMEM((plan.total_cols, wide), F32),
            ),
            flops=4 * X * 2 * X * C * wide + 4 * plan.hogel_cols * WIN * 2 * WIN * wide,
        )

    arrived = [exchange(part) for part in lines]
    finished = [hogels(half, part) for half, part in enumerate(arrived)]
    lights = [part[1] for part in finished]
    lines = [exchange(part[0]) for part in finished]
    (pencils,) = call(
        lambda *refs: pencil_back_kernel(plan, *refs),
        (pencil_shape,),
        (*lines, *pencil_tables, row_turned),
        (pltpu.VMEM((plan.hogel_rows, span, 2 * WIN), F32), *columns_scratch),
        flops=columns_flops,
    )
    tall = pltpu.VMEM((2 * X, C * lanes), BF16)
    slabs = call(
        lambda *refs: rows_inverse_kernel(plan, *refs),
        slabs_shapes,
        (exchange(pencils), *lights, weights_both, twist_behind),
        (tall, slabs_scratch),
        flops=2 * X * 2 * X * C * lanes,
    )
    return call(
        lambda *refs: unpack_kernel(plan, *refs),
        (shape_of(slm_field.shape, F32), shape_of(target_light.shape, F32)),
        swap_columns(slabs),
        (slabs_scratch,),
    )


def solution(mesh):
    return jax.shard_map(
        local,
        mesh=mesh,
        in_specs=(P(None, "rows", "cols"), P("rows", "cols", None)),
        out_specs=(P(None, "rows", "cols"), P("rows", "cols", None)),
        check_vma=False,
    )
```

```python
import math

import jax
import jax.numpy as jnp
import ml_dtypes
import numpy as np
from jax import lax
from jax.experimental import pallas as pl
from jax.experimental.pallas import tpu as pltpu
from jax.sharding import PartitionSpec as P

WIN = 256
VIEWS = 16
STRIDE = 128
BIN = 16

distance_px = 16000.0
index_ratio = 15.0

BF16 = jnp.bfloat16
F32 = jnp.float32
BOTH_MINOR = (((1,), (1,)), ((), ()))


def call(body, outs, args, scratch=(), flops=0, in_specs=None, out_specs=None):
    nbytes = sum(math.prod(a.shape) * a.dtype.itemsize for a in (*outs, *args))
    specs = {}
    if in_specs:
        whole = pl.BlockSpec(memory_space=pltpu.VMEM)
        specs["in_specs"] = [in_specs.get(n, whole) for n in range(len(args))]
    if out_specs:
        specs["out_specs"] = out_specs
    return pl.pallas_call(
        body,
        out_shape=outs,
        scratch_shapes=list(scratch),
        compiler_params=pltpu.CompilerParams(vmem_limit_bytes=24 * 2**20),
        cost_estimate=pl.CostEstimate(flops=flops, bytes_accessed=nbytes, transcendentals=0),
        **specs,
    )(*args)


def shape_of(dims, dtype):
    return jax.ShapeDtypeStruct(dims, dtype)


def high_low(table):
    table = np.asarray(table, np.float32)
    high = table.astype(ml_dtypes.bfloat16)
    low = (table - high.astype(np.float32)).astype(ml_dtypes.bfloat16)
    return np.concatenate([high, low], axis=0)


def times_i(values):
    half = values.shape[-1] // 2
    if values.shape[-1] == 128:
        lanes = lax.broadcasted_iota(jnp.int32, values.shape, values.ndim - 1)
        turned = pltpu.roll(values, half, values.ndim - 1)
        return jnp.where(lanes < half, -turned, turned)
    return jnp.concatenate([-values[..., half:], values[..., :half]], axis=-1)


def scaled(value, factor):
    return value if factor == 1.0 else value * factor


def small_dft(points, sign):
    count = len(points)
    if count == 1:
        return points
    even = small_dft(points[0::2], sign)
    odd = small_dft(points[1::2], sign)
    front, back = [], []
    for k in range(count // 2):
        re, im = odd[k]
        angle = sign * 2.0 * math.pi * k / count
        cosine, sine = math.cos(angle), math.sin(angle)
        if k == 0:
            pass
        elif 4 * k == count:
            re, im = (-im, re) if sign > 0 else (im, -re)
        elif 8 * k == count:
            re, im = cosine * (re - sign * im), cosine * (im + sign * re)
        elif 8 * k == 3 * count:
            re, im = cosine * (re + sign * im), cosine * (im - sign * re)
        else:
            re, im = re * cosine - im * sine, re * sine + im * cosine
        even_re, even_im = even[k]
        front.append((even_re + re, even_im + im))
        back.append((even_re - re, even_im - im))
    return front + back


def packed_dft(points, sign):
    count = len(points)
    if count == 1:
        return points
    even = packed_dft(points[0::2], sign)
    odd = packed_dft(points[1::2], sign)
    front, back = [], []
    for k in range(count // 2):
        term = odd[k]
        angle = sign * 2.0 * math.pi * k / count
        if 4 * k == count:
            term = times_i(term) if sign > 0 else -times_i(term)
        elif k:
            term = math.cos(angle) * term + math.sin(angle) * times_i(term)
        front.append(even[k] + term)
        back.append(even[k] - term)
    return front + back


def turn(rows, cols, period, sign):
    angles = sign * 2.0 * np.pi / period * ((np.arange(rows)[:, None] * np.arange(cols)) % period)
    return np.cos(angles), np.sin(angles)


def block_diagonal(block, copies):
    return np.kron(np.eye(copies), block)


class Plan:
    def __init__(self, rows_count, cols_count, rows_dev, cols_dev):
        self.R, self.C = rows_count, cols_count
        self.D = rows_count * cols_count
        self.X = cols_dev
        self.m = rows_dev // cols_count
        self.lanes = 2 * self.m
        self.P = 128 // self.m
        self.span = cols_dev // rows_count
        self.f = self.span // self.P
        self.total_rows = rows_dev * rows_count
        self.total_cols = cols_dev * cols_count
        self.outer = 8
        self.inner = self.D // 8
        self.shift = STRIDE // self.m
        self.hogel_rows = self.total_rows // STRIDE
        self.hogel_cols = self.total_cols // STRIDE
        self.parts = self.D // self.hogel_rows
        self.pp = WIN // self.parts
        self.views = VIEWS // self.parts
        self.own_cols = cols_dev // STRIDE

    def line_tables(self, sign):
        cosine, sine = turn(self.X, self.X, self.X, sign)
        weights = high_low(np.concatenate([cosine, sine], axis=1)).reshape(2, self.X, 2 * self.X)
        twist = turn(self.X, self.C, self.total_cols, sign)
        return weights, np.concatenate(twist, axis=1).astype(np.float32)

    def pencil_tables(self):
        cosine, sine = turn(self.m, self.m, self.m, -1.0)
        cosine, sine = block_diagonal(cosine, self.P), block_diagonal(sine, self.P)
        ahead = np.block([[cosine, sine], [-sine, cosine]])
        behind = np.block([[cosine, -sine], [sine, cosine]]) / (self.total_rows * self.total_cols)
        twist = turn(self.D, self.m, self.total_rows, -1.0)
        twist = np.stack([np.tile(part, (1, self.P)) for part in twist]).astype(np.float32)
        return high_low(ahead), high_low(behind), twist

    def row_table(self, real, imag):
        blocks = []
        for slab in range(WIN // self.m):
            rows = slice(slab * self.m, (slab + 1) * self.m)
            for left, right in ((real[rows], imag[rows]), (-imag[rows], real[rows])):
                pieces = []
                for part in range(self.parts):
                    cols = slice(part * self.pp, (part + 1) * self.pp)
                    pieces += [left[:, cols], right[:, cols]]
                blocks.append(np.concatenate(pieces, axis=1))
        return np.concatenate(blocks, axis=0)

    def group_table(self):
        return np.kron(np.eye(self.views), np.ones((BIN, BIN))).astype(np.float32)


def hogel_tables():
    positions = np.arange(WIN)
    tapers = np.sin(np.pi * (positions + 0.5) / WIN) ** 2
    angles = -2.0 * np.pi / WIN * (positions[:, None] * positions[None, :] % WIN)
    cosine = (tapers[:, None] * np.cos(angles)).astype(np.float32)
    sine = (tapers[:, None] * np.sin(angles)).astype(np.float32)
    col = np.concatenate([cosine, sine], axis=1).astype(ml_dtypes.bfloat16)
    col_turned = np.concatenate([cosine.T, sine.T], axis=1).astype(ml_dtypes.bfloat16)
    row = np.stack([cosine / WIN, sine / WIN]).astype(ml_dtypes.bfloat16)
    return col, col_turned, row


def three_pieces(values):
    first = values.astype(BF16)
    rest = values - first.astype(F32)
    second = rest.astype(BF16)
    return first, second, (rest - second.astype(F32)).astype(BF16)


def matmul(left, right):
    return jnp.dot(left, right, preferred_element_type=F32)


def partners(count):
    return sorted(range(count), key=lambda t: (t != 0, -t.bit_count()))


def gather_chunks(arrived, chunks):
    mine = lax.axis_index("cols")
    for t, chunk in zip(partners(len(arrived)), arrived):
        chunks[mine ^ t] = chunk[...]


def scatter_chunks(chunks, leaving):
    mine = lax.axis_index("cols")
    for t, chunk in zip(partners(len(leaving)), leaving):
        chunk[...] = chunks[mine ^ t]


def put_views(plan, rows):
    pad = jnp.zeros((VIEWS - 3 * plan.own_cols, plan.lanes), F32)
    pieces = [piece.astype(F32) for piece in three_pieces(rows)]
    return jnp.concatenate([*pieces, pad], axis=0).astype(BF16)


def get_views(plan, chunk):
    chunk = chunk.astype(F32)
    n = plan.own_cols
    return chunk[:n] + chunk[n : 2 * n] + chunk[2 * n : 3 * n]


def pack_kernel(plan, field, goal, *refs):
    C, m, X = plan.C, plan.m, plan.X
    leaving, (out,) = refs[:C], refs[C:]
    for c in range(C):
        rows = slice(c * m, (c + 1) * m)
        block = jnp.concatenate([field[0, rows, :], field[1, rows, :]], axis=0)
        out[c, :X, :] = block.astype(F32).T.astype(BF16)
        i, start = c // plan.parts, c % plan.parts * plan.lanes
        out[c, X:, :] = put_views(plan, goal[i, :, start : start + plan.lanes])
    scatter_chunks(out, leaving)


def unpack_kernel(plan, *refs):
    C, m, X = plan.C, plan.m, plan.X
    arrived, (out, light, slabs) = refs[:C], refs[C:]
    gather_chunks(arrived, slabs)
    for c in range(C):
        block = slabs[c, :X, :].astype(F32).T
        out[0, m * c : m * c + m, :] = block[:m]
        out[1, m * c : m * c + m, :] = block[m:]
        i, start = c // plan.parts, c % plan.parts * plan.lanes
        light[i, :, start : start + plan.lanes] = get_views(plan, slabs[c, X:, :])


def lines_forward(plan, lanes, load, emit, weights, twist, turned):
    C, X = plan.C, plan.X
    step = 64
    for start in range(0, X, step):
        points = packed_dft([load(c, start, step) for c in range(C)], -1.0)
        for k in range(C):
            cosine = twist[start : start + step, k : k + 1]
            sine = twist[start : start + step, C + k : C + k + 1]
            across = times_i(points[k])
            if k:
                value = points[k] * cosine + across * sine
                across = across * cosine - points[k] * sine
            else:
                value = points[k]
            place = slice(k * lanes, k * lanes + lanes)
            turned[start : start + step, place] = value.astype(BF16)
            turned[X + start : X + start + step, place] = across.astype(BF16)
    group = max(1, 256 // lanes)
    for first in range(0, C, group):
        result = matmul(weights[...], turned[:, first * lanes : (first + group) * lanes])
        for k in range(group):
            for r in range(plan.R):
                rows = slice(r * plan.span, (r + 1) * plan.span)
                emit((first + k) * plan.R + r, result[rows, k * lanes : (k + 1) * lanes])


def lines_inverse(plan, lanes, packed, emit, weights, twist, step):
    C, X = plan.C, plan.X
    for start in range(0, X, step):
        rows = slice(start, start + step)
        result = matmul(weights[0, rows, :], packed[...]) + matmul(weights[1, rows, :], packed[...])
        points = []
        for k in range(C):
            value = result[:, k * lanes : (k + 1) * lanes]
            if k:
                cosine, sine = twist[rows, k : k + 1], twist[rows, C + k : C + k + 1]
                value = value * cosine + times_i(value) * sine
            points.append(value)
        for c, value in enumerate(packed_dft(points, 1.0)):
            emit(c, start, step, value)


def to_planes(plan, block):
    parts = [block[p * plan.f : (p + 1) * plan.f, :] for p in range(plan.P)]
    real = jnp.concatenate([part[:, : plan.m] for part in parts], axis=1)
    imag = jnp.concatenate([part[:, plan.m :] for part in parts], axis=1)
    return real, imag


def from_planes(plan, real, imag):
    m = plan.m
    return jnp.concatenate(
        [
            jnp.concatenate([real[:, p * m : (p + 1) * m], imag[:, p * m : (p + 1) * m]], axis=1)
            for p in range(plan.P)
        ],
        axis=0,
    )


def rows_forward_kernel(plan, weights, twist, *refs):
    C, X = plan.C, plan.X
    arrived, (_, _, out, goals, turned, slabs) = refs[:C], refs[C:]
    gather_chunks(arrived, slabs)
    goals[...] = slabs[:, X:, :]

    def load(c, start, step):
        return slabs[c, start : start + step, :].astype(F32)

    def emit(d, block):
        out[d] = jnp.concatenate(to_planes(plan, block), axis=0).astype(BF16)

    lines_forward(plan, plan.lanes, load, emit, weights, twist, turned)


def rows_inverse_kernel(plan, pencils, lights, weights, twist, *refs):
    C, X, lanes = plan.C, plan.X, plan.lanes
    leaving, (packed, out) = refs[:C], refs[C:]
    for k in range(C):
        for r in range(plan.R):
            chunk = pencils[k * plan.R + r].astype(F32)
            block = from_planes(plan, chunk[: plan.f], chunk[plan.f :])
            place = slice(k * lanes, k * lanes + lanes)
            packed[r * plan.span : (r + 1) * plan.span, place] = block.astype(BF16)
            packed[X + r * plan.span : X + (r + 1) * plan.span, place] = times_i(block).astype(BF16)

    def emit(c, start, step, value):
        out[c, start : start + step, :] = value.astype(BF16)

    lines_inverse(plan, lanes, packed, emit, weights, twist, 64)
    out[:, X:, :] = lights[...]
    scatter_chunks(out, leaving)


def columns(plan, sign, load, store, steer_re, steer_im, ahead, behind, twist, scratch):
    D, f, outer, inner = plan.D, plan.f, plan.outer, plan.inner
    half_re, half_im, rounded = scratch
    for b in range(inner):
        points = [load(inner * a + b) for a in range(outer)]
        for alpha, (re, im) in enumerate(small_dft(points, -1.0)):
            angle = -2.0 * math.pi * b * alpha / D
            cosine, sine = math.cos(angle), math.sin(angle)
            if b * alpha:
                re, im = re * cosine - im * sine, re * sine + im * cosine
            half_re[alpha * inner + b] = re
            half_im[alpha * inner + b] = im
    for alpha in range(outer):
        points = [(half_re[alpha * inner + b], half_im[alpha * inner + b]) for b in range(inner)]
        for beta, (re, im) in enumerate(small_dft(points, -1.0)):
            k = alpha + outer * beta
            cosine, sine = twist[0, k : k + 1, :], twist[1, k : k + 1, :]
            for offset, part in ((0, re * cosine - im * sine), (128, re * sine + im * cosine)):
                rounded[k, :, offset : offset + 128] = part.astype(BF16)
    group = D // 2
    for start in range(0, D, group):
        place = slice(start, start + group)

        def multiply(matrix):
            left = rounded[place].reshape(group * f, 256)
            product = matmul(left, matrix[:256, :]) + matmul(left, matrix[256:, :])
            return product.reshape(group, f, 256)

        result = multiply(ahead)
        re, im = result[:, :, :128], result[:, :, 128:]
        factor_re, factor_im = steer_re[place], sign * steer_im[place]
        for offset, part in (
            (0, re * factor_re - im * factor_im),
            (128, re * factor_im + im * factor_re),
        ):
            rounded[place, :, offset : offset + 128] = part.astype(BF16)
        result = multiply(behind)
        half_re[place] = result[:, :, :128]
        half_im[place] = result[:, :, 128:]
    for alpha in range(outer):
        points = []
        for beta in range(inner):
            k = alpha + outer * beta
            cosine, sine = twist[0, k : k + 1, :], twist[1, k : k + 1, :]
            re, im = half_re[k], half_im[k]
            points.append((re * cosine + im * sine, im * cosine - re * sine))
        for b, (re, im) in enumerate(small_dft(points, 1.0)):
            angle = 2.0 * math.pi * b * alpha / D
            cosine, sine = math.cos(angle), math.sin(angle)
            if b * alpha:
                re, im = re * cosine - im * sine, re * sine + im * cosine
            half_re[alpha + outer * b] = re
            half_im[alpha + outer * b] = im
    for b in range(inner):
        points = [(half_re[alpha + outer * b], half_im[alpha + outer * b]) for alpha in range(outer)]
        for a, (re, im) in enumerate(small_dft(points, 1.0)):
            store(inner * a + b, re, im)


def pencil_forward_kernel(plan, pencils, *refs):
    steer_re, steer_im, ahead, behind, twist, row, out, windows, *scratch = refs
    f, lanes, span = plan.f, plan.lanes, plan.span

    def load(s):
        chunk = pencils[s].astype(F32)
        return chunk[:f], chunk[f:]

    def store(s, re, im):
        block = from_planes(plan, re, im).astype(BF16)
        i, slab = s // plan.shift, s % plan.shift
        windows[i, :, slab * lanes : (slab + 1) * lanes] = block
        slab += plan.shift
        windows[(i - 1) % plan.hogel_rows, :, slab * lanes : (slab + 1) * lanes] = block

    columns(plan, 1.0, load, store, steer_re, steer_im, ahead, behind, twist, scratch)
    count = plan.hogel_rows
    result = matmul(windows[...].reshape(count * span, 2 * WIN), row[...]).astype(BF16)
    for i in range(count):
        for part in range(plan.parts):
            out[i * plan.parts + part] = result[
                i * span : (i + 1) * span, part * 2 * plan.pp : (part + 1) * 2 * plan.pp
            ]


def pencil_back_kernel(plan, lines, *refs):
    steer_re, steer_im, ahead, behind, twist, row, out, windows, *scratch = refs
    lanes, span, parts = plan.lanes, plan.span, plan.parts
    count, wide = plan.hogel_rows, 2 * plan.pp
    by_part = lines[...].reshape(count, parts, span, wide)
    own = jnp.concatenate([by_part[:, n] for n in range(parts)], axis=-1)
    before = jnp.concatenate([own[-1:], own[:-1]], axis=0)
    windows[...] = (
        matmul(own.reshape(count * span, 2 * WIN), row[:, :WIN])
        + matmul(before.reshape(count * span, 2 * WIN), row[:, WIN:])
    ).reshape(count, span, WIN)

    def load(s):
        i, slab = s // plan.shift, s % plan.shift
        return to_planes(plan, windows[i, :, slab * lanes : (slab + 1) * lanes])

    def store(s, re, im):
        out[s] = jnp.concatenate([re, im], axis=0).astype(BF16)

    columns(plan, -1.0, load, store, steer_re, steer_im, ahead, behind, twist, scratch)


def hogel_kernel(plan, lines, goals, *refs):
    weights_behind, twist_behind, weights_ahead, twist_ahead, col, col_turned, same = refs[:7]
    out, lights, packed, field, spectra, bright, factors, weighted, back = refs[7:]
    C, X, lanes, pp = plan.C, plan.X, 2 * plan.pp, plan.pp
    total = plan.total_cols
    for k in range(C):
        block = lines[k * plan.R : (k + 1) * plan.R].reshape(X, lanes)
        place = slice(k * lanes, (k + 1) * lanes)
        packed[:X, place] = block
        packed[X:, place] = times_i(block.astype(F32)).astype(BF16)

    def emit_near(c, start, step, value):
        for n, part in enumerate((value, times_i(value))):
            rounded = part.astype(BF16)
            field[n, c * X + start : c * X + start + step, :] = rounded
            if c == 0 and start < STRIDE:
                field[n, total + start : total + start + step, :] = rounded

    lines_inverse(plan, lanes, packed, emit_near, weights_behind, twist_behind, 128)
    for j in range(plan.hogel_cols):
        window = slice(STRIDE * j, STRIDE * j + WIN)
        result = matmul(
            col_turned[...], jnp.concatenate([field[0, window, :], field[1, window, :]], axis=0)
        )
        spectra[j] = result
        power = result[:, :pp] * result[:, :pp] + result[:, pp:] * result[:, pp:]
        bright[j * VIEWS : (j + 1) * VIEWS, :] = power.reshape(VIEWS, BIN, pp).sum(axis=1)
    exact = lax.Precision.HIGHEST
    own = lax.broadcasted_iota(jnp.int32, (VIEWS, pp), 0) == (
        lax.broadcasted_iota(jnp.int32, (VIEWS, pp), 1) % VIEWS
    )
    for c in range(C):
        target = get_views(plan, goals[c])
        for j in range(plan.own_cols):
            h = c * plan.own_cols + j
            below = (plan.hogel_cols + h) * VIEWS
            bright[below : below + VIEWS, :] = jnp.where(own, target[j : j + 1, :], 0.0)
    spread = jnp.dot(bright[...], same[...], preferred_element_type=F32, precision=exact)
    views = plan.hogel_cols * VIEWS
    light = spread[:views] * (1.0 / (BIN * BIN))
    factors[...] = 4.0 * (light - spread[views:])
    bright[:views, :] = light
    for c in range(C):
        rows = []
        for j in range(plan.own_cols):
            h = c * plan.own_cols + j
            block = jnp.where(own, bright[h * VIEWS : (h + 1) * VIEWS, :], 0.0)
            rows.append(jnp.sum(block, axis=0, keepdims=True))
        lights[c] = put_views(plan, jnp.concatenate(rows, axis=0))
    for j in range(plan.hogel_cols):
        for view in range(VIEWS):
            factor = factors[j * VIEWS + view : j * VIEWS + view + 1, :]
            block = slice(view * BIN, (view + 1) * BIN)
            below = slice(WIN + view * BIN, WIN + (view + 1) * BIN)
            real = (spectra[j, block, :pp] * factor).astype(BF16)
            imag = (spectra[j, block, pp:] * factor).astype(BF16)
            weighted[block, :pp] = real
            weighted[block, pp:] = imag
            weighted[below, :pp] = imag
            weighted[below, pp:] = -real
        result = matmul(col[...], weighted[...])
        first, second = STRIDE * j, STRIDE * (j + 1) % total
        if j == 0:
            back[:STRIDE] = result[:STRIDE]
        else:
            back[first : first + STRIDE] = back[first : first + STRIDE] + result[:STRIDE]
        if j < plan.hogel_cols - 1:
            back[second : second + STRIDE] = result[STRIDE:]
        else:
            back[:STRIDE] = back[:STRIDE] + result[STRIDE:]

    def load(c, start, step):
        return back[c * X + start : c * X + start + step, :]

    def emit(d, block):
        out[d] = block.astype(BF16)

    lines_forward(plan, lanes, load, emit, weights_ahead, twist_ahead, packed)


def steer_table(plan):
    index = lax.axis_index(("rows", "cols"))
    shape = (plan.D, plan.f, 128)
    k = lax.broadcasted_iota(jnp.int32, shape, 0)
    line = lax.broadcasted_iota(jnp.int32, shape, 1)
    lane = lax.broadcasted_iota(jnp.int32, shape, 2)
    u = k + plan.D * (lane % plan.m)
    v = index // plan.R + plan.C * (
        plan.span * (index % plan.R) + plan.f * (lane // plan.m) + line
    )

    def freq(position, count):
        return ((position + count // 2) % count - count // 2).astype(F32) / count

    freq_rows, freq_cols = freq(u, plan.total_rows), freq(v, plan.total_cols)
    radial = freq_rows * freq_rows + freq_cols * freq_cols
    phase = (
        -2.0
        * math.pi
        * distance_px
        * radial
        / (jnp.sqrt(index_ratio * index_ratio - radial) + index_ratio)
    )
    return jnp.cos(phase), jnp.sin(phase)


def exchange(chunks):
    return lax.all_to_all(chunks, ("rows", "cols"), split_axis=0, concat_axis=0, tiled=True)


def swap_columns(chunks):
    count = lax.axis_size("cols")
    return tuple(
        lax.ppermute(chunk, "cols", [(i, i ^ t) for i in range(count)]) if t else chunk
        for t, chunk in zip(partners(count), chunks)
    )


def local(slm_field, target_light):
    rows_count, cols_count = lax.axis_size("rows"), lax.axis_size("cols")
    plan = Plan(rows_count, cols_count, slm_field.shape[1], slm_field.shape[2])
    C, D, X, lanes, f = plan.C, plan.D, plan.X, plan.lanes, plan.f
    span, wide = plan.span, 2 * plan.pp

    ahead, behind, twist = (jnp.asarray(t) for t in plan.pencil_tables())
    weights_ahead, twist_ahead = plan.line_tables(-1.0)
    weights_ahead, twist_ahead = jnp.asarray(weights_ahead[0]), jnp.asarray(twist_ahead)
    weights_behind, twist_behind = (jnp.asarray(t) for t in plan.line_tables(1.0))
    col, col_turned, row = hogel_tables()
    row = plan.row_table(row[0], row[1])
    col, col_turned, row, row_turned, same = (
        jnp.asarray(t) for t in (col, col_turned, row, row.T.copy(), plan.group_table())
    )
    steer_re, steer_im = steer_table(plan)

    slabs_shapes = (shape_of((X + VIEWS, lanes), BF16),) * C
    slabs_scratch = pltpu.VMEM((C, X + VIEWS, lanes), BF16)
    views_shape = shape_of((C, VIEWS, lanes), BF16)
    pencil_shape = shape_of((D, 2 * f, 128), BF16)
    lines_shape = shape_of((D, span, wide), BF16)
    columns_scratch = (
        pltpu.VMEM((D, f, 128), F32),
        pltpu.VMEM((D, f, 128), F32),
        pltpu.VMEM((D, f, 256), BF16),
    )
    pencil_tables = (steer_re, steer_im, ahead, behind, twist)
    columns_flops = 8 * D * f * 256 * 256 + 2 * plan.hogel_rows * span * (2 * WIN) ** 2

    apart_any = pl.BlockSpec(memory_space=pl.ANY)
    slabs = call(
        lambda *refs: pack_kernel(plan, *refs),
        slabs_shapes,
        (slm_field.astype(BF16), target_light),
        (slabs_scratch,),
    )
    tall = pltpu.VMEM((2 * X, C * lanes), BF16)
    pencils, goals = call(
        lambda *refs: rows_forward_kernel(plan, *refs),
        (pencil_shape, views_shape),
        (weights_ahead, twist_ahead, *swap_columns(slabs), steer_re, steer_im),
        (tall, slabs_scratch),
        flops=2 * X * 2 * X * C * lanes,
        in_specs={C + 2: apart_any, C + 3: apart_any},
    )
    (lines,) = call(
        lambda *refs: pencil_forward_kernel(plan, *refs),
        (lines_shape,),
        (exchange(pencils), *pencil_tables, row),
        (pltpu.VMEM((plan.hogel_rows, span, 2 * WIN), BF16), *columns_scratch),
        flops=columns_flops,
    )
    tall = pltpu.VMEM((2 * X, C * wide), BF16)
    lines, lights = call(
        lambda *refs: hogel_kernel(plan, *refs),
        (lines_shape, views_shape),
        (
            exchange(lines),
            goals,
            weights_behind,
            twist_behind,
            weights_ahead,
            twist_ahead,
            col,
            col_turned,
            same,
        ),
        (
            tall,
            pltpu.VMEM((2, plan.total_cols + STRIDE, wide), BF16),
            pltpu.VMEM((plan.hogel_cols, WIN, wide), F32),
            pltpu.VMEM((2 * plan.hogel_cols * VIEWS, plan.pp), F32),
            pltpu.VMEM((plan.hogel_cols * VIEWS, plan.pp), F32),
            pltpu.VMEM((2 * WIN, wide), BF16),
            pltpu.VMEM((plan.total_cols, wide), F32),
        ),
        flops=4 * X * 2 * X * C * wide + 4 * plan.hogel_cols * WIN * 2 * WIN * wide,
    )
    (pencils,) = call(
        lambda *refs: pencil_back_kernel(plan, *refs),
        (pencil_shape,),
        (exchange(lines), *pencil_tables, row_turned),
        (pltpu.VMEM((plan.hogel_rows, span, WIN), F32), *columns_scratch),
        flops=columns_flops,
    )
    tall = pltpu.VMEM((2 * X, C * lanes), BF16)
    slabs = call(
        lambda *refs: rows_inverse_kernel(plan, *refs),
        slabs_shapes,
        (exchange(pencils), lights, weights_behind, twist_behind),
        (tall, slabs_scratch),
        flops=2 * X * 2 * X * C * lanes,
    )
    return call(
        lambda *refs: unpack_kernel(plan, *refs),
        (shape_of(slm_field.shape, F32), shape_of(target_light.shape, F32)),
        swap_columns(slabs),
        (slabs_scratch,),
    )


def solution(mesh):
    return jax.shard_map(
        local,
        mesh=mesh,
        in_specs=(P(None, "rows", "cols"), P("rows", "cols", None)),
        out_specs=(P(None, "rows", "cols"), P("rows", "cols", None)),
        check_vma=False,
    )
```

```python
import math

import jax
import jax.numpy as jnp
import ml_dtypes
import numpy as np
from jax import lax
from jax.experimental import pallas as pl
from jax.experimental.pallas import tpu as pltpu
from jax.sharding import PartitionSpec as P

WIN = 256
VIEWS = 16
STRIDE = 128
BIN = 16

distance_px = 16000.0
index_ratio = 15.0

BF16 = jnp.bfloat16
F32 = jnp.float32
BOTH_MINOR = (((1,), (1,)), ((), ()))


def call(body, outs, args, scratch=(), flops=0, in_specs=None, out_specs=None):
    nbytes = sum(math.prod(a.shape) * a.dtype.itemsize for a in (*outs, *args))
    specs = {}
    if in_specs:
        whole = pl.BlockSpec(memory_space=pltpu.VMEM)
        specs["in_specs"] = [in_specs.get(n, whole) for n in range(len(args))]
    if out_specs:
        specs["out_specs"] = out_specs
    return pl.pallas_call(
        body,
        out_shape=outs,
        scratch_shapes=list(scratch),
        compiler_params=pltpu.CompilerParams(vmem_limit_bytes=24 * 2**20),
        cost_estimate=pl.CostEstimate(flops=flops, bytes_accessed=nbytes, transcendentals=0),
        **specs,
    )(*args)


def shape_of(dims, dtype):
    return jax.ShapeDtypeStruct(dims, dtype)


def high_low(table):
    table = np.asarray(table, np.float32)
    high = table.astype(ml_dtypes.bfloat16)
    low = (table - high.astype(np.float32)).astype(ml_dtypes.bfloat16)
    return np.concatenate([high, low], axis=0)


def times_i(values):
    half = values.shape[-1] // 2
    if values.shape[-1] == 128:
        lanes = lax.broadcasted_iota(jnp.int32, values.shape, values.ndim - 1)
        turned = pltpu.roll(values, half, values.ndim - 1)
        return jnp.where(lanes < half, -turned, turned)
    return jnp.concatenate([-values[..., half:], values[..., :half]], axis=-1)


def scaled(value, factor):
    return value if factor == 1.0 else value * factor


def small_dft(points, sign):
    count = len(points)
    if count == 1:
        return points
    even = small_dft(points[0::2], sign)
    odd = small_dft(points[1::2], sign)
    front, back = [], []
    for k in range(count // 2):
        re, im = odd[k]
        angle = sign * 2.0 * math.pi * k / count
        cosine, sine = math.cos(angle), math.sin(angle)
        if k == 0:
            pass
        elif 4 * k == count:
            re, im = (-im, re) if sign > 0 else (im, -re)
        elif 8 * k == count:
            re, im = cosine * (re - sign * im), cosine * (im + sign * re)
        elif 8 * k == 3 * count:
            re, im = cosine * (re + sign * im), cosine * (im - sign * re)
        else:
            re, im = re * cosine - im * sine, re * sine + im * cosine
        even_re, even_im = even[k]
        front.append((even_re + re, even_im + im))
        back.append((even_re - re, even_im - im))
    return front + back


def packed_dft(points, sign):
    count = len(points)
    if count == 1:
        return points
    even = packed_dft(points[0::2], sign)
    odd = packed_dft(points[1::2], sign)
    front, back = [], []
    for k in range(count // 2):
        term = odd[k]
        angle = sign * 2.0 * math.pi * k / count
        if 4 * k == count:
            term = times_i(term) if sign > 0 else -times_i(term)
        elif k:
            term = math.cos(angle) * term + math.sin(angle) * times_i(term)
        front.append(even[k] + term)
        back.append(even[k] - term)
    return front + back


def turn(rows, cols, period, sign):
    angles = sign * 2.0 * np.pi / period * ((np.arange(rows)[:, None] * np.arange(cols)) % period)
    return np.cos(angles), np.sin(angles)


def block_diagonal(block, copies):
    return np.kron(np.eye(copies), block)


class Plan:
    def __init__(self, rows_count, cols_count, rows_dev, cols_dev):
        self.R, self.C = rows_count, cols_count
        self.D = rows_count * cols_count
        self.X = cols_dev
        self.m = rows_dev // cols_count
        self.lanes = 2 * self.m
        self.P = 128 // self.m
        self.span = cols_dev // rows_count
        self.f = self.span // self.P
        self.total_rows = rows_dev * rows_count
        self.total_cols = cols_dev * cols_count
        self.outer = 8
        self.inner = self.D // 8
        self.shift = STRIDE // self.m
        self.hogel_rows = self.total_rows // STRIDE
        self.hogel_cols = self.total_cols // STRIDE
        self.parts = self.D // self.hogel_rows
        self.pp = WIN // self.parts
        self.views = VIEWS // self.parts
        self.own_cols = cols_dev // STRIDE

    def place(self, s):
        return s % self.C * self.R + s // self.C

    def line_tables(self, sign):
        cosine, sine = turn(self.X, self.X, self.X, sign)
        weights = high_low(np.concatenate([cosine, sine], axis=1)).reshape(2, self.X, 2 * self.X)
        twist = turn(self.X, self.C, self.total_cols, sign)
        return weights, np.concatenate(twist, axis=1).astype(np.float32)

    def pencil_tables(self):
        cosine, sine = turn(self.m, self.m, self.m, -1.0)
        cosine, sine = block_diagonal(cosine, self.P), block_diagonal(sine, self.P)
        ahead = np.block([[cosine, sine], [-sine, cosine]])
        behind = np.block([[cosine, -sine], [sine, cosine]]) / (self.total_rows * self.total_cols)
        twist = turn(self.D, self.m, self.total_rows, -1.0)
        twist = np.stack([np.tile(part, (1, self.P)) for part in twist]).astype(np.float32)
        return high_low(ahead), high_low(behind), twist

    def row_table(self, real, imag):
        blocks = []
        for slab in range(WIN // self.m):
            rows = slice(slab * self.m, (slab + 1) * self.m)
            for left, right in ((real[rows], imag[rows]), (-imag[rows], real[rows])):
                pieces = []
                for part in range(self.parts):
                    cols = slice(part * self.pp, (part + 1) * self.pp)
                    pieces += [left[:, cols], right[:, cols]]
                blocks.append(np.concatenate(pieces, axis=1))
        return np.concatenate(blocks, axis=0)

    def group_table(self):
        return np.kron(np.eye(self.views), np.ones((BIN, BIN))).astype(np.float32)


def hogel_tables():
    positions = np.arange(WIN)
    tapers = np.sin(np.pi * (positions + 0.5) / WIN) ** 2
    angles = -2.0 * np.pi / WIN * (positions[:, None] * positions[None, :] % WIN)
    cosine = (tapers[:, None] * np.cos(angles)).astype(np.float32)
    sine = (tapers[:, None] * np.sin(angles)).astype(np.float32)
    col = np.concatenate([cosine, sine], axis=1).astype(ml_dtypes.bfloat16)
    col_turned = np.concatenate([cosine.T, sine.T], axis=1).astype(ml_dtypes.bfloat16)
    row = np.stack([cosine / WIN, sine / WIN]).astype(ml_dtypes.bfloat16)
    return col, col_turned, row


def three_pieces(values):
    first = values.astype(BF16)
    rest = values - first.astype(F32)
    second = rest.astype(BF16)
    return first, second, (rest - second.astype(F32)).astype(BF16)


def matmul(left, right):
    return jnp.dot(left, right, preferred_element_type=F32)


def partners(count):
    return sorted(range(count), key=lambda t: (t != 0, -t.bit_count()))


def gather_chunks(arrived, chunks):
    mine = lax.axis_index("cols")
    for t, chunk in zip(partners(len(arrived)), arrived):
        chunks[mine ^ t] = chunk[...]


def scatter_chunks(chunks, leaving):
    mine = lax.axis_index("cols")
    for t, chunk in zip(partners(len(leaving)), leaving):
        chunk[...] = chunks[mine ^ t]


def put_views(plan, rows):
    pad = jnp.zeros((VIEWS - 3 * plan.own_cols, plan.lanes), F32)
    pieces = [piece.astype(F32) for piece in three_pieces(rows)]
    return jnp.concatenate([*pieces, pad], axis=0).astype(BF16)


def get_views(plan, chunk):
    chunk = chunk.astype(F32)
    n = plan.own_cols
    return chunk[:n] + chunk[n : 2 * n] + chunk[2 * n : 3 * n]


def pack_kernel(plan, field, goal, *refs):
    C, m, X = plan.C, plan.m, plan.X
    leaving, (out,) = refs[:C], refs[C:]
    for c in range(C):
        rows = slice(c * m, (c + 1) * m)
        block = jnp.concatenate([field[0, rows, :], field[1, rows, :]], axis=0)
        out[c, :X, :] = block.astype(F32).T.astype(BF16)
        i, start = c // plan.parts, c % plan.parts * plan.lanes
        out[c, X:, :] = put_views(plan, goal[i, :, start : start + plan.lanes])
    scatter_chunks(out, leaving)


def unpack_kernel(plan, *refs):
    C, m, X = plan.C, plan.m, plan.X
    arrived, (out, light, slabs) = refs[:C], refs[C:]
    gather_chunks(arrived, slabs)
    for c in range(C):
        block = slabs[c, :X, :].astype(F32).T
        out[0, m * c : m * c + m, :] = block[:m]
        out[1, m * c : m * c + m, :] = block[m:]
        i, start = c // plan.parts, c % plan.parts * plan.lanes
        light[i, :, start : start + plan.lanes] = get_views(plan, slabs[c, X:, :])


def lines_forward(plan, lanes, load, emit, weights, twist, turned):
    C, X = plan.C, plan.X
    step = 64
    for start in range(0, X, step):
        points = packed_dft([load(c, start, step) for c in range(C)], -1.0)
        for k in range(C):
            cosine = twist[start : start + step, k : k + 1]
            sine = twist[start : start + step, C + k : C + k + 1]
            across = times_i(points[k])
            if k:
                value = points[k] * cosine + across * sine
                across = across * cosine - points[k] * sine
            else:
                value = points[k]
            place = slice(k * lanes, k * lanes + lanes)
            turned[start : start + step, place] = value.astype(BF16)
            turned[X + start : X + start + step, place] = across.astype(BF16)
    group = max(1, 256 // lanes)
    for first in range(0, C, group):
        result = matmul(weights[...], turned[:, first * lanes : (first + group) * lanes])
        for k in range(group):
            for r in range(plan.R):
                rows = slice(r * plan.span, (r + 1) * plan.span)
                emit((first + k) * plan.R + r, result[rows, k * lanes : (k + 1) * lanes])


def lines_inverse(plan, lanes, product, emit, twist):
    C, X = plan.C, plan.X
    step = 64
    for start in range(0, X, step):
        rows = slice(start, start + step)
        result = product(rows)
        points = []
        for k in range(C):
            value = result[:, k * lanes : (k + 1) * lanes]
            if k:
                cosine, sine = twist[rows, k : k + 1], twist[rows, C + k : C + k + 1]
                value = value * cosine + times_i(value) * sine
            points.append(value)
        for c, value in enumerate(packed_dft(points, 1.0)):
            emit(c, start, step, value)


def to_planes(plan, block):
    parts = [block[p * plan.f : (p + 1) * plan.f, :] for p in range(plan.P)]
    real = jnp.concatenate([part[:, : plan.m] for part in parts], axis=1)
    imag = jnp.concatenate([part[:, plan.m :] for part in parts], axis=1)
    return real, imag


def from_planes(plan, real, imag):
    m = plan.m
    return jnp.concatenate(
        [
            jnp.concatenate([real[:, p * m : (p + 1) * m], imag[:, p * m : (p + 1) * m]], axis=1)
            for p in range(plan.P)
        ],
        axis=0,
    )


def rows_forward_kernel(plan, weights, twist, *refs):
    C, X = plan.C, plan.X
    arrived, (_, _, out, goals, turned, slabs) = refs[:C], refs[C:]
    gather_chunks(arrived, slabs)
    goals[...] = slabs[:, X:, :]

    def load(c, start, step):
        return slabs[c, start : start + step, :].astype(F32)

    def emit(d, block):
        out[d] = jnp.concatenate(to_planes(plan, block), axis=0).astype(BF16)

    lines_forward(plan, plan.lanes, load, emit, weights, twist, turned)


def rows_inverse_kernel(plan, pencils, lights, weights, twist, *refs):
    C, X, lanes = plan.C, plan.X, plan.lanes
    leaving, (packed, out) = refs[:C], refs[C:]
    for k in range(C):
        for r in range(plan.R):
            chunk = pencils[k * plan.R + r].astype(F32)
            block = from_planes(plan, chunk[: plan.f], chunk[plan.f :])
            place = slice(k * lanes, k * lanes + lanes)
            packed[r * plan.span : (r + 1) * plan.span, place] = block.astype(BF16)
            packed[X + r * plan.span : X + (r + 1) * plan.span, place] = times_i(block).astype(BF16)

    def emit(c, start, step, value):
        out[c, start : start + step, :] = value.astype(BF16)

    def product(rows):
        return matmul(weights[0, rows, :], packed[...]) + matmul(weights[1, rows, :], packed[...])

    lines_inverse(plan, lanes, product, emit, twist)
    out[:, X:, :] = lights[...]
    scatter_chunks(out, leaving)


def columns(plan, sign, load, store, steer_re, steer_im, ahead, behind, twist, scratch):
    D, f, outer, inner = plan.D, plan.f, plan.outer, plan.inner
    half_re, half_im, rounded = scratch
    for b in range(inner):
        points = [load(inner * a + b) for a in range(outer)]
        for alpha, (re, im) in enumerate(small_dft(points, -1.0)):
            angle = -2.0 * math.pi * b * alpha / D
            cosine, sine = math.cos(angle), math.sin(angle)
            if b * alpha:
                re, im = re * cosine - im * sine, re * sine + im * cosine
            half_re[alpha * inner + b] = re
            half_im[alpha * inner + b] = im
    for alpha in range(outer):
        points = [(half_re[alpha * inner + b], half_im[alpha * inner + b]) for b in range(inner)]
        for beta, (re, im) in enumerate(small_dft(points, -1.0)):
            k = alpha + outer * beta
            cosine, sine = twist[0, k : k + 1, :], twist[1, k : k + 1, :]
            for offset, part in ((0, re * cosine - im * sine), (128, re * sine + im * cosine)):
                rounded[k, :, offset : offset + 128] = part.astype(BF16)
    group = D // 2
    for start in range(0, D, group):
        place = slice(start, start + group)

        def multiply(matrix):
            left = rounded[place].reshape(group * f, 256)
            product = matmul(left, matrix[:256, :]) + matmul(left, matrix[256:, :])
            return product.reshape(group, f, 256)

        result = multiply(ahead)
        re, im = result[:, :, :128], result[:, :, 128:]
        factor_re, factor_im = steer_re[place], sign * steer_im[place]
        for offset, part in (
            (0, re * factor_re - im * factor_im),
            (128, re * factor_im + im * factor_re),
        ):
            rounded[place, :, offset : offset + 128] = part.astype(BF16)
        result = multiply(behind)
        half_re[place] = result[:, :, :128]
        half_im[place] = result[:, :, 128:]
    for alpha in range(outer):
        points = []
        for beta in range(inner):
            k = alpha + outer * beta
            cosine, sine = twist[0, k : k + 1, :], twist[1, k : k + 1, :]
            re, im = half_re[k], half_im[k]
            points.append((re * cosine + im * sine, im * cosine - re * sine))
        for b, (re, im) in enumerate(small_dft(points, 1.0)):
            angle = 2.0 * math.pi * b * alpha / D
            cosine, sine = math.cos(angle), math.sin(angle)
            if b * alpha:
                re, im = re * cosine - im * sine, re * sine + im * cosine
            half_re[alpha + outer * b] = re
            half_im[alpha + outer * b] = im
    for b in range(inner):
        points = [(half_re[alpha + outer * b], half_im[alpha + outer * b]) for alpha in range(outer)]
        for a, (re, im) in enumerate(small_dft(points, 1.0)):
            store(inner * a + b, re, im)


def pencil_forward_kernel(plan, pencils, *refs):
    steer_re, steer_im, ahead, behind, twist, row, out, windows, *scratch = refs
    f, lanes, span = plan.f, plan.lanes, plan.span

    def load(s):
        chunk = pencils[plan.place(s)].astype(F32)
        return chunk[:f], chunk[f:]

    def store(s, re, im):
        block = from_planes(plan, re, im).astype(BF16)
        i, slab = s // plan.shift, s % plan.shift
        windows[i, :, slab * lanes : (slab + 1) * lanes] = block
        slab += plan.shift
        windows[(i - 1) % plan.hogel_rows, :, slab * lanes : (slab + 1) * lanes] = block

    columns(plan, 1.0, load, store, steer_re, steer_im, ahead, behind, twist, scratch)
    count = plan.hogel_rows
    result = matmul(windows[...].reshape(count * span, 2 * WIN), row[...]).astype(BF16)
    for i in range(count):
        for part in range(plan.parts):
            out[plan.place(i * plan.parts + part)] = result[
                i * span : (i + 1) * span, part * 2 * plan.pp : (part + 1) * 2 * plan.pp
            ]


def pencil_back_kernel(plan, lines, *refs):
    steer_re, steer_im, ahead, behind, twist, row, out, windows, *scratch = refs
    lanes, span, parts = plan.lanes, plan.span, plan.parts
    count, wide = plan.hogel_rows, 2 * plan.pp
    result = 0.0
    for n in range(parts):
        own = jnp.stack([lines[plan.place(i * parts + n)] for i in range(count)])
        before = jnp.concatenate([own[-1:], own[:-1]], axis=0)
        depth = slice(n * wide, (n + 1) * wide)
        result = result + matmul(own.reshape(count * span, wide), row[depth, :WIN])
        result = result + matmul(before.reshape(count * span, wide), row[depth, WIN:])
    windows[...] = result.reshape(count, span, WIN)

    def load(s):
        i, slab = s // plan.shift, s % plan.shift
        return to_planes(plan, windows[i, :, slab * lanes : (slab + 1) * lanes])

    def store(s, re, im):
        out[plan.place(s)] = jnp.concatenate([re, im], axis=0).astype(BF16)

    columns(plan, -1.0, load, store, steer_re, steer_im, ahead, behind, twist, scratch)


def hogel_kernel(plan, lines, goals, *refs):
    weights_behind, twist_behind, weights_ahead, twist_ahead, col, col_turned, same = refs[:7]
    out, lights, packed, field, spectra, bright, factors, weighted, back = refs[7:]
    C, X, lanes, pp = plan.C, plan.X, 2 * plan.pp, plan.pp
    total = plan.total_cols
    for k in range(C):
        block = lines[k * plan.R : (k + 1) * plan.R].reshape(X, lanes)
        place = slice(k * lanes, (k + 1) * lanes)
        packed[:X, place] = block
        packed[X:, place] = times_i(block.astype(F32)).astype(BF16)

    def emit_near(c, start, step, value):
        for n, part in enumerate((value, times_i(value))):
            rounded = part.astype(BF16)
            field[n, c * X + start : c * X + start + step, :] = rounded
            if c == 0 and start < STRIDE:
                field[n, total + start : total + start + step, :] = rounded

    near = matmul(weights_behind[0], packed[...])
    lines_inverse(plan, lanes, lambda rows: near[rows, :], emit_near, twist_behind)
    for j in range(plan.hogel_cols):
        window = slice(STRIDE * j, STRIDE * j + WIN)
        result = matmul(
            col_turned[...], jnp.concatenate([field[0, window, :], field[1, window, :]], axis=0)
        )
        spectra[j] = result
        power = result[:, :pp] * result[:, :pp] + result[:, pp:] * result[:, pp:]
        bright[j * VIEWS : (j + 1) * VIEWS, :] = power.reshape(VIEWS, BIN, pp).sum(axis=1)
    exact = lax.Precision.HIGHEST
    own = lax.broadcasted_iota(jnp.int32, (VIEWS, pp), 0) == (
        lax.broadcasted_iota(jnp.int32, (VIEWS, pp), 1) % VIEWS
    )
    for c in range(C):
        target = get_views(plan, goals[c])
        for j in range(plan.own_cols):
            h = c * plan.own_cols + j
            below = (plan.hogel_cols + h) * VIEWS
            bright[below : below + VIEWS, :] = jnp.where(own, target[j : j + 1, :], 0.0)
    spread = jnp.dot(bright[...], same[...], preferred_element_type=F32, precision=exact)
    views = plan.hogel_cols * VIEWS
    light = spread[:views] * (1.0 / (BIN * BIN))
    factors[...] = 4.0 * (light - spread[views:])
    bright[:views, :] = light
    for c in range(C):
        rows = []
        for j in range(plan.own_cols):
            h = c * plan.own_cols + j
            block = jnp.where(own, bright[h * VIEWS : (h + 1) * VIEWS, :], 0.0)
            rows.append(jnp.sum(block, axis=0, keepdims=True))
        lights[c] = put_views(plan, jnp.concatenate(rows, axis=0))
    for j in range(plan.hogel_cols):
        for view in range(VIEWS):
            factor = factors[j * VIEWS + view : j * VIEWS + view + 1, :]
            block = slice(view * BIN, (view + 1) * BIN)
            below = slice(WIN + view * BIN, WIN + (view + 1) * BIN)
            real = (spectra[j, block, :pp] * factor).astype(BF16)
            imag = (spectra[j, block, pp:] * factor).astype(BF16)
            weighted[block, :pp] = real
            weighted[block, pp:] = imag
            weighted[below, :pp] = imag
            weighted[below, pp:] = -real
        result = matmul(col[...], weighted[...])
        first, second = STRIDE * j, STRIDE * (j + 1) % total
        if j == 0:
            back[:STRIDE] = result[:STRIDE]
        else:
            back[first : first + STRIDE] = back[first : first + STRIDE] + result[:STRIDE]
        if j < plan.hogel_cols - 1:
            back[second : second + STRIDE] = result[STRIDE:]
        else:
            back[:STRIDE] = back[:STRIDE] + result[STRIDE:]

    def load(c, start, step):
        return back[c * X + start : c * X + start + step, :]

    def emit(d, block):
        out[d] = block.astype(BF16)

    lines_forward(plan, lanes, load, emit, weights_ahead, twist_ahead, packed)


def steer_table(plan):
    index = lax.axis_index(("cols", "rows"))
    shape = (plan.D, plan.f, 128)
    k = lax.broadcasted_iota(jnp.int32, shape, 0)
    line = lax.broadcasted_iota(jnp.int32, shape, 1)
    lane = lax.broadcasted_iota(jnp.int32, shape, 2)
    u = k + plan.D * (lane % plan.m)
    v = index // plan.R + plan.C * (
        plan.span * (index % plan.R) + plan.f * (lane // plan.m) + line
    )

    def freq(position, count):
        return ((position + count // 2) % count - count // 2).astype(F32) / count

    freq_rows, freq_cols = freq(u, plan.total_rows), freq(v, plan.total_cols)
    radial = freq_rows * freq_rows + freq_cols * freq_cols
    phase = (
        -2.0
        * math.pi
        * distance_px
        * radial
        / (jnp.sqrt(index_ratio * index_ratio - radial) + index_ratio)
    )
    return jnp.cos(phase), jnp.sin(phase)


def exchange(chunks):
    return lax.all_to_all(chunks, ("cols", "rows"), split_axis=0, concat_axis=0, tiled=True)


def swap_columns(chunks):
    count = lax.axis_size("cols")
    return tuple(
        lax.ppermute(chunk, "cols", [(i, i ^ t) for i in range(count)]) if t else chunk
        for t, chunk in zip(partners(count), chunks)
    )


def local(slm_field, target_light):
    rows_count, cols_count = lax.axis_size("rows"), lax.axis_size("cols")
    plan = Plan(rows_count, cols_count, slm_field.shape[1], slm_field.shape[2])
    C, D, X, lanes, f = plan.C, plan.D, plan.X, plan.lanes, plan.f
    span, wide = plan.span, 2 * plan.pp

    ahead, behind, twist = (jnp.asarray(t) for t in plan.pencil_tables())
    weights_ahead, twist_ahead = plan.line_tables(-1.0)
    weights_ahead, twist_ahead = jnp.asarray(weights_ahead[0]), jnp.asarray(twist_ahead)
    weights_behind, twist_behind = (jnp.asarray(t) for t in plan.line_tables(1.0))
    col, col_turned, row = hogel_tables()
    row = plan.row_table(row[0], row[1])
    col, col_turned, row, row_turned, same = (
        jnp.asarray(t) for t in (col, col_turned, row, row.T.copy(), plan.group_table())
    )
    steer_re, steer_im = steer_table(plan)

    slabs_shapes = (shape_of((X + VIEWS, lanes), BF16),) * C
    slabs_scratch = pltpu.VMEM((C, X + VIEWS, lanes), BF16)
    views_shape = shape_of((C, VIEWS, lanes), BF16)
    pencil_shape = shape_of((D, 2 * f, 128), BF16)
    lines_shape = shape_of((D, span, wide), BF16)
    columns_scratch = (
        pltpu.VMEM((D, f, 128), F32),
        pltpu.VMEM((D, f, 128), F32),
        pltpu.VMEM((D, f, 256), BF16),
    )
    pencil_tables = (steer_re, steer_im, ahead, behind, twist)
    columns_flops = 8 * D * f * 256 * 256 + 2 * plan.hogel_rows * span * (2 * WIN) ** 2

    apart_any = pl.BlockSpec(memory_space=pl.ANY)
    slabs = call(
        lambda *refs: pack_kernel(plan, *refs),
        slabs_shapes,
        (slm_field.astype(BF16), target_light),
        (slabs_scratch,),
    )
    tall = pltpu.VMEM((2 * X, C * lanes), BF16)
    pencils, goals = call(
        lambda *refs: rows_forward_kernel(plan, *refs),
        (pencil_shape, views_shape),
        (weights_ahead, twist_ahead, *swap_columns(slabs), steer_re, steer_im),
        (tall, slabs_scratch),
        flops=2 * X * 2 * X * C * lanes,
        in_specs={C + 2: apart_any, C + 3: apart_any},
    )
    (lines,) = call(
        lambda *refs: pencil_forward_kernel(plan, *refs),
        (lines_shape,),
        (exchange(pencils), *pencil_tables, row),
        (pltpu.VMEM((plan.hogel_rows, span, 2 * WIN), BF16), *columns_scratch),
        flops=columns_flops,
    )
    tall = pltpu.VMEM((2 * X, C * wide), BF16)
    lines, lights = call(
        lambda *refs: hogel_kernel(plan, *refs),
        (lines_shape, views_shape),
        (
            exchange(lines),
            goals,
            weights_behind,
            twist_behind,
            weights_ahead,
            twist_ahead,
            col,
            col_turned,
            same,
        ),
        (
            tall,
            pltpu.VMEM((2, plan.total_cols + STRIDE, wide), BF16),
            pltpu.VMEM((plan.hogel_cols, WIN, wide), F32),
            pltpu.VMEM((2 * plan.hogel_cols * VIEWS, plan.pp), F32),
            pltpu.VMEM((plan.hogel_cols * VIEWS, plan.pp), F32),
            pltpu.VMEM((2 * WIN, wide), BF16),
            pltpu.VMEM((plan.total_cols, wide), F32),
        ),
        flops=4 * X * 2 * X * C * wide + 4 * plan.hogel_cols * WIN * 2 * WIN * wide,
    )
    (pencils,) = call(
        lambda *refs: pencil_back_kernel(plan, *refs),
        (pencil_shape,),
        (exchange(lines), *pencil_tables, row_turned),
        (pltpu.VMEM((plan.hogel_rows, span, WIN), F32), *columns_scratch),
        flops=columns_flops,
    )
    tall = pltpu.VMEM((2 * X, C * lanes), BF16)
    slabs = call(
        lambda *refs: rows_inverse_kernel(plan, *refs),
        slabs_shapes,
        (exchange(pencils), lights, weights_behind, twist_behind),
        (tall, slabs_scratch),
        flops=2 * X * 2 * X * C * lanes,
    )
    return call(
        lambda *refs: unpack_kernel(plan, *refs),
        (shape_of(slm_field.shape, F32), shape_of(target_light.shape, F32)),
        swap_columns(slabs),
        (slabs_scratch,),
    )


def solution(mesh):
    return jax.shard_map(
        local,
        mesh=mesh,
        in_specs=(P(None, "rows", "cols"), P("rows", "cols", None)),
        out_specs=(P(None, "rows", "cols"), P("rows", "cols", None)),
        check_vma=False,
    )
```

```python
import math

import jax
import jax.numpy as jnp
import ml_dtypes
import numpy as np
from jax import lax
from jax.experimental import pallas as pl
from jax.experimental.pallas import tpu as pltpu
from jax.sharding import PartitionSpec as P

WIN = 256
VIEWS = 16
STRIDE = 128
BIN = 16

distance_px = 16000.0
index_ratio = 15.0

BF16 = jnp.bfloat16
F32 = jnp.float32
BOTH_MINOR = (((1,), (1,)), ((), ()))


def call(body, outs, args, scratch=(), flops=0, in_specs=None, out_specs=None):
    nbytes = sum(math.prod(a.shape) * a.dtype.itemsize for a in (*outs, *args))
    specs = {}
    if in_specs:
        whole = pl.BlockSpec(memory_space=pltpu.VMEM)
        specs["in_specs"] = [in_specs.get(n, whole) for n in range(len(args))]
    if out_specs:
        specs["out_specs"] = out_specs
    return pl.pallas_call(
        body,
        out_shape=outs,
        scratch_shapes=list(scratch),
        compiler_params=pltpu.CompilerParams(vmem_limit_bytes=24 * 2**20),
        cost_estimate=pl.CostEstimate(flops=flops, bytes_accessed=nbytes, transcendentals=0),
        **specs,
    )(*args)


def shape_of(dims, dtype):
    return jax.ShapeDtypeStruct(dims, dtype)


def high_low(table):
    table = np.asarray(table, np.float32)
    high = table.astype(ml_dtypes.bfloat16)
    low = (table - high.astype(np.float32)).astype(ml_dtypes.bfloat16)
    return np.concatenate([high, low], axis=0)


def times_i(values):
    half = values.shape[-1] // 2
    if values.shape[-1] == 128:
        lanes = lax.broadcasted_iota(jnp.int32, values.shape, values.ndim - 1)
        turned = pltpu.roll(values, half, values.ndim - 1)
        return jnp.where(lanes < half, -turned, turned)
    return jnp.concatenate([-values[..., half:], values[..., :half]], axis=-1)


def rounded_with_i(value):
    rounded = value.astype(BF16)
    half = value.shape[-1] // 2
    if half % 128:
        return rounded, times_i(value.astype(F32)).astype(BF16)
    return rounded, jnp.concatenate([-rounded[:, half:], rounded[:, :half]], axis=1)


def small_dft(points, sign):
    count = len(points)
    if count == 1:
        return points
    even = small_dft(points[0::2], sign)
    odd = small_dft(points[1::2], sign)
    front, back = [], []
    for k in range(count // 2):
        re, im = odd[k]
        angle = sign * 2.0 * math.pi * k / count
        cosine, sine = math.cos(angle), math.sin(angle)
        if k == 0:
            pass
        elif 4 * k == count:
            re, im = (-im, re) if sign > 0 else (im, -re)
        elif 8 * k == count:
            re, im = cosine * (re - sign * im), cosine * (im + sign * re)
        elif 8 * k == 3 * count:
            re, im = cosine * (re + sign * im), cosine * (im - sign * re)
        else:
            re, im = re * cosine - im * sine, re * sine + im * cosine
        even_re, even_im = even[k]
        front.append((even_re + re, even_im + im))
        back.append((even_re - re, even_im - im))
    return front + back


def packed_dft(points, sign):
    count = len(points)
    if count == 1:
        return points
    even = packed_dft(points[0::2], sign)
    odd = packed_dft(points[1::2], sign)
    front, back = [], []
    for k in range(count // 2):
        term = odd[k]
        angle = sign * 2.0 * math.pi * k / count
        if 4 * k == count:
            term = times_i(term) if sign > 0 else -times_i(term)
        elif k:
            term = math.cos(angle) * term + math.sin(angle) * times_i(term)
        front.append(even[k] + term)
        back.append(even[k] - term)
    return front + back


def turn(rows, cols, period, sign):
    angles = sign * 2.0 * np.pi / period * ((np.arange(rows)[:, None] * np.arange(cols)) % period)
    return np.cos(angles), np.sin(angles)


def block_diagonal(block, copies):
    return np.kron(np.eye(copies), block)


class Plan:
    def __init__(self, rows_count, cols_count, rows_dev, cols_dev):
        self.R, self.C = rows_count, cols_count
        self.D = rows_count * cols_count
        self.X = cols_dev
        self.m = rows_dev // cols_count
        self.lanes = 2 * self.m
        self.P = 128 // self.m
        self.span = cols_dev // rows_count
        self.f = self.span // self.P
        self.total_rows = rows_dev * rows_count
        self.total_cols = cols_dev * cols_count
        self.outer = 8
        self.inner = self.D // 8
        self.shift = STRIDE // self.m
        self.hogel_rows = self.total_rows // STRIDE
        self.hogel_cols = self.total_cols // STRIDE
        self.parts = self.D // self.hogel_rows
        self.pp = WIN // self.parts
        self.views = VIEWS // self.parts
        self.own_cols = cols_dev // STRIDE

    def place(self, s):
        return s % self.C * self.R + s // self.C

    def line_tables(self, sign):
        cosine, sine = turn(self.X, self.X, self.X, sign)
        weights = high_low(np.concatenate([cosine, sine], axis=1)).reshape(2, self.X, 2 * self.X)
        twist = turn(self.X, self.C, self.total_cols, sign)
        return weights, np.concatenate(twist, axis=1).astype(np.float32)

    def pencil_tables(self):
        cosine, sine = turn(self.m, self.m, self.m, -1.0)
        cosine, sine = block_diagonal(cosine, self.P), block_diagonal(sine, self.P)
        ahead = np.block([[cosine, sine], [-sine, cosine]])
        behind = np.block([[cosine, -sine], [sine, cosine]]) / (self.total_rows * self.total_cols)
        twist = turn(self.D, self.m, self.total_rows, -1.0)
        twist = np.stack([np.tile(part, (1, self.P)) for part in twist]).astype(np.float32)
        return high_low(ahead), high_low(behind), twist

    def row_table(self, real, imag):
        blocks = []
        for slab in range(WIN // self.m):
            rows = slice(slab * self.m, (slab + 1) * self.m)
            for left, right in ((real[rows], imag[rows]), (-imag[rows], real[rows])):
                pieces = []
                for part in range(self.parts):
                    cols = slice(part * self.pp, (part + 1) * self.pp)
                    pieces += [left[:, cols], right[:, cols]]
                blocks.append(np.concatenate(pieces, axis=1))
        return np.concatenate(blocks, axis=0)

    def group_table(self):
        return np.kron(np.eye(self.views), np.ones((BIN, BIN))).astype(np.float32)


def hogel_tables():
    positions = np.arange(WIN)
    tapers = np.sin(np.pi * (positions + 0.5) / WIN) ** 2
    angles = -2.0 * np.pi / WIN * (positions[:, None] * positions[None, :] % WIN)
    cosine = (tapers[:, None] * np.cos(angles)).astype(np.float32)
    sine = (tapers[:, None] * np.sin(angles)).astype(np.float32)
    col = np.concatenate([cosine, sine], axis=1).astype(ml_dtypes.bfloat16)
    col_turned = np.concatenate([cosine.T, sine.T], axis=1).astype(ml_dtypes.bfloat16)
    row = np.stack([cosine / WIN, sine / WIN]).astype(ml_dtypes.bfloat16)
    return col, col_turned, row


def three_pieces(values):
    first = values.astype(BF16)
    rest = values - first.astype(F32)
    second = rest.astype(BF16)
    return first, second, (rest - second.astype(F32)).astype(BF16)


def matmul(left, right):
    return jnp.dot(left, right, preferred_element_type=F32)


def partners(count):
    return sorted(range(count), key=lambda t: (t != 0, -t.bit_count()))


def gather_chunks(arrived, chunks):
    mine = lax.axis_index("cols")
    for t, chunk in zip(partners(len(arrived)), arrived):
        chunks[mine ^ t] = chunk[...]


def scatter_chunks(chunks, leaving):
    mine = lax.axis_index("cols")
    for t, chunk in zip(partners(len(leaving)), leaving):
        chunk[...] = chunks[mine ^ t]


def put_views(plan, rows):
    pad = jnp.zeros((VIEWS - 3 * plan.own_cols, plan.lanes), F32)
    pieces = [piece.astype(F32) for piece in three_pieces(rows)]
    return jnp.concatenate([*pieces, pad], axis=0).astype(BF16)


def get_views(plan, chunk):
    chunk = chunk.astype(F32)
    n = plan.own_cols
    return chunk[:n] + chunk[n : 2 * n] + chunk[2 * n : 3 * n]


def pack_kernel(plan, field, goal, *refs):
    C, m, X = plan.C, plan.m, plan.X
    leaving, (out,) = refs[:C], refs[C:]
    for c in range(C):
        rows = slice(c * m, (c + 1) * m)
        block = jnp.concatenate([field[0, rows, :], field[1, rows, :]], axis=0)
        out[c, :X, :] = block.astype(F32).T.astype(BF16)
        i, start = c // plan.parts, c % plan.parts * plan.lanes
        out[c, X:, :] = put_views(plan, goal[i, :, start : start + plan.lanes])
    scatter_chunks(out, leaving)


def unpack_kernel(plan, *refs):
    C, m, X = plan.C, plan.m, plan.X
    arrived, (out, light, slabs) = refs[:C], refs[C:]
    gather_chunks(arrived, slabs)
    for c in range(C):
        block = slabs[c, :X, :].astype(F32).T
        out[0, m * c : m * c + m, :] = block[:m]
        out[1, m * c : m * c + m, :] = block[m:]
        i, start = c // plan.parts, c % plan.parts * plan.lanes
        light[i, :, start : start + plan.lanes] = get_views(plan, slabs[c, X:, :])


def lines_forward(plan, lanes, load, emit, weights, twist, turned):
    C, X = plan.C, plan.X
    step = 64
    for start in range(0, X, step):
        points = packed_dft([load(c, start, step) for c in range(C)], -1.0)
        for k in range(C):
            cosine = twist[start : start + step, k : k + 1]
            sine = twist[start : start + step, C + k : C + k + 1]
            value = points[k]
            if k:
                value = value * cosine + times_i(value) * sine
            value, across = rounded_with_i(value)
            place = slice(k * lanes, k * lanes + lanes)
            turned[start : start + step, place] = value
            turned[X + start : X + start + step, place] = across
    group = max(1, 256 // lanes)
    for first in range(0, C, group):
        result = matmul(weights[...], turned[:, first * lanes : (first + group) * lanes])
        for k in range(group):
            for r in range(plan.R):
                rows = slice(r * plan.span, (r + 1) * plan.span)
                emit((first + k) * plan.R + r, result[rows, k * lanes : (k + 1) * lanes])


def lines_inverse(plan, lanes, product, emit, twist):
    C, X = plan.C, plan.X
    step = 64
    for start in range(0, X, step):
        rows = slice(start, start + step)
        result = product(rows)
        points = []
        for k in range(C):
            value = result[:, k * lanes : (k + 1) * lanes]
            if k:
                cosine, sine = twist[rows, k : k + 1], twist[rows, C + k : C + k + 1]
                value = value * cosine + times_i(value) * sine
            points.append(value)
        for c, value in enumerate(packed_dft(points, 1.0)):
            emit(c, start, step, value)


def to_planes(plan, block):
    parts = [block[p * plan.f : (p + 1) * plan.f, :] for p in range(plan.P)]
    real = jnp.concatenate([part[:, : plan.m] for part in parts], axis=1)
    imag = jnp.concatenate([part[:, plan.m :] for part in parts], axis=1)
    return real, imag


def from_planes(plan, real, imag):
    m = plan.m
    return jnp.concatenate(
        [
            jnp.concatenate([real[:, p * m : (p + 1) * m], imag[:, p * m : (p + 1) * m]], axis=1)
            for p in range(plan.P)
        ],
        axis=0,
    )


def rows_forward_kernel(plan, weights, twist, *refs):
    C, X = plan.C, plan.X
    arrived, (_, _, out, goals, turned, slabs) = refs[:C], refs[C:]
    gather_chunks(arrived, slabs)
    goals[...] = slabs[:, X:, :]

    def load(c, start, step):
        return slabs[c, start : start + step, :].astype(F32)

    def emit(d, block):
        out[d] = jnp.concatenate(to_planes(plan, block), axis=0).astype(BF16)

    lines_forward(plan, plan.lanes, load, emit, weights, twist, turned)


def rows_inverse_kernel(plan, pencils, lights, weights, twist, *refs):
    C, X, lanes = plan.C, plan.X, plan.lanes
    leaving, (packed, out) = refs[:C], refs[C:]
    for k in range(C):
        for r in range(plan.R):
            chunk = pencils[k * plan.R + r].astype(F32)
            block = from_planes(plan, chunk[: plan.f], chunk[plan.f :])
            place = slice(k * lanes, k * lanes + lanes)
            packed[r * plan.span : (r + 1) * plan.span, place] = block.astype(BF16)
            packed[X + r * plan.span : X + (r + 1) * plan.span, place] = times_i(block).astype(BF16)

    def emit(c, start, step, value):
        out[c, start : start + step, :] = value.astype(BF16)

    def product(rows):
        return matmul(weights[0, rows, :], packed[...]) + matmul(weights[1, rows, :], packed[...])

    lines_inverse(plan, lanes, product, emit, twist)
    out[:, X:, :] = lights[...]
    scatter_chunks(out, leaving)


def columns(plan, sign, load, store, steer_re, steer_im, ahead, behind, twist, scratch):
    D, f, outer, inner = plan.D, plan.f, plan.outer, plan.inner
    half_re, half_im, rounded = scratch
    for b in range(inner):
        points = [load(inner * a + b) for a in range(outer)]
        for alpha, (re, im) in enumerate(small_dft(points, -1.0)):
            angle = -2.0 * math.pi * b * alpha / D
            cosine, sine = math.cos(angle), math.sin(angle)
            if b * alpha:
                re, im = re * cosine - im * sine, re * sine + im * cosine
            half_re[alpha * inner + b] = re
            half_im[alpha * inner + b] = im
    for alpha in range(outer):
        points = [(half_re[alpha * inner + b], half_im[alpha * inner + b]) for b in range(inner)]
        for beta, (re, im) in enumerate(small_dft(points, -1.0)):
            k = alpha + outer * beta
            cosine, sine = twist[0, k : k + 1, :], twist[1, k : k + 1, :]
            for offset, part in ((0, re * cosine - im * sine), (128, re * sine + im * cosine)):
                rounded[k, :, offset : offset + 128] = part.astype(BF16)
    group = D // 2
    for start in range(0, D, group):
        place = slice(start, start + group)

        def multiply(matrix):
            left = rounded[place].reshape(group * f, 256)
            product = matmul(left, matrix[:256, :]) + matmul(left, matrix[256:, :])
            return product.reshape(group, f, 256)

        result = multiply(ahead)
        re, im = result[:, :, :128], result[:, :, 128:]
        factor_re, factor_im = steer_re[place], sign * steer_im[place]
        for offset, part in (
            (0, re * factor_re - im * factor_im),
            (128, re * factor_im + im * factor_re),
        ):
            rounded[place, :, offset : offset + 128] = part.astype(BF16)
        result = multiply(behind)
        half_re[place] = result[:, :, :128]
        half_im[place] = result[:, :, 128:]
    for alpha in range(outer):
        points = []
        for beta in range(inner):
            k = alpha + outer * beta
            cosine, sine = twist[0, k : k + 1, :], twist[1, k : k + 1, :]
            re, im = half_re[k], half_im[k]
            points.append((re * cosine + im * sine, im * cosine - re * sine))
        for b, (re, im) in enumerate(small_dft(points, 1.0)):
            angle = 2.0 * math.pi * b * alpha / D
            cosine, sine = math.cos(angle), math.sin(angle)
            if b * alpha:
                re, im = re * cosine - im * sine, re * sine + im * cosine
            half_re[alpha + outer * b] = re
            half_im[alpha + outer * b] = im
    for b in range(inner):
        points = [(half_re[alpha + outer * b], half_im[alpha + outer * b]) for alpha in range(outer)]
        for a, (re, im) in enumerate(small_dft(points, 1.0)):
            store(inner * a + b, re, im)


def pencil_forward_kernel(plan, pencils, *refs):
    steer_re, steer_im, ahead, behind, twist, row, out, windows, *scratch = refs
    f, lanes, span = plan.f, plan.lanes, plan.span

    def load(s):
        chunk = pencils[plan.place(s)].astype(F32)
        return chunk[:f], chunk[f:]

    def store(s, re, im):
        block = from_planes(plan, re, im).astype(BF16)
        i, slab = s // plan.shift, s % plan.shift
        windows[i, :, slab * lanes : (slab + 1) * lanes] = block
        slab += plan.shift
        windows[(i - 1) % plan.hogel_rows, :, slab * lanes : (slab + 1) * lanes] = block

    columns(plan, 1.0, load, store, steer_re, steer_im, ahead, behind, twist, scratch)
    count = plan.hogel_rows
    result = matmul(windows[...].reshape(count * span, 2 * WIN), row[...]).astype(BF16)
    for i in range(count):
        for part in range(plan.parts):
            out[plan.place(i * plan.parts + part)] = result[
                i * span : (i + 1) * span, part * 2 * plan.pp : (part + 1) * 2 * plan.pp
            ]


def pencil_back_kernel(plan, lines, *refs):
    steer_re, steer_im, ahead, behind, twist, row, out, windows, *scratch = refs
    lanes, span, parts = plan.lanes, plan.span, plan.parts
    count, wide = plan.hogel_rows, 2 * plan.pp
    result = 0.0
    for n in range(parts):
        own = jnp.stack([lines[plan.place(i * parts + n)] for i in range(count)])
        before = jnp.concatenate([own[-1:], own[:-1]], axis=0)
        depth = slice(n * wide, (n + 1) * wide)
        result = result + matmul(own.reshape(count * span, wide), row[depth, :WIN])
        result = result + matmul(before.reshape(count * span, wide), row[depth, WIN:])
    windows[...] = result.reshape(count, span, WIN)

    def load(s):
        i, slab = s // plan.shift, s % plan.shift
        return to_planes(plan, windows[i, :, slab * lanes : (slab + 1) * lanes])

    def store(s, re, im):
        out[plan.place(s)] = jnp.concatenate([re, im], axis=0).astype(BF16)

    columns(plan, -1.0, load, store, steer_re, steer_im, ahead, behind, twist, scratch)


def hogel_kernel(plan, lines, goals, *refs):
    weights_behind, twist_behind, weights_ahead, twist_ahead, col, col_turned, same = refs[:7]
    out, lights, packed, field, spectra, bright, factors, weighted, back = refs[7:]
    C, X, lanes, pp = plan.C, plan.X, 2 * plan.pp, plan.pp
    total = plan.total_cols
    for k in range(C):
        block = lines[k * plan.R : (k + 1) * plan.R].reshape(X, lanes)
        place = slice(k * lanes, (k + 1) * lanes)
        packed[:X, place], packed[X:, place] = rounded_with_i(block)

    def emit_near(c, start, step, value):
        for n, rounded in enumerate(rounded_with_i(value)):
            field[n, c * X + start : c * X + start + step, :] = rounded
            if c == 0 and start < STRIDE:
                field[n, total + start : total + start + step, :] = rounded

    near = matmul(weights_behind[0], packed[...])
    lines_inverse(plan, lanes, lambda rows: near[rows, :], emit_near, twist_behind)
    for j in range(plan.hogel_cols):
        window = slice(STRIDE * j, STRIDE * j + WIN)
        result = matmul(
            col_turned[...], jnp.concatenate([field[0, window, :], field[1, window, :]], axis=0)
        )
        spectra[j] = result
        power = result[:, :pp] * result[:, :pp] + result[:, pp:] * result[:, pp:]
        bright[j * VIEWS : (j + 1) * VIEWS, :] = power.reshape(VIEWS, BIN, pp).sum(axis=1)
    exact = lax.Precision.HIGHEST
    own = lax.broadcasted_iota(jnp.int32, (VIEWS, pp), 0) == (
        lax.broadcasted_iota(jnp.int32, (VIEWS, pp), 1) % VIEWS
    )
    for c in range(C):
        target = get_views(plan, goals[c])
        for j in range(plan.own_cols):
            h = c * plan.own_cols + j
            below = (plan.hogel_cols + h) * VIEWS
            bright[below : below + VIEWS, :] = jnp.where(own, target[j : j + 1, :], 0.0)
    spread = jnp.dot(bright[...], same[...], preferred_element_type=F32, precision=exact)
    views = plan.hogel_cols * VIEWS
    light = spread[:views] * (1.0 / (BIN * BIN))
    factors[...] = 4.0 * (light - spread[views:])
    bright[:views, :] = light
    for c in range(C):
        rows = []
        for j in range(plan.own_cols):
            h = c * plan.own_cols + j
            block = jnp.where(own, bright[h * VIEWS : (h + 1) * VIEWS, :], 0.0)
            rows.append(jnp.sum(block, axis=0, keepdims=True))
        lights[c] = put_views(plan, jnp.concatenate(rows, axis=0))
    for j in range(plan.hogel_cols):
        for view in range(VIEWS):
            factor = factors[j * VIEWS + view : j * VIEWS + view + 1, :]
            block = slice(view * BIN, (view + 1) * BIN)
            below = slice(WIN + view * BIN, WIN + (view + 1) * BIN)
            real = (spectra[j, block, :pp] * factor).astype(BF16)
            imag = (spectra[j, block, pp:] * factor).astype(BF16)
            weighted[block, :pp] = real
            weighted[block, pp:] = imag
            weighted[below, :pp] = imag
            weighted[below, pp:] = -real
        result = matmul(col[...], weighted[...])
        first = slice(STRIDE * j, STRIDE * (j + 1))
        back[first] = result[:STRIDE] if j == 0 else pending + result[:STRIDE]
        pending = result[STRIDE:]
    back[:STRIDE] = back[:STRIDE] + pending

    def load(c, start, step):
        return back[c * X + start : c * X + start + step, :]

    def emit(d, block):
        out[d] = block.astype(BF16)

    lines_forward(plan, lanes, load, emit, weights_ahead, twist_ahead, packed)


def steer_table(plan):
    index = lax.axis_index(("cols", "rows"))
    shape = (plan.D, plan.f, 128)
    k = lax.broadcasted_iota(jnp.int32, shape, 0)
    line = lax.broadcasted_iota(jnp.int32, shape, 1)
    lane = lax.broadcasted_iota(jnp.int32, shape, 2)
    u = k + plan.D * (lane % plan.m)
    v = index // plan.R + plan.C * (
        plan.span * (index % plan.R) + plan.f * (lane // plan.m) + line
    )

    def freq(position, count):
        return ((position + count // 2) % count - count // 2).astype(F32) / count

    freq_rows, freq_cols = freq(u, plan.total_rows), freq(v, plan.total_cols)
    radial = freq_rows * freq_rows + freq_cols * freq_cols
    phase = (
        -2.0
        * math.pi
        * distance_px
        * radial
        / (jnp.sqrt(index_ratio * index_ratio - radial) + index_ratio)
    )
    return jnp.cos(phase), jnp.sin(phase)


def exchange(chunks):
    return lax.all_to_all(chunks, ("cols", "rows"), split_axis=0, concat_axis=0, tiled=True)


def swap_columns(chunks):
    count = lax.axis_size("cols")
    return tuple(
        lax.ppermute(chunk, "cols", [(i, i ^ t) for i in range(count)]) if t else chunk
        for t, chunk in zip(partners(count), chunks)
    )


def local(slm_field, target_light):
    rows_count, cols_count = lax.axis_size("rows"), lax.axis_size("cols")
    plan = Plan(rows_count, cols_count, slm_field.shape[1], slm_field.shape[2])
    C, D, X, lanes, f = plan.C, plan.D, plan.X, plan.lanes, plan.f
    span, wide = plan.span, 2 * plan.pp

    ahead, behind, twist = (jnp.asarray(t) for t in plan.pencil_tables())
    weights_ahead, twist_ahead = plan.line_tables(-1.0)
    weights_ahead, twist_ahead = jnp.asarray(weights_ahead[0]), jnp.asarray(twist_ahead)
    weights_behind, twist_behind = (jnp.asarray(t) for t in plan.line_tables(1.0))
    col, col_turned, row = hogel_tables()
    row = plan.row_table(row[0], row[1])
    col, col_turned, row, row_turned, same = (
        jnp.asarray(t) for t in (col, col_turned, row, row.T.copy(), plan.group_table())
    )
    steer_re, steer_im = steer_table(plan)

    slabs_shapes = (shape_of((X + VIEWS, lanes), BF16),) * C
    slabs_scratch = pltpu.VMEM((C, X + VIEWS, lanes), BF16)
    views_shape = shape_of((C, VIEWS, lanes), BF16)
    pencil_shape = shape_of((D, 2 * f, 128), BF16)
    lines_shape = shape_of((D, span, wide), BF16)
    columns_scratch = (
        pltpu.VMEM((D, f, 128), F32),
        pltpu.VMEM((D, f, 128), F32),
        pltpu.VMEM((D, f, 256), BF16),
    )
    pencil_tables = (steer_re, steer_im, ahead, behind, twist)
    columns_flops = 8 * D * f * 256 * 256 + 2 * plan.hogel_rows * span * (2 * WIN) ** 2

    apart_any = pl.BlockSpec(memory_space=pl.ANY)
    slabs = call(
        lambda *refs: pack_kernel(plan, *refs),
        slabs_shapes,
        (slm_field.astype(BF16), target_light),
        (slabs_scratch,),
    )
    tall = pltpu.VMEM((2 * X, C * lanes), BF16)
    pencils, goals = call(
        lambda *refs: rows_forward_kernel(plan, *refs),
        (pencil_shape, views_shape),
        (weights_ahead, twist_ahead, *swap_columns(slabs), steer_re, steer_im),
        (tall, slabs_scratch),
        flops=2 * X * 2 * X * C * lanes,
        in_specs={C + 2: apart_any, C + 3: apart_any},
    )
    (lines,) = call(
        lambda *refs: pencil_forward_kernel(plan, *refs),
        (lines_shape,),
        (exchange(pencils), *pencil_tables, row),
        (pltpu.VMEM((plan.hogel_rows, span, 2 * WIN), BF16), *columns_scratch),
        flops=columns_flops,
    )
    tall = pltpu.VMEM((2 * X, C * wide), BF16)
    lines, lights = call(
        lambda *refs: hogel_kernel(plan, *refs),
        (lines_shape, views_shape),
        (
            exchange(lines),
            goals,
            weights_behind,
            twist_behind,
            weights_ahead,
            twist_ahead,
            col,
            col_turned,
            same,
        ),
        (
            tall,
            pltpu.VMEM((2, plan.total_cols + STRIDE, wide), BF16),
            pltpu.VMEM((plan.hogel_cols, WIN, wide), F32),
            pltpu.VMEM((2 * plan.hogel_cols * VIEWS, plan.pp), F32),
            pltpu.VMEM((plan.hogel_cols * VIEWS, plan.pp), F32),
            pltpu.VMEM((2 * WIN, wide), BF16),
            pltpu.VMEM((plan.total_cols, wide), F32),
        ),
        flops=4 * X * 2 * X * C * wide + 4 * plan.hogel_cols * WIN * 2 * WIN * wide,
    )
    (pencils,) = call(
        lambda *refs: pencil_back_kernel(plan, *refs),
        (pencil_shape,),
        (exchange(lines), *pencil_tables, row_turned),
        (pltpu.VMEM((plan.hogel_rows, span, WIN), F32), *columns_scratch),
        flops=columns_flops,
    )
    tall = pltpu.VMEM((2 * X, C * lanes), BF16)
    slabs = call(
        lambda *refs: rows_inverse_kernel(plan, *refs),
        slabs_shapes,
        (exchange(pencils), lights, weights_behind, twist_behind),
        (tall, slabs_scratch),
        flops=2 * X * 2 * X * C * lanes,
    )
    return call(
        lambda *refs: unpack_kernel(plan, *refs),
        (shape_of(slm_field.shape, F32), shape_of(target_light.shape, F32)),
        swap_columns(slabs),
        (slabs_scratch,),
    )


def solution(mesh):
    return jax.shard_map(
        local,
        mesh=mesh,
        in_specs=(P(None, "rows", "cols"), P("rows", "cols", None)),
        out_specs=(P(None, "rows", "cols"), P("rows", "cols", None)),
        check_vma=False,
    )
```

```python
import math

import jax
import jax.numpy as jnp
import ml_dtypes
import numpy as np
from jax import lax
from jax.experimental import pallas as pl
from jax.experimental.pallas import tpu as pltpu
from jax.sharding import PartitionSpec as P

WIN = 256
VIEWS = 16
STRIDE = 128
BIN = 16

distance_px = 16000.0
index_ratio = 15.0

BF16 = jnp.bfloat16
F32 = jnp.float32
BOTH_MINOR = (((1,), (1,)), ((), ()))


def call(body, outs, args, scratch=(), flops=0, in_specs=None, out_specs=None):
    nbytes = sum(math.prod(a.shape) * a.dtype.itemsize for a in (*outs, *args))
    specs = {}
    if in_specs:
        whole = pl.BlockSpec(memory_space=pltpu.VMEM)
        specs["in_specs"] = [in_specs.get(n, whole) for n in range(len(args))]
    if out_specs:
        specs["out_specs"] = out_specs
    return pl.pallas_call(
        body,
        out_shape=outs,
        scratch_shapes=list(scratch),
        compiler_params=pltpu.CompilerParams(vmem_limit_bytes=24 * 2**20),
        cost_estimate=pl.CostEstimate(flops=flops, bytes_accessed=nbytes, transcendentals=0),
        **specs,
    )(*args)


def shape_of(dims, dtype):
    return jax.ShapeDtypeStruct(dims, dtype)


def high_low(table):
    table = np.asarray(table, np.float32)
    high = table.astype(ml_dtypes.bfloat16)
    low = (table - high.astype(np.float32)).astype(ml_dtypes.bfloat16)
    return np.concatenate([high, low], axis=0)


def times_i(values):
    half = values.shape[-1] // 2
    if values.shape[-1] == 128:
        lanes = lax.broadcasted_iota(jnp.int32, values.shape, values.ndim - 1)
        turned = pltpu.roll(values, half, values.ndim - 1)
        return jnp.where(lanes < half, -turned, turned)
    return jnp.concatenate([-values[..., half:], values[..., :half]], axis=-1)


def rounded_with_i(value):
    rounded = value.astype(BF16)
    half = value.shape[-1] // 2
    if half % 128:
        return rounded, times_i(value.astype(F32)).astype(BF16)
    return rounded, jnp.concatenate([-rounded[:, half:], rounded[:, :half]], axis=1)


def small_dft(points, sign):
    count = len(points)
    if count == 1:
        return points
    even = small_dft(points[0::2], sign)
    odd = small_dft(points[1::2], sign)
    front, back = [], []
    for k in range(count // 2):
        re, im = odd[k]
        angle = sign * 2.0 * math.pi * k / count
        cosine, sine = math.cos(angle), math.sin(angle)
        if k == 0:
            pass
        elif 4 * k == count:
            re, im = (-im, re) if sign > 0 else (im, -re)
        elif 8 * k == count:
            re, im = cosine * (re - sign * im), cosine * (im + sign * re)
        elif 8 * k == 3 * count:
            re, im = cosine * (re + sign * im), cosine * (im - sign * re)
        else:
            re, im = re * cosine - im * sine, re * sine + im * cosine
        even_re, even_im = even[k]
        front.append((even_re + re, even_im + im))
        back.append((even_re - re, even_im - im))
    return front + back


def packed_dft(points, sign):
    count = len(points)
    if count == 1:
        return points
    even = packed_dft(points[0::2], sign)
    odd = packed_dft(points[1::2], sign)
    front, back = [], []
    for k in range(count // 2):
        term = odd[k]
        angle = sign * 2.0 * math.pi * k / count
        if 4 * k == count:
            term = times_i(term) if sign > 0 else -times_i(term)
        elif k:
            term = math.cos(angle) * term + math.sin(angle) * times_i(term)
        front.append(even[k] + term)
        back.append(even[k] - term)
    return front + back


def turn(rows, cols, period, sign):
    angles = sign * 2.0 * np.pi / period * ((np.arange(rows)[:, None] * np.arange(cols)) % period)
    return np.cos(angles), np.sin(angles)


def block_diagonal(block, copies):
    return np.kron(np.eye(copies), block)


class Plan:
    def __init__(self, rows_count, cols_count, rows_dev, cols_dev):
        self.R, self.C = rows_count, cols_count
        self.D = rows_count * cols_count
        self.X = cols_dev
        self.m = rows_dev // cols_count
        self.lanes = 2 * self.m
        self.P = 128 // self.m
        self.span = cols_dev // rows_count
        self.f = self.span // self.P
        self.total_rows = rows_dev * rows_count
        self.total_cols = cols_dev * cols_count
        self.outer = 8
        self.inner = self.D // 8
        self.shift = STRIDE // self.m
        self.hogel_rows = self.total_rows // STRIDE
        self.hogel_cols = self.total_cols // STRIDE
        self.parts = self.D // self.hogel_rows
        self.pp = WIN // self.parts
        self.views = VIEWS // self.parts
        self.own_cols = cols_dev // STRIDE

    def place(self, s):
        return s % self.C * self.R + s // self.C

    def line_tables(self, sign):
        cosine, sine = turn(self.X, self.X, self.X, sign)
        weights = high_low(np.concatenate([cosine, sine], axis=1)).reshape(2, self.X, 2 * self.X)
        twist = turn(self.X, self.C, self.total_cols, sign)
        return weights, np.concatenate(twist, axis=1).astype(np.float32)

    def pencil_tables(self):
        cosine, sine = turn(self.m, self.m, self.m, -1.0)
        cosine, sine = block_diagonal(cosine, self.P), block_diagonal(sine, self.P)
        ahead = np.block([[cosine, sine], [-sine, cosine]])
        behind = np.block([[cosine, -sine], [sine, cosine]]) / (self.total_rows * self.total_cols)
        twist = turn(self.D, self.m, self.total_rows, -1.0)
        twist = np.stack([np.tile(part, (1, self.P)) for part in twist]).astype(np.float32)
        return high_low(ahead), high_low(behind), twist

    def row_table(self, real, imag):
        blocks = []
        for slab in range(WIN // self.m):
            rows = slice(slab * self.m, (slab + 1) * self.m)
            for left, right in ((real[rows], imag[rows]), (-imag[rows], real[rows])):
                pieces = []
                for part in range(self.parts):
                    cols = slice(part * self.pp, (part + 1) * self.pp)
                    pieces += [left[:, cols], right[:, cols]]
                blocks.append(np.concatenate(pieces, axis=1))
        return np.concatenate(blocks, axis=0)

    def group_table(self):
        return np.kron(np.eye(self.views), np.ones((BIN, BIN))).astype(np.float32)


def hogel_tables():
    positions = np.arange(WIN)
    tapers = np.sin(np.pi * (positions + 0.5) / WIN) ** 2
    angles = -2.0 * np.pi / WIN * (positions[:, None] * positions[None, :] % WIN)
    cosine = (tapers[:, None] * np.cos(angles)).astype(np.float32)
    sine = (tapers[:, None] * np.sin(angles)).astype(np.float32)
    col = np.concatenate([cosine, sine], axis=1).astype(ml_dtypes.bfloat16)
    col_turned = np.concatenate([cosine.T, sine.T], axis=1).astype(ml_dtypes.bfloat16)
    row = np.stack([cosine / WIN, sine / WIN]).astype(ml_dtypes.bfloat16)
    return col, col_turned, row


def three_pieces(values):
    first = values.astype(BF16)
    rest = values - first.astype(F32)
    second = rest.astype(BF16)
    return first, second, (rest - second.astype(F32)).astype(BF16)


def matmul(left, right):
    return jnp.dot(left, right, preferred_element_type=F32)


def partners(count):
    return sorted(range(count), key=lambda t: (t != 0, -t.bit_count()))


def gather_chunks(arrived, chunks):
    mine = lax.axis_index("cols")
    for t, chunk in zip(partners(len(arrived)), arrived):
        chunks[mine ^ t] = chunk[...]


def scatter_chunks(chunks, leaving):
    mine = lax.axis_index("cols")
    for t, chunk in zip(partners(len(leaving)), leaving):
        chunk[...] = chunks[mine ^ t]


def put_views(plan, rows):
    pad = jnp.zeros((VIEWS - 3 * plan.own_cols, plan.lanes), F32)
    pieces = [piece.astype(F32) for piece in three_pieces(rows)]
    return jnp.concatenate([*pieces, pad], axis=0).astype(BF16)


def get_views(plan, chunk):
    chunk = chunk.astype(F32)
    n = plan.own_cols
    return chunk[:n] + chunk[n : 2 * n] + chunk[2 * n : 3 * n]


def pack_kernel(plan, field, goal, *refs):
    C, m, X = plan.C, plan.m, plan.X
    leaving, (out,) = refs[:C], refs[C:]
    for c in range(C):
        rows = slice(c * m, (c + 1) * m)
        block = jnp.concatenate([field[0, rows, :], field[1, rows, :]], axis=0)
        out[c, :X, :] = block.astype(F32).T.astype(BF16)
        i, start = c // plan.parts, c % plan.parts * plan.lanes
        out[c, X:, :] = put_views(plan, goal[i, :, start : start + plan.lanes])
    scatter_chunks(out, leaving)


def unpack_kernel(plan, *refs):
    C, m, X = plan.C, plan.m, plan.X
    arrived, (out, light, slabs) = refs[:C], refs[C:]
    gather_chunks(arrived, slabs)
    for c in range(C):
        block = slabs[c, :X, :].astype(F32).T
        out[0, m * c : m * c + m, :] = block[:m]
        out[1, m * c : m * c + m, :] = block[m:]
        i, start = c // plan.parts, c % plan.parts * plan.lanes
        light[i, :, start : start + plan.lanes] = get_views(plan, slabs[c, X:, :])


def lines_forward(plan, lanes, load, emit, weights, twist, turned):
    C, X = plan.C, plan.X
    step = 64
    for start in range(0, X, step):
        points = packed_dft([load(c, start, step) for c in range(C)], -1.0)
        for k in range(C):
            cosine = twist[start : start + step, k : k + 1]
            sine = twist[start : start + step, C + k : C + k + 1]
            value = points[k]
            if lanes % 256:
                across = times_i(value)
                if k:
                    value, across = value * cosine + across * sine, across * cosine - value * sine
                value, across = value.astype(BF16), across.astype(BF16)
            else:
                if k:
                    value = value * cosine + times_i(value) * sine
                value, across = rounded_with_i(value)
            place = slice(k * lanes, k * lanes + lanes)
            turned[start : start + step, place] = value
            turned[X + start : X + start + step, place] = across
    group = max(1, 256 // lanes)
    for first in range(0, C, group):
        result = matmul(weights[...], turned[:, first * lanes : (first + group) * lanes])
        for k in range(group):
            for r in range(plan.R):
                rows = slice(r * plan.span, (r + 1) * plan.span)
                emit((first + k) * plan.R + r, result[rows, k * lanes : (k + 1) * lanes])


def lines_inverse(plan, lanes, product, emit, twist):
    C, X = plan.C, plan.X
    step = 64
    for start in range(0, X, step):
        rows = slice(start, start + step)
        result = product(rows)
        points = []
        for k in range(C):
            value = result[:, k * lanes : (k + 1) * lanes]
            if k:
                cosine, sine = twist[rows, k : k + 1], twist[rows, C + k : C + k + 1]
                value = value * cosine + times_i(value) * sine
            points.append(value)
        for c, value in enumerate(packed_dft(points, 1.0)):
            emit(c, start, step, value)


def to_planes(plan, block):
    parts = [block[p * plan.f : (p + 1) * plan.f, :] for p in range(plan.P)]
    real = jnp.concatenate([part[:, : plan.m] for part in parts], axis=1)
    imag = jnp.concatenate([part[:, plan.m :] for part in parts], axis=1)
    return real, imag


def from_planes(plan, real, imag):
    m = plan.m
    return jnp.concatenate(
        [
            jnp.concatenate([real[:, p * m : (p + 1) * m], imag[:, p * m : (p + 1) * m]], axis=1)
            for p in range(plan.P)
        ],
        axis=0,
    )


def rows_forward_kernel(plan, weights, twist, *refs):
    C, X = plan.C, plan.X
    arrived, (_, _, out, goals, turned, slabs) = refs[:C], refs[C:]
    gather_chunks(arrived, slabs)
    goals[...] = slabs[:, X:, :]

    def load(c, start, step):
        return slabs[c, start : start + step, :].astype(F32)

    def emit(d, block):
        out[d] = jnp.concatenate(to_planes(plan, block), axis=0).astype(BF16)

    lines_forward(plan, plan.lanes, load, emit, weights, twist, turned)


def rows_inverse_kernel(plan, pencils, lights, weights, twist, *refs):
    C, X, lanes = plan.C, plan.X, plan.lanes
    leaving, (packed, out) = refs[:C], refs[C:]
    for k in range(C):
        for r in range(plan.R):
            chunk = pencils[k * plan.R + r].astype(F32)
            block = from_planes(plan, chunk[: plan.f], chunk[plan.f :])
            place = slice(k * lanes, k * lanes + lanes)
            packed[r * plan.span : (r + 1) * plan.span, place] = block.astype(BF16)
            packed[X + r * plan.span : X + (r + 1) * plan.span, place] = times_i(block).astype(BF16)

    def emit(c, start, step, value):
        out[c, start : start + step, :] = value.astype(BF16)

    def product(rows):
        return matmul(weights[0, rows, :], packed[...]) + matmul(weights[1, rows, :], packed[...])

    lines_inverse(plan, lanes, product, emit, twist)
    out[:, X:, :] = lights[...]
    scatter_chunks(out, leaving)


def columns(plan, sign, load, store, steer_re, steer_im, ahead, behind, twist, scratch):
    D, f, outer, inner = plan.D, plan.f, plan.outer, plan.inner
    half_re, half_im, rounded = scratch
    for b in range(inner):
        points = [load(inner * a + b) for a in range(outer)]
        for alpha, (re, im) in enumerate(small_dft(points, -1.0)):
            angle = -2.0 * math.pi * b * alpha / D
            cosine, sine = math.cos(angle), math.sin(angle)
            if b * alpha:
                re, im = re * cosine - im * sine, re * sine + im * cosine
            half_re[alpha * inner + b] = re
            half_im[alpha * inner + b] = im
    for alpha in range(outer):
        points = [(half_re[alpha * inner + b], half_im[alpha * inner + b]) for b in range(inner)]
        for beta, (re, im) in enumerate(small_dft(points, -1.0)):
            k = alpha + outer * beta
            cosine, sine = twist[0, k : k + 1, :], twist[1, k : k + 1, :]
            for offset, part in ((0, re * cosine - im * sine), (128, re * sine + im * cosine)):
                rounded[k, :, offset : offset + 128] = part.astype(BF16)
    group = D // 4
    for start in range(0, D, group):
        place = slice(start, start + group)

        def multiply(matrix):
            left = rounded[place].reshape(group * f, 256)
            product = matmul(left, matrix[:256, :]) + matmul(left, matrix[256:, :])
            return product.reshape(group, f, 256)

        result = multiply(ahead)
        re, im = result[:, :, :128], result[:, :, 128:]
        factor_re, factor_im = steer_re[place], sign * steer_im[place]
        for offset, part in (
            (0, re * factor_re - im * factor_im),
            (128, re * factor_im + im * factor_re),
        ):
            rounded[place, :, offset : offset + 128] = part.astype(BF16)
        result = multiply(behind)
        half_re[place] = result[:, :, :128]
        half_im[place] = result[:, :, 128:]
    for alpha in range(outer):
        points = []
        for beta in range(inner):
            k = alpha + outer * beta
            cosine, sine = twist[0, k : k + 1, :], twist[1, k : k + 1, :]
            re, im = half_re[k], half_im[k]
            points.append((re * cosine + im * sine, im * cosine - re * sine))
        for b, (re, im) in enumerate(small_dft(points, 1.0)):
            angle = 2.0 * math.pi * b * alpha / D
            cosine, sine = math.cos(angle), math.sin(angle)
            if b * alpha:
                re, im = re * cosine - im * sine, re * sine + im * cosine
            half_re[alpha + outer * b] = re
            half_im[alpha + outer * b] = im
    for b in range(inner):
        points = [(half_re[alpha + outer * b], half_im[alpha + outer * b]) for alpha in range(outer)]
        for a, (re, im) in enumerate(small_dft(points, 1.0)):
            store(inner * a + b, re, im)


def pencil_forward_kernel(plan, pencils, *refs):
    steer_re, steer_im, ahead, behind, twist, row, out, windows, *scratch = refs
    f, lanes, span = plan.f, plan.lanes, plan.span

    def load(s):
        chunk = pencils[plan.place(s)].astype(F32)
        return chunk[:f], chunk[f:]

    def store(s, re, im):
        block = from_planes(plan, re, im).astype(BF16)
        i, slab = s // plan.shift, s % plan.shift
        windows[i, :, slab * lanes : (slab + 1) * lanes] = block
        slab += plan.shift
        windows[(i - 1) % plan.hogel_rows, :, slab * lanes : (slab + 1) * lanes] = block

    columns(plan, 1.0, load, store, steer_re, steer_im, ahead, behind, twist, scratch)
    count = plan.hogel_rows
    result = matmul(windows[...].reshape(count * span, 2 * WIN), row[...]).astype(BF16)
    for i in range(count):
        for part in range(plan.parts):
            out[plan.place(i * plan.parts + part)] = result[
                i * span : (i + 1) * span, part * 2 * plan.pp : (part + 1) * 2 * plan.pp
            ]


def pencil_back_kernel(plan, lines, *refs):
    steer_re, steer_im, ahead, behind, twist, row, out, windows, *scratch = refs
    lanes, span, parts = plan.lanes, plan.span, plan.parts
    count, wide = plan.hogel_rows, 2 * plan.pp
    result = 0.0
    for n in range(parts):
        own = jnp.stack([lines[plan.place(i * parts + n)] for i in range(count)])
        before = jnp.concatenate([own[-1:], own[:-1]], axis=0)
        depth = slice(n * wide, (n + 1) * wide)
        result = result + matmul(own.reshape(count * span, wide), row[depth, :WIN])
        result = result + matmul(before.reshape(count * span, wide), row[depth, WIN:])
    windows[...] = result.reshape(count, span, WIN)

    def load(s):
        i, slab = s // plan.shift, s % plan.shift
        return to_planes(plan, windows[i, :, slab * lanes : (slab + 1) * lanes])

    def store(s, re, im):
        out[plan.place(s)] = jnp.concatenate([re, im], axis=0).astype(BF16)

    columns(plan, -1.0, load, store, steer_re, steer_im, ahead, behind, twist, scratch)


def hogel_kernel(plan, lines, goals, *refs):
    weights_behind, twist_behind, weights_ahead, twist_ahead, col, col_turned, same = refs[:7]
    out, lights, packed, field, spectra, bright, factors, weighted, back = refs[7:]
    C, X, lanes, pp = plan.C, plan.X, 2 * plan.pp, plan.pp
    total = plan.total_cols
    for k in range(C):
        block = lines[k * plan.R : (k + 1) * plan.R].reshape(X, lanes)
        place = slice(k * lanes, (k + 1) * lanes)
        packed[:X, place], packed[X:, place] = rounded_with_i(block)

    def emit_near(c, start, step, value):
        for n, rounded in enumerate(rounded_with_i(value)):
            field[n, c * X + start : c * X + start + step, :] = rounded
            if c == 0 and start < STRIDE:
                field[n, total + start : total + start + step, :] = rounded

    near = matmul(weights_behind[0], packed[...])
    lines_inverse(plan, lanes, lambda rows: near[rows, :], emit_near, twist_behind)
    group = max(1, 512 // lanes)
    for start in range(0, plan.hogel_cols, group):
        right = []
        for j in range(start, start + group):
            window = slice(STRIDE * j, STRIDE * j + WIN)
            right.append(jnp.concatenate([field[0, window, :], field[1, window, :]], axis=0))
        result = matmul(col_turned[...], jnp.concatenate(right, axis=1))
        for j in range(start, start + group):
            spectrum = result[:, (j - start) * lanes : (j - start + 1) * lanes]
            spectra[j] = spectrum
            real, imag = spectrum[:, :pp], spectrum[:, pp:]
            power = real * real + imag * imag
            bright[j * VIEWS : (j + 1) * VIEWS, :] = power.reshape(VIEWS, BIN, pp).sum(axis=1)
    exact = lax.Precision.HIGHEST
    own = lax.broadcasted_iota(jnp.int32, (VIEWS, pp), 0) == (
        lax.broadcasted_iota(jnp.int32, (VIEWS, pp), 1) % VIEWS
    )
    for c in range(C):
        target = get_views(plan, goals[c])
        for j in range(plan.own_cols):
            h = c * plan.own_cols + j
            below = (plan.hogel_cols + h) * VIEWS
            bright[below : below + VIEWS, :] = jnp.where(own, target[j : j + 1, :], 0.0)
    spread = jnp.dot(bright[...], same[...], preferred_element_type=F32, precision=exact)
    views = plan.hogel_cols * VIEWS
    light = spread[:views] * (1.0 / (BIN * BIN))
    factors[...] = 4.0 * (light - spread[views:])
    bright[:views, :] = light
    for c in range(C):
        rows = []
        for j in range(plan.own_cols):
            h = c * plan.own_cols + j
            block = jnp.where(own, bright[h * VIEWS : (h + 1) * VIEWS, :], 0.0)
            rows.append(jnp.sum(block, axis=0, keepdims=True))
        lights[c] = put_views(plan, jnp.concatenate(rows, axis=0))
    for start in range(0, plan.hogel_cols, group):
        for j in range(start, start + group):
            left = slice((j - start) * lanes, (j - start) * lanes + pp)
            right = slice((j - start) * lanes + pp, (j - start + 1) * lanes)
            for view in range(VIEWS):
                factor = factors[j * VIEWS + view : j * VIEWS + view + 1, :]
                block = slice(view * BIN, (view + 1) * BIN)
                below = slice(WIN + view * BIN, WIN + (view + 1) * BIN)
                real = (spectra[j, block, :pp] * factor).astype(BF16)
                imag = (spectra[j, block, pp:] * factor).astype(BF16)
                weighted[block, left] = real
                weighted[block, right] = imag
                weighted[below, left] = imag
                weighted[below, right] = -real
        result = matmul(col[...], weighted[...])
        for j in range(start, start + group):
            piece = result[:, (j - start) * lanes : (j - start + 1) * lanes]
            first = slice(STRIDE * j, STRIDE * (j + 1))
            back[first] = piece[:STRIDE] if j == 0 else pending + piece[:STRIDE]
            pending = piece[STRIDE:]
    back[:STRIDE] = back[:STRIDE] + pending

    def load(c, start, step):
        return back[c * X + start : c * X + start + step, :]

    def emit(d, block):
        out[d] = block.astype(BF16)

    lines_forward(plan, lanes, load, emit, weights_ahead, twist_ahead, packed)


def steer_table(plan):
    index = lax.axis_index(("cols", "rows"))
    shape = (plan.D, plan.f, 128)
    k = lax.broadcasted_iota(jnp.int32, shape, 0)
    line = lax.broadcasted_iota(jnp.int32, shape, 1)
    lane = lax.broadcasted_iota(jnp.int32, shape, 2)
    u = k + plan.D * (lane % plan.m)
    v = index // plan.R + plan.C * (
        plan.span * (index % plan.R) + plan.f * (lane // plan.m) + line
    )

    def freq(position, count):
        return ((position + count // 2) % count - count // 2).astype(F32) / count

    freq_rows, freq_cols = freq(u, plan.total_rows), freq(v, plan.total_cols)
    radial = freq_rows * freq_rows + freq_cols * freq_cols
    phase = (
        -2.0
        * math.pi
        * distance_px
        * radial
        / (jnp.sqrt(index_ratio * index_ratio - radial) + index_ratio)
    )
    return jnp.cos(phase), jnp.sin(phase)


def exchange(chunks):
    return lax.all_to_all(chunks, ("cols", "rows"), split_axis=0, concat_axis=0, tiled=True)


def swap_columns(chunks):
    count = lax.axis_size("cols")
    return tuple(
        lax.ppermute(chunk, "cols", [(i, i ^ t) for i in range(count)]) if t else chunk
        for t, chunk in zip(partners(count), chunks)
    )


def local(slm_field, target_light):
    rows_count, cols_count = lax.axis_size("rows"), lax.axis_size("cols")
    plan = Plan(rows_count, cols_count, slm_field.shape[1], slm_field.shape[2])
    C, D, X, lanes, f = plan.C, plan.D, plan.X, plan.lanes, plan.f
    span, wide = plan.span, 2 * plan.pp

    ahead, behind, twist = (jnp.asarray(t) for t in plan.pencil_tables())
    weights_ahead, twist_ahead = plan.line_tables(-1.0)
    weights_ahead, twist_ahead = jnp.asarray(weights_ahead[0]), jnp.asarray(twist_ahead)
    weights_behind, twist_behind = (jnp.asarray(t) for t in plan.line_tables(1.0))
    col, col_turned, row = hogel_tables()
    row = plan.row_table(row[0], row[1])
    col, col_turned, row, row_turned, same = (
        jnp.asarray(t) for t in (col, col_turned, row, row.T.copy(), plan.group_table())
    )
    steer_re, steer_im = steer_table(plan)

    slabs_shapes = (shape_of((X + VIEWS, lanes), BF16),) * C
    slabs_scratch = pltpu.VMEM((C, X + VIEWS, lanes), BF16)
    views_shape = shape_of((C, VIEWS, lanes), BF16)
    pencil_shape = shape_of((D, 2 * f, 128), BF16)
    lines_shape = shape_of((D, span, wide), BF16)
    columns_scratch = (
        pltpu.VMEM((D, f, 128), F32),
        pltpu.VMEM((D, f, 128), F32),
        pltpu.VMEM((D, f, 256), BF16),
    )
    pencil_tables = (steer_re, steer_im, ahead, behind, twist)
    columns_flops = 8 * D * f * 256 * 256 + 2 * plan.hogel_rows * span * (2 * WIN) ** 2

    apart_any = pl.BlockSpec(memory_space=pl.ANY)
    slabs = call(
        lambda *refs: pack_kernel(plan, *refs),
        slabs_shapes,
        (slm_field.astype(BF16), target_light),
        (slabs_scratch,),
    )
    tall = pltpu.VMEM((2 * X, C * lanes), BF16)
    pencils, goals = call(
        lambda *refs: rows_forward_kernel(plan, *refs),
        (pencil_shape, views_shape),
        (weights_ahead, twist_ahead, *swap_columns(slabs), steer_re, steer_im),
        (tall, slabs_scratch),
        flops=2 * X * 2 * X * C * lanes,
        in_specs={C + 2: apart_any, C + 3: apart_any},
    )
    (lines,) = call(
        lambda *refs: pencil_forward_kernel(plan, *refs),
        (lines_shape,),
        (exchange(pencils), *pencil_tables, row),
        (pltpu.VMEM((plan.hogel_rows, span, 2 * WIN), BF16), *columns_scratch),
        flops=columns_flops,
    )
    tall = pltpu.VMEM((2 * X, C * wide), BF16)
    lines, lights = call(
        lambda *refs: hogel_kernel(plan, *refs),
        (lines_shape, views_shape),
        (
            exchange(lines),
            goals,
            weights_behind,
            twist_behind,
            weights_ahead,
            twist_ahead,
            col,
            col_turned,
            same,
        ),
        (
            tall,
            pltpu.VMEM((2, plan.total_cols + STRIDE, wide), BF16),
            pltpu.VMEM((plan.hogel_cols, WIN, wide), F32),
            pltpu.VMEM((2 * plan.hogel_cols * VIEWS, plan.pp), F32),
            pltpu.VMEM((plan.hogel_cols * VIEWS, plan.pp), F32),
            pltpu.VMEM((2 * WIN, 512), BF16),
            pltpu.VMEM((plan.total_cols, wide), F32),
        ),
        flops=4 * X * 2 * X * C * wide + 4 * plan.hogel_cols * WIN * 2 * WIN * wide,
    )
    (pencils,) = call(
        lambda *refs: pencil_back_kernel(plan, *refs),
        (pencil_shape,),
        (exchange(lines), *pencil_tables, row_turned),
        (pltpu.VMEM((plan.hogel_rows, span, WIN), F32), *columns_scratch),
        flops=columns_flops,
    )
    tall = pltpu.VMEM((2 * X, C * lanes), BF16)
    slabs = call(
        lambda *refs: rows_inverse_kernel(plan, *refs),
        slabs_shapes,
        (exchange(pencils), lights, weights_behind, twist_behind),
        (tall, slabs_scratch),
        flops=2 * X * 2 * X * C * lanes,
    )
    return call(
        lambda *refs: unpack_kernel(plan, *refs),
        (shape_of(slm_field.shape, F32), shape_of(target_light.shape, F32)),
        swap_columns(slabs),
        (slabs_scratch,),
    )


def solution(mesh):
    return jax.shard_map(
        local,
        mesh=mesh,
        in_specs=(P(None, "rows", "cols"), P("rows", "cols", None)),
        out_specs=(P(None, "rows", "cols"), P("rows", "cols", None)),
        check_vma=False,
    )
```

```python
import math

import jax
import jax.numpy as jnp
import ml_dtypes
import numpy as np
from jax import lax
from jax.experimental import pallas as pl
from jax.experimental.pallas import tpu as pltpu
from jax.sharding import PartitionSpec as P

WIN = 256
VIEWS = 16
STRIDE = 128
BIN = 16

distance_px = 16000.0
index_ratio = 15.0

BF16 = jnp.bfloat16
F32 = jnp.float32
BOTH_MINOR = (((1,), (1,)), ((), ()))


def call(body, outs, args, scratch=(), flops=0, in_specs=None, out_specs=None, aliases=None):
    nbytes = sum(math.prod(a.shape) * a.dtype.itemsize for a in (*outs, *args))
    specs = {"input_output_aliases": aliases or {}}
    if in_specs:
        whole = pl.BlockSpec(memory_space=pltpu.VMEM)
        specs["in_specs"] = [in_specs.get(n, whole) for n in range(len(args))]
    if out_specs:
        specs["out_specs"] = out_specs
    return pl.pallas_call(
        body,
        out_shape=outs,
        scratch_shapes=list(scratch),
        compiler_params=pltpu.CompilerParams(vmem_limit_bytes=24 * 2**20),
        cost_estimate=pl.CostEstimate(flops=flops, bytes_accessed=nbytes, transcendentals=0),
        **specs,
    )(*args)


def shape_of(dims, dtype):
    return jax.ShapeDtypeStruct(dims, dtype)


def high_low(table):
    table = np.asarray(table, np.float32)
    high = table.astype(ml_dtypes.bfloat16)
    low = (table - high.astype(np.float32)).astype(ml_dtypes.bfloat16)
    return np.concatenate([high, low], axis=0)


def times_i(values):
    half = values.shape[-1] // 2
    if values.shape[-1] == 128:
        lanes = lax.broadcasted_iota(jnp.int32, values.shape, values.ndim - 1)
        turned = pltpu.roll(values, half, values.ndim - 1)
        return jnp.where(lanes < half, -turned, turned)
    return jnp.concatenate([-values[..., half:], values[..., :half]], axis=-1)


def rounded_with_i(value):
    rounded = value.astype(BF16)
    half = value.shape[-1] // 2
    if half % 128:
        return rounded, times_i(value.astype(F32)).astype(BF16)
    return rounded, jnp.concatenate([-rounded[:, half:], rounded[:, :half]], axis=1)


def small_dft(points, sign):
    count = len(points)
    if count == 1:
        return points
    even = small_dft(points[0::2], sign)
    odd = small_dft(points[1::2], sign)
    front, back = [], []
    for k in range(count // 2):
        re, im = odd[k]
        angle = sign * 2.0 * math.pi * k / count
        cosine, sine = math.cos(angle), math.sin(angle)
        if k == 0:
            pass
        elif 4 * k == count:
            re, im = (-im, re) if sign > 0 else (im, -re)
        elif 8 * k == count:
            re, im = cosine * (re - sign * im), cosine * (im + sign * re)
        elif 8 * k == 3 * count:
            re, im = cosine * (re + sign * im), cosine * (im - sign * re)
        else:
            re, im = re * cosine - im * sine, re * sine + im * cosine
        even_re, even_im = even[k]
        front.append((even_re + re, even_im + im))
        back.append((even_re - re, even_im - im))
    return front + back


def packed_dft(points, sign):
    count = len(points)
    if count == 1:
        return points
    even = packed_dft(points[0::2], sign)
    odd = packed_dft(points[1::2], sign)
    front, back = [], []
    for k in range(count // 2):
        term = odd[k]
        angle = sign * 2.0 * math.pi * k / count
        if 4 * k == count:
            term = times_i(term) if sign > 0 else -times_i(term)
        elif k:
            term = math.cos(angle) * term + math.sin(angle) * times_i(term)
        front.append(even[k] + term)
        back.append(even[k] - term)
    return front + back


def turn(rows, cols, period, sign):
    angles = sign * 2.0 * np.pi / period * ((np.arange(rows)[:, None] * np.arange(cols)) % period)
    return np.cos(angles), np.sin(angles)


def block_diagonal(block, copies):
    return np.kron(np.eye(copies), block)


class Plan:
    def __init__(self, rows_count, cols_count, rows_dev, cols_dev):
        self.R, self.C = rows_count, cols_count
        self.D = rows_count * cols_count
        self.X = cols_dev
        self.m = rows_dev // cols_count
        self.lanes = 2 * self.m
        self.P = 128 // self.m
        self.span = cols_dev // rows_count
        self.f = self.span // self.P
        self.total_rows = rows_dev * rows_count
        self.total_cols = cols_dev * cols_count
        self.outer = 8
        self.inner = self.D // 8
        self.shift = STRIDE // self.m
        self.hogel_rows = self.total_rows // STRIDE
        self.hogel_cols = self.total_cols // STRIDE
        self.parts = self.D // self.hogel_rows
        self.pp = WIN // self.parts
        self.views = VIEWS // self.parts
        self.own_cols = cols_dev // STRIDE

    def place(self, s):
        return s % self.C * self.R + s // self.C

    def line_tables(self, sign):
        cosine, sine = turn(self.X, self.X, self.X, sign)
        weights = high_low(np.concatenate([cosine, sine], axis=1)).reshape(2, self.X, 2 * self.X)
        twist = turn(self.X, self.C, self.total_cols, sign)
        return weights, np.concatenate(twist, axis=1).astype(np.float32)

    def pencil_tables(self):
        cosine, sine = turn(self.m, self.m, self.m, -1.0)
        cosine, sine = block_diagonal(cosine, self.P), block_diagonal(sine, self.P)
        ahead = np.block([[cosine, sine], [-sine, cosine]])
        behind = np.block([[cosine, -sine], [sine, cosine]]) / (self.total_rows * self.total_cols)
        twist = turn(self.D, self.m, self.total_rows, -1.0)
        twist = np.stack([np.tile(part, (1, self.P)) for part in twist]).astype(np.float32)
        return high_low(ahead), high_low(behind), twist

    def row_table(self, real, imag):
        blocks = []
        for slab in range(WIN // self.m):
            rows = slice(slab * self.m, (slab + 1) * self.m)
            for left, right in ((real[rows], imag[rows]), (-imag[rows], real[rows])):
                pieces = []
                for part in range(self.parts):
                    cols = slice(part * self.pp, (part + 1) * self.pp)
                    pieces += [left[:, cols], right[:, cols]]
                blocks.append(np.concatenate(pieces, axis=1))
        return np.concatenate(blocks, axis=0)

    def group_table(self):
        return np.kron(np.eye(self.views), np.ones((BIN, BIN))).astype(np.float32)


def hogel_tables():
    positions = np.arange(WIN)
    tapers = np.sin(np.pi * (positions + 0.5) / WIN) ** 2
    angles = -2.0 * np.pi / WIN * (positions[:, None] * positions[None, :] % WIN)
    cosine = (tapers[:, None] * np.cos(angles)).astype(np.float32)
    sine = (tapers[:, None] * np.sin(angles)).astype(np.float32)
    col = np.concatenate([cosine, sine], axis=1).astype(ml_dtypes.bfloat16)
    col_turned = np.concatenate([cosine.T, sine.T], axis=1).astype(ml_dtypes.bfloat16)
    row = np.stack([cosine / WIN, sine / WIN]).astype(ml_dtypes.bfloat16)
    return col, col_turned, row


def three_pieces(values):
    first = values.astype(BF16)
    rest = values - first.astype(F32)
    second = rest.astype(BF16)
    return first, second, (rest - second.astype(F32)).astype(BF16)


def matmul(left, right):
    return jnp.dot(left, right, preferred_element_type=F32)


def partners(count):
    return sorted(range(count), key=lambda t: (t != 0, -t.bit_count()))


def gather_chunks(arrived, chunks):
    mine = lax.axis_index("cols")
    for t, chunk in zip(partners(len(arrived)), arrived):
        chunks[mine ^ t] = chunk[...]


def scatter_chunks(chunks, leaving):
    mine = lax.axis_index("cols")
    for t, chunk in zip(partners(len(leaving)), leaving):
        chunk[...] = chunks[mine ^ t]


def put_views(plan, rows):
    pad = jnp.zeros((VIEWS - 3 * plan.own_cols, plan.lanes), F32)
    pieces = [piece.astype(F32) for piece in three_pieces(rows)]
    return jnp.concatenate([*pieces, pad], axis=0).astype(BF16)


def get_views(plan, chunk):
    chunk = chunk.astype(F32)
    n = plan.own_cols
    return chunk[:n] + chunk[n : 2 * n] + chunk[2 * n : 3 * n]


def pack_kernel(plan, field, goal, *refs):
    C, m, X = plan.C, plan.m, plan.X
    leaving, (out,) = refs[:C], refs[C:]
    for c in range(C):
        rows = slice(c * m, (c + 1) * m)
        block = jnp.concatenate([field[0, rows, :], field[1, rows, :]], axis=0)
        out[c, :X, :] = block.astype(F32).T.astype(BF16)
        i, start = c // plan.parts, c % plan.parts * plan.lanes
        out[c, X:, :] = put_views(plan, goal[i, :, start : start + plan.lanes])
    scatter_chunks(out, leaving)


def unpack_kernel(plan, t, *refs):
    m, X, C = plan.m, plan.X, plan.C
    c = lax.axis_index("cols") ^ t
    last = t == partners(C)[-1]
    if last:
        *rest, out, light, leaving, views, sems = refs
        chunks = rest[-C:]
    else:
        *rest, out, leaving, sems = refs
        chunks = rest[-1:]
    leaving[...] = chunks[-1][:X, :].astype(F32).T
    copies = [
        pltpu.make_async_copy(
            leaving.at[pl.ds(part * m, m), :],
            out.at[part, pl.ds(pl.multiple_of(c * m, m), m), :],
            sems.at[part],
        )
        for part in range(2)
    ]
    for copy in copies:
        copy.start()
    if last:
        gather_chunks([chunk.at[pl.ds(X, VIEWS), :] for chunk in chunks], views)
        for n in range(C):
            i, start = n // plan.parts, n % plan.parts * plan.lanes
            light[i, :, start : start + plan.lanes] = get_views(plan, views[n])
    for copy in copies:
        copy.wait()


def lines_forward(plan, lanes, load, emit, weights, twist, turned):
    C, X = plan.C, plan.X
    step = 64
    for start in range(0, X, step):
        points = packed_dft([load(c, start, step) for c in range(C)], -1.0)
        for k in range(C):
            cosine = twist[start : start + step, k : k + 1]
            sine = twist[start : start + step, C + k : C + k + 1]
            value = points[k]
            if lanes % 256:
                across = times_i(value)
                if k:
                    value, across = value * cosine + across * sine, across * cosine - value * sine
                value, across = value.astype(BF16), across.astype(BF16)
            else:
                if k:
                    value = value * cosine + times_i(value) * sine
                value, across = rounded_with_i(value)
            place = slice(k * lanes, k * lanes + lanes)
            turned[start : start + step, place] = value
            turned[X + start : X + start + step, place] = across
    group = max(1, 256 // lanes)
    for first in range(0, C, group):
        result = matmul(weights[...], turned[:, first * lanes : (first + group) * lanes])
        for k in range(group):
            for r in range(plan.R):
                rows = slice(r * plan.span, (r + 1) * plan.span)
                emit((first + k) * plan.R + r, result[rows, k * lanes : (k + 1) * lanes])


def lines_inverse(plan, lanes, product, emit, twist):
    C, X = plan.C, plan.X
    step = 64
    for start in range(0, X, step):
        rows = slice(start, start + step)
        result = product(rows)
        points = []
        for k in range(C):
            value = result[:, k * lanes : (k + 1) * lanes]
            if k:
                cosine, sine = twist[rows, k : k + 1], twist[rows, C + k : C + k + 1]
                value = value * cosine + times_i(value) * sine
            points.append(value)
        for c, value in enumerate(packed_dft(points, 1.0)):
            emit(c, start, step, value)


def to_planes(plan, block):
    parts = [block[p * plan.f : (p + 1) * plan.f, :] for p in range(plan.P)]
    real = jnp.concatenate([part[:, : plan.m] for part in parts], axis=1)
    imag = jnp.concatenate([part[:, plan.m :] for part in parts], axis=1)
    return real, imag


def from_planes(plan, real, imag):
    m = plan.m
    return jnp.concatenate(
        [
            jnp.concatenate([real[:, p * m : (p + 1) * m], imag[:, p * m : (p + 1) * m]], axis=1)
            for p in range(plan.P)
        ],
        axis=0,
    )


def rows_forward_kernel(plan, weights, twist, *refs):
    C, X = plan.C, plan.X
    arrived, (_, _, out, goals, turned, slabs) = refs[:C], refs[C:]
    gather_chunks(arrived, slabs)
    goals[...] = slabs[:, X:, :]

    def load(c, start, step):
        return slabs[c, start : start + step, :].astype(F32)

    def emit(d, block):
        out[d] = jnp.concatenate(to_planes(plan, block), axis=0).astype(BF16)

    lines_forward(plan, plan.lanes, load, emit, weights, twist, turned)


def rows_inverse_kernel(plan, pencils, lights, weights, twist, *refs):
    C, X, lanes = plan.C, plan.X, plan.lanes
    leaving, (packed, out) = refs[:C], refs[C:]
    for k in range(C):
        for r in range(plan.R):
            chunk = pencils[k * plan.R + r].astype(F32)
            block = from_planes(plan, chunk[: plan.f], chunk[plan.f :])
            place = slice(k * lanes, k * lanes + lanes)
            packed[r * plan.span : (r + 1) * plan.span, place] = block.astype(BF16)
            packed[X + r * plan.span : X + (r + 1) * plan.span, place] = times_i(block).astype(BF16)

    def emit(c, start, step, value):
        out[c, start : start + step, :] = value.astype(BF16)

    def product(rows):
        return matmul(weights[0, rows, :], packed[...]) + matmul(weights[1, rows, :], packed[...])

    lines_inverse(plan, lanes, product, emit, twist)
    out[:, X:, :] = lights[...]
    scatter_chunks(out, leaving)


def columns(plan, sign, load, store, steer_re, steer_im, ahead, behind, twist, scratch):
    D, f, outer, inner = plan.D, plan.f, plan.outer, plan.inner
    half_re, half_im, rounded = scratch
    for b in range(inner):
        points = [load(inner * a + b) for a in range(outer)]
        for alpha, (re, im) in enumerate(small_dft(points, -1.0)):
            angle = -2.0 * math.pi * b * alpha / D
            cosine, sine = math.cos(angle), math.sin(angle)
            if b * alpha:
                re, im = re * cosine - im * sine, re * sine + im * cosine
            half_re[alpha * inner + b] = re
            half_im[alpha * inner + b] = im
    for alpha in range(outer):
        points = [(half_re[alpha * inner + b], half_im[alpha * inner + b]) for b in range(inner)]
        for beta, (re, im) in enumerate(small_dft(points, -1.0)):
            k = alpha + outer * beta
            cosine, sine = twist[0, k : k + 1, :], twist[1, k : k + 1, :]
            for offset, part in ((0, re * cosine - im * sine), (128, re * sine + im * cosine)):
                rounded[k, :, offset : offset + 128] = part.astype(BF16)
    group = D // 4 if sign > 0 else D // 2
    for start in range(0, D, group):
        place = slice(start, start + group)

        def multiply(matrix):
            left = rounded[place].reshape(group * f, 256)
            product = matmul(left, matrix[:256, :]) + matmul(left, matrix[256:, :])
            return product.reshape(group, f, 256)

        result = multiply(ahead)
        re, im = result[:, :, :128], result[:, :, 128:]
        factor_re, factor_im = steer_re[place], sign * steer_im[place]
        for offset, part in (
            (0, re * factor_re - im * factor_im),
            (128, re * factor_im + im * factor_re),
        ):
            rounded[place, :, offset : offset + 128] = part.astype(BF16)
        result = multiply(behind)
        half_re[place] = result[:, :, :128]
        half_im[place] = result[:, :, 128:]
    for alpha in range(outer):
        points = []
        for beta in range(inner):
            k = alpha + outer * beta
            cosine, sine = twist[0, k : k + 1, :], twist[1, k : k + 1, :]
            re, im = half_re[k], half_im[k]
            points.append((re * cosine + im * sine, im * cosine - re * sine))
        for b, (re, im) in enumerate(small_dft(points, 1.0)):
            angle = 2.0 * math.pi * b * alpha / D
            cosine, sine = math.cos(angle), math.sin(angle)
            if b * alpha:
                re, im = re * cosine - im * sine, re * sine + im * cosine
            half_re[alpha + outer * b] = re
            half_im[alpha + outer * b] = im
    for b in range(inner):
        points = [(half_re[alpha + outer * b], half_im[alpha + outer * b]) for alpha in range(outer)]
        for a, (re, im) in enumerate(small_dft(points, 1.0)):
            store(inner * a + b, re, im)


def pencil_forward_kernel(plan, pencils, *refs):
    steer_re, steer_im, ahead, behind, twist, row, out, windows, *scratch = refs
    f, lanes, span = plan.f, plan.lanes, plan.span

    def load(s):
        chunk = pencils[plan.place(s)].astype(F32)
        return chunk[:f], chunk[f:]

    def store(s, re, im):
        block = from_planes(plan, re, im).astype(BF16)
        i, slab = s // plan.shift, s % plan.shift
        windows[i, :, slab * lanes : (slab + 1) * lanes] = block
        slab += plan.shift
        windows[(i - 1) % plan.hogel_rows, :, slab * lanes : (slab + 1) * lanes] = block

    columns(plan, 1.0, load, store, steer_re, steer_im, ahead, behind, twist, scratch)
    count = plan.hogel_rows
    result = matmul(windows[...].reshape(count * span, 2 * WIN), row[...]).astype(BF16)
    for i in range(count):
        for part in range(plan.parts):
            out[plan.place(i * plan.parts + part)] = result[
                i * span : (i + 1) * span, part * 2 * plan.pp : (part + 1) * 2 * plan.pp
            ]


def pencil_back_kernel(plan, lines, *refs):
    steer_re, steer_im, ahead, behind, twist, row, out, windows, *scratch = refs
    lanes, span, parts = plan.lanes, plan.span, plan.parts
    count, wide = plan.hogel_rows, 2 * plan.pp
    result = 0.0
    for n in range(parts):
        own = jnp.stack([lines[plan.place(i * parts + n)] for i in range(count)])
        before = jnp.concatenate([own[-1:], own[:-1]], axis=0)
        depth = slice(n * wide, (n + 1) * wide)
        result = result + matmul(own.reshape(count * span, wide), row[depth, :WIN])
        result = result + matmul(before.reshape(count * span, wide), row[depth, WIN:])
    windows[...] = result.reshape(count, span, WIN)

    def load(s):
        i, slab = s // plan.shift, s % plan.shift
        return to_planes(plan, windows[i, :, slab * lanes : (slab + 1) * lanes])

    def store(s, re, im):
        out[plan.place(s)] = jnp.concatenate([re, im], axis=0).astype(BF16)

    columns(plan, -1.0, load, store, steer_re, steer_im, ahead, behind, twist, scratch)


def hogel_kernel(plan, lines, goals, *refs):
    weights_behind, twist_behind, weights_ahead, twist_ahead, col, col_turned, same = refs[:7]
    out, lights, packed, field, spectra, bright, factors, weighted, back = refs[7:]
    C, X, lanes, pp = plan.C, plan.X, 2 * plan.pp, plan.pp
    total = plan.total_cols
    for k in range(C):
        block = lines[k * plan.R : (k + 1) * plan.R].reshape(X, lanes)
        place = slice(k * lanes, (k + 1) * lanes)
        packed[:X, place], packed[X:, place] = rounded_with_i(block)

    def emit_near(c, start, step, value):
        for n, rounded in enumerate(rounded_with_i(value)):
            field[n, c * X + start : c * X + start + step, :] = rounded
            if c == 0 and start < STRIDE:
                field[n, total + start : total + start + step, :] = rounded

    near = matmul(weights_behind[0], packed[...])
    lines_inverse(plan, lanes, lambda rows: near[rows, :], emit_near, twist_behind)
    for j in range(plan.hogel_cols):
        window = slice(STRIDE * j, STRIDE * j + WIN)
        result = matmul(
            col_turned[...], jnp.concatenate([field[0, window, :], field[1, window, :]], axis=0)
        )
        spectra[j] = result
        power = result[:, :pp] * result[:, :pp] + result[:, pp:] * result[:, pp:]
        bright[j * VIEWS : (j + 1) * VIEWS, :] = power.reshape(VIEWS, BIN, pp).sum(axis=1)
    exact = lax.Precision.HIGHEST
    own = lax.broadcasted_iota(jnp.int32, (VIEWS, pp), 0) == (
        lax.broadcasted_iota(jnp.int32, (VIEWS, pp), 1) % VIEWS
    )
    for c in range(C):
        target = get_views(plan, goals[c])
        for j in range(plan.own_cols):
            h = c * plan.own_cols + j
            below = (plan.hogel_cols + h) * VIEWS
            bright[below : below + VIEWS, :] = jnp.where(own, target[j : j + 1, :], 0.0)
    spread = jnp.dot(bright[...], same[...], preferred_element_type=F32, precision=exact)
    views = plan.hogel_cols * VIEWS
    light = spread[:views] * (1.0 / (BIN * BIN))
    factors[...] = 4.0 * (light - spread[views:])
    bright[:views, :] = light
    for c in range(C):
        rows = []
        for j in range(plan.own_cols):
            h = c * plan.own_cols + j
            block = jnp.where(own, bright[h * VIEWS : (h + 1) * VIEWS, :], 0.0)
            rows.append(jnp.sum(block, axis=0, keepdims=True))
        lights[c] = put_views(plan, jnp.concatenate(rows, axis=0))
    for j in range(plan.hogel_cols):
        for view in range(VIEWS):
            factor = factors[j * VIEWS + view : j * VIEWS + view + 1, :]
            block = slice(view * BIN, (view + 1) * BIN)
            below = slice(WIN + view * BIN, WIN + (view + 1) * BIN)
            real = (spectra[j, block, :pp] * factor).astype(BF16)
            imag = (spectra[j, block, pp:] * factor).astype(BF16)
            weighted[block, :pp] = real
            weighted[block, pp:] = imag
            weighted[below, :pp] = imag
            weighted[below, pp:] = -real
        result = matmul(col[...], weighted[...])
        first = slice(STRIDE * j, STRIDE * (j + 1))
        back[first] = result[:STRIDE] if j == 0 else pending + result[:STRIDE]
        pending = result[STRIDE:]
    back[:STRIDE] = back[:STRIDE] + pending

    def load(c, start, step):
        return back[c * X + start : c * X + start + step, :]

    def emit(d, block):
        out[d] = block.astype(BF16)

    lines_forward(plan, lanes, load, emit, weights_ahead, twist_ahead, packed)


def steer_table(plan):
    index = lax.axis_index(("cols", "rows"))
    shape = (plan.D, plan.f, 128)
    k = lax.broadcasted_iota(jnp.int32, shape, 0)
    line = lax.broadcasted_iota(jnp.int32, shape, 1)
    lane = lax.broadcasted_iota(jnp.int32, shape, 2)
    u = k + plan.D * (lane % plan.m)
    v = index // plan.R + plan.C * (
        plan.span * (index % plan.R) + plan.f * (lane // plan.m) + line
    )

    def freq(position, count):
        return ((position + count // 2) % count - count // 2).astype(F32) / count

    freq_rows, freq_cols = freq(u, plan.total_rows), freq(v, plan.total_cols)
    radial = freq_rows * freq_rows + freq_cols * freq_cols
    phase = (
        -2.0
        * math.pi
        * distance_px
        * radial
        / (jnp.sqrt(index_ratio * index_ratio - radial) + index_ratio)
    )
    return jnp.cos(phase), jnp.sin(phase)


def exchange(chunks):
    return lax.all_to_all(chunks, ("cols", "rows"), split_axis=0, concat_axis=0, tiled=True)


def swap_columns(chunks):
    count = lax.axis_size("cols")
    return tuple(
        lax.ppermute(chunk, "cols", [(i, i ^ t) for i in range(count)]) if t else chunk
        for t, chunk in zip(partners(count), chunks)
    )


def local(slm_field, target_light):
    rows_count, cols_count = lax.axis_size("rows"), lax.axis_size("cols")
    plan = Plan(rows_count, cols_count, slm_field.shape[1], slm_field.shape[2])
    C, D, X, lanes, f = plan.C, plan.D, plan.X, plan.lanes, plan.f
    span, wide = plan.span, 2 * plan.pp

    ahead, behind, twist = (jnp.asarray(t) for t in plan.pencil_tables())
    weights_ahead, twist_ahead = plan.line_tables(-1.0)
    weights_ahead, twist_ahead = jnp.asarray(weights_ahead[0]), jnp.asarray(twist_ahead)
    weights_behind, twist_behind = (jnp.asarray(t) for t in plan.line_tables(1.0))
    col, col_turned, row = hogel_tables()
    row = plan.row_table(row[0], row[1])
    col, col_turned, row, row_turned, same = (
        jnp.asarray(t) for t in (col, col_turned, row, row.T.copy(), plan.group_table())
    )
    steer_re, steer_im = steer_table(plan)

    slabs_shapes = (shape_of((X + VIEWS, lanes), BF16),) * C
    slabs_scratch = pltpu.VMEM((C, X + VIEWS, lanes), BF16)
    views_shape = shape_of((C, VIEWS, lanes), BF16)
    pencil_shape = shape_of((D, 2 * f, 128), BF16)
    lines_shape = shape_of((D, span, wide), BF16)
    columns_scratch = (
        pltpu.VMEM((D, f, 128), F32),
        pltpu.VMEM((D, f, 128), F32),
        pltpu.VMEM((D, f, 256), BF16),
    )
    pencil_tables = (steer_re, steer_im, ahead, behind, twist)
    columns_flops = 8 * D * f * 256 * 256 + 2 * plan.hogel_rows * span * (2 * WIN) ** 2

    apart_any = pl.BlockSpec(memory_space=pl.ANY)
    slabs = call(
        lambda *refs: pack_kernel(plan, *refs),
        slabs_shapes,
        (slm_field.astype(BF16), target_light),
        (slabs_scratch,),
    )
    tall = pltpu.VMEM((2 * X, C * lanes), BF16)
    pencils, goals = call(
        lambda *refs: rows_forward_kernel(plan, *refs),
        (pencil_shape, views_shape),
        (weights_ahead, twist_ahead, *swap_columns(slabs), steer_re, steer_im),
        (tall, slabs_scratch),
        flops=2 * X * 2 * X * C * lanes,
        in_specs={C + 2: apart_any, C + 3: apart_any},
    )
    (lines,) = call(
        lambda *refs: pencil_forward_kernel(plan, *refs),
        (lines_shape,),
        (exchange(pencils), *pencil_tables, row),
        (pltpu.VMEM((plan.hogel_rows, span, 2 * WIN), BF16), *columns_scratch),
        flops=columns_flops,
    )
    tall = pltpu.VMEM((2 * X, C * wide), BF16)
    lines, lights = call(
        lambda *refs: hogel_kernel(plan, *refs),
        (lines_shape, views_shape),
        (
            exchange(lines),
            goals,
            weights_behind,
            twist_behind,
            weights_ahead,
            twist_ahead,
            col,
            col_turned,
            same,
        ),
        (
            tall,
            pltpu.VMEM((2, plan.total_cols + STRIDE, wide), BF16),
            pltpu.VMEM((plan.hogel_cols, WIN, wide), F32),
            pltpu.VMEM((2 * plan.hogel_cols * VIEWS, plan.pp), F32),
            pltpu.VMEM((plan.hogel_cols * VIEWS, plan.pp), F32),
            pltpu.VMEM((2 * WIN, wide), BF16),
            pltpu.VMEM((plan.total_cols, wide), F32),
        ),
        flops=4 * X * 2 * X * C * wide + 4 * plan.hogel_cols * WIN * 2 * WIN * wide,
    )
    (pencils,) = call(
        lambda *refs: pencil_back_kernel(plan, *refs),
        (pencil_shape,),
        (exchange(lines), *pencil_tables, row_turned),
        (pltpu.VMEM((plan.hogel_rows, span, WIN), F32), *columns_scratch),
        flops=columns_flops,
    )
    tall = pltpu.VMEM((2 * X, C * lanes), BF16)
    slabs = call(
        lambda *refs: rows_inverse_kernel(plan, *refs),
        slabs_shapes,
        (exchange(pencils), lights, weights_behind, twist_behind),
        (tall, slabs_scratch),
        flops=2 * X * 2 * X * C * lanes,
    )
    slabs = swap_columns(slabs)
    gradient = None
    apart = pl.BlockSpec(memory_space=pltpu.HBM)
    for n, t in enumerate(partners(C)):
        before = () if gradient is None else (gradient,)
        last = n == C - 1
        views_shapes = (shape_of(target_light.shape, F32),) if last else ()
        views_scratch = (pltpu.VMEM((C, VIEWS, lanes), BF16),) if last else ()
        gradient, *light_field = call(
            lambda *refs, t=t: unpack_kernel(plan, t, *refs),
            (shape_of(slm_field.shape, F32), *views_shapes),
            (*before, *(slabs if last else slabs[n : n + 1])),
            (pltpu.VMEM((lanes, X), F32), *views_scratch, pltpu.SemaphoreType.DMA((2,))),
            in_specs={0: apart} if before else None,
            out_specs=(apart, pl.BlockSpec(memory_space=pltpu.VMEM))[: 1 + last],
            aliases={0: 0} if before else {},
        )
    return gradient, light_field[0]


def solution(mesh):
    return jax.shard_map(
        local,
        mesh=mesh,
        in_specs=(P(None, "rows", "cols"), P("rows", "cols", None)),
        out_specs=(P(None, "rows", "cols"), P("rows", "cols", None)),
        check_vma=False,
    )
```

```python
import math

import jax
import jax.numpy as jnp
import ml_dtypes
import numpy as np
from jax import lax
from jax.experimental import pallas as pl
from jax.experimental.pallas import tpu as pltpu
from jax.sharding import PartitionSpec as P

WIN = 256
VIEWS = 16
STRIDE = 128
BIN = 16

distance_px = 16000.0
index_ratio = 15.0

BF16 = jnp.bfloat16
F32 = jnp.float32
BOTH_MINOR = (((1,), (1,)), ((), ()))


def call(body, outs, args, scratch=(), flops=0, in_specs=None, out_specs=None):
    nbytes = sum(math.prod(a.shape) * a.dtype.itemsize for a in (*outs, *args))
    specs = {}
    if in_specs:
        whole = pl.BlockSpec(memory_space=pltpu.VMEM)
        specs["in_specs"] = [in_specs.get(n, whole) for n in range(len(args))]
    if out_specs:
        specs["out_specs"] = out_specs
    return pl.pallas_call(
        body,
        out_shape=outs,
        scratch_shapes=list(scratch),
        compiler_params=pltpu.CompilerParams(vmem_limit_bytes=24 * 2**20),
        cost_estimate=pl.CostEstimate(flops=flops, bytes_accessed=nbytes, transcendentals=0),
        **specs,
    )(*args)


def shape_of(dims, dtype):
    return jax.ShapeDtypeStruct(dims, dtype)


def high_low(table):
    table = np.asarray(table, np.float32)
    high = table.astype(ml_dtypes.bfloat16)
    low = (table - high.astype(np.float32)).astype(ml_dtypes.bfloat16)
    return np.concatenate([high, low], axis=0)


def times_i(values):
    half = values.shape[-1] // 2
    if values.shape[-1] == 128:
        lanes = lax.broadcasted_iota(jnp.int32, values.shape, values.ndim - 1)
        turned = pltpu.roll(values, half, values.ndim - 1)
        return jnp.where(lanes < half, -turned, turned)
    return jnp.concatenate([-values[..., half:], values[..., :half]], axis=-1)


def rounded_with_i(value):
    rounded = value.astype(BF16)
    half = value.shape[-1] // 2
    if half % 128:
        return rounded, times_i(value.astype(F32)).astype(BF16)
    return rounded, jnp.concatenate([-rounded[:, half:], rounded[:, :half]], axis=1)


def small_dft(points, sign):
    count = len(points)
    if count == 1:
        return points
    even = small_dft(points[0::2], sign)
    odd = small_dft(points[1::2], sign)
    front, back = [], []
    for k in range(count // 2):
        re, im = odd[k]
        angle = sign * 2.0 * math.pi * k / count
        cosine, sine = math.cos(angle), math.sin(angle)
        if k == 0:
            pass
        elif 4 * k == count:
            re, im = (-im, re) if sign > 0 else (im, -re)
        elif 8 * k == count:
            re, im = cosine * (re - sign * im), cosine * (im + sign * re)
        elif 8 * k == 3 * count:
            re, im = cosine * (re + sign * im), cosine * (im - sign * re)
        else:
            re, im = re * cosine - im * sine, re * sine + im * cosine
        even_re, even_im = even[k]
        front.append((even_re + re, even_im + im))
        back.append((even_re - re, even_im - im))
    return front + back


def packed_dft(points, sign):
    count = len(points)
    if count == 1:
        return points
    even = packed_dft(points[0::2], sign)
    odd = packed_dft(points[1::2], sign)
    front, back = [], []
    for k in range(count // 2):
        term = odd[k]
        angle = sign * 2.0 * math.pi * k / count
        if 4 * k == count:
            term = times_i(term) if sign > 0 else -times_i(term)
        elif k:
            term = math.cos(angle) * term + math.sin(angle) * times_i(term)
        front.append(even[k] + term)
        back.append(even[k] - term)
    return front + back


def turn(rows, cols, period, sign):
    angles = sign * 2.0 * np.pi / period * ((np.arange(rows)[:, None] * np.arange(cols)) % period)
    return np.cos(angles), np.sin(angles)


def block_diagonal(block, copies):
    return np.kron(np.eye(copies), block)


class Plan:
    def __init__(self, rows_count, cols_count, rows_dev, cols_dev):
        self.R, self.C = rows_count, cols_count
        self.D = rows_count * cols_count
        self.X = cols_dev
        self.m = rows_dev // cols_count
        self.lanes = 2 * self.m
        self.P = 128 // self.m
        self.span = cols_dev // rows_count
        self.f = self.span // self.P
        self.total_rows = rows_dev * rows_count
        self.total_cols = cols_dev * cols_count
        self.outer = 8
        self.inner = self.D // 8
        self.shift = STRIDE // self.m
        self.hogel_rows = self.total_rows // STRIDE
        self.hogel_cols = self.total_cols // STRIDE
        self.parts = self.D // self.hogel_rows
        self.pp = WIN // self.parts
        self.views = VIEWS // self.parts
        self.own_cols = cols_dev // STRIDE

    def place(self, s):
        return s % self.C * self.R + s // self.C

    def line_tables(self, sign):
        cosine, sine = turn(self.X, self.X, self.X, sign)
        weights = high_low(np.concatenate([cosine, sine], axis=1)).reshape(2, self.X, 2 * self.X)
        twist = turn(self.X, self.C, self.total_cols, sign)
        return weights, np.concatenate(twist, axis=1).astype(np.float32)

    def pencil_tables(self):
        cosine, sine = turn(self.m, self.m, self.m, -1.0)
        cosine, sine = block_diagonal(cosine, self.P), block_diagonal(sine, self.P)
        ahead = np.block([[cosine, sine], [-sine, cosine]])
        behind = np.block([[cosine, -sine], [sine, cosine]]) / (self.total_rows * self.total_cols)
        twist = turn(self.D, self.m, self.total_rows, -1.0)
        twist = np.stack([np.tile(part, (1, self.P)) for part in twist]).astype(np.float32)
        return high_low(ahead), high_low(behind), twist

    def row_table(self, real, imag):
        blocks = []
        for slab in range(WIN // self.m):
            rows = slice(slab * self.m, (slab + 1) * self.m)
            for left, right in ((real[rows], imag[rows]), (-imag[rows], real[rows])):
                pieces = []
                for part in range(self.parts):
                    cols = slice(part * self.pp, (part + 1) * self.pp)
                    pieces += [left[:, cols], right[:, cols]]
                blocks.append(np.concatenate(pieces, axis=1))
        return np.concatenate(blocks, axis=0)

    def group_table(self):
        return np.kron(np.eye(self.views), np.ones((BIN, BIN))).astype(np.float32)


def hogel_tables():
    positions = np.arange(WIN)
    tapers = np.sin(np.pi * (positions + 0.5) / WIN) ** 2
    angles = -2.0 * np.pi / WIN * (positions[:, None] * positions[None, :] % WIN)
    cosine = (tapers[:, None] * np.cos(angles)).astype(np.float32)
    sine = (tapers[:, None] * np.sin(angles)).astype(np.float32)
    col = np.concatenate([cosine, sine], axis=1).astype(ml_dtypes.bfloat16)
    col_turned = np.concatenate([cosine.T, sine.T], axis=1).astype(ml_dtypes.bfloat16)
    row = np.stack([cosine / WIN, sine / WIN]).astype(ml_dtypes.bfloat16)
    return col, col_turned, row


def three_pieces(values):
    first = values.astype(BF16)
    rest = values - first.astype(F32)
    second = rest.astype(BF16)
    return first, second, (rest - second.astype(F32)).astype(BF16)


def matmul(left, right):
    return jnp.dot(left, right, preferred_element_type=F32)


def partners(count):
    return sorted(range(count), key=lambda t: (t != 0, -t.bit_count()))


def gather_chunks(arrived, chunks):
    mine = lax.axis_index("cols")
    for t, chunk in zip(partners(len(arrived)), arrived):
        chunks[mine ^ t] = chunk[...]


def scatter_chunks(chunks, leaving):
    mine = lax.axis_index("cols")
    for t, chunk in zip(partners(len(leaving)), leaving):
        chunk[...] = chunks[mine ^ t]


def put_views(plan, rows):
    pad = jnp.zeros((VIEWS - 3 * plan.own_cols, plan.lanes), F32)
    pieces = [piece.astype(F32) for piece in three_pieces(rows)]
    return jnp.concatenate([*pieces, pad], axis=0).astype(BF16)


def get_views(plan, chunk):
    chunk = chunk.astype(F32)
    n = plan.own_cols
    return chunk[:n] + chunk[n : 2 * n] + chunk[2 * n : 3 * n]


def pack_kernel(plan, field, goal, *refs):
    C, m, X = plan.C, plan.m, plan.X
    leaving, (out,) = refs[:C], refs[C:]
    for c in range(C):
        rows = slice(c * m, (c + 1) * m)
        block = jnp.concatenate([field[0, rows, :], field[1, rows, :]], axis=0)
        out[c, :X, :] = block.astype(F32).T.astype(BF16)
        i, start = c // plan.parts, c % plan.parts * plan.lanes
        out[c, X:, :] = put_views(plan, goal[i, :, start : start + plan.lanes])
    scatter_chunks(out, leaving)


def unpack_kernel(plan, *refs):
    C, m, X = plan.C, plan.m, plan.X
    arrived, (out, light, slabs) = refs[:C], refs[C:]
    gather_chunks(arrived, slabs)
    for c in range(C):
        block = slabs[c, :X, :].astype(F32).T
        out[0, m * c : m * c + m, :] = block[:m]
        out[1, m * c : m * c + m, :] = block[m:]
        i, start = c // plan.parts, c % plan.parts * plan.lanes
        light[i, :, start : start + plan.lanes] = get_views(plan, slabs[c, X:, :])


def lines_forward(plan, lanes, load, emit, weights, twist, turned):
    C, X = plan.C, plan.X
    step = 64
    for start in range(0, X, step):
        points = packed_dft([load(c, start, step) for c in range(C)], -1.0)
        for k in range(C):
            cosine = twist[start : start + step, k : k + 1]
            sine = twist[start : start + step, C + k : C + k + 1]
            value = points[k]
            if lanes % 256:
                across = times_i(value)
                if k:
                    value, across = value * cosine + across * sine, across * cosine - value * sine
                value, across = value.astype(BF16), across.astype(BF16)
            else:
                if k:
                    value = value * cosine + times_i(value) * sine
                value, across = rounded_with_i(value)
            place = slice(k * lanes, k * lanes + lanes)
            turned[start : start + step, place] = value
            turned[X + start : X + start + step, place] = across
    group = max(1, 256 // lanes)
    for first in range(0, C, group):
        result = matmul(weights[...], turned[:, first * lanes : (first + group) * lanes])
        for k in range(group):
            for r in range(plan.R):
                rows = slice(r * plan.span, (r + 1) * plan.span)
                emit((first + k) * plan.R + r, result[rows, k * lanes : (k + 1) * lanes])


def lines_inverse(plan, lanes, product, emit, twist):
    C, X = plan.C, plan.X
    step = 64
    for start in range(0, X, step):
        rows = slice(start, start + step)
        result = product(rows)
        points = []
        for k in range(C):
            value = result[:, k * lanes : (k + 1) * lanes]
            if k:
                cosine, sine = twist[rows, k : k + 1], twist[rows, C + k : C + k + 1]
                value = value * cosine + times_i(value) * sine
            points.append(value)
        for c, value in enumerate(packed_dft(points, 1.0)):
            emit(c, start, step, value)


def to_planes(plan, block):
    parts = [block[p * plan.f : (p + 1) * plan.f, :] for p in range(plan.P)]
    real = jnp.concatenate([part[:, : plan.m] for part in parts], axis=1)
    imag = jnp.concatenate([part[:, plan.m :] for part in parts], axis=1)
    return real, imag


def from_planes(plan, real, imag):
    m = plan.m
    return jnp.concatenate(
        [
            jnp.concatenate([real[:, p * m : (p + 1) * m], imag[:, p * m : (p + 1) * m]], axis=1)
            for p in range(plan.P)
        ],
        axis=0,
    )


def rows_forward_kernel(plan, weights, twist, *refs):
    C, X = plan.C, plan.X
    arrived, (_, _, out, goals, turned, slabs) = refs[:C], refs[C:]
    gather_chunks(arrived, slabs)
    goals[...] = slabs[:, X:, :]

    def load(c, start, step):
        return slabs[c, start : start + step, :].astype(F32)

    def emit(d, block):
        out[d] = jnp.concatenate(to_planes(plan, block), axis=0).astype(BF16)

    lines_forward(plan, plan.lanes, load, emit, weights, twist, turned)


def rows_inverse_kernel(plan, pencils, lights, weights, twist, *refs):
    C, X, lanes = plan.C, plan.X, plan.lanes
    leaving, (packed, out) = refs[:C], refs[C:]
    for k in range(C):
        for r in range(plan.R):
            chunk = pencils[k * plan.R + r].astype(F32)
            block = from_planes(plan, chunk[: plan.f], chunk[plan.f :])
            place = slice(k * lanes, k * lanes + lanes)
            packed[r * plan.span : (r + 1) * plan.span, place] = block.astype(BF16)
            packed[X + r * plan.span : X + (r + 1) * plan.span, place] = times_i(block).astype(BF16)

    def emit(c, start, step, value):
        out[c, start : start + step, :] = value.astype(BF16)

    def product(rows):
        return matmul(weights[0, rows, :], packed[...]) + matmul(weights[1, rows, :], packed[...])

    lines_inverse(plan, lanes, product, emit, twist)
    out[:, X:, :] = lights[...]
    scatter_chunks(out, leaving)


def columns(plan, sign, load, store, steer_re, steer_im, ahead, behind, twist, scratch):
    D, f, outer, inner = plan.D, plan.f, plan.outer, plan.inner
    half_re, half_im, rounded = scratch
    for b in range(inner):
        points = [load(inner * a + b) for a in range(outer)]
        for alpha, (re, im) in enumerate(small_dft(points, -1.0)):
            angle = -2.0 * math.pi * b * alpha / D
            cosine, sine = math.cos(angle), math.sin(angle)
            if b * alpha:
                re, im = re * cosine - im * sine, re * sine + im * cosine
            half_re[alpha * inner + b] = re
            half_im[alpha * inner + b] = im
    for alpha in range(outer):
        points = [(half_re[alpha * inner + b], half_im[alpha * inner + b]) for b in range(inner)]
        for beta, (re, im) in enumerate(small_dft(points, -1.0)):
            k = alpha + outer * beta
            cosine, sine = twist[0, k : k + 1, :], twist[1, k : k + 1, :]
            for offset, part in ((0, re * cosine - im * sine), (128, re * sine + im * cosine)):
                rounded[k, :, offset : offset + 128] = part.astype(BF16)
    group = D // 4 if sign > 0 else D // 2
    for start in range(0, D, group):
        place = slice(start, start + group)

        def multiply(matrix):
            left = rounded[place].reshape(group * f, 256)
            product = matmul(left, matrix[:256, :]) + matmul(left, matrix[256:, :])
            return product.reshape(group, f, 256)

        result = multiply(ahead)
        re, im = result[:, :, :128], result[:, :, 128:]
        factor_re, factor_im = steer_re[place], sign * steer_im[place]
        for offset, part in (
            (0, re * factor_re - im * factor_im),
            (128, re * factor_im + im * factor_re),
        ):
            rounded[place, :, offset : offset + 128] = part.astype(BF16)
        result = multiply(behind)
        half_re[place] = result[:, :, :128]
        half_im[place] = result[:, :, 128:]
    for alpha in range(outer):
        points = []
        for beta in range(inner):
            k = alpha + outer * beta
            cosine, sine = twist[0, k : k + 1, :], twist[1, k : k + 1, :]
            re, im = half_re[k], half_im[k]
            points.append((re * cosine + im * sine, im * cosine - re * sine))
        for b, (re, im) in enumerate(small_dft(points, 1.0)):
            angle = 2.0 * math.pi * b * alpha / D
            cosine, sine = math.cos(angle), math.sin(angle)
            if b * alpha:
                re, im = re * cosine - im * sine, re * sine + im * cosine
            half_re[alpha + outer * b] = re
            half_im[alpha + outer * b] = im
    for b in range(inner):
        points = [(half_re[alpha + outer * b], half_im[alpha + outer * b]) for alpha in range(outer)]
        for a, (re, im) in enumerate(small_dft(points, 1.0)):
            store(inner * a + b, re, im)


def pencil_forward_kernel(plan, pencils, *refs):
    steer_re, steer_im, ahead, behind, twist, row, out, windows, *scratch = refs
    f, lanes, span = plan.f, plan.lanes, plan.span

    def load(s):
        chunk = pencils[plan.place(s)].astype(F32)
        return chunk[:f], chunk[f:]

    def store(s, re, im):
        block = from_planes(plan, re, im).astype(BF16)
        i, slab = s // plan.shift, s % plan.shift
        windows[i, :, slab * lanes : (slab + 1) * lanes] = block
        slab += plan.shift
        windows[(i - 1) % plan.hogel_rows, :, slab * lanes : (slab + 1) * lanes] = block

    columns(plan, 1.0, load, store, steer_re, steer_im, ahead, behind, twist, scratch)
    count = plan.hogel_rows
    result = matmul(windows[...].reshape(count * span, 2 * WIN), row[...]).astype(BF16)
    for i in range(count):
        for part in range(plan.parts):
            out[plan.place(i * plan.parts + part)] = result[
                i * span : (i + 1) * span, part * 2 * plan.pp : (part + 1) * 2 * plan.pp
            ]


def pencil_back_kernel(plan, lines, *refs):
    steer_re, steer_im, ahead, behind, twist, row, out, windows, *scratch = refs
    lanes, span, parts = plan.lanes, plan.span, plan.parts
    count, wide = plan.hogel_rows, 2 * plan.pp
    result = 0.0
    for n in range(parts):
        own = jnp.stack([lines[plan.place(i * parts + n)] for i in range(count)])
        before = jnp.concatenate([own[-1:], own[:-1]], axis=0)
        depth = slice(n * wide, (n + 1) * wide)
        result = result + matmul(own.reshape(count * span, wide), row[depth, :WIN])
        result = result + matmul(before.reshape(count * span, wide), row[depth, WIN:])
    windows[...] = result.reshape(count, span, WIN)

    def load(s):
        i, slab = s // plan.shift, s % plan.shift
        return to_planes(plan, windows[i, :, slab * lanes : (slab + 1) * lanes])

    def store(s, re, im):
        out[plan.place(s)] = jnp.concatenate([re, im], axis=0).astype(BF16)

    columns(plan, -1.0, load, store, steer_re, steer_im, ahead, behind, twist, scratch)


def hogel_kernel(plan, lines, goals, *refs):
    weights_behind, twist_behind, weights_ahead, twist_ahead, col, col_turned, same = refs[:7]
    out, lights, packed, field, spectra, bright, factors, weighted, back = refs[7:]
    C, X, lanes, pp = plan.C, plan.X, 2 * plan.pp, plan.pp
    total = plan.total_cols
    for k in range(C):
        block = lines[k * plan.R : (k + 1) * plan.R].reshape(X, lanes)
        place = slice(k * lanes, (k + 1) * lanes)
        packed[:X, place], packed[X:, place] = rounded_with_i(block)

    def emit_near(c, start, step, value):
        for n, rounded in enumerate(rounded_with_i(value)):
            field[n, c * X + start : c * X + start + step, :] = rounded
            if c == 0 and start < STRIDE:
                field[n, total + start : total + start + step, :] = rounded

    near = matmul(weights_behind[0], packed[...])
    lines_inverse(plan, lanes, lambda rows: near[rows, :], emit_near, twist_behind)
    for j in range(plan.hogel_cols):
        window = slice(STRIDE * j, STRIDE * j + WIN)
        result = matmul(
            col_turned[...], jnp.concatenate([field[0, window, :], field[1, window, :]], axis=0)
        )
        spectra[j] = result
        power = result[:, :pp] * result[:, :pp] + result[:, pp:] * result[:, pp:]
        bright[j * VIEWS : (j + 1) * VIEWS, :] = power.reshape(VIEWS, BIN, pp).sum(axis=1)
    exact = lax.Precision.HIGHEST
    own = lax.broadcasted_iota(jnp.int32, (VIEWS, pp), 0) == (
        lax.broadcasted_iota(jnp.int32, (VIEWS, pp), 1) % VIEWS
    )
    for c in range(C):
        target = get_views(plan, goals[c])
        for j in range(plan.own_cols):
            h = c * plan.own_cols + j
            below = (plan.hogel_cols + h) * VIEWS
            bright[below : below + VIEWS, :] = jnp.where(own, target[j : j + 1, :], 0.0)
    spread = jnp.dot(bright[...], same[...], preferred_element_type=F32, precision=exact)
    views = plan.hogel_cols * VIEWS
    light = spread[:views] * (1.0 / (BIN * BIN))
    factors[...] = 4.0 * (light - spread[views:])
    bright[:views, :] = light
    for c in range(C):
        rows = []
        for j in range(plan.own_cols):
            h = c * plan.own_cols + j
            block = jnp.where(own, bright[h * VIEWS : (h + 1) * VIEWS, :], 0.0)
            rows.append(jnp.sum(block, axis=0, keepdims=True))
        lights[c] = put_views(plan, jnp.concatenate(rows, axis=0))
    for j in range(plan.hogel_cols):
        for view in range(VIEWS):
            factor = factors[j * VIEWS + view : j * VIEWS + view + 1, :]
            block = slice(view * BIN, (view + 1) * BIN)
            below = slice(WIN + view * BIN, WIN + (view + 1) * BIN)
            real = (spectra[j, block, :pp] * factor).astype(BF16)
            imag = (spectra[j, block, pp:] * factor).astype(BF16)
            weighted[block, :pp] = real
            weighted[block, pp:] = imag
            weighted[below, :pp] = imag
            weighted[below, pp:] = -real
        result = matmul(col[...], weighted[...])
        first = slice(STRIDE * j, STRIDE * (j + 1))
        back[first] = result[:STRIDE] if j == 0 else pending + result[:STRIDE]
        pending = result[STRIDE:]
    back[:STRIDE] = back[:STRIDE] + pending

    def load(c, start, step):
        return back[c * X + start : c * X + start + step, :]

    def emit(d, block):
        out[d] = block.astype(BF16)

    lines_forward(plan, lanes, load, emit, weights_ahead, twist_ahead, packed)


def steer_table(plan):
    index = lax.axis_index(("cols", "rows"))
    shape = (plan.D, plan.f, 128)
    k = lax.broadcasted_iota(jnp.int32, shape, 0)
    line = lax.broadcasted_iota(jnp.int32, shape, 1)
    lane = lax.broadcasted_iota(jnp.int32, shape, 2)
    u = k + plan.D * (lane % plan.m)
    v = index // plan.R + plan.C * (
        plan.span * (index % plan.R) + plan.f * (lane // plan.m) + line
    )

    def freq(position, count):
        return ((position + count // 2) % count - count // 2).astype(F32) / count

    freq_rows, freq_cols = freq(u, plan.total_rows), freq(v, plan.total_cols)
    radial = freq_rows * freq_rows + freq_cols * freq_cols
    phase = (
        -2.0
        * math.pi
        * distance_px
        * radial
        / (jnp.sqrt(index_ratio * index_ratio - radial) + index_ratio)
    )
    return jnp.cos(phase), jnp.sin(phase)


def exchange(chunks):
    return lax.all_to_all(chunks, ("cols", "rows"), split_axis=0, concat_axis=0, tiled=True)


def swap_columns(chunks):
    count = lax.axis_size("cols")
    return tuple(
        lax.ppermute(chunk, "cols", [(i, i ^ t) for i in range(count)]) if t else chunk
        for t, chunk in zip(partners(count), chunks)
    )


def local(slm_field, target_light):
    rows_count, cols_count = lax.axis_size("rows"), lax.axis_size("cols")
    plan = Plan(rows_count, cols_count, slm_field.shape[1], slm_field.shape[2])
    C, D, X, lanes, f = plan.C, plan.D, plan.X, plan.lanes, plan.f
    span, wide = plan.span, 2 * plan.pp

    ahead, behind, twist = (jnp.asarray(t) for t in plan.pencil_tables())
    weights_ahead, twist_ahead = plan.line_tables(-1.0)
    weights_ahead, twist_ahead = jnp.asarray(weights_ahead[0]), jnp.asarray(twist_ahead)
    weights_behind, twist_behind = (jnp.asarray(t) for t in plan.line_tables(1.0))
    col, col_turned, row = hogel_tables()
    row = plan.row_table(row[0], row[1])
    col, col_turned, row, row_turned, same = (
        jnp.asarray(t) for t in (col, col_turned, row, row.T.copy(), plan.group_table())
    )
    steer_re, steer_im = steer_table(plan)

    slabs_shapes = (shape_of((X + VIEWS, lanes), BF16),) * C
    slabs_scratch = pltpu.VMEM((C, X + VIEWS, lanes), BF16)
    views_shape = shape_of((C, VIEWS, lanes), BF16)
    pencil_shape = shape_of((D, 2 * f, 128), BF16)
    lines_shape = shape_of((D, span, wide), BF16)
    columns_scratch = (
        pltpu.VMEM((D, f, 128), F32),
        pltpu.VMEM((D, f, 128), F32),
        pltpu.VMEM((D, f, 256), BF16),
    )
    pencil_tables = (steer_re, steer_im, ahead, behind, twist)
    columns_flops = 8 * D * f * 256 * 256 + 2 * plan.hogel_rows * span * (2 * WIN) ** 2

    apart_any = pl.BlockSpec(memory_space=pl.ANY)
    slabs = call(
        lambda *refs: pack_kernel(plan, *refs),
        slabs_shapes,
        (slm_field.astype(BF16), target_light),
        (slabs_scratch,),
    )
    tall = pltpu.VMEM((2 * X, C * lanes), BF16)
    pencils, goals = call(
        lambda *refs: rows_forward_kernel(plan, *refs),
        (pencil_shape, views_shape),
        (weights_ahead, twist_ahead, *swap_columns(slabs), steer_re, steer_im),
        (tall, slabs_scratch),
        flops=2 * X * 2 * X * C * lanes,
        in_specs={C + 2: apart_any, C + 3: apart_any},
    )
    (lines,) = call(
        lambda *refs: pencil_forward_kernel(plan, *refs),
        (lines_shape,),
        (exchange(pencils), *pencil_tables, row),
        (pltpu.VMEM((plan.hogel_rows, span, 2 * WIN), BF16), *columns_scratch),
        flops=columns_flops,
    )
    tall = pltpu.VMEM((2 * X, C * wide), BF16)
    lines, lights = call(
        lambda *refs: hogel_kernel(plan, *refs),
        (lines_shape, views_shape),
        (
            exchange(lines),
            goals,
            weights_behind,
            twist_behind,
            weights_ahead,
            twist_ahead,
            col,
            col_turned,
            same,
        ),
        (
            tall,
            pltpu.VMEM((2, plan.total_cols + STRIDE, wide), BF16),
            pltpu.VMEM((plan.hogel_cols, WIN, wide), F32),
            pltpu.VMEM((2 * plan.hogel_cols * VIEWS, plan.pp), F32),
            pltpu.VMEM((plan.hogel_cols * VIEWS, plan.pp), F32),
            pltpu.VMEM((2 * WIN, wide), BF16),
            pltpu.VMEM((plan.total_cols, wide), F32),
        ),
        flops=4 * X * 2 * X * C * wide + 4 * plan.hogel_cols * WIN * 2 * WIN * wide,
    )
    (pencils,) = call(
        lambda *refs: pencil_back_kernel(plan, *refs),
        (pencil_shape,),
        (exchange(lines), *pencil_tables, row_turned),
        (pltpu.VMEM((plan.hogel_rows, span, WIN), F32), *columns_scratch),
        flops=columns_flops,
    )
    tall = pltpu.VMEM((2 * X, C * lanes), BF16)
    slabs = call(
        lambda *refs: rows_inverse_kernel(plan, *refs),
        slabs_shapes,
        (exchange(pencils), lights, weights_behind, twist_behind),
        (tall, slabs_scratch),
        flops=2 * X * 2 * X * C * lanes,
    )
    return call(
        lambda *refs: unpack_kernel(plan, *refs),
        (shape_of(slm_field.shape, F32), shape_of(target_light.shape, F32)),
        swap_columns(slabs),
        (slabs_scratch,),
    )


def solution(mesh):
    return jax.shard_map(
        local,
        mesh=mesh,
        in_specs=(P(None, "rows", "cols"), P("rows", "cols", None)),
        out_specs=(P(None, "rows", "cols"), P("rows", "cols", None)),
        check_vma=False,
    )
```

```python
import math

import jax
import jax.numpy as jnp
import ml_dtypes
import numpy as np
from jax import lax
from jax.experimental import pallas as pl
from jax.experimental.pallas import tpu as pltpu
from jax.sharding import PartitionSpec as P

WIN = 256
VIEWS = 16
STRIDE = 128
BIN = 16

distance_px = 16000.0
index_ratio = 15.0

BF16 = jnp.bfloat16
F32 = jnp.float32
BOTH_MINOR = (((1,), (1,)), ((), ()))


def call(body, outs, args, scratch=(), flops=0, in_specs=None, out_specs=None):
    nbytes = sum(math.prod(a.shape) * a.dtype.itemsize for a in (*outs, *args))
    specs = {}
    if in_specs:
        whole = pl.BlockSpec(memory_space=pltpu.VMEM)
        specs["in_specs"] = [in_specs.get(n, whole) for n in range(len(args))]
    if out_specs:
        specs["out_specs"] = out_specs
    return pl.pallas_call(
        body,
        out_shape=outs,
        scratch_shapes=list(scratch),
        compiler_params=pltpu.CompilerParams(vmem_limit_bytes=24 * 2**20),
        cost_estimate=pl.CostEstimate(flops=flops, bytes_accessed=nbytes, transcendentals=0),
        **specs,
    )(*args)


def shape_of(dims, dtype):
    return jax.ShapeDtypeStruct(dims, dtype)


def high_low(table):
    table = np.asarray(table, np.float32)
    high = table.astype(ml_dtypes.bfloat16)
    low = (table - high.astype(np.float32)).astype(ml_dtypes.bfloat16)
    return np.concatenate([high, low], axis=0)


def times_i(values):
    half = values.shape[-1] // 2
    if values.shape[-1] == 128:
        lanes = lax.broadcasted_iota(jnp.int32, values.shape, values.ndim - 1)
        turned = pltpu.roll(values, half, values.ndim - 1)
        return jnp.where(lanes < half, -turned, turned)
    return jnp.concatenate([-values[..., half:], values[..., :half]], axis=-1)


def rounded_with_i(value):
    rounded = value.astype(BF16)
    half = value.shape[-1] // 2
    if half % 128:
        return rounded, times_i(value.astype(F32)).astype(BF16)
    return rounded, jnp.concatenate([-rounded[:, half:], rounded[:, :half]], axis=1)


def small_dft(points, sign):
    count = len(points)
    if count == 1:
        return points
    even = small_dft(points[0::2], sign)
    odd = small_dft(points[1::2], sign)
    front, back = [], []
    for k in range(count // 2):
        re, im = odd[k]
        angle = sign * 2.0 * math.pi * k / count
        cosine, sine = math.cos(angle), math.sin(angle)
        if k == 0:
            pass
        elif 4 * k == count:
            re, im = (-im, re) if sign > 0 else (im, -re)
        elif 8 * k == count:
            re, im = cosine * (re - sign * im), cosine * (im + sign * re)
        elif 8 * k == 3 * count:
            re, im = cosine * (re + sign * im), cosine * (im - sign * re)
        else:
            re, im = re * cosine - im * sine, re * sine + im * cosine
        even_re, even_im = even[k]
        front.append((even_re + re, even_im + im))
        back.append((even_re - re, even_im - im))
    return front + back


def packed_dft(points, sign):
    count = len(points)
    if count == 1:
        return points
    even = packed_dft(points[0::2], sign)
    odd = packed_dft(points[1::2], sign)
    front, back = [], []
    for k in range(count // 2):
        term = odd[k]
        angle = sign * 2.0 * math.pi * k / count
        if 4 * k == count:
            term = times_i(term) if sign > 0 else -times_i(term)
        elif k:
            term = math.cos(angle) * term + math.sin(angle) * times_i(term)
        front.append(even[k] + term)
        back.append(even[k] - term)
    return front + back


def turn(rows, cols, period, sign):
    angles = sign * 2.0 * np.pi / period * ((np.arange(rows)[:, None] * np.arange(cols)) % period)
    return np.cos(angles), np.sin(angles)


def block_diagonal(block, copies):
    return np.kron(np.eye(copies), block)


class Plan:
    def __init__(self, rows_count, cols_count, rows_dev, cols_dev):
        self.R, self.C = rows_count, cols_count
        self.D = rows_count * cols_count
        self.X = cols_dev
        self.m = rows_dev // cols_count
        self.lanes = 2 * self.m
        self.P = 128 // self.m
        self.span = cols_dev // rows_count
        self.f = self.span // self.P
        self.total_rows = rows_dev * rows_count
        self.total_cols = cols_dev * cols_count
        self.outer = 8
        self.inner = self.D // 8
        self.shift = STRIDE // self.m
        self.hogel_rows = self.total_rows // STRIDE
        self.hogel_cols = self.total_cols // STRIDE
        self.parts = self.D // self.hogel_rows
        self.pp = WIN // self.parts
        self.views = VIEWS // self.parts
        self.own_cols = cols_dev // STRIDE

    def place(self, s):
        return s % self.C * self.R + s // self.C

    def line_tables(self, sign):
        cosine, sine = turn(self.X, self.X, self.X, sign)
        weights = high_low(np.concatenate([cosine, sine], axis=1)).reshape(2, self.X, 2 * self.X)
        twist = turn(self.X, self.C, self.total_cols, sign)
        return weights, np.concatenate(twist, axis=1).astype(np.float32)

    def pencil_tables(self):
        cosine, sine = turn(self.m, self.m, self.m, -1.0)
        cosine, sine = block_diagonal(cosine, self.P), block_diagonal(sine, self.P)
        ahead = np.block([[cosine, sine], [-sine, cosine]])
        behind = np.block([[cosine, -sine], [sine, cosine]]) / (self.total_rows * self.total_cols)
        twist = turn(self.D, self.m, self.total_rows, -1.0)
        twist = np.stack([np.tile(part, (1, self.P)) for part in twist]).astype(np.float32)
        return high_low(ahead), high_low(behind), twist

    def row_table(self, real, imag):
        blocks = []
        for slab in range(WIN // self.m):
            rows = slice(slab * self.m, (slab + 1) * self.m)
            for left, right in ((real[rows], imag[rows]), (-imag[rows], real[rows])):
                pieces = []
                for part in range(self.parts):
                    cols = slice(part * self.pp, (part + 1) * self.pp)
                    pieces += [left[:, cols], right[:, cols]]
                blocks.append(np.concatenate(pieces, axis=1))
        return np.concatenate(blocks, axis=0)

    def group_table(self):
        return np.kron(np.eye(self.views), np.ones((BIN, BIN))).astype(np.float32)


def hogel_tables():
    positions = np.arange(WIN)
    tapers = np.sin(np.pi * (positions + 0.5) / WIN) ** 2
    angles = -2.0 * np.pi / WIN * (positions[:, None] * positions[None, :] % WIN)
    cosine = (tapers[:, None] * np.cos(angles)).astype(np.float32)
    sine = (tapers[:, None] * np.sin(angles)).astype(np.float32)
    col = np.concatenate([cosine, sine], axis=1).astype(ml_dtypes.bfloat16)
    col_turned = np.concatenate([cosine.T, sine.T], axis=1).astype(ml_dtypes.bfloat16)
    row = np.stack([cosine / WIN, sine / WIN]).astype(ml_dtypes.bfloat16)
    return col, col_turned, row


def three_pieces(values):
    first = values.astype(BF16)
    rest = values - first.astype(F32)
    second = rest.astype(BF16)
    return first, second, (rest - second.astype(F32)).astype(BF16)


def matmul(left, right):
    return jnp.dot(left, right, preferred_element_type=F32)


def partners(count):
    return sorted(range(count), key=lambda t: (t != 0, -t.bit_count()))


def gather_chunks(arrived, chunks):
    mine = lax.axis_index("cols")
    for t, chunk in zip(partners(len(arrived)), arrived):
        chunks[mine ^ t] = chunk[...]


def scatter_chunks(chunks, leaving):
    mine = lax.axis_index("cols")
    for t, chunk in zip(partners(len(leaving)), leaving):
        chunk[...] = chunks[mine ^ t]


def put_views(plan, rows):
    pad = jnp.zeros((VIEWS - 3 * plan.own_cols, plan.lanes), F32)
    pieces = [piece.astype(F32) for piece in three_pieces(rows)]
    return jnp.concatenate([*pieces, pad], axis=0).astype(BF16)


def get_views(plan, chunk):
    chunk = chunk.astype(F32)
    n = plan.own_cols
    return chunk[:n] + chunk[n : 2 * n] + chunk[2 * n : 3 * n]


def pack_kernel(plan, field, goal, *refs):
    C, m, X = plan.C, plan.m, plan.X
    leaving, (out,) = refs[:C], refs[C:]
    for c in range(C):
        rows = slice(c * m, (c + 1) * m)
        block = jnp.concatenate([field[0, rows, :], field[1, rows, :]], axis=0)
        out[c, :X, :] = block.astype(F32).T.astype(BF16)
        i, start = c // plan.parts, c % plan.parts * plan.lanes
        out[c, X:, :] = put_views(plan, goal[i, :, start : start + plan.lanes])
    scatter_chunks(out, leaving)


def unpack_kernel(plan, *refs):
    C, m, X = plan.C, plan.m, plan.X
    arrived, (out, light, slabs) = refs[:C], refs[C:]
    gather_chunks(arrived, slabs)
    for c in range(C):
        block = slabs[c, :X, :].astype(F32).T
        out[0, m * c : m * c + m, :] = block[:m]
        out[1, m * c : m * c + m, :] = block[m:]
        i, start = c // plan.parts, c % plan.parts * plan.lanes
        light[i, :, start : start + plan.lanes] = get_views(plan, slabs[c, X:, :])


def lines_forward(plan, lanes, load, emit, weights, twist, turned):
    C, X = plan.C, plan.X
    step = 64
    for start in range(0, X, step):
        points = packed_dft([load(c, start, step) for c in range(C)], -1.0)
        for k in range(C):
            cosine = twist[start : start + step, k : k + 1]
            sine = twist[start : start + step, C + k : C + k + 1]
            value = points[k]
            if lanes % 256:
                across = times_i(value)
                if k:
                    value, across = value * cosine + across * sine, across * cosine - value * sine
                value, across = value.astype(BF16), across.astype(BF16)
            else:
                if k:
                    value = value * cosine + times_i(value) * sine
                value, across = rounded_with_i(value)
            place = slice(k * lanes, k * lanes + lanes)
            turned[start : start + step, place] = value
            turned[X + start : X + start + step, place] = across
    group = max(1, 256 // lanes)
    for first in range(0, C, group):
        result = matmul(weights[...], turned[:, first * lanes : (first + group) * lanes])
        for k in range(group):
            for r in range(plan.R):
                rows = slice(r * plan.span, (r + 1) * plan.span)
                emit((first + k) * plan.R + r, result[rows, k * lanes : (k + 1) * lanes])


def lines_inverse(plan, lanes, product, emit, twist):
    C, X = plan.C, plan.X
    step = 64
    for start in range(0, X, step):
        rows = slice(start, start + step)
        result = product(rows)
        points = []
        for k in range(C):
            value = result[:, k * lanes : (k + 1) * lanes]
            if k:
                cosine, sine = twist[rows, k : k + 1], twist[rows, C + k : C + k + 1]
                value = value * cosine + times_i(value) * sine
            points.append(value)
        for c, value in enumerate(packed_dft(points, 1.0)):
            emit(c, start, step, value)


def to_planes(plan, block):
    parts = [block[p * plan.f : (p + 1) * plan.f, :] for p in range(plan.P)]
    real = jnp.concatenate([part[:, : plan.m] for part in parts], axis=1)
    imag = jnp.concatenate([part[:, plan.m :] for part in parts], axis=1)
    return real, imag


def from_planes(plan, real, imag):
    m = plan.m
    return jnp.concatenate(
        [
            jnp.concatenate([real[:, p * m : (p + 1) * m], imag[:, p * m : (p + 1) * m]], axis=1)
            for p in range(plan.P)
        ],
        axis=0,
    )


def rows_forward_kernel(plan, weights, twist, *refs):
    C, X = plan.C, plan.X
    arrived, (_, _, out, goals, turned, slabs) = refs[:C], refs[C:]
    gather_chunks(arrived, slabs)
    goals[...] = slabs[:, X:, :]

    def load(c, start, step):
        return slabs[c, start : start + step, :].astype(F32)

    def emit(d, block):
        out[d] = jnp.concatenate(to_planes(plan, block), axis=0).astype(BF16)

    lines_forward(plan, plan.lanes, load, emit, weights, twist, turned)


def rows_inverse_kernel(plan, pencils, lights, weights, twist, *refs):
    C, X, lanes = plan.C, plan.X, plan.lanes
    leaving, (packed, out) = refs[:C], refs[C:]
    for k in range(C):
        for r in range(plan.R):
            chunk = pencils[k * plan.R + r].astype(F32)
            block = from_planes(plan, chunk[: plan.f], chunk[plan.f :])
            place = slice(k * lanes, k * lanes + lanes)
            packed[r * plan.span : (r + 1) * plan.span, place] = block.astype(BF16)
            packed[X + r * plan.span : X + (r + 1) * plan.span, place] = times_i(block).astype(BF16)

    def emit(c, start, step, value):
        out[c, start : start + step, :] = value.astype(BF16)

    def product(rows):
        return matmul(weights[0, rows, :], packed[...]) + matmul(weights[1, rows, :], packed[...])

    lines_inverse(plan, lanes, product, emit, twist)
    out[:, X:, :] = lights[...]
    scatter_chunks(out, leaving)


def columns(plan, sign, load, store, steer_re, steer_im, ahead, behind, twist, scratch):
    D, f, outer, inner = plan.D, plan.f, plan.outer, plan.inner
    half_re, half_im, rounded = scratch
    for b in range(inner):
        points = [load(inner * a + b) for a in range(outer)]
        for alpha, (re, im) in enumerate(small_dft(points, -1.0)):
            angle = -2.0 * math.pi * b * alpha / D
            cosine, sine = math.cos(angle), math.sin(angle)
            if b * alpha:
                re, im = re * cosine - im * sine, re * sine + im * cosine
            half_re[alpha * inner + b] = re
            half_im[alpha * inner + b] = im
    for alpha in range(outer):
        points = [(half_re[alpha * inner + b], half_im[alpha * inner + b]) for b in range(inner)]
        for beta, (re, im) in enumerate(small_dft(points, -1.0)):
            k = alpha + outer * beta
            cosine, sine = twist[0, k : k + 1, :], twist[1, k : k + 1, :]
            for offset, part in ((0, re * cosine - im * sine), (128, re * sine + im * cosine)):
                rounded[k, :, offset : offset + 128] = part.astype(BF16)
    group = D // 8 if sign > 0 else D
    for start in range(0, D, group):
        place = slice(start, start + group)

        def multiply(matrix):
            left = rounded[place].reshape(group * f, 256)
            product = matmul(left, matrix[:256, :]) + matmul(left, matrix[256:, :])
            return product.reshape(group, f, 256)

        result = multiply(ahead)
        re, im = result[:, :, :128], result[:, :, 128:]
        factor_re, factor_im = steer_re[place], sign * steer_im[place]
        for offset, part in (
            (0, re * factor_re - im * factor_im),
            (128, re * factor_im + im * factor_re),
        ):
            rounded[place, :, offset : offset + 128] = part.astype(BF16)
        result = multiply(behind)
        half_re[place] = result[:, :, :128]
        half_im[place] = result[:, :, 128:]
    for alpha in range(outer):
        points = []
        for beta in range(inner):
            k = alpha + outer * beta
            cosine, sine = twist[0, k : k + 1, :], twist[1, k : k + 1, :]
            re, im = half_re[k], half_im[k]
            points.append((re * cosine + im * sine, im * cosine - re * sine))
        for b, (re, im) in enumerate(small_dft(points, 1.0)):
            angle = 2.0 * math.pi * b * alpha / D
            cosine, sine = math.cos(angle), math.sin(angle)
            if b * alpha:
                re, im = re * cosine - im * sine, re * sine + im * cosine
            half_re[alpha + outer * b] = re
            half_im[alpha + outer * b] = im
    for b in range(inner):
        points = [(half_re[alpha + outer * b], half_im[alpha + outer * b]) for alpha in range(outer)]
        for a, (re, im) in enumerate(small_dft(points, 1.0)):
            store(inner * a + b, re, im)


def pencil_forward_kernel(plan, pencils, *refs):
    steer_re, steer_im, ahead, behind, twist, row, out, windows, *scratch = refs
    f, lanes, span = plan.f, plan.lanes, plan.span

    def load(s):
        chunk = pencils[plan.place(s)].astype(F32)
        return chunk[:f], chunk[f:]

    def store(s, re, im):
        block = from_planes(plan, re, im).astype(BF16)
        i, slab = s // plan.shift, s % plan.shift
        windows[i, :, slab * lanes : (slab + 1) * lanes] = block
        slab += plan.shift
        windows[(i - 1) % plan.hogel_rows, :, slab * lanes : (slab + 1) * lanes] = block

    columns(plan, 1.0, load, store, steer_re, steer_im, ahead, behind, twist, scratch)
    count = plan.hogel_rows
    result = matmul(windows[...].reshape(count * span, 2 * WIN), row[...]).astype(BF16)
    for i in range(count):
        for part in range(plan.parts):
            out[plan.place(i * plan.parts + part)] = result[
                i * span : (i + 1) * span, part * 2 * plan.pp : (part + 1) * 2 * plan.pp
            ]


def pencil_back_kernel(plan, lines, *refs):
    steer_re, steer_im, ahead, behind, twist, row, out, windows, *scratch = refs
    lanes, span, parts = plan.lanes, plan.span, plan.parts
    count, wide = plan.hogel_rows, 2 * plan.pp
    result = 0.0
    for n in range(parts):
        own = jnp.stack([lines[plan.place(i * parts + n)] for i in range(count)])
        before = jnp.concatenate([own[-1:], own[:-1]], axis=0)
        depth = slice(n * wide, (n + 1) * wide)
        result = result + matmul(own.reshape(count * span, wide), row[depth, :WIN])
        result = result + matmul(before.reshape(count * span, wide), row[depth, WIN:])
    windows[...] = result.reshape(count, span, WIN)

    def load(s):
        i, slab = s // plan.shift, s % plan.shift
        return to_planes(plan, windows[i, :, slab * lanes : (slab + 1) * lanes])

    def store(s, re, im):
        out[plan.place(s)] = jnp.concatenate([re, im], axis=0).astype(BF16)

    columns(plan, -1.0, load, store, steer_re, steer_im, ahead, behind, twist, scratch)


def hogel_kernel(plan, lines, goals, *refs):
    weights_behind, twist_behind, weights_ahead, twist_ahead, col, col_turned, same = refs[:7]
    out, lights, packed, field, spectra, bright, factors, weighted, back = refs[7:]
    C, X, lanes, pp = plan.C, plan.X, 2 * plan.pp, plan.pp
    total = plan.total_cols
    for k in range(C):
        block = lines[k * plan.R : (k + 1) * plan.R].reshape(X, lanes)
        place = slice(k * lanes, (k + 1) * lanes)
        packed[:X, place], packed[X:, place] = rounded_with_i(block)

    def emit_near(c, start, step, value):
        for n, rounded in enumerate(rounded_with_i(value)):
            field[n, c * X + start : c * X + start + step, :] = rounded
            if c == 0 and start < STRIDE:
                field[n, total + start : total + start + step, :] = rounded

    near = matmul(weights_behind[0], packed[...])
    lines_inverse(plan, lanes, lambda rows: near[rows, :], emit_near, twist_behind)
    for j in range(plan.hogel_cols):
        window = slice(STRIDE * j, STRIDE * j + WIN)
        result = matmul(
            col_turned[...], jnp.concatenate([field[0, window, :], field[1, window, :]], axis=0)
        )
        spectra[j] = result
        power = result[:, :pp] * result[:, :pp] + result[:, pp:] * result[:, pp:]
        bright[j * VIEWS : (j + 1) * VIEWS, :] = power.reshape(VIEWS, BIN, pp).sum(axis=1)
    exact = lax.Precision.HIGHEST
    own = lax.broadcasted_iota(jnp.int32, (VIEWS, pp), 0) == (
        lax.broadcasted_iota(jnp.int32, (VIEWS, pp), 1) % VIEWS
    )
    for c in range(C):
        target = get_views(plan, goals[c])
        for j in range(plan.own_cols):
            h = c * plan.own_cols + j
            below = (plan.hogel_cols + h) * VIEWS
            bright[below : below + VIEWS, :] = jnp.where(own, target[j : j + 1, :], 0.0)
    spread = jnp.dot(bright[...], same[...], preferred_element_type=F32, precision=exact)
    views = plan.hogel_cols * VIEWS
    light = spread[:views] * (1.0 / (BIN * BIN))
    factors[...] = 4.0 * (light - spread[views:])
    bright[:views, :] = light
    for c in range(C):
        rows = []
        for j in range(plan.own_cols):
            h = c * plan.own_cols + j
            block = jnp.where(own, bright[h * VIEWS : (h + 1) * VIEWS, :], 0.0)
            rows.append(jnp.sum(block, axis=0, keepdims=True))
        lights[c] = put_views(plan, jnp.concatenate(rows, axis=0))
    for j in range(plan.hogel_cols):
        for view in range(VIEWS):
            factor = factors[j * VIEWS + view : j * VIEWS + view + 1, :]
            block = slice(view * BIN, (view + 1) * BIN)
            below = slice(WIN + view * BIN, WIN + (view + 1) * BIN)
            real = (spectra[j, block, :pp] * factor).astype(BF16)
            imag = (spectra[j, block, pp:] * factor).astype(BF16)
            weighted[block, :pp] = real
            weighted[block, pp:] = imag
            weighted[below, :pp] = imag
            weighted[below, pp:] = -real
        result = matmul(col[...], weighted[...])
        first = slice(STRIDE * j, STRIDE * (j + 1))
        back[first] = result[:STRIDE] if j == 0 else pending + result[:STRIDE]
        pending = result[STRIDE:]
    back[:STRIDE] = back[:STRIDE] + pending

    def load(c, start, step):
        return back[c * X + start : c * X + start + step, :]

    def emit(d, block):
        out[d] = block.astype(BF16)

    lines_forward(plan, lanes, load, emit, weights_ahead, twist_ahead, packed)


def steer_table(plan):
    index = lax.axis_index(("cols", "rows"))
    shape = (plan.D, plan.f, 128)
    k = lax.broadcasted_iota(jnp.int32, shape, 0)
    line = lax.broadcasted_iota(jnp.int32, shape, 1)
    lane = lax.broadcasted_iota(jnp.int32, shape, 2)
    u = k + plan.D * (lane % plan.m)
    v = index // plan.R + plan.C * (
        plan.span * (index % plan.R) + plan.f * (lane // plan.m) + line
    )

    def freq(position, count):
        return ((position + count // 2) % count - count // 2).astype(F32) / count

    freq_rows, freq_cols = freq(u, plan.total_rows), freq(v, plan.total_cols)
    radial = freq_rows * freq_rows + freq_cols * freq_cols
    phase = (
        -2.0
        * math.pi
        * distance_px
        * radial
        / (jnp.sqrt(index_ratio * index_ratio - radial) + index_ratio)
    )
    return jnp.cos(phase), jnp.sin(phase)


def exchange(chunks):
    return lax.all_to_all(chunks, ("cols", "rows"), split_axis=0, concat_axis=0, tiled=True)


def swap_columns(chunks):
    count = lax.axis_size("cols")
    return tuple(
        lax.ppermute(chunk, "cols", [(i, i ^ t) for i in range(count)]) if t else chunk
        for t, chunk in zip(partners(count), chunks)
    )


def local(slm_field, target_light):
    rows_count, cols_count = lax.axis_size("rows"), lax.axis_size("cols")
    plan = Plan(rows_count, cols_count, slm_field.shape[1], slm_field.shape[2])
    C, D, X, lanes, f = plan.C, plan.D, plan.X, plan.lanes, plan.f
    span, wide = plan.span, 2 * plan.pp

    ahead, behind, twist = (jnp.asarray(t) for t in plan.pencil_tables())
    weights_ahead, twist_ahead = plan.line_tables(-1.0)
    weights_ahead, twist_ahead = jnp.asarray(weights_ahead[0]), jnp.asarray(twist_ahead)
    weights_behind, twist_behind = (jnp.asarray(t) for t in plan.line_tables(1.0))
    col, col_turned, row = hogel_tables()
    row = plan.row_table(row[0], row[1])
    col, col_turned, row, row_turned, same = (
        jnp.asarray(t) for t in (col, col_turned, row, row.T.copy(), plan.group_table())
    )
    steer_re, steer_im = steer_table(plan)

    slabs_shapes = (shape_of((X + VIEWS, lanes), BF16),) * C
    slabs_scratch = pltpu.VMEM((C, X + VIEWS, lanes), BF16)
    views_shape = shape_of((C, VIEWS, lanes), BF16)
    pencil_shape = shape_of((D, 2 * f, 128), BF16)
    lines_shape = shape_of((D, span, wide), BF16)
    columns_scratch = (
        pltpu.VMEM((D, f, 128), F32),
        pltpu.VMEM((D, f, 128), F32),
        pltpu.VMEM((D, f, 256), BF16),
    )
    pencil_tables = (steer_re, steer_im, ahead, behind, twist)
    columns_flops = 8 * D * f * 256 * 256 + 2 * plan.hogel_rows * span * (2 * WIN) ** 2

    apart_any = pl.BlockSpec(memory_space=pl.ANY)
    slabs = call(
        lambda *refs: pack_kernel(plan, *refs),
        slabs_shapes,
        (slm_field.astype(BF16), target_light),
        (slabs_scratch,),
    )
    tall = pltpu.VMEM((2 * X, C * lanes), BF16)
    pencils, goals = call(
        lambda *refs: rows_forward_kernel(plan, *refs),
        (pencil_shape, views_shape),
        (weights_ahead, twist_ahead, *swap_columns(slabs), steer_re, steer_im),
        (tall, slabs_scratch),
        flops=2 * X * 2 * X * C * lanes,
        in_specs={C + 2: apart_any, C + 3: apart_any},
    )
    (lines,) = call(
        lambda *refs: pencil_forward_kernel(plan, *refs),
        (lines_shape,),
        (exchange(pencils), *pencil_tables, row),
        (pltpu.VMEM((plan.hogel_rows, span, 2 * WIN), BF16), *columns_scratch),
        flops=columns_flops,
    )
    tall = pltpu.VMEM((2 * X, C * wide), BF16)
    lines, lights = call(
        lambda *refs: hogel_kernel(plan, *refs),
        (lines_shape, views_shape),
        (
            exchange(lines),
            goals,
            weights_behind,
            twist_behind,
            weights_ahead,
            twist_ahead,
            col,
            col_turned,
            same,
        ),
        (
            tall,
            pltpu.VMEM((2, plan.total_cols + STRIDE, wide), BF16),
            pltpu.VMEM((plan.hogel_cols, WIN, wide), F32),
            pltpu.VMEM((2 * plan.hogel_cols * VIEWS, plan.pp), F32),
            pltpu.VMEM((plan.hogel_cols * VIEWS, plan.pp), F32),
            pltpu.VMEM((2 * WIN, wide), BF16),
            pltpu.VMEM((plan.total_cols, wide), F32),
        ),
        flops=4 * X * 2 * X * C * wide + 4 * plan.hogel_cols * WIN * 2 * WIN * wide,
    )
    (pencils,) = call(
        lambda *refs: pencil_back_kernel(plan, *refs),
        (pencil_shape,),
        (exchange(lines), *pencil_tables, row_turned),
        (pltpu.VMEM((plan.hogel_rows, span, WIN), F32), *columns_scratch),
        flops=columns_flops,
    )
    tall = pltpu.VMEM((2 * X, C * lanes), BF16)
    slabs = call(
        lambda *refs: rows_inverse_kernel(plan, *refs),
        slabs_shapes,
        (exchange(pencils), lights, weights_behind, twist_behind),
        (tall, slabs_scratch),
        flops=2 * X * 2 * X * C * lanes,
    )
    return call(
        lambda *refs: unpack_kernel(plan, *refs),
        (shape_of(slm_field.shape, F32), shape_of(target_light.shape, F32)),
        swap_columns(slabs),
        (slabs_scratch,),
    )


def solution(mesh):
    return jax.shard_map(
        local,
        mesh=mesh,
        in_specs=(P(None, "rows", "cols"), P("rows", "cols", None)),
        out_specs=(P(None, "rows", "cols"), P("rows", "cols", None)),
        check_vma=False,
    )
```

```python
import math

import jax
import jax.numpy as jnp
import ml_dtypes
import numpy as np
from jax import lax
from jax.experimental import pallas as pl
from jax.experimental.pallas import tpu as pltpu
from jax.sharding import PartitionSpec as P

WIN = 256
VIEWS = 16
STRIDE = 128
BIN = 16

distance_px = 16000.0
index_ratio = 15.0

BF16 = jnp.bfloat16
F32 = jnp.float32
BOTH_MINOR = (((1,), (1,)), ((), ()))


def call(body, outs, args, scratch=(), flops=0, in_specs=None, out_specs=None):
    nbytes = sum(math.prod(a.shape) * a.dtype.itemsize for a in (*outs, *args))
    specs = {}
    if in_specs:
        whole = pl.BlockSpec(memory_space=pltpu.VMEM)
        specs["in_specs"] = [in_specs.get(n, whole) for n in range(len(args))]
    if out_specs:
        specs["out_specs"] = out_specs
    return pl.pallas_call(
        body,
        out_shape=outs,
        scratch_shapes=list(scratch),
        compiler_params=pltpu.CompilerParams(vmem_limit_bytes=24 * 2**20),
        cost_estimate=pl.CostEstimate(flops=flops, bytes_accessed=nbytes, transcendentals=0),
        **specs,
    )(*args)


def shape_of(dims, dtype):
    return jax.ShapeDtypeStruct(dims, dtype)


def high_low(table):
    table = np.asarray(table, np.float32)
    high = table.astype(ml_dtypes.bfloat16)
    low = (table - high.astype(np.float32)).astype(ml_dtypes.bfloat16)
    return np.concatenate([high, low], axis=0)


def times_i(values):
    half = values.shape[-1] // 2
    if values.shape[-1] == 128:
        lanes = lax.broadcasted_iota(jnp.int32, values.shape, values.ndim - 1)
        turned = pltpu.roll(values, half, values.ndim - 1)
        return jnp.where(lanes < half, -turned, turned)
    return jnp.concatenate([-values[..., half:], values[..., :half]], axis=-1)


def rounded_with_i(value):
    rounded = value.astype(BF16)
    half = value.shape[-1] // 2
    if half % 128:
        return rounded, times_i(value.astype(F32)).astype(BF16)
    return rounded, jnp.concatenate([-rounded[:, half:], rounded[:, :half]], axis=1)


def small_dft(points, sign):
    count = len(points)
    if count == 1:
        return points
    even = small_dft(points[0::2], sign)
    odd = small_dft(points[1::2], sign)
    front, back = [], []
    for k in range(count // 2):
        re, im = odd[k]
        angle = sign * 2.0 * math.pi * k / count
        cosine, sine = math.cos(angle), math.sin(angle)
        if k == 0:
            pass
        elif 4 * k == count:
            re, im = (-im, re) if sign > 0 else (im, -re)
        elif 8 * k == count:
            re, im = cosine * (re - sign * im), cosine * (im + sign * re)
        elif 8 * k == 3 * count:
            re, im = cosine * (re + sign * im), cosine * (im - sign * re)
        else:
            re, im = re * cosine - im * sine, re * sine + im * cosine
        even_re, even_im = even[k]
        front.append((even_re + re, even_im + im))
        back.append((even_re - re, even_im - im))
    return front + back


def packed_dft(points, sign):
    count = len(points)
    if count == 1:
        return points
    even = packed_dft(points[0::2], sign)
    odd = packed_dft(points[1::2], sign)
    front, back = [], []
    for k in range(count // 2):
        term = odd[k]
        angle = sign * 2.0 * math.pi * k / count
        if 4 * k == count:
            term = times_i(term) if sign > 0 else -times_i(term)
        elif k:
            term = math.cos(angle) * term + math.sin(angle) * times_i(term)
        front.append(even[k] + term)
        back.append(even[k] - term)
    return front + back


def turn(rows, cols, period, sign):
    angles = sign * 2.0 * np.pi / period * ((np.arange(rows)[:, None] * np.arange(cols)) % period)
    return np.cos(angles), np.sin(angles)


def block_diagonal(block, copies):
    return np.kron(np.eye(copies), block)


class Plan:
    def __init__(self, rows_count, cols_count, rows_dev, cols_dev):
        self.R, self.C = rows_count, cols_count
        self.D = rows_count * cols_count
        self.X = cols_dev
        self.m = rows_dev // cols_count
        self.lanes = 2 * self.m
        self.P = 128 // self.m
        self.span = cols_dev // rows_count
        self.f = self.span // self.P
        self.total_rows = rows_dev * rows_count
        self.total_cols = cols_dev * cols_count
        self.outer = 8
        self.inner = self.D // 8
        self.shift = STRIDE // self.m
        self.hogel_rows = self.total_rows // STRIDE
        self.hogel_cols = self.total_cols // STRIDE
        self.parts = self.D // self.hogel_rows
        self.pp = WIN // self.parts
        self.views = VIEWS // self.parts
        self.own_cols = cols_dev // STRIDE

    def place(self, s):
        return s % self.C * self.R + s // self.C

    def line_tables(self, sign):
        cosine, sine = turn(self.X, self.X, self.X, sign)
        weights = high_low(np.concatenate([cosine, sine], axis=1)).reshape(2, self.X, 2 * self.X)
        twist = turn(self.X, self.C, self.total_cols, sign)
        return weights, np.concatenate(twist, axis=1).astype(np.float32)

    def pencil_tables(self):
        cosine, sine = turn(self.m, self.m, self.m, -1.0)
        cosine, sine = block_diagonal(cosine, self.P), block_diagonal(sine, self.P)
        ahead = np.block([[cosine, sine], [-sine, cosine]])
        behind = np.block([[cosine, -sine], [sine, cosine]]) / (self.total_rows * self.total_cols)
        twist = turn(self.D, self.m, self.total_rows, -1.0)
        twist = np.stack([np.tile(part, (1, self.P)) for part in twist]).astype(np.float32)
        return high_low(ahead), high_low(behind), twist

    def row_table(self, real, imag):
        blocks = []
        for slab in range(WIN // self.m):
            rows = slice(slab * self.m, (slab + 1) * self.m)
            for left, right in ((real[rows], imag[rows]), (-imag[rows], real[rows])):
                pieces = []
                for part in range(self.parts):
                    cols = slice(part * self.pp, (part + 1) * self.pp)
                    pieces += [left[:, cols], right[:, cols]]
                blocks.append(np.concatenate(pieces, axis=1))
        return np.concatenate(blocks, axis=0)

    def group_table(self):
        return np.kron(np.eye(self.views), np.ones((BIN, BIN))).astype(np.float32)


def hogel_tables():
    positions = np.arange(WIN)
    tapers = np.sin(np.pi * (positions + 0.5) / WIN) ** 2
    angles = -2.0 * np.pi / WIN * (positions[:, None] * positions[None, :] % WIN)
    cosine = (tapers[:, None] * np.cos(angles)).astype(np.float32)
    sine = (tapers[:, None] * np.sin(angles)).astype(np.float32)
    col = np.concatenate([cosine, sine], axis=1).astype(ml_dtypes.bfloat16)
    col_turned = np.concatenate([cosine.T, sine.T], axis=1).astype(ml_dtypes.bfloat16)
    row = np.stack([cosine / WIN, sine / WIN]).astype(ml_dtypes.bfloat16)
    return col, col_turned, row


def three_pieces(values):
    first = values.astype(BF16)
    rest = values - first.astype(F32)
    second = rest.astype(BF16)
    return first, second, (rest - second.astype(F32)).astype(BF16)


def matmul(left, right):
    return jnp.dot(left, right, preferred_element_type=F32)


def partners(count):
    return sorted(range(count), key=lambda t: (t != 0, -t.bit_count()))


def gather_chunks(arrived, chunks):
    mine = lax.axis_index("cols")
    for t, chunk in zip(partners(len(arrived)), arrived):
        chunks[mine ^ t] = chunk[...]


def scatter_chunks(chunks, leaving):
    mine = lax.axis_index("cols")
    for t, chunk in zip(partners(len(leaving)), leaving):
        chunk[...] = chunks[mine ^ t]


def put_views(plan, rows):
    pad = jnp.zeros((VIEWS - 3 * plan.own_cols, plan.lanes), F32)
    pieces = [piece.astype(F32) for piece in three_pieces(rows)]
    return jnp.concatenate([*pieces, pad], axis=0).astype(BF16)


def get_views(plan, chunk):
    chunk = chunk.astype(F32)
    n = plan.own_cols
    return chunk[:n] + chunk[n : 2 * n] + chunk[2 * n : 3 * n]


def pack_kernel(plan, field, goal, *refs):
    C, m, X = plan.C, plan.m, plan.X
    leaving, (out,) = refs[:C], refs[C:]
    for c in range(C):
        rows = slice(c * m, (c + 1) * m)
        block = jnp.concatenate([field[0, rows, :], field[1, rows, :]], axis=0)
        out[c, :X, :] = block.astype(F32).T.astype(BF16)
        i, start = c // plan.parts, c % plan.parts * plan.lanes
        out[c, X:, :] = put_views(plan, goal[i, :, start : start + plan.lanes])
    scatter_chunks(out, leaving)


def unpack_kernel(plan, *refs):
    C, m, X = plan.C, plan.m, plan.X
    arrived, (out, light, slabs) = refs[:C], refs[C:]
    gather_chunks(arrived, slabs)
    for c in range(C):
        block = slabs[c, :X, :].astype(F32).T
        out[0, m * c : m * c + m, :] = block[:m]
        out[1, m * c : m * c + m, :] = block[m:]
        i, start = c // plan.parts, c % plan.parts * plan.lanes
        light[i, :, start : start + plan.lanes] = get_views(plan, slabs[c, X:, :])


def lines_forward(plan, lanes, load, emit, weights, twist, turned):
    C, X = plan.C, plan.X
    step = 64
    for start in range(0, X, step):
        points = packed_dft([load(c, start, step) for c in range(C)], -1.0)
        for k in range(C):
            cosine = twist[start : start + step, k : k + 1]
            sine = twist[start : start + step, C + k : C + k + 1]
            value = points[k]
            if lanes % 256:
                across = times_i(value)
                if k:
                    value, across = value * cosine + across * sine, across * cosine - value * sine
                value, across = value.astype(BF16), across.astype(BF16)
            else:
                if k:
                    value = value * cosine + times_i(value) * sine
                value, across = rounded_with_i(value)
            place = slice(k * lanes, k * lanes + lanes)
            turned[start : start + step, place] = value
            turned[X + start : X + start + step, place] = across
    group = max(1, 256 // lanes)
    for first in range(0, C, group):
        result = matmul(weights[...], turned[:, first * lanes : (first + group) * lanes])
        for k in range(group):
            for r in range(plan.R):
                rows = slice(r * plan.span, (r + 1) * plan.span)
                emit((first + k) * plan.R + r, result[rows, k * lanes : (k + 1) * lanes])


def lines_inverse(plan, lanes, product, emit, twist):
    C, X = plan.C, plan.X
    step = 64
    for start in range(0, X, step):
        rows = slice(start, start + step)
        result = product(rows)
        points = []
        for k in range(C):
            value = result[:, k * lanes : (k + 1) * lanes]
            if k:
                cosine, sine = twist[rows, k : k + 1], twist[rows, C + k : C + k + 1]
                value = value * cosine + times_i(value) * sine
            points.append(value)
        for c, value in enumerate(packed_dft(points, 1.0)):
            emit(c, start, step, value)


def to_planes(plan, block):
    parts = [block[p * plan.f : (p + 1) * plan.f, :] for p in range(plan.P)]
    real = jnp.concatenate([part[:, : plan.m] for part in parts], axis=1)
    imag = jnp.concatenate([part[:, plan.m :] for part in parts], axis=1)
    return real, imag


def from_planes(plan, real, imag):
    m = plan.m
    return jnp.concatenate(
        [
            jnp.concatenate([real[:, p * m : (p + 1) * m], imag[:, p * m : (p + 1) * m]], axis=1)
            for p in range(plan.P)
        ],
        axis=0,
    )


def rows_forward_kernel(plan, weights, twist, *refs):
    C, X = plan.C, plan.X
    arrived, (_, _, out, goals, turned, slabs) = refs[:C], refs[C:]
    gather_chunks(arrived, slabs)
    goals[...] = slabs[:, X:, :]

    def load(c, start, step):
        return slabs[c, start : start + step, :].astype(F32)

    def emit(d, block):
        out[d] = jnp.concatenate(to_planes(plan, block), axis=0).astype(BF16)

    lines_forward(plan, plan.lanes, load, emit, weights, twist, turned)


def rows_inverse_kernel(plan, pencils, lights, weights, twist, *refs):
    C, X, lanes = plan.C, plan.X, plan.lanes
    leaving, (packed, out) = refs[:C], refs[C:]
    for k in range(C):
        for r in range(plan.R):
            chunk = pencils[k * plan.R + r].astype(F32)
            block = from_planes(plan, chunk[: plan.f], chunk[plan.f :])
            place = slice(k * lanes, k * lanes + lanes)
            packed[r * plan.span : (r + 1) * plan.span, place] = block.astype(BF16)
            packed[X + r * plan.span : X + (r + 1) * plan.span, place] = times_i(block).astype(BF16)

    def emit(c, start, step, value):
        out[c, start : start + step, :] = value.astype(BF16)

    def product(rows):
        return matmul(weights[0, rows, :], packed[...]) + matmul(weights[1, rows, :], packed[...])

    lines_inverse(plan, lanes, product, emit, twist)
    out[:, X:, :] = lights[...]
    scatter_chunks(out, leaving)


def columns(plan, sign, load, store, steer_re, steer_im, ahead, behind, twist, scratch):
    D, f, outer, inner = plan.D, plan.f, plan.outer, plan.inner
    half_re, half_im, rounded = scratch
    for b in range(inner):
        points = [load(inner * a + b) for a in range(outer)]
        for alpha, (re, im) in enumerate(small_dft(points, -1.0)):
            angle = -2.0 * math.pi * b * alpha / D
            cosine, sine = math.cos(angle), math.sin(angle)
            if b * alpha:
                re, im = re * cosine - im * sine, re * sine + im * cosine
            half_re[alpha * inner + b] = re
            half_im[alpha * inner + b] = im
    for alpha in range(outer):
        points = [(half_re[alpha * inner + b], half_im[alpha * inner + b]) for b in range(inner)]
        for beta, (re, im) in enumerate(small_dft(points, -1.0)):
            k = alpha + outer * beta
            cosine, sine = twist[0, k : k + 1, :], twist[1, k : k + 1, :]
            for offset, part in ((0, re * cosine - im * sine), (128, re * sine + im * cosine)):
                rounded[k, :, offset : offset + 128] = part.astype(BF16)
    group = D // 4 if sign > 0 else D
    for start in range(0, D, group):
        place = slice(start, start + group)

        def multiply(matrix):
            left = rounded[place].reshape(group * f, 256)
            product = matmul(left, matrix[:256, :]) + matmul(left, matrix[256:, :])
            return product.reshape(group, f, 256)

        result = multiply(ahead)
        re, im = result[:, :, :128], result[:, :, 128:]
        factor_re, factor_im = steer_re[place], sign * steer_im[place]
        for offset, part in (
            (0, re * factor_re - im * factor_im),
            (128, re * factor_im + im * factor_re),
        ):
            rounded[place, :, offset : offset + 128] = part.astype(BF16)
        result = multiply(behind)
        half_re[place] = result[:, :, :128]
        half_im[place] = result[:, :, 128:]
    for alpha in range(outer):
        points = []
        for beta in range(inner):
            k = alpha + outer * beta
            cosine, sine = twist[0, k : k + 1, :], twist[1, k : k + 1, :]
            re, im = half_re[k], half_im[k]
            points.append((re * cosine + im * sine, im * cosine - re * sine))
        for b, (re, im) in enumerate(small_dft(points, 1.0)):
            angle = 2.0 * math.pi * b * alpha / D
            cosine, sine = math.cos(angle), math.sin(angle)
            if b * alpha:
                re, im = re * cosine - im * sine, re * sine + im * cosine
            half_re[alpha + outer * b] = re
            half_im[alpha + outer * b] = im
    for b in range(inner):
        points = [(half_re[alpha + outer * b], half_im[alpha + outer * b]) for alpha in range(outer)]
        for a, (re, im) in enumerate(small_dft(points, 1.0)):
            store(inner * a + b, re, im)


def pencil_forward_kernel(plan, pencils, *refs):
    steer_re, steer_im, ahead, behind, twist, row, out, windows, *scratch = refs
    f, lanes, span = plan.f, plan.lanes, plan.span

    def load(s):
        chunk = pencils[plan.place(s)].astype(F32)
        return chunk[:f], chunk[f:]

    def store(s, re, im):
        block = from_planes(plan, re, im).astype(BF16)
        i, slab = s // plan.shift, s % plan.shift
        windows[i, :, slab * lanes : (slab + 1) * lanes] = block
        slab += plan.shift
        windows[(i - 1) % plan.hogel_rows, :, slab * lanes : (slab + 1) * lanes] = block

    columns(plan, 1.0, load, store, steer_re, steer_im, ahead, behind, twist, scratch)
    count = plan.hogel_rows
    result = matmul(windows[...].reshape(count * span, 2 * WIN), row[...]).astype(BF16)
    for i in range(count):
        for part in range(plan.parts):
            out[plan.place(i * plan.parts + part)] = result[
                i * span : (i + 1) * span, part * 2 * plan.pp : (part + 1) * 2 * plan.pp
            ]


def pencil_back_kernel(plan, lines, *refs):
    steer_re, steer_im, ahead, behind, twist, row, out, windows, *scratch = refs
    lanes, span, parts = plan.lanes, plan.span, plan.parts
    count, wide = plan.hogel_rows, 2 * plan.pp
    result = 0.0
    for n in range(parts):
        own = jnp.stack([lines[plan.place(i * parts + n)] for i in range(count)])
        before = jnp.concatenate([own[-1:], own[:-1]], axis=0)
        depth = slice(n * wide, (n + 1) * wide)
        result = result + matmul(own.reshape(count * span, wide), row[depth, :WIN])
        result = result + matmul(before.reshape(count * span, wide), row[depth, WIN:])
    windows[...] = result.reshape(count, span, WIN)

    def load(s):
        i, slab = s // plan.shift, s % plan.shift
        return to_planes(plan, windows[i, :, slab * lanes : (slab + 1) * lanes])

    def store(s, re, im):
        out[plan.place(s)] = jnp.concatenate([re, im], axis=0).astype(BF16)

    columns(plan, -1.0, load, store, steer_re, steer_im, ahead, behind, twist, scratch)


def hogel_kernel(plan, lines, goals, *refs):
    weights_behind, twist_behind, weights_ahead, twist_ahead, col, col_turned, same = refs[:7]
    out, lights, packed, field, spectra, bright, factors, weighted, back = refs[7:]
    C, X, lanes, pp = plan.C, plan.X, 2 * plan.pp, plan.pp
    total = plan.total_cols
    for k in range(C):
        block = lines[k * plan.R : (k + 1) * plan.R].reshape(X, lanes)
        place = slice(k * lanes, (k + 1) * lanes)
        packed[:X, place], packed[X:, place] = rounded_with_i(block)

    def emit_near(c, start, step, value):
        for n, rounded in enumerate(rounded_with_i(value)):
            field[n, c * X + start : c * X + start + step, :] = rounded
            if c == 0 and start < STRIDE:
                field[n, total + start : total + start + step, :] = rounded

    near = matmul(weights_behind[0], packed[...])
    lines_inverse(plan, lanes, lambda rows: near[rows, :], emit_near, twist_behind)
    for j in range(plan.hogel_cols):
        window = slice(STRIDE * j, STRIDE * j + WIN)
        result = matmul(
            col_turned[...], jnp.concatenate([field[0, window, :], field[1, window, :]], axis=0)
        )
        spectra[j] = result
        power = result[:, :pp] * result[:, :pp] + result[:, pp:] * result[:, pp:]
        bright[j * VIEWS : (j + 1) * VIEWS, :] = power.reshape(VIEWS, BIN, pp).sum(axis=1)
    exact = lax.Precision.HIGHEST
    own = lax.broadcasted_iota(jnp.int32, (VIEWS, pp), 0) == (
        lax.broadcasted_iota(jnp.int32, (VIEWS, pp), 1) % VIEWS
    )
    for c in range(C):
        target = get_views(plan, goals[c])
        for j in range(plan.own_cols):
            h = c * plan.own_cols + j
            below = (plan.hogel_cols + h) * VIEWS
            bright[below : below + VIEWS, :] = jnp.where(own, target[j : j + 1, :], 0.0)
    spread = jnp.dot(bright[...], same[...], preferred_element_type=F32, precision=exact)
    views = plan.hogel_cols * VIEWS
    light = spread[:views] * (1.0 / (BIN * BIN))
    factors[...] = 4.0 * (light - spread[views:])
    bright[:views, :] = light
    for c in range(C):
        rows = []
        for j in range(plan.own_cols):
            h = c * plan.own_cols + j
            block = jnp.where(own, bright[h * VIEWS : (h + 1) * VIEWS, :], 0.0)
            rows.append(jnp.sum(block, axis=0, keepdims=True))
        lights[c] = put_views(plan, jnp.concatenate(rows, axis=0))
    for j in range(plan.hogel_cols):
        for view in range(VIEWS):
            factor = factors[j * VIEWS + view : j * VIEWS + view + 1, :]
            block = slice(view * BIN, (view + 1) * BIN)
            below = slice(WIN + view * BIN, WIN + (view + 1) * BIN)
            real = (spectra[j, block, :pp] * factor).astype(BF16)
            imag = (spectra[j, block, pp:] * factor).astype(BF16)
            weighted[block, :pp] = real
            weighted[block, pp:] = imag
            weighted[below, :pp] = imag
            weighted[below, pp:] = -real
        result = matmul(col[...], weighted[...])
        first = slice(STRIDE * j, STRIDE * (j + 1))
        back[first] = result[:STRIDE] if j == 0 else pending + result[:STRIDE]
        pending = result[STRIDE:]
    back[:STRIDE] = back[:STRIDE] + pending

    def load(c, start, step):
        return back[c * X + start : c * X + start + step, :]

    def emit(d, block):
        out[d] = block.astype(BF16)

    lines_forward(plan, lanes, load, emit, weights_ahead, twist_ahead, packed)


def steer_table(plan):
    index = lax.axis_index(("cols", "rows"))
    shape = (plan.D, plan.f, 128)
    k = lax.broadcasted_iota(jnp.int32, shape, 0)
    line = lax.broadcasted_iota(jnp.int32, shape, 1)
    lane = lax.broadcasted_iota(jnp.int32, shape, 2)
    u = k + plan.D * (lane % plan.m)
    v = index // plan.R + plan.C * (
        plan.span * (index % plan.R) + plan.f * (lane // plan.m) + line
    )

    def freq(position, count):
        return ((position + count // 2) % count - count // 2).astype(F32) / count

    freq_rows, freq_cols = freq(u, plan.total_rows), freq(v, plan.total_cols)
    radial = freq_rows * freq_rows + freq_cols * freq_cols
    phase = (
        -2.0
        * math.pi
        * distance_px
        * radial
        / (jnp.sqrt(index_ratio * index_ratio - radial) + index_ratio)
    )
    return jnp.cos(phase), jnp.sin(phase)


def exchange(chunks):
    return lax.all_to_all(chunks, ("cols", "rows"), split_axis=0, concat_axis=0, tiled=True)


def swap_columns(chunks):
    count = lax.axis_size("cols")
    return tuple(
        lax.ppermute(chunk, "cols", [(i, i ^ t) for i in range(count)]) if t else chunk
        for t, chunk in zip(partners(count), chunks)
    )


def local(slm_field, target_light):
    rows_count, cols_count = lax.axis_size("rows"), lax.axis_size("cols")
    plan = Plan(rows_count, cols_count, slm_field.shape[1], slm_field.shape[2])
    C, D, X, lanes, f = plan.C, plan.D, plan.X, plan.lanes, plan.f
    span, wide = plan.span, 2 * plan.pp

    ahead, behind, twist = (jnp.asarray(t) for t in plan.pencil_tables())
    weights_ahead, twist_ahead = plan.line_tables(-1.0)
    weights_ahead, twist_ahead = jnp.asarray(weights_ahead[0]), jnp.asarray(twist_ahead)
    weights_behind, twist_behind = (jnp.asarray(t) for t in plan.line_tables(1.0))
    col, col_turned, row = hogel_tables()
    row = plan.row_table(row[0], row[1])
    col, col_turned, row, row_turned, same = (
        jnp.asarray(t) for t in (col, col_turned, row, row.T.copy(), plan.group_table())
    )
    steer_re, steer_im = steer_table(plan)

    slabs_shapes = (shape_of((X + VIEWS, lanes), BF16),) * C
    slabs_scratch = pltpu.VMEM((C, X + VIEWS, lanes), BF16)
    views_shape = shape_of((C, VIEWS, lanes), BF16)
    pencil_shape = shape_of((D, 2 * f, 128), BF16)
    lines_shape = shape_of((D, span, wide), BF16)
    columns_scratch = (
        pltpu.VMEM((D, f, 128), F32),
        pltpu.VMEM((D, f, 128), F32),
        pltpu.VMEM((D, f, 256), BF16),
    )
    pencil_tables = (steer_re, steer_im, ahead, behind, twist)
    columns_flops = 8 * D * f * 256 * 256 + 2 * plan.hogel_rows * span * (2 * WIN) ** 2

    apart_any = pl.BlockSpec(memory_space=pl.ANY)
    slabs = call(
        lambda *refs: pack_kernel(plan, *refs),
        slabs_shapes,
        (slm_field.astype(BF16), target_light),
        (slabs_scratch,),
    )
    tall = pltpu.VMEM((2 * X, C * lanes), BF16)
    pencils, goals = call(
        lambda *refs: rows_forward_kernel(plan, *refs),
        (pencil_shape, views_shape),
        (weights_ahead, twist_ahead, *swap_columns(slabs), steer_re, steer_im),
        (tall, slabs_scratch),
        flops=2 * X * 2 * X * C * lanes,
        in_specs={C + 2: apart_any, C + 3: apart_any},
    )
    (lines,) = call(
        lambda *refs: pencil_forward_kernel(plan, *refs),
        (lines_shape,),
        (exchange(pencils), *pencil_tables, row),
        (pltpu.VMEM((plan.hogel_rows, span, 2 * WIN), BF16), *columns_scratch),
        flops=columns_flops,
    )
    tall = pltpu.VMEM((2 * X, C * wide), BF16)
    lines, lights = call(
        lambda *refs: hogel_kernel(plan, *refs),
        (lines_shape, views_shape),
        (
            exchange(lines),
            goals,
            weights_behind,
            twist_behind,
            weights_ahead,
            twist_ahead,
            col,
            col_turned,
            same,
        ),
        (
            tall,
            pltpu.VMEM((2, plan.total_cols + STRIDE, wide), BF16),
            pltpu.VMEM((plan.hogel_cols, WIN, wide), F32),
            pltpu.VMEM((2 * plan.hogel_cols * VIEWS, plan.pp), F32),
            pltpu.VMEM((plan.hogel_cols * VIEWS, plan.pp), F32),
            pltpu.VMEM((2 * WIN, wide), BF16),
            pltpu.VMEM((plan.total_cols, wide), F32),
        ),
        flops=4 * X * 2 * X * C * wide + 4 * plan.hogel_cols * WIN * 2 * WIN * wide,
    )
    (pencils,) = call(
        lambda *refs: pencil_back_kernel(plan, *refs),
        (pencil_shape,),
        (exchange(lines), *pencil_tables, row_turned),
        (pltpu.VMEM((plan.hogel_rows, span, WIN), F32), *columns_scratch),
        flops=columns_flops,
    )
    tall = pltpu.VMEM((2 * X, C * lanes), BF16)
    slabs = call(
        lambda *refs: rows_inverse_kernel(plan, *refs),
        slabs_shapes,
        (exchange(pencils), lights, weights_behind, twist_behind),
        (tall, slabs_scratch),
        flops=2 * X * 2 * X * C * lanes,
    )
    return call(
        lambda *refs: unpack_kernel(plan, *refs),
        (shape_of(slm_field.shape, F32), shape_of(target_light.shape, F32)),
        swap_columns(slabs),
        (slabs_scratch,),
    )


def solution(mesh):
    return jax.shard_map(
        local,
        mesh=mesh,
        in_specs=(P(None, "rows", "cols"), P("rows", "cols", None)),
        out_specs=(P(None, "rows", "cols"), P("rows", "cols", None)),
        check_vma=False,
    )
```

```python
import math

import jax
import jax.numpy as jnp
import ml_dtypes
import numpy as np
from jax import lax
from jax.experimental import pallas as pl
from jax.experimental.pallas import tpu as pltpu
from jax.sharding import PartitionSpec as P

WIN = 256
VIEWS = 16
STRIDE = 128
BIN = 16

distance_px = 16000.0
index_ratio = 15.0

BF16 = jnp.bfloat16
F32 = jnp.float32
BOTH_MINOR = (((1,), (1,)), ((), ()))


def call(body, outs, args, scratch=(), flops=0, in_specs=None, out_specs=None):
    nbytes = sum(math.prod(a.shape) * a.dtype.itemsize for a in (*outs, *args))
    specs = {}
    if in_specs:
        whole = pl.BlockSpec(memory_space=pltpu.VMEM)
        specs["in_specs"] = [in_specs.get(n, whole) for n in range(len(args))]
    if out_specs:
        specs["out_specs"] = out_specs
    return pl.pallas_call(
        body,
        out_shape=outs,
        scratch_shapes=list(scratch),
        compiler_params=pltpu.CompilerParams(vmem_limit_bytes=24 * 2**20),
        cost_estimate=pl.CostEstimate(flops=flops, bytes_accessed=nbytes, transcendentals=0),
        **specs,
    )(*args)


def shape_of(dims, dtype):
    return jax.ShapeDtypeStruct(dims, dtype)


def high_low(table):
    table = np.asarray(table, np.float32)
    high = table.astype(ml_dtypes.bfloat16)
    low = (table - high.astype(np.float32)).astype(ml_dtypes.bfloat16)
    return np.concatenate([high, low], axis=0)


def times_i(values):
    half = values.shape[-1] // 2
    if values.shape[-1] == 128:
        lanes = lax.broadcasted_iota(jnp.int32, values.shape, values.ndim - 1)
        turned = pltpu.roll(values, half, values.ndim - 1)
        return jnp.where(lanes < half, -turned, turned)
    return jnp.concatenate([-values[..., half:], values[..., :half]], axis=-1)


def rounded_with_i(value):
    rounded = value.astype(BF16)
    half = value.shape[-1] // 2
    if half % 128:
        return rounded, times_i(value.astype(F32)).astype(BF16)
    return rounded, jnp.concatenate([-rounded[:, half:], rounded[:, :half]], axis=1)


def small_dft(points, sign):
    count = len(points)
    if count == 1:
        return points
    even = small_dft(points[0::2], sign)
    odd = small_dft(points[1::2], sign)
    front, back = [], []
    for k in range(count // 2):
        re, im = odd[k]
        angle = sign * 2.0 * math.pi * k / count
        cosine, sine = math.cos(angle), math.sin(angle)
        if k == 0:
            pass
        elif 4 * k == count:
            re, im = (-im, re) if sign > 0 else (im, -re)
        elif 8 * k == count:
            re, im = cosine * (re - sign * im), cosine * (im + sign * re)
        elif 8 * k == 3 * count:
            re, im = cosine * (re + sign * im), cosine * (im - sign * re)
        else:
            re, im = re * cosine - im * sine, re * sine + im * cosine
        even_re, even_im = even[k]
        front.append((even_re + re, even_im + im))
        back.append((even_re - re, even_im - im))
    return front + back


def packed_dft(points, sign):
    count = len(points)
    if count == 1:
        return points
    even = packed_dft(points[0::2], sign)
    odd = packed_dft(points[1::2], sign)
    front, back = [], []
    for k in range(count // 2):
        term = odd[k]
        angle = sign * 2.0 * math.pi * k / count
        if 4 * k == count:
            term = times_i(term) if sign > 0 else -times_i(term)
        elif k:
            term = math.cos(angle) * term + math.sin(angle) * times_i(term)
        front.append(even[k] + term)
        back.append(even[k] - term)
    return front + back


def turn(rows, cols, period, sign):
    angles = sign * 2.0 * np.pi / period * ((np.arange(rows)[:, None] * np.arange(cols)) % period)
    return np.cos(angles), np.sin(angles)


def block_diagonal(block, copies):
    return np.kron(np.eye(copies), block)


class Plan:
    def __init__(self, rows_count, cols_count, rows_dev, cols_dev):
        self.R, self.C = rows_count, cols_count
        self.D = rows_count * cols_count
        self.X = cols_dev
        self.m = rows_dev // cols_count
        self.lanes = 2 * self.m
        self.P = 128 // self.m
        self.span = cols_dev // rows_count
        self.f = self.span // self.P
        self.total_rows = rows_dev * rows_count
        self.total_cols = cols_dev * cols_count
        self.outer = 8
        self.inner = self.D // 8
        self.shift = STRIDE // self.m
        self.hogel_rows = self.total_rows // STRIDE
        self.hogel_cols = self.total_cols // STRIDE
        self.parts = self.D // self.hogel_rows
        self.pp = WIN // self.parts
        self.views = VIEWS // self.parts
        self.own_cols = cols_dev // STRIDE

    def place(self, s):
        return s % self.C * self.R + s // self.C

    def line_tables(self, sign):
        cosine, sine = turn(self.X, self.X, self.X, sign)
        weights = high_low(np.concatenate([cosine, sine], axis=1)).reshape(2, self.X, 2 * self.X)
        twist = turn(self.X, self.C, self.total_cols, sign)
        return weights, np.concatenate(twist, axis=1).astype(np.float32)

    def pencil_tables(self):
        cosine, sine = turn(self.m, self.m, self.m, -1.0)
        cosine, sine = block_diagonal(cosine, self.P), block_diagonal(sine, self.P)
        ahead = np.block([[cosine, sine], [-sine, cosine]])
        behind = np.block([[cosine, -sine], [sine, cosine]]) / (self.total_rows * self.total_cols)
        twist = turn(self.D, self.m, self.total_rows, -1.0)
        twist = np.stack([np.tile(part, (1, self.P)) for part in twist]).astype(np.float32)
        return high_low(ahead), high_low(behind), twist

    def row_table(self, real, imag):
        blocks = []
        for slab in range(WIN // self.m):
            rows = slice(slab * self.m, (slab + 1) * self.m)
            for left, right in ((real[rows], imag[rows]), (-imag[rows], real[rows])):
                pieces = []
                for part in range(self.parts):
                    cols = slice(part * self.pp, (part + 1) * self.pp)
                    pieces += [left[:, cols], right[:, cols]]
                blocks.append(np.concatenate(pieces, axis=1))
        return np.concatenate(blocks, axis=0)

    def group_table(self):
        return np.kron(np.eye(self.views), np.ones((BIN, BIN))).astype(np.float32)


def hogel_tables():
    positions = np.arange(WIN)
    tapers = np.sin(np.pi * (positions + 0.5) / WIN) ** 2
    angles = -2.0 * np.pi / WIN * (positions[:, None] * positions[None, :] % WIN)
    cosine = (tapers[:, None] * np.cos(angles)).astype(np.float32)
    sine = (tapers[:, None] * np.sin(angles)).astype(np.float32)
    col = np.concatenate([cosine, sine], axis=1).astype(ml_dtypes.bfloat16)
    col_turned = np.concatenate([cosine.T, sine.T], axis=1).astype(ml_dtypes.bfloat16)
    row = np.stack([cosine / WIN, sine / WIN]).astype(ml_dtypes.bfloat16)
    return col, col_turned, row


def three_pieces(values):
    first = values.astype(BF16)
    rest = values - first.astype(F32)
    second = rest.astype(BF16)
    return first, second, (rest - second.astype(F32)).astype(BF16)


def matmul(left, right):
    return jnp.dot(left, right, preferred_element_type=F32)


def partners(count):
    return sorted(range(count), key=lambda t: (t != 0, -t.bit_count()))


def gather_chunks(arrived, chunks):
    mine = lax.axis_index("cols")
    for t, chunk in zip(partners(len(arrived)), arrived):
        chunks[mine ^ t] = chunk[...]


def scatter_chunks(chunks, leaving):
    mine = lax.axis_index("cols")
    for t, chunk in zip(partners(len(leaving)), leaving):
        chunk[...] = chunks[mine ^ t]


def put_views(plan, rows):
    pad = jnp.zeros((VIEWS - 3 * plan.own_cols, plan.lanes), F32)
    pieces = [piece.astype(F32) for piece in three_pieces(rows)]
    return jnp.concatenate([*pieces, pad], axis=0).astype(BF16)


def get_views(plan, chunk):
    chunk = chunk.astype(F32)
    n = plan.own_cols
    return chunk[:n] + chunk[n : 2 * n] + chunk[2 * n : 3 * n]


def pack_kernel(plan, field, goal, *refs):
    C, m, X = plan.C, plan.m, plan.X
    leaving, (out,) = refs[:C], refs[C:]
    for c in range(C):
        rows = slice(c * m, (c + 1) * m)
        block = jnp.concatenate([field[0, rows, :], field[1, rows, :]], axis=0)
        out[c, :X, :] = block.astype(F32).T.astype(BF16)
        i, start = c // plan.parts, c % plan.parts * plan.lanes
        out[c, X:, :] = put_views(plan, goal[i, :, start : start + plan.lanes])
    scatter_chunks(out, leaving)


def unpack_kernel(plan, *refs):
    C, m, X = plan.C, plan.m, plan.X
    arrived, (out, light, slabs) = refs[:C], refs[C:]
    gather_chunks(arrived, slabs)
    for c in range(C):
        block = slabs[c, :X, :].astype(F32).T
        out[0, m * c : m * c + m, :] = block[:m]
        out[1, m * c : m * c + m, :] = block[m:]
        i, start = c // plan.parts, c % plan.parts * plan.lanes
        light[i, :, start : start + plan.lanes] = get_views(plan, slabs[c, X:, :])


def lines_forward(plan, lanes, load, emit, weights, twist, turned):
    C, X = plan.C, plan.X
    step = 64
    for start in range(0, X, step):
        points = packed_dft([load(c, start, step) for c in range(C)], -1.0)
        for k in range(C):
            cosine = twist[start : start + step, k : k + 1]
            sine = twist[start : start + step, C + k : C + k + 1]
            value = points[k]
            if lanes % 256:
                across = times_i(value)
                if k:
                    value, across = value * cosine + across * sine, across * cosine - value * sine
                value, across = value.astype(BF16), across.astype(BF16)
            else:
                if k:
                    value = value * cosine + times_i(value) * sine
                value, across = rounded_with_i(value)
            place = slice(k * lanes, k * lanes + lanes)
            turned[start : start + step, place] = value
            turned[X + start : X + start + step, place] = across
    group = max(1, 256 // lanes)
    for first in range(0, C, group):
        result = matmul(weights[...], turned[:, first * lanes : (first + group) * lanes])
        for k in range(group):
            for r in range(plan.R):
                rows = slice(r * plan.span, (r + 1) * plan.span)
                emit((first + k) * plan.R + r, result[rows, k * lanes : (k + 1) * lanes])


def lines_inverse(plan, lanes, product, emit, twist):
    C, X = plan.C, plan.X
    step = 64
    for start in range(0, X, step):
        rows = slice(start, start + step)
        result = product(rows)
        points = []
        for k in range(C):
            value = result[:, k * lanes : (k + 1) * lanes]
            if k:
                cosine, sine = twist[rows, k : k + 1], twist[rows, C + k : C + k + 1]
                value = value * cosine + times_i(value) * sine
            points.append(value)
        for c, value in enumerate(packed_dft(points, 1.0)):
            emit(c, start, step, value)


def to_planes(plan, block):
    parts = [block[p * plan.f : (p + 1) * plan.f, :] for p in range(plan.P)]
    real = jnp.concatenate([part[:, : plan.m] for part in parts], axis=1)
    imag = jnp.concatenate([part[:, plan.m :] for part in parts], axis=1)
    return real, imag


def from_planes(plan, real, imag):
    m = plan.m
    return jnp.concatenate(
        [
            jnp.concatenate([real[:, p * m : (p + 1) * m], imag[:, p * m : (p + 1) * m]], axis=1)
            for p in range(plan.P)
        ],
        axis=0,
    )


def rows_forward_kernel(plan, weights, twist, *refs):
    C, X = plan.C, plan.X
    arrived, (_, _, out, goals, turned, slabs) = refs[:C], refs[C:]
    gather_chunks(arrived, slabs)
    goals[...] = slabs[:, X:, :]

    def load(c, start, step):
        return slabs[c, start : start + step, :].astype(F32)

    def emit(d, block):
        out[d] = jnp.concatenate(to_planes(plan, block), axis=0).astype(BF16)

    lines_forward(plan, plan.lanes, load, emit, weights, twist, turned)


def rows_inverse_kernel(plan, pencils, lights, weights, twist, *refs):
    C, X, lanes = plan.C, plan.X, plan.lanes
    leaving, (packed, out) = refs[:C], refs[C:]
    for k in range(C):
        for r in range(plan.R):
            chunk = pencils[k * plan.R + r].astype(F32)
            block = from_planes(plan, chunk[: plan.f], chunk[plan.f :])
            place = slice(k * lanes, k * lanes + lanes)
            packed[r * plan.span : (r + 1) * plan.span, place] = block.astype(BF16)
            packed[X + r * plan.span : X + (r + 1) * plan.span, place] = times_i(block).astype(BF16)

    def emit(c, start, step, value):
        out[c, start : start + step, :] = value.astype(BF16)

    def product(rows):
        return matmul(weights[0, rows, :], packed[...]) + matmul(weights[1, rows, :], packed[...])

    lines_inverse(plan, lanes, product, emit, twist)
    out[:, X:, :] = lights[...]
    scatter_chunks(out, leaving)


def columns(plan, sign, load, store, steer_re, steer_im, ahead, behind, twist, scratch):
    D, f, outer, inner = plan.D, plan.f, plan.outer, plan.inner
    half_re, half_im, rounded = scratch
    for b in range(inner):
        points = [load(inner * a + b) for a in range(outer)]
        for alpha, (re, im) in enumerate(small_dft(points, -1.0)):
            angle = -2.0 * math.pi * b * alpha / D
            cosine, sine = math.cos(angle), math.sin(angle)
            if b * alpha:
                re, im = re * cosine - im * sine, re * sine + im * cosine
            half_re[alpha * inner + b] = re
            half_im[alpha * inner + b] = im
    for alpha in range(outer):
        points = [(half_re[alpha * inner + b], half_im[alpha * inner + b]) for b in range(inner)]
        for beta, (re, im) in enumerate(small_dft(points, -1.0)):
            k = alpha + outer * beta
            cosine, sine = twist[0, k : k + 1, :], twist[1, k : k + 1, :]
            for offset, part in ((0, re * cosine - im * sine), (128, re * sine + im * cosine)):
                rounded[k, :, offset : offset + 128] = part.astype(BF16)
    group = D // 4 if sign > 0 else D
    for start in range(0, D, group):
        place = slice(start, start + group)

        def multiply(matrix):
            left = rounded[place].reshape(group * f, 256)
            product = matmul(left, matrix[:256, :])
            return product.reshape(group, f, 256)

        result = multiply(ahead)
        re, im = result[:, :, :128], result[:, :, 128:]
        factor_re, factor_im = steer_re[place], sign * steer_im[place]
        for offset, part in (
            (0, re * factor_re - im * factor_im),
            (128, re * factor_im + im * factor_re),
        ):
            rounded[place, :, offset : offset + 128] = part.astype(BF16)
        result = multiply(behind)
        half_re[place] = result[:, :, :128]
        half_im[place] = result[:, :, 128:]
    for alpha in range(outer):
        points = []
        for beta in range(inner):
            k = alpha + outer * beta
            cosine, sine = twist[0, k : k + 1, :], twist[1, k : k + 1, :]
            re, im = half_re[k], half_im[k]
            points.append((re * cosine + im * sine, im * cosine - re * sine))
        for b, (re, im) in enumerate(small_dft(points, 1.0)):
            angle = 2.0 * math.pi * b * alpha / D
            cosine, sine = math.cos(angle), math.sin(angle)
            if b * alpha:
                re, im = re * cosine - im * sine, re * sine + im * cosine
            half_re[alpha + outer * b] = re
            half_im[alpha + outer * b] = im
    for b in range(inner):
        points = [(half_re[alpha + outer * b], half_im[alpha + outer * b]) for alpha in range(outer)]
        for a, (re, im) in enumerate(small_dft(points, 1.0)):
            store(inner * a + b, re, im)


def pencil_forward_kernel(plan, pencils, *refs):
    steer_re, steer_im, ahead, behind, twist, row, out, windows, *scratch = refs
    f, lanes, span = plan.f, plan.lanes, plan.span

    def load(s):
        chunk = pencils[plan.place(s)].astype(F32)
        return chunk[:f], chunk[f:]

    def store(s, re, im):
        block = from_planes(plan, re, im).astype(BF16)
        i, slab = s // plan.shift, s % plan.shift
        windows[i, :, slab * lanes : (slab + 1) * lanes] = block
        slab += plan.shift
        windows[(i - 1) % plan.hogel_rows, :, slab * lanes : (slab + 1) * lanes] = block

    columns(plan, 1.0, load, store, steer_re, steer_im, ahead, behind, twist, scratch)
    count = plan.hogel_rows
    result = matmul(windows[...].reshape(count * span, 2 * WIN), row[...]).astype(BF16)
    for i in range(count):
        for part in range(plan.parts):
            out[plan.place(i * plan.parts + part)] = result[
                i * span : (i + 1) * span, part * 2 * plan.pp : (part + 1) * 2 * plan.pp
            ]


def pencil_back_kernel(plan, lines, *refs):
    steer_re, steer_im, ahead, behind, twist, row, out, windows, *scratch = refs
    lanes, span, parts = plan.lanes, plan.span, plan.parts
    count, wide = plan.hogel_rows, 2 * plan.pp
    result = 0.0
    for n in range(parts):
        own = jnp.stack([lines[plan.place(i * parts + n)] for i in range(count)])
        before = jnp.concatenate([own[-1:], own[:-1]], axis=0)
        depth = slice(n * wide, (n + 1) * wide)
        result = result + matmul(own.reshape(count * span, wide), row[depth, :WIN])
        result = result + matmul(before.reshape(count * span, wide), row[depth, WIN:])
    windows[...] = result.reshape(count, span, WIN)

    def load(s):
        i, slab = s // plan.shift, s % plan.shift
        return to_planes(plan, windows[i, :, slab * lanes : (slab + 1) * lanes])

    def store(s, re, im):
        out[plan.place(s)] = jnp.concatenate([re, im], axis=0).astype(BF16)

    columns(plan, -1.0, load, store, steer_re, steer_im, ahead, behind, twist, scratch)


def hogel_kernel(plan, lines, goals, *refs):
    weights_behind, twist_behind, weights_ahead, twist_ahead, col, col_turned, same = refs[:7]
    out, lights, packed, field, spectra, bright, factors, weighted, back = refs[7:]
    C, X, lanes, pp = plan.C, plan.X, 2 * plan.pp, plan.pp
    total = plan.total_cols
    for k in range(C):
        block = lines[k * plan.R : (k + 1) * plan.R].reshape(X, lanes)
        place = slice(k * lanes, (k + 1) * lanes)
        packed[:X, place], packed[X:, place] = rounded_with_i(block)

    def emit_near(c, start, step, value):
        for n, rounded in enumerate(rounded_with_i(value)):
            field[n, c * X + start : c * X + start + step, :] = rounded
            if c == 0 and start < STRIDE:
                field[n, total + start : total + start + step, :] = rounded

    near = matmul(weights_behind[0], packed[...])
    lines_inverse(plan, lanes, lambda rows: near[rows, :], emit_near, twist_behind)
    for j in range(plan.hogel_cols):
        window = slice(STRIDE * j, STRIDE * j + WIN)
        result = matmul(
            col_turned[...], jnp.concatenate([field[0, window, :], field[1, window, :]], axis=0)
        )
        spectra[j] = result
        power = result[:, :pp] * result[:, :pp] + result[:, pp:] * result[:, pp:]
        bright[j * VIEWS : (j + 1) * VIEWS, :] = power.reshape(VIEWS, BIN, pp).sum(axis=1)
    exact = lax.Precision.HIGHEST
    own = lax.broadcasted_iota(jnp.int32, (VIEWS, pp), 0) == (
        lax.broadcasted_iota(jnp.int32, (VIEWS, pp), 1) % VIEWS
    )
    for c in range(C):
        target = get_views(plan, goals[c])
        for j in range(plan.own_cols):
            h = c * plan.own_cols + j
            below = (plan.hogel_cols + h) * VIEWS
            bright[below : below + VIEWS, :] = jnp.where(own, target[j : j + 1, :], 0.0)
    spread = jnp.dot(bright[...], same[...], preferred_element_type=F32, precision=exact)
    views = plan.hogel_cols * VIEWS
    light = spread[:views] * (1.0 / (BIN * BIN))
    factors[...] = 4.0 * (light - spread[views:])
    bright[:views, :] = light
    for c in range(C):
        rows = []
        for j in range(plan.own_cols):
            h = c * plan.own_cols + j
            block = jnp.where(own, bright[h * VIEWS : (h + 1) * VIEWS, :], 0.0)
            rows.append(jnp.sum(block, axis=0, keepdims=True))
        lights[c] = put_views(plan, jnp.concatenate(rows, axis=0))
    for j in range(plan.hogel_cols):
        for view in range(VIEWS):
            factor = factors[j * VIEWS + view : j * VIEWS + view + 1, :]
            block = slice(view * BIN, (view + 1) * BIN)
            below = slice(WIN + view * BIN, WIN + (view + 1) * BIN)
            real = (spectra[j, block, :pp] * factor).astype(BF16)
            imag = (spectra[j, block, pp:] * factor).astype(BF16)
            weighted[block, :pp] = real
            weighted[block, pp:] = imag
            weighted[below, :pp] = imag
            weighted[below, pp:] = -real
        result = matmul(col[...], weighted[...])
        first = slice(STRIDE * j, STRIDE * (j + 1))
        back[first] = result[:STRIDE] if j == 0 else pending + result[:STRIDE]
        pending = result[STRIDE:]
    back[:STRIDE] = back[:STRIDE] + pending

    def load(c, start, step):
        return back[c * X + start : c * X + start + step, :]

    def emit(d, block):
        out[d] = block.astype(BF16)

    lines_forward(plan, lanes, load, emit, weights_ahead, twist_ahead, packed)


def steer_table(plan):
    index = lax.axis_index(("cols", "rows"))
    shape = (plan.D, plan.f, 128)
    k = lax.broadcasted_iota(jnp.int32, shape, 0)
    line = lax.broadcasted_iota(jnp.int32, shape, 1)
    lane = lax.broadcasted_iota(jnp.int32, shape, 2)
    u = k + plan.D * (lane % plan.m)
    v = index // plan.R + plan.C * (
        plan.span * (index % plan.R) + plan.f * (lane // plan.m) + line
    )

    def freq(position, count):
        return ((position + count // 2) % count - count // 2).astype(F32) / count

    freq_rows, freq_cols = freq(u, plan.total_rows), freq(v, plan.total_cols)
    radial = freq_rows * freq_rows + freq_cols * freq_cols
    phase = (
        -2.0
        * math.pi
        * distance_px
        * radial
        / (jnp.sqrt(index_ratio * index_ratio - radial) + index_ratio)
    )
    return jnp.cos(phase), jnp.sin(phase)


def exchange(chunks):
    return lax.all_to_all(chunks, ("cols", "rows"), split_axis=0, concat_axis=0, tiled=True)


def swap_columns(chunks):
    count = lax.axis_size("cols")
    return tuple(
        lax.ppermute(chunk, "cols", [(i, i ^ t) for i in range(count)]) if t else chunk
        for t, chunk in zip(partners(count), chunks)
    )


def local(slm_field, target_light):
    rows_count, cols_count = lax.axis_size("rows"), lax.axis_size("cols")
    plan = Plan(rows_count, cols_count, slm_field.shape[1], slm_field.shape[2])
    C, D, X, lanes, f = plan.C, plan.D, plan.X, plan.lanes, plan.f
    span, wide = plan.span, 2 * plan.pp

    ahead, behind, twist = (jnp.asarray(t) for t in plan.pencil_tables())
    weights_ahead, twist_ahead = plan.line_tables(-1.0)
    weights_ahead, twist_ahead = jnp.asarray(weights_ahead[0]), jnp.asarray(twist_ahead)
    weights_behind, twist_behind = (jnp.asarray(t) for t in plan.line_tables(1.0))
    col, col_turned, row = hogel_tables()
    row = plan.row_table(row[0], row[1])
    col, col_turned, row, row_turned, same = (
        jnp.asarray(t) for t in (col, col_turned, row, row.T.copy(), plan.group_table())
    )
    steer_re, steer_im = steer_table(plan)

    slabs_shapes = (shape_of((X + VIEWS, lanes), BF16),) * C
    slabs_scratch = pltpu.VMEM((C, X + VIEWS, lanes), BF16)
    views_shape = shape_of((C, VIEWS, lanes), BF16)
    pencil_shape = shape_of((D, 2 * f, 128), BF16)
    lines_shape = shape_of((D, span, wide), BF16)
    columns_scratch = (
        pltpu.VMEM((D, f, 128), F32),
        pltpu.VMEM((D, f, 128), F32),
        pltpu.VMEM((D, f, 256), BF16),
    )
    pencil_tables = (steer_re, steer_im, ahead, behind, twist)
    columns_flops = 8 * D * f * 256 * 256 + 2 * plan.hogel_rows * span * (2 * WIN) ** 2

    apart_any = pl.BlockSpec(memory_space=pl.ANY)
    slabs = call(
        lambda *refs: pack_kernel(plan, *refs),
        slabs_shapes,
        (slm_field.astype(BF16), target_light),
        (slabs_scratch,),
    )
    tall = pltpu.VMEM((2 * X, C * lanes), BF16)
    pencils, goals = call(
        lambda *refs: rows_forward_kernel(plan, *refs),
        (pencil_shape, views_shape),
        (weights_ahead, twist_ahead, *swap_columns(slabs), steer_re, steer_im),
        (tall, slabs_scratch),
        flops=2 * X * 2 * X * C * lanes,
        in_specs={C + 2: apart_any, C + 3: apart_any},
    )
    (lines,) = call(
        lambda *refs: pencil_forward_kernel(plan, *refs),
        (lines_shape,),
        (exchange(pencils), *pencil_tables, row),
        (pltpu.VMEM((plan.hogel_rows, span, 2 * WIN), BF16), *columns_scratch),
        flops=columns_flops,
    )
    tall = pltpu.VMEM((2 * X, C * wide), BF16)
    lines, lights = call(
        lambda *refs: hogel_kernel(plan, *refs),
        (lines_shape, views_shape),
        (
            exchange(lines),
            goals,
            weights_behind,
            twist_behind,
            weights_ahead,
            twist_ahead,
            col,
            col_turned,
            same,
        ),
        (
            tall,
            pltpu.VMEM((2, plan.total_cols + STRIDE, wide), BF16),
            pltpu.VMEM((plan.hogel_cols, WIN, wide), F32),
            pltpu.VMEM((2 * plan.hogel_cols * VIEWS, plan.pp), F32),
            pltpu.VMEM((plan.hogel_cols * VIEWS, plan.pp), F32),
            pltpu.VMEM((2 * WIN, wide), BF16),
            pltpu.VMEM((plan.total_cols, wide), F32),
        ),
        flops=4 * X * 2 * X * C * wide + 4 * plan.hogel_cols * WIN * 2 * WIN * wide,
    )
    (pencils,) = call(
        lambda *refs: pencil_back_kernel(plan, *refs),
        (pencil_shape,),
        (exchange(lines), *pencil_tables, row_turned),
        (pltpu.VMEM((plan.hogel_rows, span, WIN), F32), *columns_scratch),
        flops=columns_flops,
    )
    tall = pltpu.VMEM((2 * X, C * lanes), BF16)
    slabs = call(
        lambda *refs: rows_inverse_kernel(plan, *refs),
        slabs_shapes,
        (exchange(pencils), lights, weights_behind, twist_behind),
        (tall, slabs_scratch),
        flops=2 * X * 2 * X * C * lanes,
    )
    return call(
        lambda *refs: unpack_kernel(plan, *refs),
        (shape_of(slm_field.shape, F32), shape_of(target_light.shape, F32)),
        swap_columns(slabs),
        (slabs_scratch,),
    )


def solution(mesh):
    return jax.shard_map(
        local,
        mesh=mesh,
        in_specs=(P(None, "rows", "cols"), P("rows", "cols", None)),
        out_specs=(P(None, "rows", "cols"), P("rows", "cols", None)),
        check_vma=False,
    )
```
